32 devices in a mesh: fsdp: 32 (over z, y, x, core).
Axes of the slice: x: 2, y: 2, z: 4, core: 2. Of those that a mesh axis runs over, the one named last changes fastest.
Arguments:
- inputs: bfloat16 [2, 32, 512, 1024], P(None, 'fsdp'), may hold values from -6 to 6
- timesteps: int32 [2, 32], P(None, 'fsdp'), may hold values from 0 to 4999
- segments: int32 [2, 32, 512], P(None, 'fsdp'), may hold values from 0 to 31, never falling along the last dimension, each value on 1 to 256 neighbouring positions
- cotangent: bfloat16 [2, 32, 512, 1024], P(None, 'fsdp'), may hold values from -6 to 6
- query_weight: bfloat16 [1024, 1024], P('fsdp'), may hold values from -0.1875 to 0.1875
- key_weight: bfloat16 [1024, 1024], P('fsdp'), may hold values from -0.1875 to 0.1875
- value_weight: bfloat16 [1024, 1024], P('fsdp'), may hold values from -0.1875 to 0.1875
- output_weight: bfloat16 [1024, 1024], P('fsdp'), may hold values from -0.75 to 0.75
- inner_weight: bfloat16 [1024, 4096], P('fsdp'), may hold values from -0.1875 to 0.1875
- outer_weight: bfloat16 [4096, 1024], P('fsdp'), may hold values from -0.09375 to 0.09375
- time_weight: bfloat16 [1024, 1024], P('fsdp'), may hold values from -0.1875 to 0.1875
- query_bias: bfloat16 [1024], P('fsdp'), may hold values from -3 to 3
- value_bias: bfloat16 [1024], P('fsdp'), may hold values from -3 to 3
- output_bias: bfloat16 [1024], P('fsdp'), may hold values from -3 to 3
- inner_bias: bfloat16 [4096], P('fsdp'), may hold values from -3 to 3
- outer_bias: bfloat16 [1024], P('fsdp'), may hold values from -3 to 3
- first_gain: bfloat16 [1024], P('fsdp'), may hold values from 0.5 to 1.5
- first_shift: bfloat16 [1024], P('fsdp'), may hold values from -2 to 2
- second_gain: bfloat16 [1024], P('fsdp'), may hold values from 0.5 to 1.5
- second_shift: bfloat16 [1024], P('fsdp'), may hold values from -2 to 2
Outputs:
- layer_output: bfloat16 [2, 32, 512, 1024], P(None, 'fsdp')
- input_grad: float32 [2, 32, 512, 1024], P(None, 'fsdp')
- query_weight_grad: float32 [1024, 1024], P('fsdp')
- key_weight_grad: float32 [1024, 1024], P('fsdp')
- value_weight_grad: float32 [1024, 1024], P('fsdp')
- output_weight_grad: float32 [1024, 1024], P('fsdp')
- inner_weight_grad: float32 [1024, 4096], P('fsdp')
- outer_weight_grad: float32 [4096, 1024], P('fsdp')
- time_weight_grad: float32 [1024, 1024], P('fsdp')
- query_bias_grad: float32 [1024], P('fsdp')
- value_bias_grad: float32 [1024], P('fsdp')
- output_bias_grad: float32 [1024], P('fsdp')
- inner_bias_grad: float32 [4096], P('fsdp')
- outer_bias_grad: float32 [1024], P('fsdp')
- first_gain_grad: float32 [1024], P('fsdp')
- first_shift_grad: float32 [1024], P('fsdp')
- second_gain_grad: float32 [1024], P('fsdp')
- second_shift_grad: float32 [1024], P('fsdp')
The draws below stay inside these ranges and needn't reach their ends.
Inputs may be any that keep to these rules, and one draw needn't show every extreme that they name: `segments`: within a row the segment numbers never fall; each document holds 1 to 256 positions, and in every row one document holds exactly 256.
All inputs are finite; a program needn't handle non-finite values.
Results may differ from the reference program's by a relative error of at most 0.022.
Values may be sent and summed in bfloat16 or wider, within the bound.
No kernel may reach another device: no remote copies, remote signals or barrier semaphores. Data moves between devices by JAX's collectives and lax.ppermute only.
A program may use at most 256 MiB of HBM per device.

```python
import math
import jax
import jax.numpy as jnp
import numpy as np
from jax import lax

D = 1024
H = 16
FF = 4096
HD = 64
TSTEPS = 5000
ROW_LEN = 512
MB = 2
ROWS = 32


def place_ends(values, key, smallest, high):
    longest = values.shape.index(max(values.shape))
    spots = []
    for shift in (0, 1):
        where = [jax.random.randint(jax.random.fold_in(key, axis), (), 0, length) for axis, length in enumerate(values.shape)]
        where[longest] = (where[longest] + shift) % values.shape[longest]
        spots.append(tuple(where))
    return values.at[spots[0]].set(smallest).at[spots[1]].set(high)


def with_spikes(array, rng, source, target, shards_of, factor):
    owner, partner = [(jnp.arange(array.shape[axis_at]) // (array.shape[axis_at] // shards_of)).reshape([-1 if axis == axis_at else 1 for axis in range(array.ndim)]) for axis_at in (source, target)]
    chosen = jax.random.permutation(rng, shards_of)[partner]
    strong = (owner == chosen) | (owner == (partner + shards_of // 2) % shards_of)
    return jnp.where(strong, factor * array, array)


def block_levels(stream_key, extent, pieces, smallest, top_value):
    loudness, own = 1.0, jax.random.fold_in(stream_key, 6)
    for dim, blocks in pieces:
        draws = jnp.exp(jax.random.uniform(jax.random.fold_in(own, dim), (blocks,), jnp.float32, smallest / len(pieces), top_value / len(pieces)))
        loudness = loudness * jnp.repeat(draws, extent[dim] // blocks).reshape([-1 if axis == dim else 1 for axis in range(len(extent))])
    return loudness


def split_up(count, total, reach, slope):
    loads = [(1 << 20) // math.isqrt(rank ** slope) + 1 for rank in range(2, count + 1)]
    spare, holding = total - reach - (count - 1), [1] * (count - 1)
    while spare > 0:
        free = [i for i in range(count - 1) if holding[i] < reach]
        whole, remaining = sum([loads[i] for i in free]), spare
        for i in free:
            extra = min(reach - holding[i], max(1, remaining * loads[i] // whole), spare)
            holding[i] = holding[i] + extra
            spare = spare - extra
    return np.array([reach] + holding)


def uneven(rng, count, total, reach, skew):
    if count == 2:
        one = jax.random.randint(rng, (), max(1, total - reach), min(reach, total - 1) + 1)
        return jnp.stack([one, total - one])
    lengths = jnp.asarray(split_up(count, total, reach, skew), jnp.int32)
    couples = (count - 1) // 2
    source_of, receiver = lengths[1:1 + 2 * couples:2], lengths[2:2 + 2 * couples:2]
    room = jnp.minimum(source_of - 1, reach - receiver)
    shifted = jax.random.randint(jax.random.fold_in(rng, 1), (couples,), 0, 1 << 20) % (room + 1)
    lengths = lengths.at[1:1 + 2 * couples:2].set(source_of - shifted).at[2:2 + 2 * couples:2].set(receiver + shifted)
    return lengths[jax.random.permutation(jax.random.fold_in(rng, 2), count)]


def gaussian(stream_key, extent, scale, reach, pieces=(), kind=jnp.bfloat16):
    array = scale * jax.random.normal(stream_key, extent, jnp.float32)
    if pieces:
        array = array * block_levels(stream_key, extent, pieces, -0.22, 0.18)
    return jnp.clip(array, -reach, reach).astype(kind)


def heavy_noise(rng, extent, scale, reach, pieces, heavy, kind=jnp.bfloat16):
    result = scale * jax.random.normal(rng, extent, jnp.float32)
    if pieces:
        result = result * block_levels(rng, extent, pieces, -0.22, 0.18)
    return jnp.clip(with_spikes(result, jax.random.fold_in(rng, 3), *heavy), -reach, reach).astype(kind)


def setup_inputs(seed: int = 0) -> dict:
    splits = jax.random.split(jax.random.key(seed), 21)
    return {
        "inputs": heavy_noise(splits[0], (MB, ROWS, ROW_LEN, D), 1.0, 6.0, ((1, 32),), (1, 3, 32, 2.75)),
        "timesteps": place_ends(jax.random.randint(splits[1], (MB, ROWS), 0, TSTEPS), jax.random.fold_in(splits[1], 1), 0, TSTEPS - 1).astype(jnp.int32),
        "segments": jax.vmap(lambda own: jnp.searchsorted(jnp.cumsum(uneven(own, ROW_LEN // 16, ROW_LEN, ROW_LEN // 2, 2)), jnp.arange(ROW_LEN), side="right"))(jax.random.split(splits[2], MB * ROWS)).reshape((MB, ROWS, ROW_LEN)).astype(jnp.int32),
        "cotangent": gaussian(splits[3], (MB, ROWS, ROW_LEN, D), 1.0, 6.0, ((1, 32),)),
        "query_weight": gaussian(splits[4], (D, D), D ** -0.5, 0.1875, ((0, 32),)),
        "key_weight": gaussian(splits[5], (D, D), D ** -0.5, 0.1875, ((0, 32),)),
        "value_weight": gaussian(splits[6], (D, D), D ** -0.5, 0.1875, ((0, 32),)),
        "output_weight": gaussian(splits[7], (D, D), (D // 16) ** -0.5, 0.75, ((0, 32),)),
        "inner_weight": gaussian(splits[8], (D, FF), D ** -0.5, 0.1875, ((0, 32),)),
        "outer_weight": gaussian(splits[9], (FF, D), FF ** -0.5, 0.09375, ((0, 32),)),
        "time_weight": gaussian(splits[10], (D, D), D ** -0.5, 0.1875, ((0, 32),)),
        "query_bias": gaussian(splits[11], (D,), 0.5, 3.0, ((0, 32),)),
        "value_bias": gaussian(splits[12], (D,), 0.5, 3.0, ((0, 32),)),
        "output_bias": gaussian(splits[13], (D,), 0.5, 3.0, ((0, 32),)),
        "inner_bias": gaussian(splits[14], (FF,), 0.5, 3.0, ((0, 32),)),
        "outer_bias": gaussian(splits[15], (D,), 0.5, 3.0, ((0, 32),)),
        "first_gain": jnp.clip(1.0 + 0.1 * jax.random.normal(splits[16], (D,), jnp.float32), 0.5, 1.5).astype(jnp.bfloat16),
        "first_shift": gaussian(splits[17], (D,), 0.3, 2.0, ((0, 32),)),
        "second_gain": jnp.clip(1.0 + 0.1 * jax.random.normal(splits[18], (D,), jnp.float32), 0.5, 1.5).astype(jnp.bfloat16),
        "second_shift": gaussian(splits[19], (D,), 0.3, 2.0, ((0, 32),)),
    }


@jax.custom_vjp
def low(v):
    return lax.optimization_barrier(v.astype(jnp.bfloat16)).astype(jnp.float32)

@jax.custom_vjp
def low_back(v):
    return v

def low_keep(v):
    return (low(v), None)

def low_pass(kept, grad):
    return (grad,)

def back_keep(v):
    return (v, None)

def back_low(kept, grad):
    return (low(grad),)
low.defvjp(low_keep, low_pass)
low_back.defvjp(back_keep, back_low)

def product(operand, factor):
    return jnp.dot(operand, factor, precision=lax.Precision.HIGHEST)

def features(step_ids):
    half_width = D // 2
    freqs = jnp.exp(-math.log(10000.0) * jnp.arange(half_width, dtype=jnp.float32) / half_width)
    angles = step_ids.astype(jnp.float32)[..., None] * freqs
    return jnp.concatenate([jnp.sin(angles), jnp.cos(angles)], axis=-1)

def layer_norm(values_in, gain, shift):
    center = values_in - lax.optimization_barrier(jnp.mean(values_in, axis=-1, keepdims=True))
    spread = lax.optimization_barrier(jnp.mean(center * center, axis=-1, keepdims=True))
    return center * lax.rsqrt(spread + 1e-05) * gain + shift

def attend(queries, key_rows, values, segment_ids):
    row_length = queries.shape[0]
    query_heads = queries.reshape(row_length, H, HD)
    key_heads = key_rows.reshape(row_length, H, HD)
    value_heads = values.reshape(row_length, H, HD)
    scores = jnp.einsum('qhd,khd->hqk', query_heads, key_heads, precision=lax.Precision.HIGHEST) * (1.0 / math.sqrt(HD))
    scores = low_back(scores)
    same_doc = segment_ids[:, None] == segment_ids[None, :]
    scores = jnp.where(same_doc[None], scores, -1e+30)
    soft_low = low(jax.nn.softmax(scores, axis=-1))
    context = jnp.einsum('hqk,khd->qhd', soft_low, value_heads, precision=lax.Precision.HIGHEST)
    return low(low_back(context.reshape(row_length, D)))
checked_attend = jax.checkpoint(attend)

def layer(params, inputs, feats, segment_ids):
    query_weight, key_weight, value_weight, output_weight, inner_weight, outer_weight, time_weight, query_bias, value_bias, output_bias, inner_bias, outer_bias, first_gain, first_shift, second_gain, second_shift = params
    temb = product(low(feats), time_weight)
    stream = inputs + temb[:, None, :]
    stream_low = low(stream)
    queries = low(low_back(product(stream_low, query_weight) + query_bias))
    key_rows = low(low_back(product(stream_low, key_weight)))
    values = low(low_back(product(stream_low, value_weight) + value_bias))
    context = lax.map(lambda member: checked_attend(*member), (queries, key_rows, values, segment_ids))
    branch = low_back(product(context, output_weight) + output_bias)
    first = layer_norm(stream + branch, first_gain, first_shift)
    inner_pre = low_back(product(low(first), inner_weight) + inner_bias)
    active_low = low(jax.nn.gelu(inner_pre, approximate=False))
    outer = low_back(product(active_low, outer_weight) + outer_bias)
    return layer_norm(first + outer, second_gain, second_shift)

def reference(inputs, timesteps, segments, cotangent, query_weight, key_weight, value_weight, output_weight, inner_weight, outer_weight, time_weight, query_bias, value_bias, output_bias, inner_bias, outer_bias, first_gain, first_shift, second_gain, second_shift):
    params = tuple((weight_arg.astype(jnp.float32) for weight_arg in (query_weight, key_weight, value_weight, output_weight, inner_weight, outer_weight, time_weight, query_bias, value_bias, output_bias, inner_bias, outer_bias, first_gain, first_shift, second_gain, second_shift)))
    group_rows = math.gcd(max(1, 4096 // ROW_LEN), MB * ROWS)
    block_count = MB * ROWS // group_rows
    blocks = (inputs.astype(jnp.float32).reshape(block_count, group_rows, ROW_LEN, D), features(timesteps).reshape(block_count, group_rows, D), segments.reshape(block_count, group_rows, ROW_LEN), cotangent.astype(jnp.float32).reshape(block_count, group_rows, ROW_LEN, D))

    def step_block(totals, block):
        block_inputs, block_feats, block_segments, block_cotangent = block

        def local_layer(weights_now, rows_now):
            return layer(weights_now, rows_now, block_feats, block_segments)
        result_rows, pullback = jax.vjp(local_layer, params, block_inputs)
        param_grads, row_grads = pullback(block_cotangent)
        totals = jax.tree.map(jnp.add, totals, param_grads)
        return (totals, (result_rows.astype(jnp.bfloat16), row_grads))
    zero_grads = tuple((jnp.zeros_like(weight_arg) for weight_arg in params))
    totals, (result_rows, row_grads) = lax.scan(step_block, zero_grads, blocks)
    layer_output = result_rows.reshape(MB, ROWS, ROW_LEN, D)
    input_grad = row_grads.reshape(MB, ROWS, ROW_LEN, D)
    return (layer_output, input_grad, totals[0], totals[1], totals[2], totals[3], totals[4], totals[5], totals[6], totals[7], totals[8], totals[9], totals[10], totals[11], totals[12], totals[13], totals[14], totals[15])
```

```python
import functools
import math

import jax
import jax.numpy as jnp
from jax import lax
from jax.experimental import pallas as pl
from jax.experimental.pallas import tpu as pltpu
from jax.sharding import PartitionSpec as P

D = 1024
H = 16


INV_ROOT_TWO = 0.7071067811865476
INV_ROOT_TAU = 0.3989422804014327
F32 = jnp.float32
BF16 = jnp.bfloat16


def matmul(operand, factor):
    return jnp.dot(operand, factor, preferred_element_type=F32)


def matmul_left(operand, factor):
    return lax.dot_general(
        operand, factor, (((0,), (0,)), ((), ())), preferred_element_type=F32
    )


def matmul_right(operand, factor):
    return lax.dot_general(
        operand, factor, (((1,), (1,)), ((), ())), preferred_element_type=F32
    )


def features(step_ids):
    half_width = D // 2
    freqs = jnp.exp(-math.log(10000.0) * jnp.arange(half_width, dtype=F32) / half_width)
    angles = step_ids.astype(F32)[..., None] * freqs
    return jnp.concatenate([jnp.sin(angles), jnp.cos(angles)], axis=-1)


def normalize(values_in):
    center = values_in - jnp.mean(values_in, axis=-1, keepdims=True)
    spread = lax.rsqrt(jnp.mean(center * center, axis=-1, keepdims=True) + 1e-05)
    return (center * spread, spread)


def norm_back(grad_normed, normed, spread):
    mean_grad = jnp.mean(grad_normed, axis=-1, keepdims=True)
    mean_cross = jnp.mean(grad_normed * normed, axis=-1, keepdims=True)
    return spread * (grad_normed - mean_grad - normed * mean_cross)


class Net:
    def __init__(self, n):
        self.n = n
        self.bits = n.bit_length() - 1
        chip = self.bits - 1
        sizes = [(chip + 2 - i) // 3 for i in range(3)]
        groups, top = [], self.bits - 1
        for size in sizes:
            groups.append(tuple(range(top, top - size, -1)))
            top -= size
        self.outer, self.middle, self.near = groups
        self.core = (0,)

    def masks(self, group):
        found = []
        for pick in range(1, 1 << len(group)):
            mask = 0
            for place, bit in enumerate(group):
                if pick >> place & 1:
                    mask |= 1 << bit
            found.append(mask)
        return found

    def swap(self, array, mask):
        return lax.ppermute(array, "fsdp", [(i, i ^ mask) for i in range(self.n)])

    def gather(self, shard, order):
        masks = self.masks(order[0])
        first = jnp.stack([shard] + [self.swap(shard, mask) for mask in masks])
        pieces = [([0] + masks, first)]
        for group in order[1:]:
            fresh = []
            for mask in self.masks(group):
                for sources, array in pieces:
                    fresh.append(([source ^ mask for source in sources], self.swap(array, mask)))
            pieces += fresh
        return pieces

    def take(self, term, bits, mask, present, me):
        present = list(present)
        for bit in bits:
            place = present.index(bit)
            low = 1 << (len(present) - 1 - place)
            value = (me >> bit & 1) ^ (mask >> bit & 1)
            rest = term.shape[1:]
            term = term.reshape((1 << place, 2, low) + rest)
            term = lax.dynamic_index_in_dim(term, value, 1, keepdims=False)
            term = term.reshape((low << place,) + rest)
            present.remove(bit)
        return term

    def scatter(self, halves, order, me):
        keep, send = halves
        terms, present = [keep, self.swap(send, 1)], list(range(self.bits - 1, 0, -1))
        for group in order:
            received = []
            for mask in self.masks(group):
                parts = [self.take(term, group, mask, present, me).astype(F32) for term in terms]
                received.append(self.swap(sum(parts[1:], parts[0]).astype(keep.dtype), mask))
            terms = [self.take(term, group, 0, present, me) for term in terms] + received
            present = [bit for bit in present if bit not in group]
        parts = [term.astype(F32)[0] for term in terms]
        return sum(parts[1:], parts[0])

    def scatter_whole(self, whole, order, me):
        present = list(range(self.bits - 1, -1, -1))
        halves = [self.take(whole, self.core, mask, present, me) for mask in (0, 1)]
        return self.scatter(halves, order, me)


class Weights:
    def __init__(self, net, me, wanted):
        self.arrays, self.plans, self.shapes = [], [], []
        seen = {}
        for pieces, which in wanted:
            rows, columns = pieces[0][1].shape[-2:]
            plan = []
            if rows % 16:
                blocks = jnp.concatenate([array[:, which] for _, array in pieces])
                order = jnp.asarray([s for own, _ in pieces for s in own], jnp.int32)
                place = jnp.zeros((net.n,), jnp.int32).at[order ^ me].set(jnp.arange(net.n))
                whole = blocks[place].reshape(net.n * rows // 16, 16, columns)
                plan.append((len(self.arrays), None, None))
                self.arrays.append(whole)
                self.shapes.append(whole.shape)
            else:
                for own, array in pieces:
                    if id(array) not in seen:
                        seen[id(array)] = len(self.arrays)
                        self.arrays.append(array)
                    for j, source in enumerate(own):
                        plan.append((seen[id(array)], (j, which), source))
                self.shapes.append((net.n, rows, columns))
            self.plans.append(plan)
        self.slots = max(len(plan) for plan in self.plans)

    def scratch(self):
        return [pltpu.VMEM(shape, BF16) for shape in self.shapes] + [
            pltpu.SemaphoreType.DMA((len(self.plans), self.slots))
        ]

    def copies(self, w, me, array_refs, held_ref, sems):
        found = []
        for slot, (array, index, source) in enumerate(self.plans[w]):
            if index is None:
                pair = (array_refs[array], held_ref)
            else:
                pair = (array_refs[array].at[index], held_ref.at[me ^ source])
            found.append(pltpu.make_async_copy(*pair, sems.at[w, slot]))
        return found

    def start(self, w, *refs):
        for copy in self.copies(w, *refs):
            copy.start()

    def wait(self, w, *refs):
        for copy in self.copies(w, *refs):
            copy.wait()


def flat(held):
    return held.reshape(-1, held.shape[-1])


SMEM_SPEC = pl.BlockSpec(memory_space=pltpu.SMEM)
ANY_SPEC = pl.BlockSpec(memory_space=pl.ANY)


def full_spec(shape):
    return pl.BlockSpec(shape, lambda *_: (0,) * len(shape))


def tile_spec(tile, columns):
    return pl.BlockSpec((tile, columns), lambda i: (i, 0))


def call(body, name, grid, ins, outs, scratch, flops, vmem, read, exps=0):
    return pl.pallas_call(
        body,
        grid=grid,
        in_specs=[spec for _, spec in ins],
        out_specs=[spec for _, _, spec in outs],
        out_shape=[jax.ShapeDtypeStruct(shape, dtype) for shape, dtype, _ in outs],
        scratch_shapes=scratch,
        compiler_params=pltpu.CompilerParams(
            vmem_limit_bytes=vmem << 20,
            dimension_semantics=("arbitrary",) * len(grid),
        ),
        cost_estimate=pl.CostEstimate(flops=flops, bytes_accessed=read, transcendentals=exps),
        name=name,
    )(*[array for array, _ in ins])


def project_body(weights, tile, row_length, me_ref, *refs):
    count = len(weights.arrays)
    arrays, refs = refs[:count], refs[count:]
    feats_ref, x_ref, qb_ref, vb_ref = refs[:4]
    temb_ref, low_ref, q_ref, k_ref, v_ref = refs[4:9]
    tw, qw, kw, vw, sems = refs[9:14]
    me, step = me_ref[0], pl.program_id(0)

    @pl.when(step == 0)
    def _():
        for w, held in enumerate((tw, qw, kw, vw)):
            weights.start(w, me, arrays, held, sems)
        weights.wait(0, me, arrays, tw, sems)
        temb_ref[...] = matmul(feats_ref[...], flat(tw[...]))
        for w, held in ((1, qw), (2, kw), (3, vw)):
            weights.wait(w, me, arrays, held, sems)

    row = step * tile // row_length
    low = (x_ref[...].astype(F32) + temb_ref[pl.ds(row, 1), :]).astype(BF16)
    low_ref[...] = low
    q_ref[...] = (matmul(low, flat(qw[...])) + qb_ref[...]).astype(BF16)
    k_ref[...] = matmul(low, flat(kw[...])).astype(BF16)
    v_ref[...] = (matmul(low, flat(vw[...])) + vb_ref[...]).astype(BF16)


def project(net, me, flow_tq, flow_kv, feats, x, query_bias, value_bias, row_length):
    tokens, width = x.shape
    tile = min(256, row_length)
    weights = Weights(net, me, [(flow_tq, 0), (flow_tq, 1), (flow_kv, 0), (flow_kv, 1)])
    ins = (
        [(me.reshape(1), SMEM_SPEC)]
        + [(array, ANY_SPEC) for array in weights.arrays]
        + [(feats, full_spec(feats.shape)), (x, tile_spec(tile, width))]
        + [(bias, full_spec((1, width))) for bias in (query_bias, value_bias)]
    )
    outs = [(feats.shape, F32, full_spec(feats.shape))]
    outs += [((tokens, width), BF16, tile_spec(tile, width))] * 4
    return call(
        functools.partial(project_body, weights, tile, row_length),
        "project",
        (tokens // tile,),
        ins,
        outs,
        weights.scratch(),
        6 * tokens * width * width,
        40,
        8 * width * width + 10 * tokens * width,
    )


def same_document(segc_ref, segr_ref, bias_ref):
    @pl.when(pl.program_id(1) == 0)
    def _():
        bias_ref[...] = jnp.where(segc_ref[0] == segr_ref[0], 0.0, -1e30)


def own_lanes(shape, head, head_dim):
    lanes = lax.broadcasted_iota(jnp.int32, shape, len(shape) - 1)
    return (lanes // head_dim) == head


def attend_body(head_dim, segc_ref, segr_ref, q_ref, k_ref, v_ref, out_ref, log_ref, bias_ref):
    same_document(segc_ref, segr_ref, bias_ref)
    queries, key_rows, values = q_ref[...], k_ref[...], v_ref[...]
    scale = 1.0 / math.sqrt(head_dim)
    per = queries.shape[1] // head_dim
    total = None
    for head in range(per):
        mine = own_lanes(queries.shape, head, head_dim)
        keys_own = jnp.where(mine, key_rows * BF16(scale), BF16(0))
        scores = matmul_right(keys_own, queries) + bias_ref[...]
        top = jnp.max(scores, axis=0, keepdims=True)
        raised = jnp.exp(scores - top)
        amount = jnp.sum(raised, axis=0, keepdims=True)
        log_ref[0, 0, pl.ds(head, 1), :] = top + jnp.log(amount)
        soft_low = (raised * (1.0 / amount)).astype(BF16)
        context = matmul_left(soft_low, values)
        total = context if total is None else jnp.where(mine, context, total)
    out_ref[...] = total.astype(BF16)


def attend_back_body(
    head_dim, segc_ref, segr_ref, q_ref, k_ref, v_ref, log_ref, g_ref, gq_ref, gk_ref, gv_ref, bias_ref
):
    same_document(segc_ref, segr_ref, bias_ref)
    queries, key_rows, values, grads = q_ref[...], k_ref[...], v_ref[...], g_ref[...]
    scale = 1.0 / math.sqrt(head_dim)
    per = queries.shape[1] // head_dim
    totals = None
    for head in range(per):
        mine = own_lanes(queries.shape, head, head_dim)
        keys_own = jnp.where(mine, key_rows * BF16(scale), BF16(0))
        scores = matmul_right(keys_own, queries) + bias_ref[...]
        soft = jnp.exp(scores - log_ref[0, 0, pl.ds(head, 1), :])
        grad_soft = matmul_right(jnp.where(mine, values, BF16(0)), grads)
        inner_sum = jnp.sum(soft * grad_soft, axis=0, keepdims=True)
        grad_scores = (soft * (grad_soft - inner_sum)).astype(BF16)
        parts = (
            matmul_left(grad_scores, key_rows),
            matmul(grad_scores, queries),
            matmul(soft.astype(BF16), grads),
        )
        if totals is None:
            totals = parts
        else:
            totals = tuple(jnp.where(mine, part, total) for part, total in zip(parts, totals))
    gq_ref[...] = (totals[0] * scale).astype(BF16)
    gk_ref[...] = (totals[1] * scale).astype(BF16)
    gv_ref[...] = totals[2].astype(BF16)


def attention_specs(rows, row_length, lanes):
    segc = pl.BlockSpec((1, row_length, 1), lambda i, j: (i, 0, 0))
    segr = pl.BlockSpec((1, 1, row_length), lambda i, j: (i, 0, 0))
    block = pl.BlockSpec((row_length, lanes), lambda i, j: (i, j))
    return segc, segr, block


def attend(queries, key_rows, values, segments):
    rows, row_length = segments.shape
    tokens, width = queries.shape
    head_dim = width // H
    lanes = 128
    blocks, per = width // lanes, lanes // head_dim
    segc, segr, block = attention_specs(rows, row_length, lanes)
    log_spec = pl.BlockSpec((1, 1, per, row_length), lambda i, j: (i, j, 0, 0))
    return call(
        functools.partial(attend_body, head_dim),
        "attend",
        (rows, blocks),
        [(segments[:, :, None], segc), (segments[:, None, :], segr)]
        + [(array, block) for array in (queries, key_rows, values)],
        [
            ((tokens, width), BF16, block),
            ((rows, blocks, per, row_length), F32, log_spec),
        ],
        [pltpu.VMEM((row_length, row_length), F32)],
        4 * tokens * row_length * width * 4,
        32,
        8 * tokens * width,
        tokens * row_length * H,
    )


def attend_back(queries, key_rows, values, segments, log_total, grad_context):
    rows, row_length = segments.shape
    tokens, width = queries.shape
    head_dim = width // H
    lanes = 128
    blocks, per = width // lanes, lanes // head_dim
    segc, segr, block = attention_specs(rows, row_length, lanes)
    log_spec = pl.BlockSpec((1, 1, per, row_length), lambda i, j: (i, j, 0, 0))
    return call(
        functools.partial(attend_back_body, head_dim),
        "attend_back",
        (rows, blocks),
        [(segments[:, :, None], segc), (segments[:, None, :], segr)]
        + [(array, block) for array in (queries, key_rows, values)]
        + [(log_total, log_spec), (grad_context, block)],
        [((tokens, width), BF16, block)] * 3,
        [pltpu.VMEM((row_length, row_length), F32)],
        10 * tokens * row_length * width * 4,
        32,
        14 * tokens * width,
        tokens * row_length * H,
    )


def add_to(ref, value, step):
    part = jnp.sum(value, axis=0, keepdims=True)

    @pl.when(step == 0)
    def _():
        ref[...] = part

    @pl.when(step != 0)
    def _():
        ref[...] += part


def ffn_body(weights, tile, row_length, chunk, me_ref, *refs):
    count = len(weights.arrays)
    arrays, refs = refs[:count], refs[count:]
    (context_ref, x_ref, temb_ref, cot_ref, ob_ref, ib_ref, ub_ref) = refs[:7]
    (fg_ref, fs_ref, sg_ref, ss_ref) = refs[7:11]
    (out_ref, first_low_ref, normed_ref, spread_ref, active_ref, slope_ref) = refs[11:17]
    (gs_ref, gs_low_ref, sgg_ref, ssg_ref, obg_ref) = refs[17:22]
    ow, iw, uw, sems = refs[22:26]
    acc_ref = refs[26]
    me, step = me_ref[0], pl.program_id(0)

    @pl.when(step == 0)
    def _():
        for w, held in enumerate((ow, iw, uw)):
            weights.start(w, me, arrays, held, sems)
        weights.wait(0, me, arrays, ow, sems)

    row = step * tile // row_length
    stream = x_ref[...].astype(F32) + temb_ref[pl.ds(row, 1), :]
    mixed = stream + (matmul(context_ref[...], flat(ow[...])) + ob_ref[...])
    normed, spread = normalize(mixed)
    normed_ref[...] = normed
    spread_ref[...] = spread
    first = normed * fg_ref[...] + fs_ref[...]
    first_low_ref[...] = first.astype(BF16)
    acc_ref[...] = first + ub_ref[...]

    @pl.when(step == 0)
    def _():
        for w, held in ((1, iw), (2, uw)):
            weights.wait(w, me, arrays, held, sems)

    unit = uw.shape[1]
    hidden = iw.shape[2]

    @pl.loop(0, hidden // chunk)
    def _(j):
        columns = pl.ds(pl.multiple_of(j * chunk, chunk), chunk)
        pre = matmul(first_low_ref[...], flat(iw[:, :, columns])) + ib_ref[:, columns]
        normal_cdf = 0.5 * (1.0 + lax.erf(pre * INV_ROOT_TWO))
        normal_pdf = jnp.exp(-0.5 * pre * pre) * INV_ROOT_TAU
        active = (pre * normal_cdf).astype(BF16)
        active_ref[:, columns] = active
        slope_ref[:, columns] = (normal_cdf + pre * normal_pdf).astype(BF16)
        acc_ref[...] += matmul(active, flat(uw[pl.ds(j * (chunk // unit), chunk // unit)]))

    normed_second, spread_second = normalize(acc_ref[...])
    out_ref[...] = (normed_second * sg_ref[...] + ss_ref[...]).astype(BF16)
    grad_out = cot_ref[...].astype(F32)
    add_to(sgg_ref, grad_out * normed_second, step)
    add_to(ssg_ref, grad_out, step)
    grad_second = norm_back(grad_out * sg_ref[...], normed_second, spread_second)
    gs_ref[...] = grad_second
    low = grad_second.astype(BF16)
    gs_low_ref[...] = low
    add_to(obg_ref, low.astype(F32), step)


def ffn(net, me, flows, context, x, temb, cotangent, vectors, row_length):
    tokens, width = x.shape
    hidden = vectors[1].shape[1]
    tile = min(256, row_length)
    weights = Weights(net, me, [(flow, 0) for flow in flows])
    tiled, wide = tile_spec(tile, width), tile_spec(tile, hidden)
    ins = (
        [(me.reshape(1), SMEM_SPEC)]
        + [(array, ANY_SPEC) for array in weights.arrays]
        + [(context, tiled), (x, tiled), (temb, full_spec(temb.shape)), (cotangent, tiled)]
        + [(vector, full_spec(vector.shape)) for vector in vectors]
    )
    row = ((1, width), F32, full_spec((1, width)))
    outs = [
        ((tokens, width), BF16, tiled),
        ((tokens, width), BF16, tiled),
        ((tokens, width), F32, tiled),
        ((tokens, 1), F32, tile_spec(tile, 1)),
        ((tokens, hidden), BF16, wide),
        ((tokens, hidden), BF16, wide),
        ((tokens, width), F32, tiled),
        ((tokens, width), BF16, tiled),
        row,
        row,
        row,
    ]
    return call(
        functools.partial(ffn_body, weights, tile, row_length, 512),
        "ffn",
        (tokens // tile,),
        ins,
        outs,
        weights.scratch() + [pltpu.VMEM((tile, width), F32)],
        2 * tokens * width * (2 * hidden + width),
        60,
        4 * width * hidden + 4 * tokens * hidden + 20 * tokens * width,
        2 * tokens * hidden,
    )


def ffn_back_body(weights, chunk, me_ref, *refs):
    count = len(weights.arrays)
    arrays, refs = refs[:count], refs[count:]
    (gs_ref, gs_low_ref, slope_ref, normed_ref, spread_ref, fg_ref) = refs[:6]
    (gi_ref, gm_ref, gm_low_ref, gc_ref) = refs[6:10]
    (ibg_ref, fgg_ref, fsg_ref, obg_ref) = refs[10:14]
    ow, iw, uw, sems = refs[14:18]
    acc_ref = refs[18]
    me, step = me_ref[0], pl.program_id(0)

    @pl.when(step == 0)
    def _():
        for w, held in ((2, uw), (1, iw), (0, ow)):
            weights.start(w, me, arrays, held, sems)
        for w, held in ((2, uw), (1, iw)):
            weights.wait(w, me, arrays, held, sems)

    acc_ref[...] = gs_ref[...]
    unit = uw.shape[1]
    hidden = iw.shape[2]

    @pl.loop(0, hidden // chunk)
    def _(j):
        columns = pl.ds(pl.multiple_of(j * chunk, chunk), chunk)
        held = flat(uw[pl.ds(j * (chunk // unit), chunk // unit)])
        grad_active = matmul_right(gs_low_ref[...], held)
        low = (grad_active * slope_ref[:, columns].astype(F32)).astype(BF16)
        gi_ref[:, columns] = low
        acc_ref[...] += matmul_right(low, flat(iw[:, :, columns]))

    add_to(ibg_ref, gi_ref[...].astype(F32), step)
    grad_first, normed = acc_ref[...], normed_ref[...]
    add_to(fgg_ref, grad_first * normed, step)
    add_to(fsg_ref, grad_first, step)
    grad_mixed = norm_back(grad_first * fg_ref[...], normed, spread_ref[...])
    gm_ref[...] = grad_mixed
    low = grad_mixed.astype(BF16)
    gm_low_ref[...] = low
    add_to(obg_ref, low.astype(F32), step)

    @pl.when(step == 0)
    def _():
        weights.wait(0, me, arrays, ow, sems)

    gc_ref[...] = matmul_right(low, flat(ow[...])).astype(BF16)


def ffn_back(net, me, flows, gs, gs_low, slope, normed, spread, first_gain):
    tokens, width = gs.shape
    hidden = slope.shape[1]
    tile = min(256, tokens)
    weights = Weights(net, me, [(flow, 0) for flow in flows])
    tiled, wide = tile_spec(tile, width), tile_spec(tile, hidden)
    ins = (
        [(me.reshape(1), SMEM_SPEC)]
        + [(array, ANY_SPEC) for array in weights.arrays]
        + [(gs, tiled), (gs_low, tiled), (slope, wide), (normed, tiled)]
        + [(spread, tile_spec(tile, 1)), (first_gain, full_spec(first_gain.shape))]
    )
    row = ((1, width), F32, full_spec((1, width)))
    outs = [
        ((tokens, hidden), BF16, wide),
        ((tokens, width), F32, tiled),
        ((tokens, width), BF16, tiled),
        ((tokens, width), BF16, tiled),
        ((1, hidden), F32, full_spec((1, hidden))),
        row,
        row,
        row,
    ]
    return call(
        functools.partial(ffn_back_body, weights, 512),
        "ffn_back",
        (tokens // tile,),
        ins,
        outs,
        weights.scratch() + [pltpu.VMEM((tile, width), F32)],
        2 * tokens * width * (2 * hidden + width),
        60,
        4 * width * hidden + 4 * tokens * hidden + 20 * tokens * width,
    )


def product_body(rows, me_ref, a_ref, b_ref, keep_ref, send_ref):
    core = me_ref[0] & 1
    total = matmul_left(a_ref[...], b_ref[...])
    total = total.reshape(-1, 2, rows, total.shape[-1])
    low, high = total[:, 0], total[:, 1]
    keep_ref[...] = jnp.where(core == 0, low, high).astype(BF16)
    send_ref[...] = jnp.where(core == 0, high, low).astype(BF16)


def product(net, me, left, right, tile=512, lanes=512):
    tokens, width = left.shape
    columns = right.shape[1]
    rows = width // net.n
    lanes = min(lanes, columns)
    shape = (net.n // 2, rows, columns)
    block = pl.BlockSpec((tile // (2 * rows), rows, lanes), lambda i, j: (i, 0, j))
    return call(
        functools.partial(product_body, rows),
        "product",
        (width // tile, columns // lanes),
        [
            (me.reshape(1), SMEM_SPEC),
            (left, pl.BlockSpec((tokens, tile), lambda i, j: (0, i))),
            (right, pl.BlockSpec((tokens, lanes), lambda i, j: (0, j))),
        ],
        [(shape, BF16, block), (shape, BF16, block)],
        [],
        2 * tokens * width * columns,
        48,
        2 * (tokens * width + tokens * columns + width * columns),
    )


def stream_back_body(weights, tile, row_length, me_ref, *refs):
    count = len(weights.arrays)
    arrays, refs = refs[:count], refs[count:]
    gm_ref, gq_ref, gk_ref, gv_ref, out_ref, gt_ref, qbg_ref, vbg_ref = refs[:8]
    qw, kw, vw, sems = refs[8:12]
    me, step = me_ref[0], pl.program_id(0)

    @pl.when(step == 0)
    def _():
        for w, held in enumerate((qw, kw, vw)):
            weights.start(w, me, arrays, held, sems)
        for w, held in enumerate((qw, kw, vw)):
            weights.wait(w, me, arrays, held, sems)

    add_to(qbg_ref, gq_ref[...].astype(F32), step)
    add_to(vbg_ref, gv_ref[...].astype(F32), step)
    total = (
        gm_ref[...]
        + matmul_right(gq_ref[...], flat(qw[...]))
        + matmul_right(gk_ref[...], flat(kw[...]))
        + matmul_right(gv_ref[...], flat(vw[...]))
    )
    out_ref[...] = total
    row = pl.ds(step * tile // row_length, 1)
    part = jnp.sum(total, axis=0, keepdims=True)
    opens = lax.rem(step * tile, row_length) == 0
    gt_ref[row, :] = part + jnp.where(opens, 0.0, gt_ref[row, :])


def stream_back(net, me, flow_tq, flow_kv, gm, gq, gk, gv, rows):
    tokens, width = gm.shape
    row_length = tokens // rows
    tile = min(256, row_length)
    weights = Weights(net, me, [(flow_tq, 1), (flow_kv, 0), (flow_kv, 1)])
    tiled = tile_spec(tile, width)
    row = ((1, width), F32, full_spec((1, width)))
    return call(
        functools.partial(stream_back_body, weights, tile, row_length),
        "stream_back",
        (tokens // tile,),
        [(me.reshape(1), SMEM_SPEC)]
        + [(array, ANY_SPEC) for array in weights.arrays]
        + [(array, tiled) for array in (gm, gq, gk, gv)],
        [((tokens, width), F32, tiled), ((rows, width), F32, full_spec((rows, width))), row, row],
        weights.scratch(),
        6 * tokens * width * width,
        40,
        6 * width * width + 14 * tokens * width,
    )


def in_order(net, me, pieces):
    blocks = jnp.concatenate([array for _, array in pieces])
    order = jnp.asarray([source for own, _ in pieces for source in own], jnp.int32)
    place = jnp.zeros((net.n,), jnp.int32).at[order].set(jnp.arange(net.n, dtype=jnp.int32))
    return blocks[place[jnp.arange(net.n) ^ me]]


def on_device(
    net,
    inputs,
    timesteps,
    segments,
    cotangent,
    query_weight,
    key_weight,
    value_weight,
    output_weight,
    inner_weight,
    outer_weight,
    time_weight,
    *vectors,
):
    n = net.n
    me = lax.axis_index("fsdp").astype(jnp.int32)
    batch_count, row_count, row_length, model_width = inputs.shape
    rows = batch_count * row_count
    tokens = rows * row_length
    order_a = (net.outer, net.middle, net.near, net.core)
    order_b = (net.outer, net.near, net.middle, net.core)
    back_a = (net.near, net.middle, net.outer)
    back_b = (net.middle, net.near, net.outer)

    feats = features(timesteps.reshape(rows)).astype(BF16)
    sizes = [vector.shape[0] for vector in vectors]
    small = jnp.concatenate(list(vectors) + [feats.reshape(-1)])[None]

    small = in_order(net, me, net.gather(small, order_a))[:, 0]
    flow_tq = net.gather(jnp.stack([time_weight, query_weight]), order_a)
    flow_kv = net.gather(jnp.stack([key_weight, value_weight]), order_b)
    flow_o = net.gather(output_weight[None], order_a)
    flow_i = net.gather(inner_weight[None], order_b)
    flow_u = net.gather(outer_weight[None], order_a)

    gathered, start = [], 0
    for size in sizes:
        gathered.append(small[:, start : start + size].reshape(1, -1).astype(F32))
        start += size
    (query_bias, value_bias, output_bias, inner_bias, outer_bias) = gathered[:5]
    (first_gain, first_shift, second_gain, second_shift) = gathered[5:]
    feats_all = small[:, start:].reshape(n * rows, model_width)

    segments = segments.reshape(rows, row_length)
    x = inputs.reshape(tokens, model_width)
    temb, stream_low, queries, key_rows, values = project(
        net, me, flow_tq, flow_kv, feats, x, query_bias, value_bias, row_length
    )
    context, log_total = attend(queries, key_rows, values, segments)
    (
        layer_output,
        first_low,
        normed_first,
        spread_first,
        active_low,
        slope,
        grad_second,
        grad_second_low,
        second_gain_grad,
        second_shift_grad,
        outer_bias_grad,
    ) = ffn(
        net,
        me,
        (flow_o, flow_i, flow_u),
        context,
        x,
        temb,
        cotangent.reshape(tokens, model_width),
        (output_bias, inner_bias, outer_bias, first_gain, first_shift, second_gain, second_shift),
        row_length,
    )
    outer_halves = product(net, me, active_low, grad_second_low)
    (
        grad_inner_low,
        grad_mixed,
        grad_mixed_low,
        grad_context,
        inner_bias_grad,
        first_gain_grad,
        first_shift_grad,
        output_bias_grad,
    ) = ffn_back(
        net,
        me,
        (flow_o, flow_i, flow_u),
        grad_second,
        grad_second_low,
        slope,
        normed_first,
        spread_first,
        first_gain,
    )
    inner_halves = product(net, me, first_low, grad_inner_low)
    output_halves = product(net, me, context, grad_mixed_low)
    grad_queries, grad_keys, grad_values = attend_back(
        queries, key_rows, values, segments, log_total, grad_context
    )
    query_halves = product(net, me, stream_low, grad_queries)
    key_halves = product(net, me, stream_low, grad_keys)
    value_halves = product(net, me, stream_low, grad_values)
    grad_stream, grad_temb, query_bias_grad, value_bias_grad = stream_back(
        net, me, flow_tq, flow_kv, grad_mixed, grad_queries, grad_keys, grad_values, rows
    )

    outer_weight_grad = net.scatter(outer_halves, back_a, me)
    inner_weight_grad = net.scatter(inner_halves, back_b, me)
    output_weight_grad = net.scatter(output_halves, back_a, me)
    query_weight_grad = net.scatter(query_halves, back_a, me)
    key_weight_grad = net.scatter(key_halves, back_b, me)
    value_weight_grad = net.scatter(value_halves, back_a, me)
    temb_all = in_order(net, me, net.gather(grad_temb, order_a)).reshape(n * rows, model_width)
    own = model_width // n
    feats_own = lax.dynamic_slice_in_dim(feats_all, me * own, own, 1)
    time_weight_grad = lax.dot_general(
        feats_own.astype(F32),
        temb_all,
        (((0,), (0,)), ((), ())),
        precision=lax.Precision.HIGHEST,
    )
    vector_grads = [
        query_bias_grad,
        value_bias_grad,
        output_bias_grad,
        inner_bias_grad,
        outer_bias_grad,
        first_gain_grad,
        first_shift_grad,
        second_gain_grad,
        second_shift_grad,
    ]
    vector_sums = jnp.concatenate([grad.reshape(n, -1) for grad in vector_grads], axis=1)
    vector_sums = net.scatter_whole(vector_sums[:, None], back_a, me)[0]
    vector_outs, start = [], 0
    for size in sizes:
        vector_outs.append(vector_sums[start : start + size])
        start += size

    shape = inputs.shape
    return (
        layer_output.reshape(shape),
        grad_stream.reshape(shape),
        query_weight_grad,
        key_weight_grad,
        value_weight_grad,
        output_weight_grad,
        inner_weight_grad,
        outer_weight_grad,
        time_weight_grad,
    ) + tuple(vector_outs)


def solution(mesh):
    matrix, vector = P("fsdp", None), P("fsdp")
    batch = P(None, "fsdp", None, None)
    return jax.shard_map(
        functools.partial(on_device, Net(mesh.shape["fsdp"])),
        mesh=mesh,
        in_specs=(batch, P(None, "fsdp"), P(None, "fsdp", None), batch)
        + (matrix,) * 7
        + (vector,) * 9,
        out_specs=(batch, batch) + (matrix,) * 7 + (vector,) * 9,
        check_vma=False,
    )
```

```python
import functools
import math

import jax
import jax.numpy as jnp
from jax import lax
from jax.experimental import pallas as pl
from jax.experimental.pallas import tpu as pltpu
from jax.sharding import PartitionSpec as P

D = 1024
H = 16


INV_ROOT_TWO = 0.7071067811865476
INV_ROOT_TAU = 0.3989422804014327
F32 = jnp.float32
BF16 = jnp.bfloat16


def matmul(operand, factor):
    return jnp.dot(operand, factor, preferred_element_type=F32)


def matmul_left(operand, factor):
    return lax.dot_general(
        operand, factor, (((0,), (0,)), ((), ())), preferred_element_type=F32
    )


def matmul_right(operand, factor):
    return lax.dot_general(
        operand, factor, (((1,), (1,)), ((), ())), preferred_element_type=F32
    )


def features(step_ids):
    half_width = D // 2
    freqs = jnp.exp(-math.log(10000.0) * jnp.arange(half_width, dtype=F32) / half_width)
    angles = step_ids.astype(F32)[..., None] * freqs
    return jnp.concatenate([jnp.sin(angles), jnp.cos(angles)], axis=-1)


def normalize(values_in):
    center = values_in - jnp.mean(values_in, axis=-1, keepdims=True)
    spread = lax.rsqrt(jnp.mean(center * center, axis=-1, keepdims=True) + 1e-05)
    return (center * spread, spread)


def norm_back(grad_normed, normed, spread):
    mean_grad = jnp.mean(grad_normed, axis=-1, keepdims=True)
    mean_cross = jnp.mean(grad_normed * normed, axis=-1, keepdims=True)
    return spread * (grad_normed - mean_grad - normed * mean_cross)


class Net:
    def __init__(self, n):
        self.n = n
        self.bits = n.bit_length() - 1
        chip = self.bits - 1
        sizes = [(chip + 2 - i) // 3 for i in range(3)]
        groups, top = [], self.bits - 1
        for size in sizes:
            groups.append(tuple(range(top, top - size, -1)))
            top -= size
        self.outer, self.middle, self.near = groups
        self.core = (0,)

    def masks(self, group):
        found = []
        for pick in range(1, 1 << len(group)):
            mask = 0
            for place, bit in enumerate(group):
                if pick >> place & 1:
                    mask |= 1 << bit
            found.append(mask)
        return found

    def swap(self, array, mask):
        return lax.ppermute(array, "fsdp", [(i, i ^ mask) for i in range(self.n)])

    def gather_far(self, shard):
        return [shard] + [self.swap(shard, mask) for mask in self.masks(self.outer)]

    def stacked(self, parts):
        return ([0] + self.masks(self.outer), jnp.stack(parts))

    def gather_near(self, own):
        sources, array = own
        return [
            [(mask, self.swap(array, mask)) for mask in self.masks(group)]
            for group in (self.near, self.middle)
        ]

    def gather_corner(self, own, near):
        sources, half = own[0], len(own[0]) // 2
        pieces, corners, sent = [own], [], []
        for group in near:
            pieces += [([s ^ mask for s in sources], array) for mask, array in group]
        for mask_x, array_x in near[0]:
            for mask_y, array_y in near[1]:
                low, high = array_y[:half], array_x[half:]
                sent += [low, high]
                corner = mask_x ^ mask_y
                corners.append(([s ^ corner for s in sources[:half]], self.swap(low, mask_x)))
                corners.append(([s ^ corner for s in sources[half:]], self.swap(high, mask_y)))
        return pieces, corners, sent

    def gather_core(self, pieces):
        return pieces + [([s ^ 1 for s in own], self.swap(array, 1)) for own, array in pieces]

    def inner_masks(self):
        near, middle = self.masks(self.near), self.masks(self.middle)
        return near + middle + [x | y for x in near for y in middle]

    def gather_round(self, sources, array, masks):
        array = jnp.concatenate([array] + [self.swap(array, mask) for mask in masks])
        return [source ^ mask for mask in [0] + masks for source in sources], array

    def take(self, term, bits, mask, present, me):
        present = list(present)
        for bit in bits:
            place = present.index(bit)
            low = 1 << (len(present) - 1 - place)
            value = (me >> bit & 1) ^ (mask >> bit & 1)
            rest = term.shape[1:]
            term = term.reshape((1 << place, 2, low) + rest)
            term = lax.dynamic_index_in_dim(term, value, 1, keepdims=False)
            term = term.reshape((low << place,) + rest)
            present.remove(bit)
        return term

    def scatter_core(self, halves):
        keep, send = halves
        return [keep, self.swap(send, 1)], list(range(self.bits - 1, 0, -1))

    def added(self, parts, dtype):
        parts = [part.astype(F32) for part in parts]
        return sum(parts[1:], parts[0]).astype(dtype)

    def scatter_step(self, state, group, me):
        terms, present = state
        sent = []
        for mask in self.masks(group):
            parts = [self.take(term, group, mask, present, me) for term in terms]
            sent.append(self.added(parts, terms[0].dtype))
        received = [self.swap(part, mask) for part, mask in zip(sent, self.masks(group))]
        terms = [self.take(term, group, 0, present, me) for term in terms] + received
        return (terms, [bit for bit in present if bit not in group]), sent

    def scatter_corner(self, state, me):
        terms, present = state
        left = [bit for bit in present if bit not in self.near]
        found, sent = [], []
        for mask_x in self.masks(self.near):
            row = [self.take(term, self.near, mask_x, present, me) for term in terms]
            for mask_y in self.masks(self.middle):
                parts = [self.take(term, self.middle, mask_y, left, me) for term in row]
                half = parts[0].shape[0] // 2
                low = self.added([part[:half] for part in parts], terms[0].dtype)
                high = self.added([part[half:] for part in parts], terms[0].dtype)
                sent += [low, high]
                found.append((mask_x, mask_y, self.swap(low, mask_x), self.swap(high, mask_y)))
        return found, sent

    def scatter_near(self, state, corner, me):
        terms, present = state
        left = [bit for bit in present if bit not in self.near]
        mine, received, sent = [self.take(t, self.near, 0, present, me) for t in terms], [], []
        for mask_x in self.masks(self.near):
            row = [self.take(term, self.near, mask_x, present, me) for term in terms]
            parts = [self.take(term, self.middle, 0, left, me) for term in row]
            for mask, _, _, high in corner:
                if mask == mask_x:
                    parts.append(jnp.concatenate([jnp.zeros_like(high), high]))
            sent.append((self.added(parts, terms[0].dtype), mask_x))
        for mask_y in self.masks(self.middle):
            parts = [self.take(term, self.middle, mask_y, left, me) for term in mine]
            for _, mask, low, _ in corner:
                if mask == mask_y:
                    parts.append(jnp.concatenate([low, jnp.zeros_like(low)]))
            sent.append((self.added(parts, terms[0].dtype), mask_y))
        received = [self.swap(part, mask) for part, mask in sent]
        terms = [self.take(term, self.middle, 0, left, me) for term in mine] + received
        left = [bit for bit in left if bit not in self.middle]
        return (terms, left), [part for part, _ in sent]

    def scatter_far(self, state, me):
        return self.scatter_step(state, self.outer, me)

    def scatter_end(self, state):
        return self.added(state[0], F32)[0]

    def scatter(self, halves, order, me):
        state = self.scatter_core(halves)
        for group in order:
            state, _ = self.scatter_step(state, group, me)
        return self.scatter_end(state)

    def scatter_whole(self, whole, order, me):
        present = list(range(self.bits - 1, -1, -1))
        halves = [self.take(whole, self.core, mask, present, me) for mask in (0, 1)]
        return self.scatter(halves, order, me)


def after(values, others):
    leaves, tree = jax.tree.flatten(values)
    arrays = [leaf for leaf in leaves if not isinstance(leaf, int)]
    others = [leaf for leaf in jax.tree.leaves(others) if not isinstance(leaf, int)]
    tied = iter(lax.optimization_barrier(tuple(arrays + others)))
    return jax.tree.unflatten(
        tree, [leaf if isinstance(leaf, int) else next(tied) for leaf in leaves]
    )


class Weights:
    def __init__(self, net, me, wanted):
        self.arrays, self.plans, self.shapes = [], [], []
        seen = {}
        for pieces, place, rows in wanted:
            columns = pieces[0][1].shape[-1]
            plan = []
            if rows % 16:
                blocks = jnp.concatenate([array[:, place : place + rows] for _, array in pieces])
                order = jnp.asarray([s for own, _ in pieces for s in own], jnp.int32)
                spot = jnp.zeros((net.n,), jnp.int32).at[order ^ me].set(jnp.arange(net.n))
                whole = blocks[spot].reshape(net.n * rows // 16, 16, columns)
                plan.append((len(self.arrays), None, None))
                self.arrays.append(whole)
                self.shapes.append(whole.shape)
            else:
                for own, array in pieces:
                    if id(array) not in seen:
                        seen[id(array)] = len(self.arrays)
                        self.arrays.append(array)
                    for j, source in enumerate(own):
                        plan.append((seen[id(array)], (j, pl.ds(place, rows)), source))
                self.shapes.append((net.n, rows, columns))
            self.plans.append(plan)
        self.slots = max(len(plan) for plan in self.plans)

    def scratch(self):
        return [pltpu.VMEM(shape, BF16) for shape in self.shapes] + [
            pltpu.SemaphoreType.DMA((len(self.plans), self.slots))
        ]

    def copies(self, w, me, array_refs, held_ref, sems):
        found = []
        for slot, (array, index, source) in enumerate(self.plans[w]):
            if index is None:
                pair = (array_refs[array], held_ref)
            else:
                pair = (array_refs[array].at[index], held_ref.at[me ^ source])
            found.append(pltpu.make_async_copy(*pair, sems.at[w, slot]))
        return found

    def start(self, w, *refs):
        for copy in self.copies(w, *refs):
            copy.start()

    def wait(self, w, *refs):
        for copy in self.copies(w, *refs):
            copy.wait()


def flat(held):
    return held.reshape(-1, held.shape[-1])


SMEM_SPEC = pl.BlockSpec(memory_space=pltpu.SMEM)
ANY_SPEC = pl.BlockSpec(memory_space=pltpu.HBM)


def full_spec(shape):
    return pl.BlockSpec(shape, lambda *_: (0,) * len(shape))


def tile_spec(tile, columns):
    return pl.BlockSpec((tile, columns), lambda i: (i, 0))


def call(body, name, grid, ins, outs, scratch, us, bases=()):
    count = len(ins)

    def run(*refs):
        body(*refs[:count], *refs[count + len(bases) :])

    return pl.pallas_call(
        run,
        grid=grid,
        in_specs=[spec for _, spec in ins] + [ANY_SPEC] * len(bases),
        out_specs=[spec for _, _, spec in outs],
        out_shape=[jax.ShapeDtypeStruct(shape, dtype) for shape, dtype, _ in outs],
        scratch_shapes=scratch,
        input_output_aliases={count + i: i for i in range(len(bases))},
        compiler_params=pltpu.CompilerParams(
            vmem_limit_bytes=60 << 20,
            dimension_semantics=("arbitrary",) * len(grid),
        ),
        cost_estimate=pl.CostEstimate(
            flops=int(us * 2e10), bytes_accessed=int(us * 5e7), transcendentals=0
        ),
        name=name,
    )(*[array for array, _ in ins], *bases)


def sum_body(groups, me_ref, *refs):
    step = pl.program_id(0)
    outs = refs[len(refs) - len(groups) :]
    for out_ref, addends in zip(outs, groups):
        total = None
        for place, (low, high) in addends:
            part = refs[place][...].astype(F32)
            if low is not None:
                part = jnp.where((step >= low) & (step < high), part, 0.0)
            total = part if total is None else total + part
        out_ref[...] = total.astype(out_ref.dtype)


def sum_call(me, name, grid, ins, groups, outs, body=None):
    grid_spec = pltpu.PrefetchScalarGridSpec(
        num_scalar_prefetch=1,
        grid=(grid,),
        in_specs=[
            pl.BlockSpec(block, lambda i, me_ref, place=place: place(i, me_ref[0]))
            for _, block, place in ins
        ],
        out_specs=[
            pl.BlockSpec(block, lambda i, me_ref, place=place: place(i, me_ref[0]))
            for _, _, block, place in outs
        ],
    )
    return pl.pallas_call(
        body or functools.partial(sum_body, groups),
        grid_spec=grid_spec,
        out_shape=[jax.ShapeDtypeStruct(shape, dtype) for shape, dtype, _, _ in outs],
        compiler_params=pltpu.CompilerParams(
            vmem_limit_bytes=60 << 20, dimension_semantics=("arbitrary",)
        ),
        cost_estimate=pl.CostEstimate(flops=1000, bytes_accessed=1000, transcendentals=0),
        name=name,
    )(me.reshape(1), *[array for array, _, _ in ins])


class Reduction:
    def __init__(self, net, me, keep, send):
        self.net, self.me = net, me
        self.terms = [keep, net.swap(send, 1)]
        self.rows, self.columns = keep.shape[1:]
        self.plain = len(net.near) == 1 and len(net.middle) == 1 and self.rows % 8 == 0
        self.state = None

    def block(self):
        return (1, self.rows, self.columns)

    def hold(self, others):
        if self.plain:
            self.terms = after(self.terms, others)
        else:
            state = self.state or (self.terms, list(range(self.net.bits - 1, 0, -1)))
            self.state = held(state, others)
            if getattr(self, "corner_pieces", None) is not None:
                self.corner_pieces = after(self.corner_pieces, others)
        return self

    def corner(self):
        net = self.net
        if not self.plain:
            state = self.state or (self.terms, list(range(net.bits - 1, 0, -1)))
            self.state = state
            self.corner_pieces, sent = net.scatter_corner(state, self.me)
            return sent
        far = 1 << (len(net.outer) - 1)

        def place(shift):
            return lambda i, me: ((i + shift) * 4 + (me >> 1 & 3 ^ 3), 0, 0)

        ins = [(term, self.block(), place(shift)) for shift in (0, far) for term in self.terms]
        out = ((far, self.rows, self.columns), BF16, self.block(), lambda i, me: (i, 0, 0))
        always = (None, None)
        groups = [[(0, always), (1, always)], [(2, always), (3, always)]]
        low, high = sum_call(self.me, "corner_sum", far, ins, groups, [out, out])
        self.terms += [net.swap(low, 1 << net.near[0]), net.swap(high, 1 << net.middle[0])]
        return [low, high]

    def near(self):
        net = self.net
        if not self.plain:
            self.state, sent = net.scatter_near(self.state, self.corner_pieces, self.me)
            self.corner_pieces = None
            return sent
        far = 1 << (len(net.outer) - 1)
        keep, other, low, high = self.terms

        def place(flip):
            return lambda i, me: (i * 4 + (me >> 1 & 3 ^ flip), 0, 0)

        ins = [(term, self.block(), place(flip)) for flip in (1, 2) for term in (keep, other)]
        ins.append((high, self.block(), lambda i, me: (jnp.maximum(i - far, 0), 0, 0)))
        ins.append((low, self.block(), lambda i, me: (jnp.minimum(i, far - 1), 0, 0)))
        always = (None, None)
        groups = [
            [(0, always), (1, always), (4, (far, 2 * far))],
            [(2, always), (3, always), (5, (0, far))],
        ]
        out = ((2 * far, self.rows, self.columns), BF16, self.block(), lambda i, me: (i, 0, 0))
        sent = sum_call(self.me, "near_sum", 2 * far, ins, groups, [out, out])
        received = [
            net.swap(part, 1 << group[0]) for part, group in zip(sent, (net.near, net.middle))
        ]
        self.terms = [keep, other] + received
        return sent

    def sources(self, flip, step_block):
        keep, other, row, column = self.terms[:4]
        found = []
        for term in (keep, other):
            found.append((term, lambda me: ((me >> 3 ^ flip) * 4 + (me >> 1 & 3))))
        for term in (row, column):
            found.append((term, lambda me: (me >> 3 ^ flip)))
        return [
            (term, step_block[0], lambda i, me, at=at: step_block[1](i, at(me)))
            for term, at in found
        ]

    def far(self):
        net = self.net
        if not self.plain:
            self.state, sent = net.scatter_step(self.state, net.outer, self.me)
            return sent
        parts = 4
        lanes = self.columns // parts
        step_block = ((1, self.rows, lanes), lambda i, at: (at, 0, i))
        masks = net.masks(net.outer)
        ins, groups = [], []
        for mask in masks:
            groups.append([(len(ins) + j, (None, None)) for j in range(4)])
            ins += self.sources(mask >> 3, step_block)
        out = ((1, self.rows, self.columns), BF16, step_block[0], lambda i, me: (0, 0, i))
        sent = sum_call(self.me, "far_sum", parts, ins, groups, [out] * len(masks))
        self.terms += [net.swap(part, mask) for part, mask in zip(sent, masks)]
        return sent

    def end(self, lots, unit):
        if not self.plain:
            total = self.net.scatter_end(self.state)
            results, start = [], 0
            for count in lots:
                blocks = [
                    total[(start + j) * unit : (start + j + 1) * unit] for j in range(count)
                ]
                results.append(jnp.concatenate(blocks, axis=1))
                start += count
            return results
        step_block = ((1, unit, self.columns), lambda i, at: (at, i, 0))
        ins = self.sources(0, step_block)
        ins += [(term, step_block[0], lambda i, me: (0, i, 0)) for term in self.terms[4:]]
        outs, bounds, start = [], [], 0
        for count in lots:

            def place(i, me, start=start, count=count):
                return (0, jnp.clip(i - start, 0, count - 1))

            outs.append(((unit, count * self.columns), F32, (unit, self.columns), place))
            bounds.append((start, start + count))
            start += count

        def body(me_ref, *refs):
            step, addends = pl.program_id(0), refs[: len(ins)]
            total = addends[0][0].astype(F32)
            for ref in addends[1:]:
                total = total + ref[0].astype(F32)
            for out_ref, (low, high) in zip(refs[len(ins) :], bounds):

                @pl.when((step >= low) & (step < high))
                def _():
                    out_ref[...] = total

        return sum_call(self.me, "end_sum", start, ins, None, outs, body)


def pack_body(step, me_ref, lines_ref, inner_ref, *refs):
    shards, out_ref = refs[:-1], refs[-1]
    start = 0
    for ref in shards:
        out_ref[start : start + ref.shape[0]] = ref[...]
        start += ref.shape[0]
    me, width = me_ref[0], out_ref.shape[1]

    def spread(ref, offset):
        count = ref.shape[1]
        lanes = lax.broadcasted_iota(jnp.int32, (count, width), 1)
        spots = lax.broadcasted_iota(jnp.int32, (count, width), 0) + offset
        return matmul(ref[...], jnp.where(lanes == spots, 1.0, 0.0).astype(BF16))

    vectors = spread(lines_ref, me * step)
    place = me * inner_ref.shape[1]
    inner = spread(inner_ref, lax.rem(place, width))
    row = lax.broadcasted_iota(jnp.int32, inner.shape, 0)
    inner = jnp.where(row == place // width, inner, 0.0)
    out_ref[start:] = jnp.concatenate([vectors, inner]).astype(BF16)


def pack(me, shards, lines, inner):
    step, width = shards[0].shape
    return call(
        functools.partial(pack_body, step),
        "pack",
        (1,),
        [(me.reshape(1), SMEM_SPEC)]
        + [(array, full_spec(array.shape)) for array in (lines, inner, *shards)],
        [((len(shards) * step + 16, width), BF16, full_spec((len(shards) * step + 16, width)))],
        [],
        1,
    )[0]


def project_body(weights, tile, row_length, me_ref, *refs):
    count = len(weights.arrays)
    arrays, refs = refs[:count], refs[count:]
    feats_ref, x_ref = refs[:2]
    temb_ref, lines_ref, low_ref, q_ref, k_ref, v_ref = refs[2:8]
    tw, qw, kw, vw, lw, sems = refs[8:14]
    me, step = me_ref[0], pl.program_id(0)

    @pl.when(step == 0)
    def _():
        for w, held in enumerate((tw, qw, kw, vw, lw)):
            weights.start(w, me, arrays, held, sems)
        weights.wait(0, me, arrays, tw, sems)
        temb_ref[...] = matmul(feats_ref[...], flat(tw[...]))
        weights.wait(4, me, arrays, lw, sems)
        lines_ref[...] = jnp.sum(lw[...].astype(F32), axis=0)
        for w, held in ((1, qw), (2, kw), (3, vw)):
            weights.wait(w, me, arrays, held, sems)

    row = step * tile // row_length
    low = (x_ref[...].astype(F32) + temb_ref[pl.ds(row, 1), :]).astype(BF16)
    low_ref[...] = low
    q_ref[...] = (matmul(low, flat(qw[...])) + lines_ref[0:1]).astype(BF16)
    k_ref[...] = matmul(low, flat(kw[...])).astype(BF16)
    v_ref[...] = (matmul(low, flat(vw[...])) + lines_ref[1:2]).astype(BF16)


def project(net, me, flow, feats, x, row_length):
    tokens, width = x.shape
    tile = min(256, row_length)
    r = width // net.n
    weights = Weights(net, me, [(flow, w * r, r) for w in range(4)] + [(flow, 4 * r, 16)])
    ins = (
        [(me.reshape(1), SMEM_SPEC)]
        + [(array, ANY_SPEC) for array in weights.arrays]
        + [(feats, full_spec(feats.shape)), (x, tile_spec(tile, width))]
    )
    outs = [(feats.shape, F32, full_spec(feats.shape))]
    outs += [((16, width), F32, full_spec((16, width)))]
    outs += [((tokens, width), BF16, tile_spec(tile, width))] * 4
    return call(
        functools.partial(project_body, weights, tile, row_length),
        "project",
        (tokens // tile,),
        ins,
        outs,
        weights.scratch(),
        14,
    )


def same_document(segc_ref, segr_ref, bias_ref, block):
    @pl.when(block == 0)
    def _():
        bias_ref[...] = jnp.where(segc_ref[0] == segr_ref[0], 0.0, -1e30)


def own_lanes(shape, head, head_dim):
    lanes = lax.broadcasted_iota(jnp.int32, shape, len(shape) - 1)
    return (lanes // head_dim) == head


def attend_body(head_dim, segc_ref, segr_ref, q_ref, k_ref, v_ref, out_ref, log_ref, bias_ref):
    same_document(segc_ref, segr_ref, bias_ref, pl.program_id(1))
    queries, key_rows, values = q_ref[...], k_ref[...], v_ref[...]
    scale = 1.0 / math.sqrt(head_dim)
    per = queries.shape[1] // head_dim
    total = None
    for head in range(per):
        mine = own_lanes(queries.shape, head, head_dim)
        keys_own = jnp.where(mine, key_rows * BF16(scale), BF16(0))
        scores = matmul_right(keys_own, queries) + bias_ref[...]
        top = jnp.max(scores, axis=0, keepdims=True)
        raised = jnp.exp(scores - top)
        amount = jnp.sum(raised, axis=0, keepdims=True)
        log_ref[0, 0, pl.ds(head, 1), :] = top + jnp.log(amount)
        soft_low = (raised * (1.0 / amount)).astype(BF16)
        context = matmul_left(soft_low, values)
        total = context if total is None else jnp.where(mine, context, total)
    out_ref[...] = total.astype(BF16)


def attend_back_body(
    head_dim, segc_ref, segr_ref, q_ref, k_ref, v_ref, log_ref, g_ref, gq_ref, gk_ref, gv_ref, sums_ref, bias_ref
):
    same_document(segc_ref, segr_ref, bias_ref, pl.program_id(1))
    queries, key_rows, values, grads = q_ref[...], k_ref[...], v_ref[...], g_ref[...]
    scale = 1.0 / math.sqrt(head_dim)
    per = queries.shape[1] // head_dim
    totals = None
    for head in range(per):
        mine = own_lanes(queries.shape, head, head_dim)
        keys_own = jnp.where(mine, key_rows * BF16(scale), BF16(0))
        scores = matmul_right(keys_own, queries) + bias_ref[...]
        soft = jnp.exp(scores - log_ref[0, 0, pl.ds(head, 1), :])
        grad_soft = matmul_right(jnp.where(mine, values, BF16(0)), grads)
        inner_sum = jnp.sum(soft * grad_soft, axis=0, keepdims=True)
        grad_scores = (soft * (grad_soft - inner_sum)).astype(BF16)
        parts = (
            matmul_left(grad_scores, key_rows),
            matmul(grad_scores, queries),
            matmul(soft.astype(BF16), grads),
        )
        if totals is None:
            totals = parts
        else:
            totals = tuple(jnp.where(mine, part, total) for part, total in zip(parts, totals))
    gq = (totals[0] * scale).astype(BF16)
    gv = totals[2].astype(BF16)
    gq_ref[...] = gq
    gk_ref[...] = (totals[1] * scale).astype(BF16)
    gv_ref[...] = gv
    sums = [jnp.sum(part.astype(F32), axis=0, keepdims=True) for part in (gq, gv)]
    sums_ref[...] = jnp.concatenate(sums + [jnp.zeros_like(sums[0])] * 6)


def attention_args(segments, start, lanes, head_dim):
    row_length, per = segments.shape[1], lanes // head_dim
    segc = pl.BlockSpec((1, row_length, 1), lambda i, j: (start + i, 0, 0))
    segr = pl.BlockSpec((1, 1, row_length), lambda i, j: (start + i, 0, 0))
    block = pl.BlockSpec((row_length, lanes), lambda i, j: (start + i, j))
    log_spec = pl.BlockSpec((1, 1, per, row_length), lambda i, j: (start + i, j, 0, 0))
    return [(segments[:, :, None], segc), (segments[:, None, :], segr)], block, log_spec


def attend(queries, key_rows, values, segments, lanes=128):
    rows, row_length = segments.shape
    tokens, width = queries.shape
    head_dim = width // H
    blocks, per = width // lanes, lanes // head_dim
    masks, block, log_spec = attention_args(segments, 0, lanes, head_dim)
    return call(
        functools.partial(attend_body, head_dim),
        "attend",
        (rows, blocks),
        masks + [(array, block) for array in (queries, key_rows, values)],
        [
            ((tokens, width), BF16, block),
            ((rows, blocks, per, row_length), F32, log_spec),
        ],
        [pltpu.VMEM((row_length, row_length), F32)],
        24,
    )


def attend_back(queries, key_rows, values, segments, log_total, grad_context, row, bases=(), lanes=128):
    rows, row_length = segments.shape
    tokens, width = queries.shape
    head_dim = width // H
    masks, block, log_spec = attention_args(segments, row, lanes, head_dim)
    return call(
        functools.partial(attend_back_body, head_dim),
        "attend_back",
        (1, width // lanes),
        masks
        + [(array, block) for array in (queries, key_rows, values)]
        + [(log_total, log_spec), (grad_context, block)],
        [((tokens, width), BF16, block)] * 3
        + [((8, width), F32, pl.BlockSpec((8, lanes), lambda i, j: (0, j)))],
        [pltpu.VMEM((row_length, row_length), F32)],
        19,
        bases,
    )


def add_to(ref, value, step):
    part = jnp.sum(value, axis=0, keepdims=True)

    @pl.when(step == 0)
    def _():
        ref[...] = part

    @pl.when(step != 0)
    def _():
        ref[...] += part


def add_lines(ref, values, step):
    zero = jnp.zeros((1, ref.shape[1]), F32)
    sums = {line: jnp.sum(value, axis=0, keepdims=True) for line, value in values.items()}
    part = jnp.concatenate([sums.get(line, zero) for line in range(ref.shape[0])])

    @pl.when(step == 0)
    def _():
        ref[...] = part

    @pl.when(step != 0)
    def _():
        ref[...] += part


def ffn_in_body(weights, row, chunk, me_ref, *refs):
    count = len(weights.arrays)
    arrays, refs = refs[:count], refs[count:]
    context_ref, x_ref, temb_ref, lines_ref = refs[:4]
    first_low_ref, normed_ref, spread_ref, active_ref, slope_ref = refs[4:9]
    ow, iws, sems = refs[9], refs[10:14], refs[14]
    me, step = me_ref[0], pl.program_id(0)

    @pl.when(step == 0)
    def _():
        for w, held in enumerate((ow,) + iws):
            weights.start(w, me, arrays, held, sems)
        weights.wait(0, me, arrays, ow, sems)

    stream = x_ref[...].astype(F32) + temb_ref[row : row + 1, :]
    mixed = stream + (matmul(context_ref[...], flat(ow[...])) + lines_ref[2:3])
    normed, spread = normalize(mixed)
    normed_ref[...] = normed
    spread_ref[...] = spread
    first = normed * lines_ref[4:5] + lines_ref[5:6]
    first_low_ref[...] = first.astype(BF16)
    width = ow.shape[2]
    for k, iw in enumerate(iws):

        @pl.when(step == 0)
        def _():
            weights.wait(k + 1, me, arrays, iw, sems)

        @pl.loop(0, width // chunk)
        def _(j):
            inner = pl.ds(pl.multiple_of(j * chunk, chunk), chunk)
            columns = pl.ds(pl.multiple_of(k * width + j * chunk, chunk), chunk)
            pre = matmul(first_low_ref[...], flat(iw[:, :, inner])) + lines_ref[8 + k : 9 + k, inner]
            normal_cdf = 0.5 * (1.0 + lax.erf(pre * INV_ROOT_TWO))
            normal_pdf = jnp.exp(-0.5 * pre * pre) * INV_ROOT_TAU
            active_ref[:, columns] = (pre * normal_cdf).astype(BF16)
            slope_ref[:, columns] = (normal_cdf + pre * normal_pdf).astype(BF16)


def ffn_in(net, me, flow, context, x, temb, lines, hidden, row, row_length, bases=(), tile=256, chunk=512):
    tokens, width = x.shape
    r = width // net.n
    weights = Weights(net, me, [(flow, w * r, r) for w in range(1 + hidden // width)])
    tile = min(tile, row_length)
    start = row * (row_length // tile)
    tiled, wide, thin = (
        pl.BlockSpec((tile, columns), lambda i: (start + i, 0)) for columns in (width, hidden, 1)
    )
    ins = (
        [(me.reshape(1), SMEM_SPEC)]
        + [(array, ANY_SPEC) for array in weights.arrays]
        + [(context, tiled), (x, tiled)]
        + [(array, full_spec(array.shape)) for array in (temb, lines)]
    )
    outs = [
        ((tokens, width), BF16, tiled),
        ((tokens, width), F32, tiled),
        ((tokens, 1), F32, thin),
        ((tokens, hidden), BF16, wide),
        ((tokens, hidden), BF16, wide),
    ]
    return call(
        functools.partial(ffn_in_body, weights, row, chunk),
        "ffn_in",
        (row_length // tile,),
        ins,
        outs,
        weights.scratch(),
        16,
        bases,
    )


def ffn_out_body(weights, me_ref, *refs):
    count = len(weights.arrays)
    arrays, refs = refs[:count], refs[count:]
    active_ref, normed_ref, cot_ref, lines_ref = refs[:4]
    out_ref, gs_ref, gs_low_ref, sums_ref = refs[4:8]
    uw, sems = refs[8:10]
    me, step = me_ref[0], pl.program_id(0)

    @pl.when(step == 0)
    def _():
        weights.start(0, me, arrays, uw, sems)
        weights.wait(0, me, arrays, uw, sems)

    first = normed_ref[...] * lines_ref[4:5] + lines_ref[5:6]
    second = first + (matmul(active_ref[...], flat(uw[...])) + lines_ref[3:4])
    normed_second, spread_second = normalize(second)
    out_ref[...] = (normed_second * lines_ref[6:7] + lines_ref[7:8]).astype(BF16)
    grad_out = cot_ref[...].astype(F32)
    grad_second = norm_back(grad_out * lines_ref[6:7], normed_second, spread_second)
    gs_ref[...] = grad_second
    low = grad_second.astype(BF16)
    gs_low_ref[...] = low
    add_lines(sums_ref, {3: low.astype(F32), 6: grad_out * normed_second, 7: grad_out}, step)


def ffn_out(net, me, flow, active, normed, cotangent, vectors, tile=256):
    tokens, width = normed.shape
    hidden = active.shape[1]
    weights = Weights(net, me, [(flow, 0, hidden // net.n)])
    tiled, wide = tile_spec(tile, width), tile_spec(tile, hidden)
    ins = (
        [(me.reshape(1), SMEM_SPEC)]
        + [(array, ANY_SPEC) for array in weights.arrays]
        + [(active, wide), (normed, tiled), (cotangent, tiled)]
        + [(vector, full_spec(vector.shape)) for vector in vectors]
    )
    outs = [
        ((tokens, width), BF16, tiled),
        ((tokens, width), F32, tiled),
        ((tokens, width), BF16, tiled),
        ((8, width), F32, full_spec((8, width))),
    ]
    return call(
        functools.partial(ffn_out_body, weights),
        "ffn_out",
        (tokens // tile,),
        ins,
        outs,
        weights.scratch(),
        20,
    )


def ffn_back_body(weights, chunk, me_ref, *refs):
    count = len(weights.arrays)
    arrays, refs = refs[:count], refs[count:]
    (gs_ref, gs_low_ref, slope_ref, normed_ref, spread_ref, lines_ref) = refs[:6]
    (gi_ref, gm_ref, gm_low_ref, gc_ref, ibg_ref, sums_ref) = refs[6:12]
    uw, ow, iws, sems, acc_ref = refs[12], refs[13], refs[14:18], refs[18], refs[19]
    me, step = me_ref[0], pl.program_id(0)
    helds = (uw, ow) + iws

    @pl.when(step == 0)
    def _():
        for w in (0, 2, 3, 4, 5, 1):
            weights.start(w, me, arrays, helds[w], sems)
        weights.wait(0, me, arrays, uw, sems)

    acc_ref[...] = gs_ref[...]
    unit = uw.shape[1]
    width = ow.shape[2]
    for k, iw in enumerate(iws):

        @pl.when(step == 0)
        def _():
            weights.wait(k + 2, me, arrays, iw, sems)

        @pl.loop(0, width // chunk)
        def _(j):
            inner = pl.ds(pl.multiple_of(j * chunk, chunk), chunk)
            columns = pl.ds(pl.multiple_of(k * width + j * chunk, chunk), chunk)
            span = chunk // unit
            held = flat(uw[pl.ds(k * (width // unit) + j * span, span)])
            grad_active = matmul_right(gs_low_ref[...], held)
            low = (grad_active * slope_ref[:, columns].astype(F32)).astype(BF16)
            gi_ref[:, columns] = low
            acc_ref[...] += matmul_right(low, flat(iw[:, :, inner]))

    add_to(ibg_ref, gi_ref[...].astype(F32), step)
    grad_first, normed = acc_ref[...], normed_ref[...]
    grad_mixed = norm_back(grad_first * lines_ref[4:5], normed, spread_ref[...])
    gm_ref[...] = grad_mixed
    low = grad_mixed.astype(BF16)
    gm_low_ref[...] = low
    add_lines(sums_ref, {2: low.astype(F32), 4: grad_first * normed, 5: grad_first}, step)

    @pl.when(step == 0)
    def _():
        weights.wait(1, me, arrays, ow, sems)

    gc_ref[...] = matmul_right(low, flat(ow[...])).astype(BF16)


def ffn_back(net, me, flow_u, flow_io, gs, gs_low, slope, normed, spread, lines, tile=256, chunk=512):
    tokens, width = gs.shape
    hidden = slope.shape[1]
    r = width // net.n
    weights = Weights(
        net,
        me,
        [(flow_u, 0, hidden // net.n)]
        + [(flow_io, w * r, r) for w in range(1 + hidden // width)],
    )
    tile = min(tile, tokens)
    tiled, wide = tile_spec(tile, width), tile_spec(tile, hidden)
    ins = (
        [(me.reshape(1), SMEM_SPEC)]
        + [(array, ANY_SPEC) for array in weights.arrays]
        + [(gs, tiled), (gs_low, tiled), (slope, wide), (normed, tiled)]
        + [(spread, tile_spec(tile, 1)), (lines, full_spec(lines.shape))]
    )
    outs = [
        ((tokens, hidden), BF16, wide),
        ((tokens, width), F32, tiled),
        ((tokens, width), BF16, tiled),
        ((tokens, width), BF16, tiled),
        ((1, hidden), F32, full_spec((1, hidden))),
        ((8, width), F32, full_spec((8, width))),
    ]
    return call(
        functools.partial(ffn_back_body, weights, chunk),
        "ffn_back",
        (tokens // tile,),
        ins,
        outs,
        weights.scratch() + [pltpu.VMEM((tile, width), F32)],
        45,
    )


def deal(me_ref, total, rows, keep_ref, send_ref, kind=0):
    core = me_ref[0] & 1
    total = total.reshape(-1, 2, rows, total.shape[-1])
    low, high = total[:, 0], total[:, 1]
    place = slice(kind * rows, (kind + 1) * rows)
    keep_ref[:, place] = jnp.where(core == 0, low, high).astype(BF16)
    send_ref[:, place] = jnp.where(core == 0, high, low).astype(BF16)


def product_body(rows, me_ref, a_ref, b_ref, keep_ref, send_ref):
    deal(me_ref, matmul_left(a_ref[...], b_ref[...]), rows, keep_ref, send_ref)


def product(net, me, left, right, tile=512):
    tokens, width = left.shape
    columns = right.shape[1]
    rows = width // net.n
    shape = (net.n // 2, rows, columns)
    block = pl.BlockSpec((tile // (2 * rows), rows, columns), lambda i: (i, 0, 0))
    return call(
        functools.partial(product_body, rows),
        "product",
        (width // tile,),
        [
            (me.reshape(1), SMEM_SPEC),
            (left, pl.BlockSpec((tokens, tile), lambda i: (0, i))),
            (right, full_spec((tokens, columns))),
        ],
        [(shape, BF16, block), (shape, BF16, block)],
        [],
        15,
    )


def inner_body(rows, me_ref, context_ref, first_ref, gm_ref, gi_ref, keep_ref, send_ref):
    total = matmul_left(first_ref[...], gi_ref[...])
    width = gm_ref.shape[1]
    deal(me_ref, matmul_left(context_ref[...], gm_ref[...]), rows, keep_ref, send_ref, 0)
    for k in range(total.shape[1] // width):
        part = total[:, k * width : (k + 1) * width]
        deal(me_ref, part, rows, keep_ref, send_ref, k + 1)


def inner_product(net, me, context, first_low, gm_low, gi, tile=256):
    tokens, width = context.shape
    hidden = gi.shape[1]
    rows = width // net.n
    kinds = 1 + hidden // width
    shape = (net.n // 2, kinds * rows, width)
    block = pl.BlockSpec((tile // (2 * rows), kinds * rows, width), lambda i: (i, 0, 0))
    left = pl.BlockSpec((tokens, tile), lambda i: (0, i))
    return call(
        functools.partial(inner_body, rows),
        "inner_product",
        (width // tile,),
        [
            (me.reshape(1), SMEM_SPEC),
            (context, left),
            (first_low, left),
            (gm_low, full_spec((tokens, width))),
            (gi, full_spec((tokens, hidden))),
        ],
        [(shape, BF16, block), (shape, BF16, block)],
        [],
        18,
    )


def triple_body(rows, me_ref, lines_ref, a_ref, q_ref, k_ref, v_ref, keep_ref, send_ref):
    for w, ref in enumerate((q_ref, k_ref, v_ref)):
        deal(me_ref, matmul_left(a_ref[...], ref[...]), rows, keep_ref, send_ref, w)
    core = me_ref[0] & 1
    low, high = lines_ref[:, 0:8], lines_ref[:, 8:16]
    place = slice(3 * rows, 3 * rows + 8)
    keep_ref[:, place] = jnp.where(core == 0, low, high).astype(BF16)
    send_ref[:, place] = jnp.where(core == 0, high, low).astype(BF16)


def triple_product(net, me, lines, left, gq, gk, gv, tile=256):
    tokens, width = left.shape
    rows = width // net.n
    shape = (net.n // 2, 3 * rows + 8, width)
    chips = tile // (2 * rows)
    block = pl.BlockSpec((chips, 3 * rows + 8, width), lambda i: (i, 0, 0))
    full = full_spec((tokens, width))
    return call(
        functools.partial(triple_body, rows),
        "triple_product",
        (width // tile,),
        [
            (me.reshape(1), SMEM_SPEC),
            (lines, pl.BlockSpec((chips, 16, width), lambda i: (i, 0, 0))),
            (left, pl.BlockSpec((tokens, tile), lambda i: (0, i))),
            (gq, full),
            (gk, full),
            (gv, full),
        ],
        [(shape, BF16, block), (shape, BF16, block)],
        [],
        13,
    )


def stream_back_body(weights, me_ref, *refs):
    count = len(weights.arrays)
    arrays, refs = refs[:count], refs[count:]
    gm_ref, gq_ref, gk_ref, gv_ref = refs[:4]
    out_ref, gt_ref = refs[4:6]
    qw, kw, vw, sems = refs[6:10]
    me, step = me_ref[0], pl.program_id(0)

    @pl.when(step == 0)
    def _():
        for w, held in enumerate((qw, kw, vw)):
            weights.start(w, me, arrays, held, sems)
        for w, held in enumerate((qw, kw, vw)):
            weights.wait(w, me, arrays, held, sems)

    total = (
        gm_ref[...]
        + matmul_right(gq_ref[...], flat(qw[...]))
        + matmul_right(gk_ref[...], flat(kw[...]))
        + matmul_right(gv_ref[...], flat(vw[...]))
    )
    out_ref[...] = total
    add_to(gt_ref, total, step)


def stream_back(net, me, flow, gm, gq, gk, gv, row, row_length, base=None, tile=256):
    tokens, width = gm.shape
    tile = min(tile, row_length)
    r = width // net.n
    weights = Weights(net, me, [(flow, w * r, r) for w in (1, 2, 3)])
    start = row * (row_length // tile)
    tiled = pl.BlockSpec((tile, width), lambda i: (start + i, 0))
    ins = (
        [(me.reshape(1), SMEM_SPEC)]
        + [(array, ANY_SPEC) for array in weights.arrays]
        + [(array, tiled) for array in (gm, gq, gk, gv)]
    )
    return call(
        functools.partial(stream_back_body, weights),
        "stream_back",
        (row_length // tile,),
        ins,
        [((tokens, width), F32, tiled), ((1, width), F32, full_spec((1, width)))],
        weights.scratch(),
        10,
        () if base is None else (base,),
    )


def in_order(net, me, sources, blocks):
    order = jnp.asarray(sources, jnp.int32)
    spot = jnp.zeros((net.n,), jnp.int32).at[order].set(jnp.arange(net.n, dtype=jnp.int32))
    return blocks[spot[jnp.arange(net.n) ^ me]]


def held(state, others):
    return after(state[0], others), state[1]


def stream_ends(state, unit):
    if not state.plain:
        total = state.net.scatter_end(state.state)
        return [total[w * unit : (w + 1) * unit] for w in range(3)] + [total[3 * unit]]
    rows, columns = state.rows, state.columns
    step_block = ((1, rows, columns), lambda i, at: (at, 0, 0))
    ins = state.sources(0, step_block)
    ins += [(term, step_block[0], lambda i, me: (0, 0, 0)) for term in state.terms[4:]]
    shapes = [(unit, columns)] * 3 + [(8, columns)]
    outs = [(shape, F32, shape, lambda i, me: (0, 0)) for shape in shapes]

    def body(me_ref, *refs):
        total = refs[0][0].astype(F32)
        for ref in refs[1 : len(ins)]:
            total = total + ref[0].astype(F32)
        start = 0
        for out_ref in refs[len(ins) :]:
            count = out_ref.shape[0]
            out_ref[...] = total[start : start + count]
            start += count

    results = sum_call(state.me, "stream_end", 1, ins, None, outs, body)
    return list(results[:3]) + [results[3][0]]


def on_device(
    net,
    inputs,
    timesteps,
    segments,
    cotangent,
    query_weight,
    key_weight,
    value_weight,
    output_weight,
    inner_weight,
    outer_weight,
    time_weight,
    *vectors,
):
    n = net.n
    me = lax.axis_index("fsdp").astype(jnp.int32)
    batch_count, row_count, row_length, model_width = inputs.shape
    rows = batch_count * row_count
    tokens = rows * row_length
    feats = features(timesteps.reshape(rows)).astype(BF16)
    order = (0, 1, 2, 4, 5, 6, 7, 8, 3)
    sizes = [vectors[i].shape[0] for i in order]
    small = sum(
        jnp.pad(vectors[i].astype(F32)[None], ((line, 7 - line), (0, 0)))
        for line, i in enumerate(order[:8])
    )
    inner_line = jnp.broadcast_to(vectors[3][None], (8, sizes[-1]))
    r = model_width // n

    shards = (time_weight, query_weight, key_weight, value_weight)
    far = net.gather_far(pack(me, shards, small.astype(BF16), inner_line))
    hidden = inner_weight.shape[1]
    inner_blocks = [
        inner_weight[:, start : start + model_width] for start in range(0, hidden, model_width)
    ]
    shard_io = after(jnp.concatenate([output_weight] + inner_blocks), far)
    far_io = net.gather_far(shard_io)
    far = net.stacked(far)
    near = net.gather_near(far)
    near, far_io = after((near, far_io), ())
    pieces, corners, _ = net.gather_corner(far, near)
    flow = net.gather_core(pieces)
    far_io, corners = after((net.stacked(far_io), corners), ())
    near_io = net.gather_near(far_io)
    flow += net.gather_core(corners)

    segments = segments.reshape(rows, row_length)
    x = inputs.reshape(tokens, model_width)
    feats_in = after(feats, far_io)
    temb, lines, stream_low, queries, key_rows, values = project(
        net, me, flow, feats_in, x, row_length
    )
    near_io, queries, shard_u = after((near_io, queries, outer_weight), ())
    pieces, corners, sent = net.gather_corner(far_io, near_io)
    flow_io = net.gather_core(pieces[:1])
    far_u = net.gather_far(shard_u)
    queries = after(queries, sent)
    context, log_total = attend(queries, key_rows, values, segments)
    far_u, corners, context = after((far_u, corners, context), ())
    flow_io += net.gather_core(corners) + net.gather_core(pieces[1:])
    far_u = net.stacked(far_u)
    near_u = net.gather_near(far_u)
    context = after(context, far_u)
    fed, sent = (), ()
    for row in range(rows):
        if row == 1:
            near_u, fed = after((near_u, fed), ())
            pieces, corners, sent = net.gather_corner(far_u, near_u)
            fed = after(fed, sent)
        fed = ffn_in(
            net, me, flow_io, context, x, temb, lines, hidden, row, row_length, fed
        )
    first_low, normed_first, spread_first, active_low, slope = fed
    corners, active_low = after((corners, active_low), ())
    flow_u = net.gather_core(pieces) + net.gather_core(corners)
    (
        layer_output,
        grad_second,
        grad_second_low,
        sums_out,
    ) = ffn_out(
        net,
        me,
        flow_u,
        active_low,
        normed_first,
        cotangent.reshape(tokens, model_width),
        (lines,),
    )
    outer_halves = product(net, me, active_low, grad_second_low)
    outer_sum = Reduction(net, me, *outer_halves)
    slope = after(slope, outer_halves)
    (
        grad_inner_low,
        grad_mixed,
        grad_mixed_low,
        grad_context,
        inner_bias_grad,
        sums_back,
    ) = ffn_back(
        net,
        me,
        flow_u,
        flow_io,
        grad_second,
        grad_second_low,
        slope,
        normed_first,
        spread_first,
        lines,
    )
    sent = outer_sum.hold(grad_mixed_low).corner()
    grad_mixed_low = after(grad_mixed_low, sent)
    inner_halves = inner_product(net, me, context, first_low, grad_mixed_low, grad_inner_low)
    inner_sum = Reduction(net, me, *inner_halves)
    sent = outer_sum.hold(inner_halves).near()
    grad_context = after(grad_context, (inner_halves, sent))
    back = (queries, key_rows, values, segments, log_total, grad_context)
    found, sums_rows = None, 0.0
    for row in range(rows):
        if row == 1:
            sent = inner_sum.hold(found[1]).corner() + list(outer_sum.hold(found[1]).far())
            found = after(found, sent)
        found = attend_back(*back, row, found or ())
        sums_rows += found[3]
        found = found[:3]
    grad_queries, grad_keys, grad_values = found
    sent = inner_sum.hold(grad_queries).near()
    (outer_weight_grad,) = outer_sum.hold(grad_queries).end([1], outer_weight.shape[0])
    sums = sums_rows + sums_out + sums_back
    sums = sums.reshape(8, n, r).transpose(1, 0, 2).reshape(n, 8 * r)
    sums = jnp.concatenate([sums, inner_bias_grad.reshape(n, -1)], axis=1)
    sums = jnp.pad(sums, ((0, 0), (0, model_width - sums.shape[1]))).astype(BF16)
    sums = jnp.broadcast_to(sums[:, None], (n, 8, model_width)).reshape(n // 2, 16, model_width)
    stream_low, sums = after((stream_low, sums), (sent, outer_weight_grad))
    stream_halves = triple_product(
        net, me, sums, stream_low, grad_queries, grad_keys, grad_values
    )
    stream_sum = Reduction(net, me, *stream_halves)
    grad_mixed = after(grad_mixed, stream_halves)
    back = (flow, grad_mixed, grad_queries, grad_keys, grad_values)
    grad_stream, part = stream_back(net, me, *back, 0, row_length)
    grad_temb = [part]
    for row in range(1, rows):
        if row == 1:
            sent = stream_sum.hold(part).corner() + list(inner_sum.hold(part).far())
            grad_stream = after(grad_stream, sent)
        grad_stream, part = stream_back(net, me, *back, row, row_length, grad_stream)
        grad_temb.append(part)
    sent = stream_sum.hold(part).near()
    ends = jnp.concatenate([feats.astype(F32), jnp.concatenate(grad_temb)], axis=1)[None]
    output_weight_grad, inner_weight_grad = inner_sum.hold(sent).end([1, hidden // model_width], r)
    ends = after(ends, output_weight_grad)
    sources, ends = net.gather_round([0], ends, net.masks(net.core))
    sources, ends = net.gather_round(sources, ends, net.inner_masks())
    stream_sum.far()
    sources, ends = net.gather_round(sources, ends, net.masks(net.outer))
    ends = in_order(net, me, sources, ends).reshape(n * rows, 2 * model_width)
    query_weight_grad, key_weight_grad, value_weight_grad, vector_sums = stream_ends(
        stream_sum, r
    )
    feats_all, temb_all = ends[:, :model_width], ends[:, model_width:]
    own = model_width // n
    feats_own = lax.dynamic_slice_in_dim(feats_all, me * own, own, 1)
    time_weight_grad = lax.dot_general(
        feats_own,
        temb_all,
        (((0,), (0,)), ((), ())),
        precision=lax.Precision.HIGHEST,
    )
    parts, start = {}, 0
    for i, size in zip(order, sizes):
        parts[i] = vector_sums[start : start + size]
        start += size
    vector_outs = [parts[i] for i in range(len(order))]

    shape = inputs.shape
    return (
        layer_output.reshape(shape),
        grad_stream.reshape(shape),
        query_weight_grad,
        key_weight_grad,
        value_weight_grad,
        output_weight_grad,
        inner_weight_grad,
        outer_weight_grad,
        time_weight_grad,
    ) + tuple(vector_outs)


def solution(mesh):
    matrix, vector = P("fsdp", None), P("fsdp")
    batch = P(None, "fsdp", None, None)
    return jax.shard_map(
        functools.partial(on_device, Net(mesh.shape["fsdp"])),
        mesh=mesh,
        in_specs=(batch, P(None, "fsdp"), P(None, "fsdp", None), batch)
        + (matrix,) * 7
        + (vector,) * 9,
        out_specs=(batch, batch) + (matrix,) * 7 + (vector,) * 9,
        check_vma=False,
    )
```

```python
import functools
import math

import jax
import jax.numpy as jnp
from jax import lax
from jax.experimental import pallas as pl
from jax.experimental.pallas import tpu as pltpu
from jax.sharding import PartitionSpec as P

D = 1024
H = 16


INV_ROOT_TWO = 0.7071067811865476
INV_ROOT_TAU = 0.3989422804014327
F32 = jnp.float32
BF16 = jnp.bfloat16


def matmul(operand, factor):
    return jnp.dot(operand, factor, preferred_element_type=F32)


def matmul_left(operand, factor):
    return lax.dot_general(
        operand, factor, (((0,), (0,)), ((), ())), preferred_element_type=F32
    )


def matmul_right(operand, factor):
    return lax.dot_general(
        operand, factor, (((1,), (1,)), ((), ())), preferred_element_type=F32
    )


def features(step_ids):
    half_width = D // 2
    freqs = jnp.exp(-math.log(10000.0) * jnp.arange(half_width, dtype=F32) / half_width)
    angles = step_ids.astype(F32)[..., None] * freqs
    return jnp.concatenate([jnp.sin(angles), jnp.cos(angles)], axis=-1)


def normalize(values_in):
    center = values_in - jnp.mean(values_in, axis=-1, keepdims=True)
    spread = lax.rsqrt(jnp.mean(center * center, axis=-1, keepdims=True) + 1e-05)
    return (center * spread, spread)


def norm_back(grad_normed, normed, spread):
    mean_grad = jnp.mean(grad_normed, axis=-1, keepdims=True)
    mean_cross = jnp.mean(grad_normed * normed, axis=-1, keepdims=True)
    return spread * (grad_normed - mean_grad - normed * mean_cross)


def halves_body(low_in, high_in, low_out, high_out):
    low_out[...] = low_in[...]
    high_out[...] = high_in[...]


def halves(low_of, high_of):
    count, half = low_of.shape[0], low_of.shape[0] // 2
    block = (1,) + low_of.shape[1:]
    return pl.pallas_call(
        halves_body,
        grid=(half,),
        in_specs=[
            pl.BlockSpec(block, lambda i: (i, 0, 0)),
            pl.BlockSpec(block, lambda i: (half + i, 0, 0)),
        ],
        out_specs=[pl.BlockSpec(block, lambda i: (i, 0, 0))] * 2,
        out_shape=[jax.ShapeDtypeStruct((half,) + low_of.shape[1:], low_of.dtype)] * 2,
        compiler_params=pltpu.CompilerParams(vmem_limit_bytes=60 << 20),
        cost_estimate=pl.CostEstimate(flops=1000, bytes_accessed=1000, transcendentals=0),
        name="halves",
    )(low_of, high_of)


class Net:
    def __init__(self, n):
        self.n = n
        self.bits = n.bit_length() - 1
        chip = self.bits - 1
        sizes = [(chip + 2 - i) // 3 for i in range(3)]
        groups, top = [], self.bits - 1
        for size in sizes:
            groups.append(tuple(range(top, top - size, -1)))
            top -= size
        self.outer, self.middle, self.near = groups
        self.core = (0,)

    def masks(self, group):
        found = []
        for pick in range(1, 1 << len(group)):
            mask = 0
            for place, bit in enumerate(group):
                if pick >> place & 1:
                    mask |= 1 << bit
            found.append(mask)
        return found

    def swap(self, array, mask):
        return lax.ppermute(array, "fsdp", [(i, i ^ mask) for i in range(self.n)])

    def gather_far(self, shard):
        return [shard] + [self.swap(shard, mask) for mask in self.masks(self.outer)]

    def stacked(self, parts):
        return ([0] + self.masks(self.outer), jnp.stack(parts))

    def gather_near(self, own):
        sources, array = own
        return [
            [(mask, self.swap(array, mask)) for mask in self.masks(group)]
            for group in (self.near, self.middle)
        ]

    def gather_corner(self, own, near):
        sources, half = own[0], len(own[0]) // 2
        pieces, corners, sent = [own], [], []
        for group in near:
            pieces += [([s ^ mask for s in sources], array) for mask, array in group]
        for mask_x, array_x in near[0]:
            for mask_y, array_y in near[1]:
                low, high = halves(array_y, array_x)
                sent += [low, high]
                corner = mask_x ^ mask_y
                corners.append(([s ^ corner for s in sources[:half]], self.swap(low, mask_x)))
                corners.append(([s ^ corner for s in sources[half:]], self.swap(high, mask_y)))
        return pieces, corners, sent

    def gather_core(self, pieces):
        return pieces + [([s ^ 1 for s in own], self.swap(array, 1)) for own, array in pieces]

    def inner_masks(self):
        near, middle = self.masks(self.near), self.masks(self.middle)
        return near + middle + [x | y for x in near for y in middle]

    def gather_round(self, sources, array, masks):
        array = jnp.concatenate([array] + [self.swap(array, mask) for mask in masks])
        return [source ^ mask for mask in [0] + masks for source in sources], array

    def take(self, term, bits, mask, present, me):
        present = list(present)
        for bit in bits:
            place = present.index(bit)
            low = 1 << (len(present) - 1 - place)
            value = (me >> bit & 1) ^ (mask >> bit & 1)
            rest = term.shape[1:]
            term = term.reshape((1 << place, 2, low) + rest)
            term = lax.dynamic_index_in_dim(term, value, 1, keepdims=False)
            term = term.reshape((low << place,) + rest)
            present.remove(bit)
        return term

    def scatter_core(self, halves):
        keep, send = halves
        return [keep, self.swap(send, 1)], list(range(self.bits - 1, 0, -1))

    def added(self, parts, dtype):
        parts = [part.astype(F32) for part in parts]
        return sum(parts[1:], parts[0]).astype(dtype)

    def scatter_step(self, state, group, me):
        terms, present = state
        sent = []
        for mask in self.masks(group):
            parts = [self.take(term, group, mask, present, me) for term in terms]
            sent.append(self.added(parts, terms[0].dtype))
        received = [self.swap(part, mask) for part, mask in zip(sent, self.masks(group))]
        terms = [self.take(term, group, 0, present, me) for term in terms] + received
        return (terms, [bit for bit in present if bit not in group]), sent

    def scatter_corner(self, state, me):
        terms, present = state
        left = [bit for bit in present if bit not in self.near]
        found, sent = [], []
        for mask_x in self.masks(self.near):
            row = [self.take(term, self.near, mask_x, present, me) for term in terms]
            for mask_y in self.masks(self.middle):
                parts = [self.take(term, self.middle, mask_y, left, me) for term in row]
                half = parts[0].shape[0] // 2
                low = self.added([part[:half] for part in parts], terms[0].dtype)
                high = self.added([part[half:] for part in parts], terms[0].dtype)
                sent += [low, high]
                found.append((mask_x, mask_y, self.swap(low, mask_x), self.swap(high, mask_y)))
        return found, sent

    def scatter_near(self, state, corner, me):
        terms, present = state
        left = [bit for bit in present if bit not in self.near]
        mine, received, sent = [self.take(t, self.near, 0, present, me) for t in terms], [], []
        for mask_x in self.masks(self.near):
            row = [self.take(term, self.near, mask_x, present, me) for term in terms]
            parts = [self.take(term, self.middle, 0, left, me) for term in row]
            for mask, _, _, high in corner:
                if mask == mask_x:
                    parts.append(jnp.concatenate([jnp.zeros_like(high), high]))
            sent.append((self.added(parts, terms[0].dtype), mask_x))
        for mask_y in self.masks(self.middle):
            parts = [self.take(term, self.middle, mask_y, left, me) for term in mine]
            for _, mask, low, _ in corner:
                if mask == mask_y:
                    parts.append(jnp.concatenate([low, jnp.zeros_like(low)]))
            sent.append((self.added(parts, terms[0].dtype), mask_y))
        received = [self.swap(part, mask) for part, mask in sent]
        terms = [self.take(term, self.middle, 0, left, me) for term in mine] + received
        left = [bit for bit in left if bit not in self.middle]
        return (terms, left), [part for part, _ in sent]

    def scatter_far(self, state, me):
        return self.scatter_step(state, self.outer, me)

    def scatter_end(self, state):
        return self.added(state[0], F32)[0]

    def scatter(self, halves, order, me):
        state = self.scatter_core(halves)
        for group in order:
            state, _ = self.scatter_step(state, group, me)
        return self.scatter_end(state)

    def scatter_whole(self, whole, order, me):
        present = list(range(self.bits - 1, -1, -1))
        halves = [self.take(whole, self.core, mask, present, me) for mask in (0, 1)]
        return self.scatter(halves, order, me)


def after(values, others):
    leaves, tree = jax.tree.flatten(values)
    arrays = [leaf for leaf in leaves if not isinstance(leaf, int)]
    others = [leaf for leaf in jax.tree.leaves(others) if not isinstance(leaf, int)]
    tied = iter(lax.optimization_barrier(tuple(arrays + others)))
    return jax.tree.unflatten(
        tree, [leaf if isinstance(leaf, int) else next(tied) for leaf in leaves]
    )


class Weights:
    def __init__(self, net, me, wanted):
        self.arrays, self.plans, self.shapes = [], [], []
        seen = {}
        for pieces, places, rows in wanted:
            places = (places,) if isinstance(places, int) else tuple(places)
            columns = pieces[0][1].shape[-1]
            plan = []
            if rows % 16:
                blocks = [
                    jnp.concatenate([array[:, place : place + rows] for _, array in pieces])
                    for place in places
                ]
                blocks = jnp.concatenate(blocks, axis=2)
                order = jnp.asarray([s for own, _ in pieces for s in own], jnp.int32)
                spot = jnp.zeros((net.n,), jnp.int32).at[order ^ me].set(jnp.arange(net.n))
                whole = blocks[spot].reshape(net.n * rows // 16, 16, len(places) * columns)
                plan.append((len(self.arrays), None, None, None))
                self.arrays.append(whole)
                self.shapes.append(whole.shape)
            else:
                for own, array in pieces:
                    if id(array) not in seen:
                        seen[id(array)] = len(self.arrays)
                        self.arrays.append(array)
                    for j, source in enumerate(own):
                        for k, place in enumerate(places):
                            aim = pl.ds(k * columns, columns)
                            plan.append((seen[id(array)], (j, pl.ds(place, rows)), source, aim))
                self.shapes.append((net.n, rows, len(places) * columns))
            self.plans.append(plan)
        self.slots = max(len(plan) for plan in self.plans)

    def scratch(self):
        return [pltpu.VMEM(shape, BF16) for shape in self.shapes] + [
            pltpu.SemaphoreType.DMA((len(self.plans), self.slots))
        ]

    def copies(self, w, me, array_refs, held_ref, sems):
        found = []
        for slot, (array, index, source, aim) in enumerate(self.plans[w]):
            if index is None:
                pair = (array_refs[array], held_ref)
            else:
                pair = (array_refs[array].at[index], held_ref.at[me ^ source, :, aim])
            found.append(pltpu.make_async_copy(*pair, sems.at[w, slot]))
        return found

    def start(self, w, *refs):
        for copy in self.copies(w, *refs):
            copy.start()

    def wait(self, w, *refs):
        for copy in self.copies(w, *refs):
            copy.wait()


def flat(held):
    return held.reshape(-1, held.shape[-1])


SMEM_SPEC = pl.BlockSpec(memory_space=pltpu.SMEM)
ANY_SPEC = pl.BlockSpec(memory_space=pltpu.HBM)


def full_spec(shape):
    return pl.BlockSpec(shape, lambda *_: (0,) * len(shape))


def tile_spec(tile, columns):
    return pl.BlockSpec((tile, columns), lambda i: (i, 0))


def call(body, name, grid, ins, outs, scratch, us, bases=()):
    count = len(ins)

    def run(*refs):
        body(*refs[:count], *refs[count + len(bases) :])

    return pl.pallas_call(
        run,
        grid=grid,
        in_specs=[spec for _, spec in ins] + [ANY_SPEC] * len(bases),
        out_specs=[spec for _, _, spec in outs],
        out_shape=[jax.ShapeDtypeStruct(shape, dtype) for shape, dtype, _ in outs],
        scratch_shapes=scratch,
        input_output_aliases={count + i: i for i in range(len(bases))},
        compiler_params=pltpu.CompilerParams(
            vmem_limit_bytes=60 << 20,
            dimension_semantics=("arbitrary",) * len(grid),
        ),
        cost_estimate=pl.CostEstimate(
            flops=int(us * 2e10), bytes_accessed=int(us * 5e7), transcendentals=0
        ),
        name=name,
    )(*[array for array, _ in ins], *bases)


def sum_body(groups, me_ref, *refs):
    step = pl.program_id(0)
    outs = refs[len(refs) - len(groups) :]
    for out_ref, addends in zip(outs, groups):
        total = None
        for place, (low, high) in addends:
            part = refs[place][...].astype(F32)
            if low is not None:
                part = jnp.where((step >= low) & (step < high), part, 0.0)
            total = part if total is None else total + part
        out_ref[...] = total.astype(out_ref.dtype)


def sum_call(me, name, grid, ins, groups, outs, body=None, us=0.01):
    grid_spec = pltpu.PrefetchScalarGridSpec(
        num_scalar_prefetch=1,
        grid=(grid,),
        in_specs=[
            pl.BlockSpec(block, lambda i, me_ref, place=place: place(i, me_ref[0]))
            for _, block, place in ins
        ],
        out_specs=[
            pl.BlockSpec(block, lambda i, me_ref, place=place: place(i, me_ref[0]))
            for _, _, block, place in outs
        ],
    )
    return pl.pallas_call(
        body or functools.partial(sum_body, groups),
        grid_spec=grid_spec,
        out_shape=[jax.ShapeDtypeStruct(shape, dtype) for shape, dtype, _, _ in outs],
        compiler_params=pltpu.CompilerParams(
            vmem_limit_bytes=60 << 20, dimension_semantics=("arbitrary",)
        ),
        cost_estimate=pl.CostEstimate(flops=int(us * 2e10), bytes_accessed=int(us * 5e7), transcendentals=0),
        name=name,
    )(me.reshape(1), *[array for array, _, _ in ins])


class Reduction:
    def __init__(self, net, me, keep, send):
        self.net, self.me = net, me
        self.terms = [keep, net.swap(send, 1)]
        self.rows, self.columns = keep.shape[1:]
        self.plain = len(net.near) == 1 and len(net.middle) == 1 and self.rows % 8 == 0
        self.state = None

    def block(self):
        return (1, self.rows, self.columns)

    def hold(self, others):
        if self.plain:
            self.terms = after(self.terms, others)
        else:
            state = self.state or (self.terms, list(range(self.net.bits - 1, 0, -1)))
            self.state = held(state, others)
            if getattr(self, "corner_pieces", None) is not None:
                self.corner_pieces = after(self.corner_pieces, others)
        return self

    def corner(self):
        net = self.net
        if not self.plain:
            state = self.state or (self.terms, list(range(net.bits - 1, 0, -1)))
            self.state = state
            self.corner_pieces, sent = net.scatter_corner(state, self.me)
            return sent
        far = 1 << (len(net.outer) - 1)

        def place(shift):
            return lambda i, me: ((i + shift) * 4 + (me >> 1 & 3 ^ 3), 0, 0)

        ins = [(term, self.block(), place(shift)) for shift in (0, far) for term in self.terms]
        out = ((far, self.rows, self.columns), BF16, self.block(), lambda i, me: (i, 0, 0))
        always = (None, None)
        groups = [[(0, always), (1, always)], [(2, always), (3, always)]]
        low, high = sum_call(self.me, "corner_sum", far, ins, groups, [out, out])
        self.terms += [net.swap(low, 1 << net.near[0]), net.swap(high, 1 << net.middle[0])]
        return [low, high]

    def near(self):
        net = self.net
        if not self.plain:
            self.state, sent = net.scatter_near(self.state, self.corner_pieces, self.me)
            self.corner_pieces = None
            return sent
        far = 1 << (len(net.outer) - 1)
        keep, other, low, high = self.terms

        def place(flip):
            return lambda i, me: (i * 4 + (me >> 1 & 3 ^ flip), 0, 0)

        ins = [(term, self.block(), place(flip)) for flip in (1, 2) for term in (keep, other)]
        ins.append((high, self.block(), lambda i, me: (jnp.maximum(i - far, 0), 0, 0)))
        ins.append((low, self.block(), lambda i, me: (jnp.minimum(i, far - 1), 0, 0)))
        always = (None, None)
        groups = [
            [(0, always), (1, always), (4, (far, 2 * far))],
            [(2, always), (3, always), (5, (0, far))],
        ]
        out = ((2 * far, self.rows, self.columns), BF16, self.block(), lambda i, me: (i, 0, 0))
        sent = sum_call(self.me, "near_sum", 2 * far, ins, groups, [out, out])
        received = [
            net.swap(part, 1 << group[0]) for part, group in zip(sent, (net.near, net.middle))
        ]
        self.terms = [keep, other] + received
        return sent

    def sources(self, flip, step_block):
        keep, other, row, column = self.terms[:4]
        found = []
        for term in (keep, other):
            found.append((term, lambda me: ((me >> 3 ^ flip) * 4 + (me >> 1 & 3))))
        for term in (row, column):
            found.append((term, lambda me: (me >> 3 ^ flip)))
        return [
            (term, step_block[0], lambda i, me, at=at: step_block[1](i, at(me)))
            for term, at in found
        ]

    def far(self):
        net = self.net
        if not self.plain:
            self.state, sent = net.scatter_step(self.state, net.outer, self.me)
            return sent
        parts = 4
        lanes = self.columns // parts
        step_block = ((1, self.rows, lanes), lambda i, at: (at, 0, i))
        masks = net.masks(net.outer)
        ins, groups = [], []
        for mask in masks:
            groups.append([(len(ins) + j, (None, None)) for j in range(4)])
            ins += self.sources(mask >> 3, step_block)
        out = ((1, self.rows, self.columns), BF16, step_block[0], lambda i, me: (0, 0, i))
        sent = sum_call(self.me, "far_sum", parts, ins, groups, [out] * len(masks))
        self.terms += [net.swap(part, mask) for part, mask in zip(sent, masks)]
        return sent

    def received(self):
        return self.terms[-1] if self.plain else self.state[0][-1]

    def end(self, lots, unit):
        if not self.plain:
            total = self.net.scatter_end(self.state)
            results, start = [], 0
            for count in lots:
                blocks = [
                    total[(start + j) * unit : (start + j + 1) * unit] for j in range(count)
                ]
                results.append(jnp.concatenate(blocks, axis=1))
                start += count
            return results
        step_block = ((1, unit, self.columns), lambda i, at: (at, i, 0))
        ins = self.sources(0, step_block)
        ins += [(term, step_block[0], lambda i, me: (0, i, 0)) for term in self.terms[4:]]
        outs, bounds, start = [], [], 0
        for count in lots:

            def place(i, me, start=start, count=count):
                return (0, jnp.clip(i - start, 0, count - 1))

            outs.append(((unit, count * self.columns), F32, (unit, self.columns), place))
            bounds.append((start, start + count))
            start += count

        def body(me_ref, *refs):
            step, addends = pl.program_id(0), refs[: len(ins)]
            total = addends[0][0].astype(F32)
            for ref in addends[1:]:
                total = total + ref[0].astype(F32)
            for out_ref, (low, high) in zip(refs[len(ins) :], bounds):

                @pl.when((step >= low) & (step < high))
                def _():
                    out_ref[...] = total

        return sum_call(self.me, "end_sum", start, ins, None, outs, body, 4)


def pack_body(step, me_ref, lines_ref, inner_ref, *refs):
    shards, out_ref = refs[:-1], refs[-1]
    start = 0
    for ref in shards:
        out_ref[start : start + ref.shape[0]] = ref[...]
        start += ref.shape[0]
    me, width = me_ref[0], out_ref.shape[1]

    def spread(ref, offset):
        count = ref.shape[1]
        lanes = lax.broadcasted_iota(jnp.int32, (count, width), 1)
        spots = lax.broadcasted_iota(jnp.int32, (count, width), 0) + offset
        return matmul(ref[...], jnp.where(lanes == spots, 1.0, 0.0).astype(BF16))

    vectors = spread(lines_ref, me * step)
    place = me * inner_ref.shape[1]
    inner = spread(inner_ref, lax.rem(place, width))
    row = lax.broadcasted_iota(jnp.int32, inner.shape, 0)
    inner = jnp.where(row == place // width, inner, 0.0)
    out_ref[start:] = jnp.concatenate([vectors, inner]).astype(BF16)


def pack(me, shards, lines, inner):
    step, width = shards[0].shape
    return call(
        functools.partial(pack_body, step),
        "pack",
        (1,),
        [(me.reshape(1), SMEM_SPEC)]
        + [(array, full_spec(array.shape)) for array in (lines, inner, *shards)],
        [((len(shards) * step + 16, width), BF16, full_spec((len(shards) * step + 16, width)))],
        [],
        1,
    )[0]


def project_body(weights, tile, row_length, me_ref, *refs):
    count = len(weights.arrays)
    arrays, refs = refs[:count], refs[count:]
    feats_ref, x_ref = refs[:2]
    temb_ref, lines_ref, low_ref, q_ref, k_ref, v_ref = refs[2:8]
    tw, qw, kw, vw, lw, sems = refs[8:14]
    me, step = me_ref[0], pl.program_id(0)

    @pl.when(step == 0)
    def _():
        for w, held in enumerate((tw, qw, kw, vw, lw)):
            weights.start(w, me, arrays, held, sems)
        weights.wait(0, me, arrays, tw, sems)
        temb_ref[...] = matmul(feats_ref[...], flat(tw[...]))
        weights.wait(4, me, arrays, lw, sems)
        lines_ref[...] = jnp.sum(lw[...].astype(F32), axis=0)
        for w, held in ((1, qw), (2, kw), (3, vw)):
            weights.wait(w, me, arrays, held, sems)

    row = step * tile // row_length
    low = (x_ref[...].astype(F32) + temb_ref[pl.ds(row, 1), :]).astype(BF16)
    low_ref[...] = low
    q_ref[...] = (matmul(low, flat(qw[...])) + lines_ref[0:1]).astype(BF16)
    k_ref[...] = matmul(low, flat(kw[...])).astype(BF16)
    v_ref[...] = (matmul(low, flat(vw[...])) + lines_ref[1:2]).astype(BF16)


def project(net, me, flow, feats, x, row_length):
    tokens, width = x.shape
    tile = min(256, row_length)
    r = width // net.n
    weights = Weights(net, me, [(flow, w * r, r) for w in range(4)] + [(flow, 4 * r, 16)])
    ins = (
        [(me.reshape(1), SMEM_SPEC)]
        + [(array, ANY_SPEC) for array in weights.arrays]
        + [(feats, full_spec(feats.shape)), (x, tile_spec(tile, width))]
    )
    outs = [(feats.shape, F32, full_spec(feats.shape))]
    outs += [((16, width), F32, full_spec((16, width)))]
    outs += [((tokens, width), BF16, tile_spec(tile, width))] * 4
    return call(
        functools.partial(project_body, weights, tile, row_length),
        "project",
        (tokens // tile,),
        ins,
        outs,
        weights.scratch(),
        14,
    )


def same_document(segc_ref, segr_ref, bias_ref, block):
    @pl.when(block == 0)
    def _():
        bias_ref[...] = jnp.where(segc_ref[0] == segr_ref[0], 0.0, -1e30)


def own_lanes(shape, head, head_dim):
    lanes = lax.broadcasted_iota(jnp.int32, shape, len(shape) - 1)
    return (lanes // head_dim) == head


def attend_body(head_dim, segc_ref, segr_ref, q_ref, k_ref, v_ref, out_ref, log_ref, bias_ref):
    same_document(segc_ref, segr_ref, bias_ref, pl.program_id(1))
    queries, key_rows, values = q_ref[...], k_ref[...], v_ref[...]
    scale = 1.0 / math.sqrt(head_dim)
    per = queries.shape[1] // head_dim
    total = None
    for head in range(per):
        mine = own_lanes(queries.shape, head, head_dim)
        keys_own = jnp.where(mine, key_rows * BF16(scale), BF16(0))
        scores = matmul_right(keys_own, queries) + bias_ref[...]
        top = jnp.max(scores, axis=0, keepdims=True)
        raised = jnp.exp(scores - top)
        amount = jnp.sum(raised, axis=0, keepdims=True)
        log_ref[0, 0, pl.ds(head, 1), :] = top + jnp.log(amount)
        soft_low = (raised * (1.0 / amount)).astype(BF16)
        context = matmul_left(soft_low, values)
        total = context if total is None else jnp.where(mine, context, total)
    out_ref[...] = total.astype(BF16)


def attend_back_body(
    head_dim, segc_ref, segr_ref, q_ref, k_ref, v_ref, log_ref, g_ref, gq_ref, gk_ref, gv_ref, sums_ref, rows_ref, bias_ref
):
    same_document(segc_ref, segr_ref, bias_ref, pl.program_id(1))
    queries, key_rows, values, grads = q_ref[...], k_ref[...], v_ref[...], g_ref[...]
    scale = 1.0 / math.sqrt(head_dim)
    per = queries.shape[1] // head_dim
    totals = None
    for head in range(per):
        mine = own_lanes(queries.shape, head, head_dim)
        keys_own = jnp.where(mine, key_rows * BF16(scale), BF16(0))
        scores = matmul_right(keys_own, queries) + bias_ref[...]
        soft = jnp.exp(scores - log_ref[0, 0, pl.ds(head, 1), :])
        grad_soft = matmul_right(jnp.where(mine, values, BF16(0)), grads)
        inner_sum = jnp.sum(soft * grad_soft, axis=0, keepdims=True)
        grad_scores = (soft * (grad_soft - inner_sum)).astype(BF16)
        parts = (
            matmul_left(grad_scores, key_rows),
            matmul(grad_scores, queries),
            matmul(soft.astype(BF16), grads),
        )
        if totals is None:
            totals = parts
        else:
            totals = tuple(jnp.where(mine, part, total) for part, total in zip(parts, totals))
    gq = (totals[0] * scale).astype(BF16)
    gv = totals[2].astype(BF16)
    gq_ref[...] = gq
    gk = (totals[1] * scale).astype(BF16)
    gk_ref[...] = gk
    gv_ref[...] = gv
    sums = [jnp.sum(part.astype(F32), axis=0, keepdims=True) for part in (gq, gk, gv)]
    zero = jnp.zeros_like(sums[0])
    sums_ref[...] = jnp.concatenate([sums[0], sums[2]] + [zero] * 6)
    rows_ref[...] = jnp.concatenate(sums + [zero] * 5)


def attention_args(segments, start, lanes, head_dim):
    row_length, per = segments.shape[1], lanes // head_dim
    segc = pl.BlockSpec((1, row_length, 1), lambda i, j: (start + i, 0, 0))
    segr = pl.BlockSpec((1, 1, row_length), lambda i, j: (start + i, 0, 0))
    block = pl.BlockSpec((row_length, lanes), lambda i, j: (start + i, j))
    log_spec = pl.BlockSpec((1, 1, per, row_length), lambda i, j: (start + i, j, 0, 0))
    return [(segments[:, :, None], segc), (segments[:, None, :], segr)], block, log_spec


def attend(queries, key_rows, values, segments, lanes=256):
    rows, row_length = segments.shape
    tokens, width = queries.shape
    head_dim = width // H
    blocks, per = width // lanes, lanes // head_dim
    masks, block, log_spec = attention_args(segments, 0, lanes, head_dim)
    return call(
        functools.partial(attend_body, head_dim),
        "attend",
        (rows, blocks),
        masks + [(array, block) for array in (queries, key_rows, values)],
        [
            ((tokens, width), BF16, block),
            ((rows, blocks, per, row_length), F32, log_spec),
        ],
        [pltpu.VMEM((row_length, row_length), F32)],
        24,
    )


def attend_back(queries, key_rows, values, segments, log_total, grad_context, row, bases=(), lanes=256):
    rows, row_length = segments.shape
    tokens, width = queries.shape
    head_dim = width // H
    masks, block, log_spec = attention_args(segments, row, lanes, head_dim)
    return call(
        functools.partial(attend_back_body, head_dim),
        "attend_back",
        (1, width // lanes),
        masks
        + [(array, block) for array in (queries, key_rows, values)]
        + [(log_total, log_spec), (grad_context, block)],
        [((tokens, width), BF16, block)] * 3
        + [((8, width), F32, pl.BlockSpec((8, lanes), lambda i, j: (0, j)))] * 2,
        [pltpu.VMEM((row_length, row_length), F32)],
        19,
        bases,
    )


def add_to(ref, value, step):
    part = jnp.sum(value, axis=0, keepdims=True)

    @pl.when(step == 0)
    def _():
        ref[...] = part

    @pl.when(step != 0)
    def _():
        ref[...] += part


def add_lines(ref, values, step):
    zero = jnp.zeros((1, ref.shape[1]), F32)
    sums = {line: jnp.sum(value, axis=0, keepdims=True) for line, value in values.items()}
    part = jnp.concatenate([sums.get(line, zero) for line in range(ref.shape[0])])

    @pl.when(step == 0)
    def _():
        ref[...] = part

    @pl.when(step != 0)
    def _():
        ref[...] += part


def ffn_in_body(weights, tile, row_length, chunk, me_ref, *refs):
    count = len(weights.arrays)
    arrays, refs = refs[:count], refs[count:]
    context_ref, x_ref, temb_ref, lines_ref = refs[:4]
    first_low_ref, normed_ref, spread_ref, active_ref, slope_ref = refs[4:9]
    ow, iw, sems = refs[9:12]
    me, step = me_ref[0], pl.program_id(0)

    @pl.when(step == 0)
    def _():
        for w, held in enumerate((ow, iw)):
            weights.start(w, me, arrays, held, sems)
        weights.wait(0, me, arrays, ow, sems)

    row = step * tile // row_length
    stream = x_ref[...].astype(F32) + temb_ref[pl.ds(row, 1), :]
    mixed = stream + (matmul(context_ref[...], flat(ow[...])) + lines_ref[2:3])
    normed, spread = normalize(mixed)
    normed_ref[...] = normed
    spread_ref[...] = spread
    first = normed * lines_ref[4:5] + lines_ref[5:6]
    low = first.astype(BF16)
    first_low_ref[...] = low

    @pl.when(step == 0)
    def _():
        weights.wait(1, me, arrays, iw, sems)

    width, hidden = ow.shape[2], iw.shape[2]

    def inner(start):
        pre = matmul(low, flat(iw[:, :, start : start + chunk]))
        line, place = 8 + start // width, start % width
        return pre + lines_ref[line : line + 1, place : place + chunk]

    later = inner(0)
    for start in range(0, hidden, chunk):
        pre = later
        if start + chunk < hidden:
            later = inner(start + chunk)
        columns = slice(start, start + chunk)
        normal_cdf = 0.5 * (1.0 + lax.erf(pre * INV_ROOT_TWO))
        normal_pdf = jnp.exp(-0.5 * pre * pre) * INV_ROOT_TAU
        active_ref[:, columns] = (pre * normal_cdf).astype(BF16)
        slope_ref[:, columns] = (normal_cdf + pre * normal_pdf).astype(BF16)


def ffn_in(net, me, flow, context, x, temb, lines, hidden, row_length, tile=256, chunk=512):
    tokens, width = x.shape
    r = width // net.n
    blocks = range(r, r + hidden // width * r, r)
    weights = Weights(net, me, [(flow, 0, r), (flow, blocks, r)])
    tile = min(tile, row_length)
    tiled, wide, thin = (tile_spec(tile, columns) for columns in (width, hidden, 1))
    ins = (
        [(me.reshape(1), SMEM_SPEC)]
        + [(array, ANY_SPEC) for array in weights.arrays]
        + [(context, tiled), (x, tiled)]
        + [(array, full_spec(array.shape)) for array in (temb, lines)]
    )
    outs = [
        ((tokens, width), BF16, tiled),
        ((tokens, width), F32, tiled),
        ((tokens, 1), F32, thin),
        ((tokens, hidden), BF16, wide),
        ((tokens, hidden), BF16, wide),
    ]
    return call(
        functools.partial(ffn_in_body, weights, tile, row_length, chunk),
        "ffn_in",
        (tokens // tile,),
        ins,
        outs,
        weights.scratch(),
        30,
    )


def ffn_out_body(weights, me_ref, *refs):
    count = len(weights.arrays)
    arrays, refs = refs[:count], refs[count:]
    active_ref, normed_ref, cot_ref, lines_ref = refs[:4]
    out_ref, gs_ref, gs_low_ref, sums_ref = refs[4:8]
    uw, sems = refs[8:10]
    me, step = me_ref[0], pl.program_id(0)

    @pl.when(step == 0)
    def _():
        weights.start(0, me, arrays, uw, sems)
        weights.wait(0, me, arrays, uw, sems)

    first = normed_ref[...] * lines_ref[4:5] + lines_ref[5:6]
    second = first + (matmul(active_ref[...], flat(uw[...])) + lines_ref[3:4])
    normed_second, spread_second = normalize(second)
    out_ref[...] = (normed_second * lines_ref[6:7] + lines_ref[7:8]).astype(BF16)
    grad_out = cot_ref[...].astype(F32)
    grad_second = norm_back(grad_out * lines_ref[6:7], normed_second, spread_second)
    gs_ref[...] = grad_second
    low = grad_second.astype(BF16)
    gs_low_ref[...] = low
    add_lines(sums_ref, {3: low.astype(F32), 6: grad_out * normed_second, 7: grad_out}, step)


def ffn_out(net, me, flow, active, normed, cotangent, vectors, tile=256):
    tokens, width = normed.shape
    hidden = active.shape[1]
    weights = Weights(net, me, [(flow, 0, hidden // net.n)])
    tiled, wide = tile_spec(tile, width), tile_spec(tile, hidden)
    ins = (
        [(me.reshape(1), SMEM_SPEC)]
        + [(array, ANY_SPEC) for array in weights.arrays]
        + [(active, wide), (normed, tiled), (cotangent, tiled)]
        + [(vector, full_spec(vector.shape)) for vector in vectors]
    )
    outs = [
        ((tokens, width), BF16, tiled),
        ((tokens, width), F32, tiled),
        ((tokens, width), BF16, tiled),
        ((8, width), F32, full_spec((8, width))),
    ]
    return call(
        functools.partial(ffn_out_body, weights),
        "ffn_out",
        (tokens // tile,),
        ins,
        outs,
        weights.scratch(),
        20,
    )


def ffn_back_body(weights, tile, row_length, chunk, me_ref, *refs):
    count = len(weights.arrays)
    arrays, refs = refs[:count], refs[count:]
    (gs_ref, gs_low_ref, slope_ref, normed_ref, spread_ref, lines_ref) = refs[:6]
    (gi_ref, gm_ref, gm_low_ref, gc_ref, ibg_ref, sums_ref, rows_ref) = refs[6:13]
    uw, ow, iw, sems = refs[13:17]
    me, step = me_ref[0], pl.program_id(0)

    @pl.when(step == 0)
    def _():
        for w, held in ((0, uw), (2, iw), (1, ow)):
            weights.start(w, me, arrays, held, sems)
        weights.wait(0, me, arrays, uw, sems)

    unit = uw.shape[1]
    hidden = iw.shape[2]
    for start in range(0, hidden, chunk):
        columns = slice(start, start + chunk)
        held = flat(uw[start // unit : (start + chunk) // unit])
        grad_active = matmul_right(gs_low_ref[...], held)
        gi_ref[:, columns] = (grad_active * slope_ref[:, columns].astype(F32)).astype(BF16)

    @pl.when(step == 0)
    def _():
        weights.wait(2, me, arrays, iw, sems)

    grad_first = gs_ref[...] + matmul_right(gi_ref[...], flat(iw[...]))
    add_to(ibg_ref, gi_ref[...].astype(F32), step)
    normed = normed_ref[...]
    grad_mixed = norm_back(grad_first * lines_ref[4:5], normed, spread_ref[...])
    gm_ref[...] = grad_mixed

    @pl.when(step == 0)
    def _():
        rows_ref[...] = jnp.zeros_like(rows_ref)

    row = pl.ds(step * tile // row_length, 1)
    rows_ref[row, :] += jnp.sum(grad_mixed, axis=0, keepdims=True)
    low = grad_mixed.astype(BF16)
    gm_low_ref[...] = low
    add_lines(sums_ref, {2: low.astype(F32), 4: grad_first * normed, 5: grad_first}, step)

    @pl.when(step == 0)
    def _():
        weights.wait(1, me, arrays, ow, sems)

    gc_ref[...] = matmul_right(low, flat(ow[...])).astype(BF16)


def ffn_back(net, me, flow_u, flow_io, gs, gs_low, slope, normed, spread, lines, row_length, tile=256, chunk=1024):
    tokens, width = gs.shape
    hidden = slope.shape[1]
    r = width // net.n
    weights = Weights(
        net,
        me,
        [
            (flow_u, 0, hidden // net.n),
            (flow_io, 0, r),
            (flow_io, range(r, r + hidden // width * r, r), r),
        ],
    )
    tile = min(tile, row_length)
    tiled, wide = tile_spec(tile, width), tile_spec(tile, hidden)
    ins = (
        [(me.reshape(1), SMEM_SPEC)]
        + [(array, ANY_SPEC) for array in weights.arrays]
        + [(gs, tiled), (gs_low, tiled), (slope, wide), (normed, tiled)]
        + [(spread, tile_spec(tile, 1)), (lines, full_spec(lines.shape))]
    )
    outs = [
        ((tokens, hidden), BF16, wide),
        ((tokens, width), F32, tiled),
        ((tokens, width), BF16, tiled),
        ((tokens, width), BF16, tiled),
        ((1, hidden), F32, full_spec((1, hidden))),
        ((8, width), F32, full_spec((8, width))),
        ((8, width), F32, full_spec((8, width))),
    ]
    return call(
        functools.partial(ffn_back_body, weights, tile, row_length, chunk),
        "ffn_back",
        (tokens // tile,),
        ins,
        outs,
        weights.scratch(),
        38,
    )


def deal(me_ref, total, rows, keep_ref, send_ref, kind=0):
    core = me_ref[0] & 1
    total = total.reshape(-1, 2, rows, total.shape[-1])
    low, high = total[:, 0], total[:, 1]
    place = slice(kind * rows, (kind + 1) * rows)
    keep_ref[:, place] = jnp.where(core == 0, low, high).astype(BF16)
    send_ref[:, place] = jnp.where(core == 0, high, low).astype(BF16)


def product_body(rows, me_ref, a_ref, b_ref, keep_ref, send_ref):
    deal(me_ref, matmul_left(a_ref[...], b_ref[...]), rows, keep_ref, send_ref)


def product(net, me, left, right, tile=1024):
    tokens, width = left.shape
    columns = right.shape[1]
    rows = width // net.n
    shape = (net.n // 2, rows, columns)
    block = pl.BlockSpec((tile // (2 * rows), rows, columns), lambda i: (i, 0, 0))
    return call(
        functools.partial(product_body, rows),
        "product",
        (width // tile,),
        [
            (me.reshape(1), SMEM_SPEC),
            (left, pl.BlockSpec((tokens, tile), lambda i: (0, i))),
            (right, full_spec((tokens, columns))),
        ],
        [(shape, BF16, block), (shape, BF16, block)],
        [],
        15,
    )


def inner_body(rows, me_ref, context_ref, first_ref, gm_ref, gi_ref, keep_ref, send_ref):
    total = matmul_left(first_ref[...], gi_ref[...])
    width = gm_ref.shape[1]
    deal(me_ref, matmul_left(context_ref[...], gm_ref[...]), rows, keep_ref, send_ref, 0)
    for k in range(total.shape[1] // width):
        part = total[:, k * width : (k + 1) * width]
        deal(me_ref, part, rows, keep_ref, send_ref, k + 1)


def inner_product(net, me, context, first_low, gm_low, gi, tile=256):
    tokens, width = context.shape
    hidden = gi.shape[1]
    rows = width // net.n
    kinds = 1 + hidden // width
    shape = (net.n // 2, kinds * rows, width)
    block = pl.BlockSpec((tile // (2 * rows), kinds * rows, width), lambda i: (i, 0, 0))
    left = pl.BlockSpec((tokens, tile), lambda i: (0, i))
    return call(
        functools.partial(inner_body, rows),
        "inner_product",
        (width // tile,),
        [
            (me.reshape(1), SMEM_SPEC),
            (context, left),
            (first_low, left),
            (gm_low, full_spec((tokens, width))),
            (gi, full_spec((tokens, hidden))),
        ],
        [(shape, BF16, block), (shape, BF16, block)],
        [],
        18,
    )


def triple_body(rows, me_ref, lines_ref, a_ref, q_ref, k_ref, v_ref, keep_ref, send_ref):
    for w, ref in enumerate((q_ref, k_ref, v_ref)):
        deal(me_ref, matmul_left(a_ref[...], ref[...]), rows, keep_ref, send_ref, w)
    core = me_ref[0] & 1
    low, high = lines_ref[:, 0:8], lines_ref[:, 8:16]
    place = slice(3 * rows, 3 * rows + 8)
    keep_ref[:, place] = jnp.where(core == 0, low, high).astype(BF16)
    send_ref[:, place] = jnp.where(core == 0, high, low).astype(BF16)


def triple_product(net, me, lines, left, gq, gk, gv, tile=256):
    tokens, width = left.shape
    rows = width // net.n
    shape = (net.n // 2, 3 * rows + 8, width)
    chips = tile // (2 * rows)
    block = pl.BlockSpec((chips, 3 * rows + 8, width), lambda i: (i, 0, 0))
    full = full_spec((tokens, width))
    return call(
        functools.partial(triple_body, rows),
        "triple_product",
        (width // tile,),
        [
            (me.reshape(1), SMEM_SPEC),
            (lines, pl.BlockSpec((chips, 16, width), lambda i: (i, 0, 0))),
            (left, pl.BlockSpec((tokens, tile), lambda i: (0, i))),
            (gq, full),
            (gk, full),
            (gv, full),
        ],
        [(shape, BF16, block), (shape, BF16, block)],
        [],
        13,
    )


def stream_back_body(weights, rows, me_ref, *refs):
    count = len(weights.arrays)
    arrays, refs = refs[:count], refs[count:]
    gm_ref, gq_ref, gk_ref, gv_ref = refs[:4]
    sum_refs, refs = refs[4 : 4 + rows], refs[4 + rows :]
    out_ref, outs = refs[0], refs[1:]
    qw, kw, vw, sems = outs[-4:]
    me, step = me_ref[0], pl.program_id(0)

    @pl.when(step == 0)
    def _():
        for w, held in enumerate((qw, kw, vw)):
            weights.start(w, me, arrays, held, sems)
        for w, held in enumerate((qw, kw, vw)):
            weights.wait(w, me, arrays, held, sems)
        if sum_refs:
            total = sum_refs[0][...]
            for w, held in enumerate((qw, kw, vw)):
                lines = [ref[w : w + 1] for ref in sum_refs[1:]]
                lines += [jnp.zeros_like(lines[0])] * (8 - len(lines))
                total += matmul_right(jnp.concatenate(lines).astype(BF16), flat(held[...]))
            outs[0][...] = total

    out_ref[...] = (
        gm_ref[...]
        + matmul_right(gq_ref[...], flat(qw[...]))
        + matmul_right(gk_ref[...], flat(kw[...]))
        + matmul_right(gv_ref[...], flat(vw[...]))
    )


def stream_back(net, me, flow, gm, gq, gk, gv, row, row_length, base=None, sums=(), tile=256):
    tokens, width = gm.shape
    tile = min(tile, row_length)
    r = width // net.n
    weights = Weights(net, me, [(flow, w * r, r) for w in (1, 2, 3)])
    start = row * (row_length // tile)
    tiled = pl.BlockSpec((tile, width), lambda i: (start + i, 0))
    ins = (
        [(me.reshape(1), SMEM_SPEC)]
        + [(array, ANY_SPEC) for array in weights.arrays]
        + [(array, tiled) for array in (gm, gq, gk, gv)]
        + [(array, full_spec((8, width))) for array in sums]
    )
    outs = [((tokens, width), F32, tiled)]
    if sums:
        outs.append(((8, width), F32, full_spec((8, width))))
    return call(
        functools.partial(stream_back_body, weights, len(sums)),
        "stream_back",
        (row_length // tile,),
        ins,
        outs,
        weights.scratch(),
        10,
        () if base is None else (base,),
    )


def in_order(net, me, sources, blocks):
    order = jnp.asarray(sources, jnp.int32)
    spot = jnp.zeros((net.n,), jnp.int32).at[order].set(jnp.arange(net.n, dtype=jnp.int32))
    return blocks[spot[jnp.arange(net.n) ^ me]]


def held(state, others):
    return after(state[0], others), state[1]


def stream_ends(state, unit):
    if not state.plain:
        total = state.net.scatter_end(state.state)
        return [total[w * unit : (w + 1) * unit] for w in range(3)] + [total[3 * unit]]
    rows, columns = state.rows, state.columns
    step_block = ((1, rows, columns), lambda i, at: (at, 0, 0))
    ins = state.sources(0, step_block)
    ins += [(term, step_block[0], lambda i, me: (0, 0, 0)) for term in state.terms[4:]]
    shapes = [(unit, columns)] * 3 + [(8, columns)]
    outs = [(shape, F32, shape, lambda i, me: (0, 0)) for shape in shapes]

    def body(me_ref, *refs):
        total = refs[0][0].astype(F32)
        for ref in refs[1 : len(ins)]:
            total = total + ref[0].astype(F32)
        start = 0
        for out_ref in refs[len(ins) :]:
            count = out_ref.shape[0]
            out_ref[...] = total[start : start + count]
            start += count

    results = sum_call(state.me, "stream_end", 1, ins, None, outs, body)
    return list(results[:3]) + [results[3][0]]


def on_device(
    net,
    inputs,
    timesteps,
    segments,
    cotangent,
    query_weight,
    key_weight,
    value_weight,
    output_weight,
    inner_weight,
    outer_weight,
    time_weight,
    *vectors,
):
    n = net.n
    me = lax.axis_index("fsdp").astype(jnp.int32)
    batch_count, row_count, row_length, model_width = inputs.shape
    rows = batch_count * row_count
    tokens = rows * row_length
    feats = features(timesteps.reshape(rows)).astype(BF16)
    order = (0, 1, 2, 4, 5, 6, 7, 8, 3)
    sizes = [vectors[i].shape[0] for i in order]
    small = sum(
        jnp.pad(vectors[i].astype(F32)[None], ((line, 7 - line), (0, 0)))
        for line, i in enumerate(order[:8])
    )
    inner_line = jnp.broadcast_to(vectors[3][None], (8, sizes[-1]))
    r = model_width // n

    shards = (time_weight, query_weight, key_weight, value_weight)
    far = net.gather_far(pack(me, shards, small.astype(BF16), inner_line))
    hidden = inner_weight.shape[1]
    inner_blocks = [
        inner_weight[:, start : start + model_width] for start in range(0, hidden, model_width)
    ]
    shard_io = after(jnp.concatenate([output_weight] + inner_blocks), far)
    far_io = net.gather_far(shard_io)
    far = net.stacked(far)
    near = net.gather_near(far)
    pieces, corners, _ = net.gather_corner(far, near)
    flow = net.gather_core(pieces)
    far_io, corners, shard_u = after((net.stacked(far_io), corners, outer_weight), ())
    near_io = net.gather_near(far_io)
    flow += net.gather_core(corners)
    far_u = net.gather_far(after(shard_u, flow))

    segments = segments.reshape(rows, row_length)
    x = inputs.reshape(tokens, model_width)
    feats_in = after(feats, far_io)
    temb, lines, stream_low, queries, key_rows, values = project(
        net, me, flow, feats_in, x, row_length
    )
    far_u = net.stacked(after(far_u, queries))
    near_io, queries = after((near_io, queries), far_u)
    pieces, corners, sent = net.gather_corner(far_io, near_io)
    far_u = after(far_u, sent)
    near_u = net.gather_near(far_u)
    queries = after(queries, (sent, far_u))
    context, log_total = attend(queries, key_rows, values, segments)
    corners, context, pieces = after((corners, context, pieces), ())
    flow_io = net.gather_core(pieces) + net.gather_core(corners)
    near_u, flow_io = after((near_u, flow_io), ())
    pieces, corners, sent = net.gather_corner(far_u, near_u)
    context = after(context, sent)
    first_low, normed_first, spread_first, active_low, slope = ffn_in(
        net, me, flow_io, context, x, temb, lines, hidden, row_length
    )
    corners, active_low = after((corners, active_low), ())
    flow_u = net.gather_core(pieces) + net.gather_core(corners)
    (
        layer_output,
        grad_second,
        grad_second_low,
        sums_out,
    ) = ffn_out(
        net,
        me,
        flow_u,
        active_low,
        normed_first,
        cotangent.reshape(tokens, model_width),
        (lines,),
    )
    outer_halves = product(net, me, active_low, grad_second_low)
    outer_sum = Reduction(net, me, *outer_halves)
    slope = after(slope, outer_halves)
    (
        grad_inner_low,
        grad_mixed,
        grad_mixed_low,
        grad_context,
        inner_bias_grad,
        sums_back,
        mixed_rows,
    ) = ffn_back(
        net,
        me,
        flow_u,
        flow_io,
        grad_second,
        grad_second_low,
        slope,
        normed_first,
        spread_first,
        lines,
        row_length,
    )
    sent = outer_sum.hold(grad_mixed_low).corner()
    grad_mixed_low = after(grad_mixed_low, sent)
    inner_halves = inner_product(net, me, context, first_low, grad_mixed_low, grad_inner_low)
    inner_sum = Reduction(net, me, *inner_halves)
    sent = outer_sum.hold(inner_halves).near()
    grad_context = after(grad_context, (inner_halves, sent))
    back = (queries, key_rows, values, segments, log_total, grad_context)
    found, sums_rows, row_sums = None, 0.0, [mixed_rows]
    for row in range(rows):
        if row == 1:
            sent = inner_sum.hold(found[1]).corner() + list(outer_sum.hold(found[1]).far())
            found = after(found, sent)
        found = attend_back(*back, row, found or ())
        sums_rows += found[3]
        row_sums.append(found[4])
        found = found[:3]
    grad_queries, grad_keys, grad_values = found
    sent = inner_sum.hold(grad_queries).near()
    (outer_weight_grad,) = outer_sum.hold(grad_queries).end([1], outer_weight.shape[0])
    sums = sums_rows + sums_out + sums_back
    sums = sums.reshape(8, n, r).transpose(1, 0, 2).reshape(n, 8 * r)
    sums = jnp.concatenate([sums, inner_bias_grad.reshape(n, -1)], axis=1)
    sums = jnp.pad(sums, ((0, 0), (0, model_width - sums.shape[1]))).astype(BF16)
    sums = jnp.broadcast_to(sums[:, None], (n, 8, model_width)).reshape(n // 2, 16, model_width)
    stream_low, sums = after((stream_low, sums), (sent, outer_weight_grad))
    stream_halves = triple_product(
        net, me, sums, stream_low, grad_queries, grad_keys, grad_values
    )
    stream_sum = Reduction(net, me, *stream_halves)
    grad_mixed = after(grad_mixed, stream_halves)
    back = (flow, grad_mixed, grad_queries, grad_keys, grad_values)
    grad_stream, grad_temb = stream_back(net, me, *back, 0, row_length, sums=row_sums)
    ends = jnp.concatenate([feats.astype(F32), grad_temb[:rows]], axis=1)[None]
    sources, ends = net.gather_round([0], ends, net.masks(net.core))
    sent = inner_sum.hold(grad_temb).far()
    sent = list(sent) + stream_sum.hold((grad_temb, sent)).corner()
    ends, grad_stream = after((ends, grad_stream), sent)
    for row in range(1, rows):
        (grad_stream,) = stream_back(net, me, *back, row, row_length, grad_stream)
    sent = stream_sum.hold(grad_stream).near()
    output_weight_grad, inner_weight_grad = inner_sum.hold(sent).end([1, hidden // model_width], r)
    ends = after(ends, (sent, output_weight_grad))
    sources, ends = net.gather_round(sources, ends, net.inner_masks())
    stream_sum.hold(ends).far()
    sources, ends = net.gather_round(
        sources, after(ends, stream_sum.received()), net.masks(net.outer)
    )
    ends = in_order(net, me, sources, ends).reshape(n * rows, 2 * model_width)
    query_weight_grad, key_weight_grad, value_weight_grad, vector_sums = stream_ends(
        stream_sum, r
    )
    feats_all, temb_all = ends[:, :model_width], ends[:, model_width:]
    own = model_width // n
    feats_own = lax.dynamic_slice_in_dim(feats_all, me * own, own, 1)
    time_weight_grad = lax.dot_general(
        feats_own,
        temb_all,
        (((0,), (0,)), ((), ())),
        precision=lax.Precision.HIGHEST,
    )
    parts, start = {}, 0
    for i, size in zip(order, sizes):
        parts[i] = vector_sums[start : start + size]
        start += size
    vector_outs = [parts[i] for i in range(len(order))]

    shape = inputs.shape
    return (
        layer_output.reshape(shape),
        grad_stream.reshape(shape),
        query_weight_grad,
        key_weight_grad,
        value_weight_grad,
        output_weight_grad,
        inner_weight_grad,
        outer_weight_grad,
        time_weight_grad,
    ) + tuple(vector_outs)


def solution(mesh):
    matrix, vector = P("fsdp", None), P("fsdp")
    batch = P(None, "fsdp", None, None)
    return jax.shard_map(
        functools.partial(on_device, Net(mesh.shape["fsdp"])),
        mesh=mesh,
        in_specs=(batch, P(None, "fsdp"), P(None, "fsdp", None), batch)
        + (matrix,) * 7
        + (vector,) * 9,
        out_specs=(batch, batch) + (matrix,) * 7 + (vector,) * 9,
        check_vma=False,
    )
```

```python
import functools
import math

import jax
import jax.numpy as jnp
from jax import lax
from jax.experimental import pallas as pl
from jax.experimental.pallas import tpu as pltpu
from jax.sharding import PartitionSpec as P

D = 1024
H = 16


INV_ROOT_TWO = 0.7071067811865476
INV_ROOT_TAU = 0.3989422804014327
F32 = jnp.float32
BF16 = jnp.bfloat16


def matmul(operand, factor):
    return jnp.dot(operand, factor, preferred_element_type=F32)


def matmul_left(operand, factor):
    return lax.dot_general(
        operand, factor, (((0,), (0,)), ((), ())), preferred_element_type=F32
    )


def matmul_right(operand, factor):
    return lax.dot_general(
        operand, factor, (((1,), (1,)), ((), ())), preferred_element_type=F32
    )


def features(step_ids):
    half_width = D // 2
    freqs = jnp.exp(-math.log(10000.0) * jnp.arange(half_width, dtype=F32) / half_width)
    angles = step_ids.astype(F32)[..., None] * freqs
    return jnp.concatenate([jnp.sin(angles), jnp.cos(angles)], axis=-1)


def own_features(step_ids, first, count):
    half_width = D // 2
    columns = first + jnp.arange(count, dtype=jnp.int32)
    places = (columns % half_width).astype(F32)
    freqs = jnp.exp(-math.log(10000.0) * places / half_width)
    angles = step_ids[:, None] * freqs
    return jnp.where(columns < half_width, jnp.sin(angles), jnp.cos(angles))


def normalize(values_in):
    center = values_in - jnp.mean(values_in, axis=-1, keepdims=True)
    spread = lax.rsqrt(jnp.mean(center * center, axis=-1, keepdims=True) + 1e-05)
    return (center * spread, spread)


def norm_back(grad_normed, normed, spread):
    mean_grad = jnp.mean(grad_normed, axis=-1, keepdims=True)
    mean_cross = jnp.mean(grad_normed * normed, axis=-1, keepdims=True)
    return spread * (grad_normed - mean_grad - normed * mean_cross)


def halves_body(low_in, high_in, low_out, high_out):
    low_out[...] = low_in[...]
    high_out[...] = high_in[...]


def halves(low_of, high_of):
    count, half = low_of.shape[0], low_of.shape[0] // 2
    block = (1,) + low_of.shape[1:]
    return pl.pallas_call(
        halves_body,
        grid=(half,),
        in_specs=[
            pl.BlockSpec(block, lambda i: (i, 0, 0)),
            pl.BlockSpec(block, lambda i: (half + i, 0, 0)),
        ],
        out_specs=[pl.BlockSpec(block, lambda i: (i, 0, 0))] * 2,
        out_shape=[jax.ShapeDtypeStruct((half,) + low_of.shape[1:], low_of.dtype)] * 2,
        compiler_params=pltpu.CompilerParams(vmem_limit_bytes=16 << 20),
        cost_estimate=pl.CostEstimate(flops=1000, bytes_accessed=1000, transcendentals=0),
        name="halves",
    )(low_of, high_of)


class Net:
    def __init__(self, n):
        self.n = n
        self.bits = n.bit_length() - 1
        chip = self.bits - 1
        sizes = [(chip + 2 - i) // 3 for i in range(3)]
        groups, top = [], self.bits - 1
        for size in sizes:
            groups.append(tuple(range(top, top - size, -1)))
            top -= size
        self.outer, self.middle, self.near = groups
        self.core = (0,)

    def masks(self, group):
        found = []
        for pick in range(1, 1 << len(group)):
            mask = 0
            for place, bit in enumerate(group):
                if pick >> place & 1:
                    mask |= 1 << bit
            found.append(mask)
        return found

    def swap(self, array, mask):
        return lax.ppermute(array, "fsdp", [(i, i ^ mask) for i in range(self.n)])

    def gather_far(self, shard):
        return [shard] + [self.swap(shard, mask) for mask in self.masks(self.outer)]

    def stacked(self, parts):
        return ([0] + self.masks(self.outer), jnp.stack(parts))

    def gather_near(self, own):
        sources, array = own
        return [
            [(mask, self.swap(array, mask)) for mask in self.masks(group)]
            for group in (self.near, self.middle)
        ]

    def gather_corner(self, own, near):
        sources, half = own[0], len(own[0]) // 2
        pieces, corners, sent = [own], [], []
        for group in near:
            pieces += [([s ^ mask for s in sources], array) for mask, array in group]
        for mask_x, array_x in near[0]:
            for mask_y, array_y in near[1]:
                low, high = halves(array_y, array_x)
                sent += [low, high]
                corner = mask_x ^ mask_y
                corners.append(([s ^ corner for s in sources[:half]], self.swap(low, mask_x)))
                corners.append(([s ^ corner for s in sources[half:]], self.swap(high, mask_y)))
        return pieces, corners, sent

    def gather_core(self, pieces):
        return pieces + [([s ^ 1 for s in own], self.swap(array, 1)) for own, array in pieces]

    def inner_masks(self):
        near, middle = self.masks(self.near), self.masks(self.middle)
        return near + middle + [x | y for x in near for y in middle]

    def gather_round(self, sources, array, masks):
        array = jnp.concatenate([array] + [self.swap(array, mask) for mask in masks])
        return [source ^ mask for mask in [0] + masks for source in sources], array

    def take(self, term, bits, mask, present, me):
        present = list(present)
        for bit in bits:
            place = present.index(bit)
            low = 1 << (len(present) - 1 - place)
            value = (me >> bit & 1) ^ (mask >> bit & 1)
            rest = term.shape[1:]
            term = term.reshape((1 << place, 2, low) + rest)
            term = lax.dynamic_index_in_dim(term, value, 1, keepdims=False)
            term = term.reshape((low << place,) + rest)
            present.remove(bit)
        return term

    def scatter_core(self, halves):
        keep, send = halves
        return [keep, self.swap(send, 1)], list(range(self.bits - 1, 0, -1))

    def added(self, parts, dtype):
        parts = [part.astype(F32) for part in parts]
        return sum(parts[1:], parts[0]).astype(dtype)

    def scatter_step(self, state, group, me):
        terms, present = state
        sent = []
        for mask in self.masks(group):
            parts = [self.take(term, group, mask, present, me) for term in terms]
            sent.append(self.added(parts, terms[0].dtype))
        received = [self.swap(part, mask) for part, mask in zip(sent, self.masks(group))]
        terms = [self.take(term, group, 0, present, me) for term in terms] + received
        return (terms, [bit for bit in present if bit not in group]), sent

    def scatter_corner(self, state, me):
        terms, present = state
        left = [bit for bit in present if bit not in self.near]
        found, sent = [], []
        for mask_x in self.masks(self.near):
            row = [self.take(term, self.near, mask_x, present, me) for term in terms]
            for mask_y in self.masks(self.middle):
                parts = [self.take(term, self.middle, mask_y, left, me) for term in row]
                half = parts[0].shape[0] // 2
                low = self.added([part[:half] for part in parts], terms[0].dtype)
                high = self.added([part[half:] for part in parts], terms[0].dtype)
                sent += [low, high]
                found.append((mask_x, mask_y, self.swap(low, mask_x), self.swap(high, mask_y)))
        return found, sent

    def scatter_near(self, state, corner, me):
        terms, present = state
        left = [bit for bit in present if bit not in self.near]
        mine, received, sent = [self.take(t, self.near, 0, present, me) for t in terms], [], []
        for mask_x in self.masks(self.near):
            row = [self.take(term, self.near, mask_x, present, me) for term in terms]
            parts = [self.take(term, self.middle, 0, left, me) for term in row]
            for mask, _, _, high in corner:
                if mask == mask_x:
                    parts.append(jnp.concatenate([jnp.zeros_like(high), high]))
            sent.append((self.added(parts, terms[0].dtype), mask_x))
        for mask_y in self.masks(self.middle):
            parts = [self.take(term, self.middle, mask_y, left, me) for term in mine]
            for _, mask, low, _ in corner:
                if mask == mask_y:
                    parts.append(jnp.concatenate([low, jnp.zeros_like(low)]))
            sent.append((self.added(parts, terms[0].dtype), mask_y))
        received = [self.swap(part, mask) for part, mask in sent]
        terms = [self.take(term, self.middle, 0, left, me) for term in mine] + received
        left = [bit for bit in left if bit not in self.middle]
        return (terms, left), [part for part, _ in sent]

    def scatter_far(self, state, me):
        return self.scatter_step(state, self.outer, me)

    def scatter_end(self, state):
        return self.added(state[0], F32)[0]

    def scatter(self, halves, order, me):
        state = self.scatter_core(halves)
        for group in order:
            state, _ = self.scatter_step(state, group, me)
        return self.scatter_end(state)

    def scatter_whole(self, whole, order, me):
        present = list(range(self.bits - 1, -1, -1))
        halves = [self.take(whole, self.core, mask, present, me) for mask in (0, 1)]
        return self.scatter(halves, order, me)


def after(values, others):
    leaves, tree = jax.tree.flatten(values)
    arrays = [leaf for leaf in leaves if not isinstance(leaf, int)]
    others = [leaf for leaf in jax.tree.leaves(others) if not isinstance(leaf, int)]
    tied = iter(lax.optimization_barrier(tuple(arrays + others)))
    return jax.tree.unflatten(
        tree, [leaf if isinstance(leaf, int) else next(tied) for leaf in leaves]
    )


class Weights:
    def __init__(self, net, me, wanted):
        self.arrays, self.plans, self.shapes = [], [], []
        seen = {}
        for pieces, places, rows in wanted:
            places = (places,) if isinstance(places, int) else tuple(places)
            columns = pieces[0][1].shape[-1]
            plan = []
            if rows % 16:
                blocks = [
                    jnp.concatenate([array[:, place : place + rows] for _, array in pieces])
                    for place in places
                ]
                blocks = jnp.concatenate(blocks, axis=2)
                order = jnp.asarray([s for own, _ in pieces for s in own], jnp.int32)
                spot = jnp.zeros((net.n,), jnp.int32).at[order ^ me].set(jnp.arange(net.n))
                whole = blocks[spot].reshape(net.n * rows // 16, 16, len(places) * columns)
                plan.append((len(self.arrays), None, None, None))
                self.arrays.append(whole)
                self.shapes.append(whole.shape)
            else:
                for own, array in pieces:
                    if id(array) not in seen:
                        seen[id(array)] = len(self.arrays)
                        self.arrays.append(array)
                    for j, source in enumerate(own):
                        for k, place in enumerate(places):
                            aim = pl.ds(k * columns, columns)
                            plan.append((seen[id(array)], (j, pl.ds(place, rows)), source, aim))
                self.shapes.append((net.n, rows, len(places) * columns))
            self.plans.append(plan)
        self.slots = max(len(plan) for plan in self.plans)

    def scratch(self):
        return [pltpu.VMEM(shape, BF16) for shape in self.shapes] + [
            pltpu.SemaphoreType.DMA((len(self.plans), self.slots))
        ]

    def copies(self, w, me, array_refs, held_ref, sems):
        found = []
        for slot, (array, index, source, aim) in enumerate(self.plans[w]):
            if index is None:
                pair = (array_refs[array], held_ref)
            else:
                pair = (array_refs[array].at[index], held_ref.at[me ^ source, :, aim])
            found.append(pltpu.make_async_copy(*pair, sems.at[w, slot]))
        return found

    def start(self, w, *refs):
        for copy in self.copies(w, *refs):
            copy.start()

    def wait(self, w, *refs):
        for copy in self.copies(w, *refs):
            copy.wait()


def flat(held):
    return held.reshape(-1, held.shape[-1])


SMEM_SPEC = pl.BlockSpec(memory_space=pltpu.SMEM)
ANY_SPEC = pl.BlockSpec(memory_space=pltpu.HBM)


def full_spec(shape):
    return pl.BlockSpec(shape, lambda *_: (0,) * len(shape))


def tile_spec(tile, columns):
    return pl.BlockSpec((tile, columns), lambda i: (i, 0))


def call(body, name, grid, ins, outs, scratch, us, bases=()):
    count = len(ins)

    def run(*refs):
        body(*refs[:count], *refs[count + len(bases) :])

    return pl.pallas_call(
        run,
        grid=grid,
        in_specs=[spec for _, spec in ins] + [ANY_SPEC] * len(bases),
        out_specs=[spec for _, _, spec in outs],
        out_shape=[jax.ShapeDtypeStruct(shape, dtype) for shape, dtype, _ in outs],
        scratch_shapes=scratch,
        input_output_aliases={count + i: i for i in range(len(bases))},
        compiler_params=pltpu.CompilerParams(
            vmem_limit_bytes=60 << 20,
            dimension_semantics=("arbitrary",) * len(grid),
        ),
        cost_estimate=pl.CostEstimate(
            flops=int(us * 2e10), bytes_accessed=int(us * 5e7), transcendentals=0
        ),
        name=name,
    )(*[array for array, _ in ins], *bases)


def sum_body(groups, me_ref, *refs):
    step = pl.program_id(0)
    outs = refs[len(refs) - len(groups) :]
    for out_ref, addends in zip(outs, groups):
        total = None
        for place, (low, high) in addends:
            part = refs[place][...].astype(F32)
            if low is not None:
                part = jnp.where((step >= low) & (step < high), part, 0.0)
            total = part if total is None else total + part
        out_ref[...] = total.astype(out_ref.dtype)


def sum_call(me, name, grid, ins, groups, outs, body=None, us=0.01):
    grid_spec = pltpu.PrefetchScalarGridSpec(
        num_scalar_prefetch=1,
        grid=(grid,),
        in_specs=[
            pl.BlockSpec(block, lambda i, me_ref, place=place: place(i, me_ref[0]))
            for _, block, place in ins
        ],
        out_specs=[
            pl.BlockSpec(block, lambda i, me_ref, place=place: place(i, me_ref[0]))
            for _, _, block, place in outs
        ],
    )
    return pl.pallas_call(
        body or functools.partial(sum_body, groups),
        grid_spec=grid_spec,
        out_shape=[jax.ShapeDtypeStruct(shape, dtype) for shape, dtype, _, _ in outs],
        compiler_params=pltpu.CompilerParams(
            vmem_limit_bytes=60 << 20, dimension_semantics=("arbitrary",)
        ),
        cost_estimate=pl.CostEstimate(flops=int(us * 2e10), bytes_accessed=int(us * 5e7), transcendentals=0),
        name=name,
    )(me.reshape(1), *[array for array, _, _ in ins])


class Reduction:
    def __init__(self, net, me, keep, send):
        self.net, self.me = net, me
        self.terms = [keep, net.swap(send, 1)]
        self.rows, self.columns = keep.shape[1:]
        self.plain = len(net.near) == 1 and len(net.middle) == 1 and self.rows % 8 == 0
        self.state = None

    def block(self):
        return (1, self.rows, self.columns)

    def hold(self, others):
        if self.plain:
            self.terms = after(self.terms, others)
        else:
            state = self.state or (self.terms, list(range(self.net.bits - 1, 0, -1)))
            self.state = held(state, others)
            if getattr(self, "corner_pieces", None) is not None:
                self.corner_pieces = after(self.corner_pieces, others)
        return self

    def corner(self):
        net = self.net
        if not self.plain:
            state = self.state or (self.terms, list(range(net.bits - 1, 0, -1)))
            self.state = state
            self.corner_pieces, sent = net.scatter_corner(state, self.me)
            return sent
        far = 1 << (len(net.outer) - 1)

        def place(shift):
            return lambda i, me: ((i + shift) * 4 + (me >> 1 & 3 ^ 3), 0, 0)

        ins = [(term, self.block(), place(shift)) for shift in (0, far) for term in self.terms]
        out = ((far, self.rows, self.columns), BF16, self.block(), lambda i, me: (i, 0, 0))
        always = (None, None)
        groups = [[(0, always), (1, always)], [(2, always), (3, always)]]
        low, high = sum_call(self.me, "corner_sum", far, ins, groups, [out, out])
        self.terms += [net.swap(low, 1 << net.near[0]), net.swap(high, 1 << net.middle[0])]
        return [low, high]

    def near(self):
        net = self.net
        if not self.plain:
            self.state, sent = net.scatter_near(self.state, self.corner_pieces, self.me)
            self.corner_pieces = None
            return sent
        far = 1 << (len(net.outer) - 1)
        keep, other, low, high = self.terms

        def place(flip):
            return lambda i, me: (i * 4 + (me >> 1 & 3 ^ flip), 0, 0)

        ins = [(term, self.block(), place(flip)) for flip in (1, 2) for term in (keep, other)]
        ins.append((high, self.block(), lambda i, me: (jnp.maximum(i - far, 0), 0, 0)))
        ins.append((low, self.block(), lambda i, me: (jnp.minimum(i, far - 1), 0, 0)))
        always = (None, None)
        groups = [
            [(0, always), (1, always), (4, (far, 2 * far))],
            [(2, always), (3, always), (5, (0, far))],
        ]
        out = ((2 * far, self.rows, self.columns), BF16, self.block(), lambda i, me: (i, 0, 0))
        sent = sum_call(self.me, "near_sum", 2 * far, ins, groups, [out, out])
        received = [
            net.swap(part, 1 << group[0]) for part, group in zip(sent, (net.near, net.middle))
        ]
        self.terms = [keep, other] + received
        return sent

    def sources(self, flip, step_block):
        keep, other, row, column = self.terms[:4]
        found = []
        for term in (keep, other):
            found.append((term, lambda me: ((me >> 3 ^ flip) * 4 + (me >> 1 & 3))))
        for term in (row, column):
            found.append((term, lambda me: (me >> 3 ^ flip)))
        return [
            (term, step_block[0], lambda i, me, at=at: step_block[1](i, at(me)))
            for term, at in found
        ]

    def far(self):
        net = self.net
        if not self.plain:
            self.state, sent = net.scatter_step(self.state, net.outer, self.me)
            return sent
        parts = 2 if self.rows % 32 == 0 else 1
        step_block = ((1, self.rows // parts, self.columns), lambda i, at: (at, i, 0))
        masks = net.masks(net.outer)
        ins, groups = [], []
        for mask in masks:
            groups.append([(len(ins) + j, (None, None)) for j in range(4)])
            ins += self.sources(mask >> 3, step_block)
        out = ((1, self.rows, self.columns), BF16, step_block[0], lambda i, me: (0, i, 0))
        sent = sum_call(self.me, "far_sum", parts, ins, groups, [out] * len(masks))
        self.terms += [net.swap(part, mask) for part, mask in zip(sent, masks)]
        return sent

    def received(self):
        return self.terms[-1] if self.plain else self.state[0][-1]

    def end(self, lots, unit):
        if not self.plain:
            total = self.net.scatter_end(self.state)
            results, start = [], 0
            for count in lots:
                blocks = [
                    total[(start + j) * unit : (start + j + 1) * unit] for j in range(count)
                ]
                results.append(jnp.concatenate(blocks, axis=1))
                start += count
            return results
        step_block = ((1, unit, self.columns), lambda i, at: (at, i, 0))
        ins = self.sources(0, step_block)
        ins += [(term, step_block[0], lambda i, me: (0, i, 0)) for term in self.terms[4:]]
        outs, bounds, start = [], [], 0
        for count in lots:

            def place(i, me, start=start, count=count):
                return (0, jnp.clip(i - start, 0, count - 1))

            outs.append(((unit, count * self.columns), F32, (unit, self.columns), place))
            bounds.append((start, start + count))
            start += count

        def body(me_ref, *refs):
            step, addends = pl.program_id(0), refs[: len(ins)]
            total = addends[0][0].astype(F32)
            for ref in addends[1:]:
                total = total + ref[0].astype(F32)
            for out_ref, (low, high) in zip(refs[len(ins) :], bounds):

                @pl.when((step >= low) & (step < high))
                def _():
                    out_ref[...] = total

        return sum_call(self.me, "end_sum", start, ins, None, outs, body, 4)


def pack_body(sizes, me_ref, small_ref, *refs):
    shards, out_ref = refs[:-1], refs[-1]
    start = 0
    for ref in shards:
        out_ref[start : start + ref.shape[0]] = ref[...]
        start += ref.shape[0]
    me, width = me_ref[0], out_ref.shape[1]

    small = small_ref[...]
    step, inner_size, steps = sizes

    def spread(first, count, offset):
        spots = lax.broadcasted_iota(jnp.int32, (small.shape[1], width), 0) - first
        lanes = lax.broadcasted_iota(jnp.int32, (small.shape[1], width), 1)
        hits = (spots >= 0) & (spots < count) & (lanes == spots + offset)
        return matmul(small, jnp.where(hits, 1.0, 0.0).astype(BF16))

    vectors = spread(0, step, me * step)
    place = me * inner_size
    inner = spread(step, inner_size, lax.rem(place, width))
    row = lax.broadcasted_iota(jnp.int32, inner.shape, 0)
    inner = jnp.where(row == place // width, inner, 0.0)
    times = spread(step + inner_size, steps, me * steps)
    out_ref[start:] = jnp.concatenate([vectors, inner + times]).astype(BF16)


def pack(me, shards, vectors, inner, times):
    step, width = shards[0].shape
    sizes = (step, inner.shape[0], times.shape[0])
    small = 0.0
    for line, vector in enumerate(vectors):
        small += jnp.pad(vector.astype(F32)[None], ((line, 7 - line), (0, 256 - step)))
    rest = 256 - sizes[1] - step
    small += jnp.pad(inner.astype(F32)[None], ((0, 0), (step, rest)))
    for line, digits in ((4, times // 64), (5, times % 64)):
        left = step + sizes[1]
        right = 256 - left - sizes[2]
        small += jnp.pad(digits.astype(F32)[None], ((line, 7 - line), (left, right)))
    small = small.astype(BF16)
    rows = len(shards) * step + 16
    return call(
        functools.partial(pack_body, sizes),
        "pack",
        (1,),
        [(me.reshape(1), SMEM_SPEC)]
        + [(array, full_spec(array.shape)) for array in (small, *shards)],
        [((rows, width), BF16, full_spec((rows, width)))],
        [],
        1,
    )[0]


def project_body(weights, tile, row_length, me_ref, *refs):
    count = len(weights.arrays)
    arrays, refs = refs[:count], refs[count:]
    feats_ref, x_ref = refs[:2]
    temb_ref, lines_ref, low_ref, q_ref, k_ref, v_ref = refs[2:8]
    tw, qw, kw, vw, lw, sems = refs[8:14]
    me, step = me_ref[0], pl.program_id(0)

    @pl.when(step == 0)
    def _():
        for w, held in enumerate((tw, qw, kw, vw, lw)):
            weights.start(w, me, arrays, held, sems)
        weights.wait(0, me, arrays, tw, sems)
        temb_ref[...] = matmul(feats_ref[...], flat(tw[...]))
        weights.wait(4, me, arrays, lw, sems)
        lines_ref[...] = jnp.sum(lw[...].astype(F32), axis=0)
        for w, held in ((1, qw), (2, kw), (3, vw)):
            weights.wait(w, me, arrays, held, sems)

    row = step * tile // row_length
    low = (x_ref[...].astype(F32) + temb_ref[pl.ds(row, 1), :]).astype(BF16)
    low_ref[...] = low
    q_ref[...] = (matmul(low, flat(qw[...])) + lines_ref[0:1]).astype(BF16)
    k_ref[...] = matmul(low, flat(kw[...])).astype(BF16)
    v_ref[...] = (matmul(low, flat(vw[...])) + lines_ref[1:2]).astype(BF16)


def project(net, me, flow, feats, x, row_length):
    tokens, width = x.shape
    tile = min(256, row_length)
    r = width // net.n
    weights = Weights(net, me, [(flow, w * r, r) for w in range(4)] + [(flow, 4 * r, 16)])
    ins = (
        [(me.reshape(1), SMEM_SPEC)]
        + [(array, ANY_SPEC) for array in weights.arrays]
        + [(feats, full_spec(feats.shape)), (x, tile_spec(tile, width))]
    )
    outs = [(feats.shape, F32, full_spec(feats.shape))]
    outs += [((16, width), F32, full_spec((16, width)))]
    outs += [((tokens, width), BF16, tile_spec(tile, width))] * 4
    return call(
        functools.partial(project_body, weights, tile, row_length),
        "project",
        (tokens // tile,),
        ins,
        outs,
        weights.scratch(),
        14,
    )


def same_document(segc_ref, segr_ref, bias_ref, block):
    @pl.when(block == 0)
    def _():
        bias_ref[...] = jnp.where(segc_ref[0] == segr_ref[0], 0.0, -1e30)


def own_lanes(shape, head, head_dim):
    lanes = lax.broadcasted_iota(jnp.int32, shape, len(shape) - 1)
    return (lanes // head_dim) == head


def attend_body(head_dim, segc_ref, segr_ref, q_ref, k_ref, v_ref, out_ref, log_ref, bias_ref):
    same_document(segc_ref, segr_ref, bias_ref, pl.program_id(1))
    queries, key_rows, values = q_ref[...], k_ref[...], v_ref[...]
    scale = 1.0 / math.sqrt(head_dim)
    per = queries.shape[1] // head_dim
    total = None
    for head in range(per):
        mine = own_lanes(queries.shape, head, head_dim)
        keys_own = jnp.where(mine, key_rows * BF16(scale), BF16(0))
        scores = matmul_right(keys_own, queries) + bias_ref[...]
        top = jnp.max(scores, axis=0, keepdims=True)
        raised = jnp.exp(scores - top)
        amount = jnp.sum(raised, axis=0, keepdims=True)
        log_ref[0, 0, pl.ds(head, 1), :] = top + jnp.log(amount)
        soft_low = (raised * (1.0 / amount)).astype(BF16)
        context = matmul_left(soft_low, values)
        total = context if total is None else jnp.where(mine, context, total)
    out_ref[...] = total.astype(BF16)


def attend_back_body(
    head_dim, segc_ref, segr_ref, q_ref, k_ref, v_ref, log_ref, g_ref, gq_ref, gk_ref, gv_ref, sums_ref, rows_ref, bias_ref
):
    same_document(segc_ref, segr_ref, bias_ref, pl.program_id(1))
    queries, key_rows, values, grads = q_ref[...], k_ref[...], v_ref[...], g_ref[...]
    scale = 1.0 / math.sqrt(head_dim)
    per = queries.shape[1] // head_dim
    totals = None
    for head in range(per):
        mine = own_lanes(queries.shape, head, head_dim)
        keys_own = jnp.where(mine, key_rows * BF16(scale), BF16(0))
        scores = matmul_right(keys_own, queries) + bias_ref[...]
        soft = jnp.exp(scores - log_ref[0, 0, pl.ds(head, 1), :])
        grad_soft = matmul_right(jnp.where(mine, values, BF16(0)), grads)
        inner_sum = jnp.sum(soft * grad_soft, axis=0, keepdims=True)
        grad_scores = (soft * (grad_soft - inner_sum)).astype(BF16)
        parts = (
            matmul_left(grad_scores, key_rows),
            matmul(grad_scores, queries),
            matmul(soft.astype(BF16), grads),
        )
        if totals is None:
            totals = parts
        else:
            totals = tuple(jnp.where(mine, part, total) for part, total in zip(parts, totals))
    gq = (totals[0] * scale).astype(BF16)
    gv = totals[2].astype(BF16)
    gq_ref[...] = gq
    gk = (totals[1] * scale).astype(BF16)
    gk_ref[...] = gk
    gv_ref[...] = gv
    sums = [jnp.sum(part.astype(F32), axis=0, keepdims=True) for part in (gq, gk, gv)]
    zero = jnp.zeros_like(sums[0])
    sums_ref[...] = jnp.concatenate([sums[0], sums[2]] + [zero] * 6)
    rows_ref[...] = jnp.concatenate(sums + [zero] * 5)


def attention_args(segments, start, lanes, head_dim):
    row_length, per = segments.shape[1], lanes // head_dim
    segc = pl.BlockSpec((1, row_length, 1), lambda i, j: (start + i, 0, 0))
    segr = pl.BlockSpec((1, 1, row_length), lambda i, j: (start + i, 0, 0))
    block = pl.BlockSpec((row_length, lanes), lambda i, j: (start + i, j))
    log_spec = pl.BlockSpec((1, 1, per, row_length), lambda i, j: (start + i, j, 0, 0))
    return [(segments[:, :, None], segc), (segments[:, None, :], segr)], block, log_spec


def attend(queries, key_rows, values, segments, lanes=256):
    rows, row_length = segments.shape
    tokens, width = queries.shape
    head_dim = width // H
    blocks, per = width // lanes, lanes // head_dim
    masks, block, log_spec = attention_args(segments, 0, lanes, head_dim)
    return call(
        functools.partial(attend_body, head_dim),
        "attend",
        (rows, blocks),
        masks + [(array, block) for array in (queries, key_rows, values)],
        [
            ((tokens, width), BF16, block),
            ((rows, blocks, per, row_length), F32, log_spec),
        ],
        [pltpu.VMEM((row_length, row_length), F32)],
        24,
    )


def attend_back(queries, key_rows, values, segments, log_total, grad_context, row, bases=(), lanes=256):
    rows, row_length = segments.shape
    tokens, width = queries.shape
    head_dim = width // H
    masks, block, log_spec = attention_args(segments, row, lanes, head_dim)
    return call(
        functools.partial(attend_back_body, head_dim),
        "attend_back",
        (1, width // lanes),
        masks
        + [(array, block) for array in (queries, key_rows, values)]
        + [(log_total, log_spec), (grad_context, block)],
        [((tokens, width), BF16, block)] * 3
        + [((8, width), F32, pl.BlockSpec((8, lanes), lambda i, j: (0, j)))] * 2,
        [pltpu.VMEM((row_length, row_length), F32)],
        19,
        bases,
    )


def add_to(ref, value, step):
    part = jnp.sum(value, axis=0, keepdims=True)

    @pl.when(step == 0)
    def _():
        ref[...] = part

    @pl.when(step != 0)
    def _():
        ref[...] += part


def add_lines(ref, values, step):
    zero = jnp.zeros((1, ref.shape[1]), F32)
    sums = {line: jnp.sum(value, axis=0, keepdims=True) for line, value in values.items()}
    part = jnp.concatenate([sums.get(line, zero) for line in range(ref.shape[0])])

    @pl.when(step == 0)
    def _():
        ref[...] = part

    @pl.when(step != 0)
    def _():
        ref[...] += part


def ffn_in_body(weights, tile, row_length, chunk, me_ref, *refs):
    count = len(weights.arrays)
    arrays, refs = refs[:count], refs[count:]
    context_ref, x_ref, temb_ref, lines_ref = refs[:4]
    first_low_ref, normed_ref, spread_ref, active_ref, slope_ref = refs[4:9]
    ow, iw, sems = refs[9:12]
    me, step = me_ref[0], pl.program_id(0)

    @pl.when(step == 0)
    def _():
        for w, held in enumerate((ow, iw)):
            weights.start(w, me, arrays, held, sems)
        weights.wait(0, me, arrays, ow, sems)

    row = step * tile // row_length
    stream = x_ref[...].astype(F32) + temb_ref[pl.ds(row, 1), :]
    mixed = stream + (matmul(context_ref[...], flat(ow[...])) + lines_ref[2:3])
    normed, spread = normalize(mixed)
    normed_ref[...] = normed
    spread_ref[...] = spread
    first = normed * lines_ref[4:5] + lines_ref[5:6]
    low = first.astype(BF16)
    first_low_ref[...] = low

    @pl.when(step == 0)
    def _():
        weights.wait(1, me, arrays, iw, sems)

    width, hidden = ow.shape[2], iw.shape[2]

    def inner(start):
        pre = matmul(low, flat(iw[:, :, start : start + chunk]))
        line, place = 8 + start // width, start % width
        return pre + lines_ref[line : line + 1, place : place + chunk]

    later = inner(0)
    for start in range(0, hidden, chunk):
        pre = later
        if start + chunk < hidden:
            later = inner(start + chunk)
        columns = slice(start, start + chunk)
        normal_cdf = 0.5 * (1.0 + lax.erf(pre * INV_ROOT_TWO))
        normal_pdf = jnp.exp(-0.5 * pre * pre) * INV_ROOT_TAU
        active_ref[:, columns] = (pre * normal_cdf).astype(BF16)
        slope_ref[:, columns] = (normal_cdf + pre * normal_pdf).astype(BF16)


def ffn_in(net, me, flow, context, x, temb, lines, hidden, row_length, tile=256, chunk=512):
    tokens, width = x.shape
    r = width // net.n
    blocks = range(r, r + hidden // width * r, r)
    weights = Weights(net, me, [(flow, 0, r), (flow, blocks, r)])
    tile = min(tile, row_length)
    tiled, wide, thin = (tile_spec(tile, columns) for columns in (width, hidden, 1))
    ins = (
        [(me.reshape(1), SMEM_SPEC)]
        + [(array, ANY_SPEC) for array in weights.arrays]
        + [(context, tiled), (x, tiled)]
        + [(array, full_spec(array.shape)) for array in (temb, lines)]
    )
    outs = [
        ((tokens, width), BF16, tiled),
        ((tokens, width), F32, tiled),
        ((tokens, 1), F32, thin),
        ((tokens, hidden), BF16, wide),
        ((tokens, hidden), BF16, wide),
    ]
    return call(
        functools.partial(ffn_in_body, weights, tile, row_length, chunk),
        "ffn_in",
        (tokens // tile,),
        ins,
        outs,
        weights.scratch(),
        30,
    )


def ffn_out_body(weights, me_ref, *refs):
    count = len(weights.arrays)
    arrays, refs = refs[:count], refs[count:]
    active_ref, normed_ref, cot_ref, lines_ref = refs[:4]
    out_ref, gs_ref, gs_low_ref, sums_ref = refs[4:8]
    uw, sems = refs[8:10]
    me, step = me_ref[0], pl.program_id(0)

    @pl.when(step == 0)
    def _():
        weights.start(0, me, arrays, uw, sems)
        weights.wait(0, me, arrays, uw, sems)

    first = normed_ref[...] * lines_ref[4:5] + lines_ref[5:6]
    second = first + (matmul(active_ref[...], flat(uw[...])) + lines_ref[3:4])
    normed_second, spread_second = normalize(second)
    out_ref[...] = (normed_second * lines_ref[6:7] + lines_ref[7:8]).astype(BF16)
    grad_out = cot_ref[...].astype(F32)
    grad_second = norm_back(grad_out * lines_ref[6:7], normed_second, spread_second)
    gs_ref[...] = grad_second
    low = grad_second.astype(BF16)
    gs_low_ref[...] = low
    add_lines(sums_ref, {3: low.astype(F32), 6: grad_out * normed_second, 7: grad_out}, step)


def ffn_out(net, me, flow, active, normed, cotangent, vectors, tile=256):
    tokens, width = normed.shape
    hidden = active.shape[1]
    weights = Weights(net, me, [(flow, 0, hidden // net.n)])
    tiled, wide = tile_spec(tile, width), tile_spec(tile, hidden)
    ins = (
        [(me.reshape(1), SMEM_SPEC)]
        + [(array, ANY_SPEC) for array in weights.arrays]
        + [(active, wide), (normed, tiled), (cotangent, tiled)]
        + [(vector, full_spec(vector.shape)) for vector in vectors]
    )
    outs = [
        ((tokens, width), BF16, tiled),
        ((tokens, width), F32, tiled),
        ((tokens, width), BF16, tiled),
        ((8, width), F32, full_spec((8, width))),
    ]
    return call(
        functools.partial(ffn_out_body, weights),
        "ffn_out",
        (tokens // tile,),
        ins,
        outs,
        weights.scratch(),
        20,
    )


def ffn_back_body(weights, tile, row_length, chunk, me_ref, *refs):
    count = len(weights.arrays)
    arrays, refs = refs[:count], refs[count:]
    (gs_ref, gs_low_ref, slope_ref, normed_ref, spread_ref, lines_ref) = refs[:6]
    (gi_ref, gm_ref, gm_low_ref, gc_ref, ibg_ref, sums_ref, rows_ref) = refs[6:13]
    uw, ow, iw, sems = refs[13:17]
    me, step = me_ref[0], pl.program_id(0)

    @pl.when(step == 0)
    def _():
        for w, held in ((0, uw), (2, iw), (1, ow)):
            weights.start(w, me, arrays, held, sems)
        weights.wait(0, me, arrays, uw, sems)

    unit = uw.shape[1]
    hidden = iw.shape[2]
    for start in range(0, hidden, chunk):
        columns = slice(start, start + chunk)
        held = flat(uw[start // unit : (start + chunk) // unit])
        grad_active = matmul_right(gs_low_ref[...], held)
        gi_ref[:, columns] = (grad_active * slope_ref[:, columns].astype(F32)).astype(BF16)

    @pl.when(step == 0)
    def _():
        weights.wait(2, me, arrays, iw, sems)

    grad_first = gs_ref[...] + matmul_right(gi_ref[...], flat(iw[...]))
    add_to(ibg_ref, gi_ref[...].astype(F32), step)
    normed = normed_ref[...]
    grad_mixed = norm_back(grad_first * lines_ref[4:5], normed, spread_ref[...])
    gm_ref[...] = grad_mixed

    @pl.when(step == 0)
    def _():
        rows_ref[...] = jnp.zeros_like(rows_ref)

    row = pl.ds(step * tile // row_length, 1)
    rows_ref[row, :] += jnp.sum(grad_mixed, axis=0, keepdims=True)
    low = grad_mixed.astype(BF16)
    gm_low_ref[...] = low
    add_lines(sums_ref, {2: low.astype(F32), 4: grad_first * normed, 5: grad_first}, step)

    @pl.when(step == 0)
    def _():
        weights.wait(1, me, arrays, ow, sems)

    gc_ref[...] = matmul_right(low, flat(ow[...])).astype(BF16)


def ffn_back(net, me, flow_u, flow_io, gs, gs_low, slope, normed, spread, lines, row_length, tile=256, chunk=1024):
    tokens, width = gs.shape
    hidden = slope.shape[1]
    r = width // net.n
    weights = Weights(
        net,
        me,
        [
            (flow_u, 0, hidden // net.n),
            (flow_io, 0, r),
            (flow_io, range(r, r + hidden // width * r, r), r),
        ],
    )
    tile = min(tile, row_length)
    tiled, wide = tile_spec(tile, width), tile_spec(tile, hidden)
    ins = (
        [(me.reshape(1), SMEM_SPEC)]
        + [(array, ANY_SPEC) for array in weights.arrays]
        + [(gs, tiled), (gs_low, tiled), (slope, wide), (normed, tiled)]
        + [(spread, tile_spec(tile, 1)), (lines, full_spec(lines.shape))]
    )
    outs = [
        ((tokens, hidden), BF16, wide),
        ((tokens, width), F32, tiled),
        ((tokens, width), BF16, tiled),
        ((tokens, width), BF16, tiled),
        ((1, hidden), F32, full_spec((1, hidden))),
        ((8, width), F32, full_spec((8, width))),
        ((8, width), F32, full_spec((8, width))),
    ]
    return call(
        functools.partial(ffn_back_body, weights, tile, row_length, chunk),
        "ffn_back",
        (tokens // tile,),
        ins,
        outs,
        weights.scratch(),
        38,
    )


def deal(me_ref, total, rows, keep_ref, send_ref, kind=0):
    core = me_ref[0] & 1
    total = total.reshape(-1, 2, rows, total.shape[-1])
    low, high = total[:, 0], total[:, 1]
    place = slice(kind * rows, (kind + 1) * rows)
    keep_ref[:, place] = jnp.where(core == 0, low, high).astype(BF16)
    send_ref[:, place] = jnp.where(core == 0, high, low).astype(BF16)


def product_body(rows, me_ref, a_ref, b_ref, keep_ref, send_ref):
    deal(me_ref, matmul_left(a_ref[...], b_ref[...]), rows, keep_ref, send_ref)


def product(net, me, left, right, tile=1024):
    tokens, width = left.shape
    columns = right.shape[1]
    rows = width // net.n
    shape = (net.n // 2, rows, columns)
    block = pl.BlockSpec((tile // (2 * rows), rows, columns), lambda i: (i, 0, 0))
    return call(
        functools.partial(product_body, rows),
        "product",
        (width // tile,),
        [
            (me.reshape(1), SMEM_SPEC),
            (left, pl.BlockSpec((tokens, tile), lambda i: (0, i))),
            (right, full_spec((tokens, columns))),
        ],
        [(shape, BF16, block), (shape, BF16, block)],
        [],
        15,
    )


def inner_body(rows, me_ref, context_ref, first_ref, gm_ref, gi_ref, keep_ref, send_ref):
    total = matmul_left(first_ref[...], gi_ref[...])
    width = gm_ref.shape[1]
    deal(me_ref, matmul_left(context_ref[...], gm_ref[...]), rows, keep_ref, send_ref, 0)
    for k in range(total.shape[1] // width):
        part = total[:, k * width : (k + 1) * width]
        deal(me_ref, part, rows, keep_ref, send_ref, k + 1)


def inner_product(net, me, context, first_low, gm_low, gi, tile=256):
    tokens, width = context.shape
    hidden = gi.shape[1]
    rows = width // net.n
    kinds = 1 + hidden // width
    shape = (net.n // 2, kinds * rows, width)
    block = pl.BlockSpec((tile // (2 * rows), kinds * rows, width), lambda i: (i, 0, 0))
    left = pl.BlockSpec((tokens, tile), lambda i: (0, i))
    return call(
        functools.partial(inner_body, rows),
        "inner_product",
        (width // tile,),
        [
            (me.reshape(1), SMEM_SPEC),
            (context, left),
            (first_low, left),
            (gm_low, full_spec((tokens, width))),
            (gi, full_spec((tokens, hidden))),
        ],
        [(shape, BF16, block), (shape, BF16, block)],
        [],
        18,
    )


def triple_body(rows, me_ref, lines_ref, a_ref, q_ref, k_ref, v_ref, keep_ref, send_ref):
    for w, ref in enumerate((q_ref, k_ref, v_ref)):
        deal(me_ref, matmul_left(a_ref[...], ref[...]), rows, keep_ref, send_ref, w)
    core = me_ref[0] & 1
    low, high = lines_ref[:, 0:8], lines_ref[:, 8:16]
    place = slice(3 * rows, 3 * rows + 8)
    keep_ref[:, place] = jnp.where(core == 0, low, high).astype(BF16)
    send_ref[:, place] = jnp.where(core == 0, high, low).astype(BF16)


def triple_product(net, me, lines, left, gq, gk, gv, tile=256):
    tokens, width = left.shape
    rows = width // net.n
    shape = (net.n // 2, 3 * rows + 8, width)
    chips = tile // (2 * rows)
    block = pl.BlockSpec((chips, 3 * rows + 8, width), lambda i: (i, 0, 0))
    full = full_spec((tokens, width))
    return call(
        functools.partial(triple_body, rows),
        "triple_product",
        (width // tile,),
        [
            (me.reshape(1), SMEM_SPEC),
            (lines, pl.BlockSpec((chips, 16, width), lambda i: (i, 0, 0))),
            (left, pl.BlockSpec((tokens, tile), lambda i: (0, i))),
            (gq, full),
            (gk, full),
            (gv, full),
        ],
        [(shape, BF16, block), (shape, BF16, block)],
        [],
        13,
    )


def stream_back_body(weights, rows, me_ref, *refs):
    count = len(weights.arrays)
    arrays, refs = refs[:count], refs[count:]
    gm_ref, gq_ref, gk_ref, gv_ref = refs[:4]
    sum_refs, refs = refs[4 : 4 + rows], refs[4 + rows :]
    out_ref, outs = refs[0], refs[1:]
    qw, kw, vw, sems = outs[-4:]
    me, step = me_ref[0], pl.program_id(0)

    @pl.when(step == 0)
    def _():
        for w, held in enumerate((qw, kw, vw)):
            weights.start(w, me, arrays, held, sems)
        for w, held in enumerate((qw, kw, vw)):
            weights.wait(w, me, arrays, held, sems)
        if sum_refs:
            total = sum_refs[0][...]
            for w, held in enumerate((qw, kw, vw)):
                lines = [ref[w : w + 1] for ref in sum_refs[1:]]
                lines += [jnp.zeros_like(lines[0])] * (8 - len(lines))
                total += matmul_right(jnp.concatenate(lines).astype(BF16), flat(held[...]))
            outs[0][...] = total

    out_ref[...] = (
        gm_ref[...]
        + matmul_right(gq_ref[...], flat(qw[...]))
        + matmul_right(gk_ref[...], flat(kw[...]))
        + matmul_right(gv_ref[...], flat(vw[...]))
    )


def stream_back(net, me, flow, gm, gq, gk, gv, row, row_length, base=None, sums=(), tile=256):
    tokens, width = gm.shape
    tile = min(tile, row_length)
    r = width // net.n
    weights = Weights(net, me, [(flow, w * r, r) for w in (1, 2, 3)])
    start = row * (row_length // tile)
    tiled = pl.BlockSpec((tile, width), lambda i: (start + i, 0))
    ins = (
        [(me.reshape(1), SMEM_SPEC)]
        + [(array, ANY_SPEC) for array in weights.arrays]
        + [(array, tiled) for array in (gm, gq, gk, gv)]
        + [(array, full_spec((8, width))) for array in sums]
    )
    outs = [((tokens, width), F32, tiled)]
    if sums:
        outs.append(((8, width), F32, full_spec((8, width))))
    return call(
        functools.partial(stream_back_body, weights, len(sums)),
        "stream_back",
        (row_length // tile,),
        ins,
        outs,
        weights.scratch(),
        10,
        () if base is None else (base,),
    )


def in_order(net, me, sources, blocks):
    order = jnp.asarray(sources, jnp.int32)
    spot = jnp.zeros((net.n,), jnp.int32).at[order].set(jnp.arange(net.n, dtype=jnp.int32))
    return blocks[spot[jnp.arange(net.n) ^ me]]


def held(state, others):
    return after(state[0], others), state[1]


def stream_ends(state, unit, sizes):
    if not state.plain:
        total = state.net.scatter_end(state.state)
        found, start = [total[w * unit : (w + 1) * unit] for w in range(3)], 0
        for size in sizes:
            found.append(total[3 * unit, start : start + size])
            start += size
        return found
    rows, columns = state.rows, state.columns
    step_block = ((1, rows, columns), lambda i, at: (at, 0, 0))
    ins = state.sources(0, step_block)
    ins += [(term, step_block[0], lambda i, me: (0, 0, 0)) for term in state.terms[4:]]
    shapes = [(unit, columns)] * 3 + [(1, size) for size in sizes]
    outs = [(shape, F32, shape, lambda i, me: (0, 0)) for shape in shapes]

    def body(me_ref, *refs):
        total = refs[0][0].astype(F32)
        for ref in refs[1 : len(ins)]:
            total = total + ref[0].astype(F32)
        outs = refs[len(ins) :]
        for w in range(3):
            outs[w][...] = total[w * unit : (w + 1) * unit]
        start = 0
        for out_ref, size in zip(outs[3:], sizes):
            out_ref[...] = total[3 * unit : 3 * unit + 1, start : start + size]
            start += size

    results = sum_call(state.me, "stream_end", 1, ins, None, outs, body)
    return list(results[:3]) + [result[0] for result in results[3:]]


def on_device(
    net,
    inputs,
    timesteps,
    segments,
    cotangent,
    query_weight,
    key_weight,
    value_weight,
    output_weight,
    inner_weight,
    outer_weight,
    time_weight,
    *vectors,
):
    n = net.n
    me = lax.axis_index("fsdp").astype(jnp.int32)
    batch_count, row_count, row_length, model_width = inputs.shape
    rows = batch_count * row_count
    tokens = rows * row_length
    feats = features(timesteps.reshape(rows)).astype(BF16)
    order = (0, 1, 2, 4, 5, 6, 7, 8, 3)
    sizes = [vectors[i].shape[0] for i in order]
    r = model_width // n

    shards = (time_weight, query_weight, key_weight, value_weight)
    lines = [vectors[i] for i in order[:8]]
    far = net.gather_far(pack(me, shards, lines, vectors[3], timesteps.reshape(rows)))
    hidden = inner_weight.shape[1]
    inner_blocks = [
        inner_weight[:, start : start + model_width] for start in range(0, hidden, model_width)
    ]
    shard_io = after(jnp.concatenate([output_weight] + inner_blocks), far)
    far_io = net.gather_far(shard_io)
    far = net.stacked(far)
    near = net.gather_near(far)
    pieces, corners, _ = net.gather_corner(far, near)
    flow = net.gather_core(pieces)
    far_io, corners, shard_u = after((net.stacked(far_io), corners, outer_weight), ())
    near_io = net.gather_near(far_io)
    flow += net.gather_core(corners)
    far_u = net.gather_far(after(shard_u, flow))

    segments = segments.reshape(rows, row_length)
    x = inputs.reshape(tokens, model_width)
    feats_in = after(feats, far_io)
    temb, lines, stream_low, queries, key_rows, values = project(
        net, me, flow, feats_in, x, row_length
    )
    far_u = net.stacked(after(far_u, queries))
    near_u = net.gather_near(far_u)
    near_io, queries = after((near_io, queries), far_u)
    pieces, corners, sent = net.gather_corner(far_io, near_io)
    queries = after(queries, sent)
    context, log_total = attend(queries, key_rows, values, segments)
    near_u, context, pieces = after((near_u, context, pieces), ())
    flow_io = net.gather_core(pieces)
    pieces, corners_u, sent = net.gather_corner(far_u, near_u)
    context, corners = after((context, corners), sent)
    flow_io += net.gather_core(corners)
    corners = corners_u
    first_low, normed_first, spread_first, active_low, slope = ffn_in(
        net, me, flow_io, context, x, temb, lines, hidden, row_length
    )
    corners, active_low = after((corners, active_low), ())
    flow_u = net.gather_core(pieces) + net.gather_core(corners)
    (
        layer_output,
        grad_second,
        grad_second_low,
        sums_out,
    ) = ffn_out(
        net,
        me,
        flow_u,
        active_low,
        normed_first,
        cotangent.reshape(tokens, model_width),
        (lines,),
    )
    outer_halves = product(net, me, active_low, grad_second_low)
    outer_sum = Reduction(net, me, *outer_halves)
    slope = after(slope, outer_halves)
    (
        grad_inner_low,
        grad_mixed,
        grad_mixed_low,
        grad_context,
        inner_bias_grad,
        sums_back,
        mixed_rows,
    ) = ffn_back(
        net,
        me,
        flow_u,
        flow_io,
        grad_second,
        grad_second_low,
        slope,
        normed_first,
        spread_first,
        lines,
        row_length,
    )
    sent = outer_sum.hold(grad_mixed_low).corner()
    grad_mixed_low = after(grad_mixed_low, sent)
    inner_halves = inner_product(net, me, context, first_low, grad_mixed_low, grad_inner_low)
    inner_sum = Reduction(net, me, *inner_halves)
    sent = outer_sum.hold(inner_halves).near()
    grad_context = after(grad_context, (inner_halves, sent))
    back = (queries, key_rows, values, segments, log_total, grad_context)
    found, sums_rows, row_sums = None, 0.0, [mixed_rows]
    for row in range(rows):
        if row == 1:
            sent = list(inner_sum.hold(found[1]).corner())
            sent += list(outer_sum.hold((found[1], sent)).far())
            found = after(found, sent)
        found = attend_back(*back, row, found or ())
        sums_rows += found[3]
        row_sums.append(found[4])
        found = found[:3]
    grad_queries, grad_keys, grad_values = found
    sent = inner_sum.hold(grad_queries).near()
    outer_sum.hold(grad_queries)
    sums = sums_rows + sums_out + sums_back
    sums = sums.reshape(8, n, r).transpose(1, 0, 2).reshape(n, 8 * r)
    sums = jnp.concatenate([sums, inner_bias_grad.reshape(n, -1)], axis=1)
    sums = jnp.pad(sums, ((0, 0), (0, model_width - sums.shape[1]))).astype(BF16)
    sums = jnp.broadcast_to(sums[:, None], (n, 8, model_width)).reshape(n // 2, 16, model_width)
    stream_low, sums = after((stream_low, sums), (sent, outer_sum.received()))
    stream_halves = triple_product(
        net, me, sums, stream_low, grad_queries, grad_keys, grad_values
    )
    stream_sum = Reduction(net, me, *stream_halves)
    grad_mixed = after(grad_mixed, stream_halves)
    back = (flow, grad_mixed, grad_queries, grad_keys, grad_values)
    grad_stream, grad_temb = stream_back(net, me, *back, 0, row_length, sums=row_sums)
    ends = grad_temb[:rows][None]
    sources, ends = net.gather_round([0], ends, net.masks(net.core))
    sent = list(stream_sum.hold(grad_temb).corner())
    sent += list(inner_sum.hold((grad_temb, sent)).far())
    ends = after(ends, sent)
    sent = stream_sum.hold(sent).near()
    grad_stream = after(grad_stream, sent)
    for row in range(1, rows):
        (grad_stream,) = stream_back(net, me, *back, row, row_length, grad_stream)
    inner_sum.hold(grad_stream), outer_sum.hold(grad_stream)
    output_weight_grad, inner_weight_grad = inner_sum.end([1, hidden // model_width], r)
    (outer_weight_grad,) = outer_sum.end([1], outer_weight.shape[0])
    ends = after(ends, (grad_stream, inner_sum.received()))
    sources, ends = net.gather_round(sources, ends, net.masks(net.near))
    sent = stream_sum.hold(grad_stream).far()
    sources, ends = net.gather_round(sources, after(ends, sent), net.masks(net.middle))
    sources, ends = net.gather_round(
        sources, after(ends, stream_sum.received()), net.masks(net.outer)
    )
    temb_all = in_order(net, me, sources, ends).reshape(n * rows, model_width)
    query_weight_grad, key_weight_grad, value_weight_grad, *parts = stream_ends(
        stream_sum, r, sizes
    )
    own = model_width // n
    steps_all = (lines[12] * 64.0 + lines[13])[: n * rows]
    feats_own = own_features(steps_all, me * own, own).astype(BF16).astype(F32)
    time_weight_grad = lax.dot_general(
        feats_own,
        temb_all,
        (((0,), (0,)), ((), ())),
        precision=lax.Precision.HIGHEST,
    )
    parts = dict(zip(order, parts))
    vector_outs = [parts[i] for i in range(len(order))]

    shape = inputs.shape
    return (
        layer_output.reshape(shape),
        grad_stream.reshape(shape),
        query_weight_grad,
        key_weight_grad,
        value_weight_grad,
        output_weight_grad,
        inner_weight_grad,
        outer_weight_grad,
        time_weight_grad,
    ) + tuple(vector_outs)


def solution(mesh):
    matrix, vector = P("fsdp", None), P("fsdp")
    batch = P(None, "fsdp", None, None)
    return jax.shard_map(
        functools.partial(on_device, Net(mesh.shape["fsdp"])),
        mesh=mesh,
        in_specs=(batch, P(None, "fsdp"), P(None, "fsdp", None), batch)
        + (matrix,) * 7
        + (vector,) * 9,
        out_specs=(batch, batch) + (matrix,) * 7 + (vector,) * 9,
        check_vma=False,
    )
```

```python
import functools
import math

import jax
import jax.numpy as jnp
from jax import lax
from jax.experimental import pallas as pl
from jax.experimental.pallas import tpu as pltpu
from jax.sharding import PartitionSpec as P

D = 1024
H = 16


INV_ROOT_TWO = 0.7071067811865476
INV_ROOT_TAU = 0.3989422804014327
F32 = jnp.float32
BF16 = jnp.bfloat16


def matmul(operand, factor):
    return jnp.dot(operand, factor, preferred_element_type=F32)


def matmul_left(operand, factor):
    return lax.dot_general(
        operand, factor, (((0,), (0,)), ((), ())), preferred_element_type=F32
    )


def matmul_right(operand, factor):
    return lax.dot_general(
        operand, factor, (((1,), (1,)), ((), ())), preferred_element_type=F32
    )


def features(step_ids):
    half_width = D // 2
    freqs = jnp.exp(-math.log(10000.0) * jnp.arange(half_width, dtype=F32) / half_width)
    angles = step_ids.astype(F32)[..., None] * freqs
    return jnp.concatenate([jnp.sin(angles), jnp.cos(angles)], axis=-1)


def own_features(step_ids, first, count):
    half_width = D // 2
    columns = first + jnp.arange(count, dtype=jnp.int32)
    places = (columns % half_width).astype(F32)
    freqs = jnp.exp(-math.log(10000.0) * places / half_width)
    angles = step_ids[:, None] * freqs
    return jnp.where(columns < half_width, jnp.sin(angles), jnp.cos(angles))


def normalize(values_in):
    center = values_in - jnp.mean(values_in, axis=-1, keepdims=True)
    spread = lax.rsqrt(jnp.mean(center * center, axis=-1, keepdims=True) + 1e-05)
    return (center * spread, spread)


def norm_back(grad_normed, normed, spread):
    mean_grad = jnp.mean(grad_normed, axis=-1, keepdims=True)
    mean_cross = jnp.mean(grad_normed * normed, axis=-1, keepdims=True)
    return spread * (grad_normed - mean_grad - normed * mean_cross)


def halves_body(low_in, high_in, low_out, high_out):
    low_out[...] = low_in[...]
    high_out[...] = high_in[...]


def halves(low_of, high_of):
    count, half = low_of.shape[0], low_of.shape[0] // 2
    block = (1,) + low_of.shape[1:]
    return pl.pallas_call(
        halves_body,
        grid=(half,),
        in_specs=[
            pl.BlockSpec(block, lambda i: (i, 0, 0)),
            pl.BlockSpec(block, lambda i: (half + i, 0, 0)),
        ],
        out_specs=[pl.BlockSpec(block, lambda i: (i, 0, 0))] * 2,
        out_shape=[jax.ShapeDtypeStruct((half,) + low_of.shape[1:], low_of.dtype)] * 2,
        compiler_params=pltpu.CompilerParams(vmem_limit_bytes=16 << 20),
        cost_estimate=pl.CostEstimate(flops=1000, bytes_accessed=1000, transcendentals=0),
        name="halves",
    )(low_of, high_of)


class Net:
    def __init__(self, n):
        self.n = n
        self.bits = n.bit_length() - 1
        chip = self.bits - 1
        sizes = [(chip + 2 - i) // 3 for i in range(3)]
        groups, top = [], self.bits - 1
        for size in sizes:
            groups.append(tuple(range(top, top - size, -1)))
            top -= size
        self.outer, self.middle, self.near = groups
        self.core = (0,)

    def masks(self, group):
        found = []
        for pick in range(1, 1 << len(group)):
            mask = 0
            for place, bit in enumerate(group):
                if pick >> place & 1:
                    mask |= 1 << bit
            found.append(mask)
        return found

    def swap(self, array, mask):
        return lax.ppermute(array, "fsdp", [(i, i ^ mask) for i in range(self.n)])

    def gather_far(self, shard):
        return [shard] + [self.swap(shard, mask) for mask in self.masks(self.outer)]

    def stacked(self, parts, me):
        low = self.bits - len(self.outer)
        masks = [mask >> low for mask in [0] + self.masks(self.outer)]
        count, shape = len(parts), parts[0].shape

        def body(me_ref, *refs):
            step, out_ref = pl.program_id(0), refs[-1]
            for mask, ref in zip(masks, refs):

                @pl.when(step == me_ref[0] >> low ^ mask)
                def _():
                    out_ref[0] = ref[...]

        whole = pl.BlockSpec(shape, lambda i: (0, 0))
        return pl.pallas_call(
            body,
            grid=(count,),
            in_specs=[pl.BlockSpec(memory_space=pltpu.SMEM)] + [whole] * count,
            out_specs=pl.BlockSpec((1,) + shape, lambda i: (i, 0, 0)),
            out_shape=jax.ShapeDtypeStruct((count,) + shape, parts[0].dtype),
            compiler_params=pltpu.CompilerParams(vmem_limit_bytes=16 << 20),
            cost_estimate=pl.CostEstimate(flops=1000, bytes_accessed=1000, transcendentals=0),
            name="stacked",
        )(me.reshape(1), *parts)

    def gather_near(self, own):
        return [
            [(mask, self.swap(own, mask)) for mask in self.masks(group)]
            for group in (self.near, self.middle)
        ]

    def gather_corner(self, own, near):
        half = own.shape[0] // 2
        pieces, corners, sent = [(0, 0, own)], [], []
        for group in near:
            pieces += [(0, mask, array) for mask, array in group]
        for mask_x, array_x in near[0]:
            for mask_y, array_y in near[1]:
                low, high = halves(array_y, array_x)
                sent += [low, high]
                corners.append((0, mask_x ^ mask_y, self.swap(low, mask_x)))
                corners.append((half, mask_x ^ mask_y, self.swap(high, mask_y)))
        return pieces, corners, sent

    def gather_core(self, pieces):
        return pieces + [(first, mask ^ 1, self.swap(array, 1)) for first, mask, array in pieces]

    def inner_masks(self):
        near, middle = self.masks(self.near), self.masks(self.middle)
        return near + middle + [x | y for x in near for y in middle]

    def gather_round(self, sources, array, masks):
        array = jnp.concatenate([array] + [self.swap(array, mask) for mask in masks])
        return [source ^ mask for mask in [0] + masks for source in sources], array

    def take(self, term, bits, mask, present, me):
        present = list(present)
        for bit in bits:
            place = present.index(bit)
            low = 1 << (len(present) - 1 - place)
            value = (me >> bit & 1) ^ (mask >> bit & 1)
            rest = term.shape[1:]
            term = term.reshape((1 << place, 2, low) + rest)
            term = lax.dynamic_index_in_dim(term, value, 1, keepdims=False)
            term = term.reshape((low << place,) + rest)
            present.remove(bit)
        return term

    def scatter_core(self, halves):
        keep, send = halves
        return [keep, self.swap(send, 1)], list(range(self.bits - 1, 0, -1))

    def added(self, parts, dtype):
        parts = [part.astype(F32) for part in parts]
        return sum(parts[1:], parts[0]).astype(dtype)

    def scatter_step(self, state, group, me):
        terms, present = state
        sent = []
        for mask in self.masks(group):
            parts = [self.take(term, group, mask, present, me) for term in terms]
            sent.append(self.added(parts, terms[0].dtype))
        received = [self.swap(part, mask) for part, mask in zip(sent, self.masks(group))]
        terms = [self.take(term, group, 0, present, me) for term in terms] + received
        return (terms, [bit for bit in present if bit not in group]), sent

    def scatter_corner(self, state, me):
        terms, present = state
        left = [bit for bit in present if bit not in self.near]
        found, sent = [], []
        for mask_x in self.masks(self.near):
            row = [self.take(term, self.near, mask_x, present, me) for term in terms]
            for mask_y in self.masks(self.middle):
                parts = [self.take(term, self.middle, mask_y, left, me) for term in row]
                half = parts[0].shape[0] // 2
                low = self.added([part[:half] for part in parts], terms[0].dtype)
                high = self.added([part[half:] for part in parts], terms[0].dtype)
                sent += [low, high]
                found.append((mask_x, mask_y, self.swap(low, mask_x), self.swap(high, mask_y)))
        return found, sent

    def scatter_near(self, state, corner, me):
        terms, present = state
        left = [bit for bit in present if bit not in self.near]
        mine, received, sent = [self.take(t, self.near, 0, present, me) for t in terms], [], []
        for mask_x in self.masks(self.near):
            row = [self.take(term, self.near, mask_x, present, me) for term in terms]
            parts = [self.take(term, self.middle, 0, left, me) for term in row]
            for mask, _, _, high in corner:
                if mask == mask_x:
                    parts.append(jnp.concatenate([jnp.zeros_like(high), high]))
            sent.append((self.added(parts, terms[0].dtype), mask_x))
        for mask_y in self.masks(self.middle):
            parts = [self.take(term, self.middle, mask_y, left, me) for term in mine]
            for _, mask, low, _ in corner:
                if mask == mask_y:
                    parts.append(jnp.concatenate([low, jnp.zeros_like(low)]))
            sent.append((self.added(parts, terms[0].dtype), mask_y))
        received = [self.swap(part, mask) for part, mask in sent]
        terms = [self.take(term, self.middle, 0, left, me) for term in mine] + received
        left = [bit for bit in left if bit not in self.middle]
        return (terms, left), [part for part, _ in sent]

    def scatter_far(self, state, me):
        return self.scatter_step(state, self.outer, me)

    def scatter_end(self, state):
        return self.added(state[0], F32)[0]

    def scatter(self, halves, order, me):
        state = self.scatter_core(halves)
        for group in order:
            state, _ = self.scatter_step(state, group, me)
        return self.scatter_end(state)

    def scatter_whole(self, whole, order, me):
        present = list(range(self.bits - 1, -1, -1))
        halves = [self.take(whole, self.core, mask, present, me) for mask in (0, 1)]
        return self.scatter(halves, order, me)


def after(values, others):
    leaves, tree = jax.tree.flatten(values)
    arrays = [leaf for leaf in leaves if not isinstance(leaf, int)]
    others = [leaf for leaf in jax.tree.leaves(others) if not isinstance(leaf, int)]
    tied = iter(lax.optimization_barrier(tuple(arrays + others)))
    return jax.tree.unflatten(
        tree, [leaf if isinstance(leaf, int) else next(tied) for leaf in leaves]
    )


class Weights:
    def __init__(self, net, me, wanted):
        self.arrays, self.plans, self.shapes = [], [], []
        seen = {}
        outer = 1 << len(net.outer)
        low = net.n // outer
        self.low = low
        for pieces, places, rows in wanted:
            places = (places,) if isinstance(places, int) else tuple(places)
            columns = pieces[0][2].shape[-1]
            plan = []
            if rows % 16:
                blocks = [
                    jnp.concatenate([array[:, place : place + rows] for _, _, array in pieces])
                    for place in places
                ]
                blocks = jnp.concatenate(blocks, axis=2)
                order = [
                    (first + j) * low + (me % low ^ mask)
                    for first, mask, array in pieces
                    for j in range(array.shape[0])
                ]
                spot = jnp.zeros((net.n,), jnp.int32).at[jnp.stack(order)].set(jnp.arange(net.n))
                whole = blocks[spot].reshape(outer, low * rows // 16, 16, len(places) * columns)
                plan.append((len(self.arrays), None, None, None))
                self.arrays.append(whole)
                self.shapes.append(whole.shape)
            else:
                for first, mask, array in pieces:
                    if id(array) not in seen:
                        seen[id(array)] = len(self.arrays)
                        self.arrays.append(array)
                    for k, place in enumerate(places):
                        own = (slice(None), pl.ds(place, rows))
                        aim = (pl.ds(first, array.shape[0]), pl.ds(k * columns, columns))
                        plan.append((seen[id(array)], own, mask, aim))
                self.shapes.append((outer, low, rows, len(places) * columns))
            self.plans.append(plan)
        self.slots = max(len(plan) for plan in self.plans)

    def scratch(self):
        return [pltpu.VMEM(shape, BF16) for shape in self.shapes] + [
            pltpu.SemaphoreType.DMA((len(self.plans), self.slots))
        ]

    def copies(self, w, me, array_refs, held_ref, sems):
        found = []
        for slot, (array, own, mask, aim) in enumerate(self.plans[w]):
            if own is None:
                pair = (array_refs[array], held_ref)
            else:
                spot = me % self.low ^ mask
                pair = (array_refs[array].at[own], held_ref.at[aim[0], spot, :, aim[1]])
            found.append(pltpu.make_async_copy(*pair, sems.at[w, slot]))
        return found

    def start(self, w, *refs):
        for copy in self.copies(w, *refs):
            copy.start()

    def wait(self, w, *refs):
        for copy in self.copies(w, *refs):
            copy.wait()


def flat(held):
    return held.reshape(-1, held.shape[-1])


SMEM_SPEC = pl.BlockSpec(memory_space=pltpu.SMEM)
ANY_SPEC = pl.BlockSpec(memory_space=pltpu.HBM)


def full_spec(shape):
    return pl.BlockSpec(shape, lambda *_: (0,) * len(shape))


def tile_spec(tile, columns):
    return pl.BlockSpec((tile, columns), lambda i: (i, 0))


def call(body, name, grid, ins, outs, scratch, us, bases=()):
    count = len(ins)

    def run(*refs):
        body(*refs[:count], *refs[count + len(bases) :])

    return pl.pallas_call(
        run,
        grid=grid,
        in_specs=[spec for _, spec in ins] + [ANY_SPEC] * len(bases),
        out_specs=[spec for _, _, spec in outs],
        out_shape=[jax.ShapeDtypeStruct(shape, dtype) for shape, dtype, _ in outs],
        scratch_shapes=scratch,
        input_output_aliases={count + i: i for i in range(len(bases))},
        compiler_params=pltpu.CompilerParams(
            vmem_limit_bytes=60 << 20,
            dimension_semantics=("arbitrary",) * len(grid),
        ),
        cost_estimate=pl.CostEstimate(
            flops=int(us * 2e10), bytes_accessed=int(us * 5e7), transcendentals=0
        ),
        name=name,
    )(*[array for array, _ in ins], *bases)


def sum_body(groups, me_ref, *refs):
    step = pl.program_id(0)
    outs = refs[len(refs) - len(groups) :]
    for out_ref, addends in zip(outs, groups):
        total = None
        for place, (low, high) in addends:
            part = refs[place][...].astype(F32)
            if low is not None:
                part = jnp.where((step >= low) & (step < high), part, 0.0)
            total = part if total is None else total + part
        out_ref[...] = total.astype(out_ref.dtype)


def sum_call(me, name, grid, ins, groups, outs, body=None, us=0.01):
    grid_spec = pltpu.PrefetchScalarGridSpec(
        num_scalar_prefetch=1,
        grid=(grid,),
        in_specs=[
            pl.BlockSpec(block, lambda i, me_ref, place=place: place(i, me_ref[0]))
            for _, block, place in ins
        ],
        out_specs=[
            pl.BlockSpec(block, lambda i, me_ref, place=place: place(i, me_ref[0]))
            for _, _, block, place in outs
        ],
    )
    return pl.pallas_call(
        body or functools.partial(sum_body, groups),
        grid_spec=grid_spec,
        out_shape=[jax.ShapeDtypeStruct(shape, dtype) for shape, dtype, _, _ in outs],
        compiler_params=pltpu.CompilerParams(
            vmem_limit_bytes=60 << 20, dimension_semantics=("arbitrary",)
        ),
        cost_estimate=pl.CostEstimate(flops=int(us * 2e10), bytes_accessed=int(us * 5e7), transcendentals=0),
        name=name,
    )(me.reshape(1), *[array for array, _, _ in ins])


class Reduction:
    def __init__(self, net, me, keep, send):
        self.net, self.me = net, me
        self.terms = [keep, net.swap(send, 1)]
        self.rows, self.columns = keep.shape[1:]
        self.plain = len(net.near) == 1 and len(net.middle) == 1 and self.rows % 8 == 0
        self.state = None

    def block(self):
        return (1, self.rows, self.columns)

    def hold(self, others):
        if self.plain:
            self.terms = after(self.terms, others)
        else:
            state = self.state or (self.terms, list(range(self.net.bits - 1, 0, -1)))
            self.state = held(state, others)
            if getattr(self, "corner_pieces", None) is not None:
                self.corner_pieces = after(self.corner_pieces, others)
        return self

    def corner(self):
        net = self.net
        if not self.plain:
            state = self.state or (self.terms, list(range(net.bits - 1, 0, -1)))
            self.state = state
            self.corner_pieces, sent = net.scatter_corner(state, self.me)
            return sent
        far = 1 << (len(net.outer) - 1)

        def place(shift):
            return lambda i, me: ((i + shift) * 4 + (me >> 1 & 3 ^ 3), 0, 0)

        ins = [(term, self.block(), place(shift)) for shift in (0, far) for term in self.terms]
        out = ((far, self.rows, self.columns), BF16, self.block(), lambda i, me: (i, 0, 0))
        always = (None, None)
        groups = [[(0, always), (1, always)], [(2, always), (3, always)]]
        low, high = sum_call(self.me, "corner_sum", far, ins, groups, [out, out])
        self.terms += [net.swap(low, 1 << net.near[0]), net.swap(high, 1 << net.middle[0])]
        return [low, high]

    def near(self):
        net = self.net
        if not self.plain:
            self.state, sent = net.scatter_near(self.state, self.corner_pieces, self.me)
            self.corner_pieces = None
            return sent
        far = 1 << (len(net.outer) - 1)
        keep, other, low, high = self.terms

        def place(flip):
            return lambda i, me: (i * 4 + (me >> 1 & 3 ^ flip), 0, 0)

        ins = [(term, self.block(), place(flip)) for flip in (1, 2) for term in (keep, other)]
        ins.append((high, self.block(), lambda i, me: (jnp.maximum(i - far, 0), 0, 0)))
        ins.append((low, self.block(), lambda i, me: (jnp.minimum(i, far - 1), 0, 0)))
        always = (None, None)
        groups = [
            [(0, always), (1, always), (4, (far, 2 * far))],
            [(2, always), (3, always), (5, (0, far))],
        ]
        out = ((2 * far, self.rows, self.columns), BF16, self.block(), lambda i, me: (i, 0, 0))
        sent = sum_call(self.me, "near_sum", 2 * far, ins, groups, [out, out])
        received = [
            net.swap(part, 1 << group[0]) for part, group in zip(sent, (net.near, net.middle))
        ]
        self.terms = [keep, other] + received
        return sent

    def sources(self, flip, step_block):
        keep, other, row, column = self.terms[:4]
        found = []
        for term in (keep, other):
            found.append((term, lambda me: ((me >> 3 ^ flip) * 4 + (me >> 1 & 3))))
        for term in (row, column):
            found.append((term, lambda me: (me >> 3 ^ flip)))
        return [
            (term, step_block[0], lambda i, me, at=at: step_block[1](i, at(me)))
            for term, at in found
        ]

    def far(self):
        net = self.net
        if not self.plain:
            self.state, sent = net.scatter_step(self.state, net.outer, self.me)
            return sent
        parts = 2 if self.rows % 32 == 0 else 1
        step_block = ((1, self.rows // parts, self.columns), lambda i, at: (at, i, 0))
        masks = net.masks(net.outer)
        ins, groups = [], []
        for mask in masks:
            groups.append([(len(ins) + j, (None, None)) for j in range(4)])
            ins += self.sources(mask >> 3, step_block)
        out = ((1, self.rows, self.columns), BF16, step_block[0], lambda i, me: (0, i, 0))
        sent = sum_call(self.me, "far_sum", parts, ins, groups, [out] * len(masks))
        self.terms += [net.swap(part, mask) for part, mask in zip(sent, masks)]
        return sent

    def received(self):
        return self.terms[-1] if self.plain else self.state[0][-1]

    def end(self, lots, unit):
        if not self.plain:
            total = self.net.scatter_end(self.state)
            results, start = [], 0
            for count in lots:
                blocks = [
                    total[(start + j) * unit : (start + j + 1) * unit] for j in range(count)
                ]
                results.append(jnp.concatenate(blocks, axis=1))
                start += count
            return results
        step_block = ((1, unit, self.columns), lambda i, at: (at, i, 0))
        ins = self.sources(0, step_block)
        ins += [(term, step_block[0], lambda i, me: (0, i, 0)) for term in self.terms[4:]]
        outs, bounds, start = [], [], 0
        for count in lots:

            def place(i, me, start=start, count=count):
                return (0, jnp.clip(i - start, 0, count - 1))

            outs.append(((unit, count * self.columns), F32, (unit, self.columns), place))
            bounds.append((start, start + count))
            start += count

        def body(me_ref, *refs):
            step, addends = pl.program_id(0), refs[: len(ins)]
            total = addends[0][0].astype(F32)
            for ref in addends[1:]:
                total = total + ref[0].astype(F32)
            for out_ref, (low, high) in zip(refs[len(ins) :], bounds):

                @pl.when((step >= low) & (step < high))
                def _():
                    out_ref[...] = total

        return sum_call(self.me, "end_sum", start, ins, None, outs, body, 4)


def pack_body(sizes, me_ref, times_ref, small_ref, *refs):
    shards, out_ref = refs[:-1], refs[-1]
    start = 0
    for ref in shards:
        out_ref[start : start + ref.shape[0]] = ref[...]
        start += ref.shape[0]
    me, width = me_ref[0], out_ref.shape[1]

    small = small_ref[...]
    step, inner_size, steps = sizes

    def spread(first, count, offset):
        spots = lax.broadcasted_iota(jnp.int32, (small.shape[1], width), 0) - first
        lanes = lax.broadcasted_iota(jnp.int32, (small.shape[1], width), 1)
        hits = (spots >= 0) & (spots < count) & (lanes == spots + offset)
        return matmul(small, jnp.where(hits, 1.0, 0.0).astype(BF16))

    vectors = spread(0, step, me * step)
    place = me * inner_size
    inner = spread(step, inner_size, lax.rem(place, width))
    row = lax.broadcasted_iota(jnp.int32, inner.shape, 0)
    inner = jnp.where(row == place // width, inner, 0.0)
    lane = lax.broadcasted_iota(jnp.int32, inner.shape, 1)
    for j in range(steps):
        time = times_ref[j]
        digit = jnp.where(row == 4, time >> 6, jnp.where(row == 5, time & 63, 0))
        inner += jnp.where(lane == me * steps + j, digit, 0).astype(F32)
    out_ref[start:] = jnp.concatenate([vectors, inner]).astype(BF16)


def pack(me, shards, vectors, inner, times):
    step, width = shards[0].shape
    sizes = (step, inner.shape[0], times.shape[0])
    small = 0.0
    for line, vector in enumerate(vectors):
        small += jnp.pad(vector.astype(F32)[None], ((line, 7 - line), (0, 256 - step)))
    rest = 256 - sizes[1] - step
    small += jnp.pad(inner.astype(F32)[None], ((0, 0), (step, rest)))
    small = small.astype(BF16)
    rows = len(shards) * step + 16
    return call(
        functools.partial(pack_body, sizes),
        "pack",
        (1,),
        [(me.reshape(1), SMEM_SPEC), (times, SMEM_SPEC)]
        + [(array, full_spec(array.shape)) for array in (small, *shards)],
        [((rows, width), BF16, full_spec((rows, width)))],
        [],
        1,
    )[0]


def project_body(weights, tile, row_length, me_ref, *refs):
    count = len(weights.arrays)
    arrays, refs = refs[:count], refs[count:]
    feats_ref, x_ref = refs[:2]
    temb_ref, lines_ref, low_ref, q_ref, k_ref, v_ref = refs[2:8]
    tw, qw, kw, vw, lw, sems = refs[8:14]
    me, step = me_ref[0], pl.program_id(0)

    @pl.when(step == 0)
    def _():
        for w, held in enumerate((tw, qw, kw, vw, lw)):
            weights.start(w, me, arrays, held, sems)
        weights.wait(0, me, arrays, tw, sems)
        temb_ref[...] = matmul(feats_ref[...], flat(tw[...]))
        weights.wait(4, me, arrays, lw, sems)
        lines_ref[...] = jnp.sum(lw[...].astype(F32), axis=(0, 1))
        for w, held in ((1, qw), (2, kw), (3, vw)):
            weights.wait(w, me, arrays, held, sems)

    row = step * tile // row_length
    low = (x_ref[...].astype(F32) + temb_ref[pl.ds(row, 1), :]).astype(BF16)
    low_ref[...] = low
    q_ref[...] = (matmul(low, flat(qw[...])) + lines_ref[0:1]).astype(BF16)
    k_ref[...] = matmul(low, flat(kw[...])).astype(BF16)
    v_ref[...] = (matmul(low, flat(vw[...])) + lines_ref[1:2]).astype(BF16)


def project(net, me, flow, feats, x, row_length):
    tokens, width = x.shape
    tile = min(256, row_length)
    r = width // net.n
    weights = Weights(net, me, [(flow, w * r, r) for w in range(4)] + [(flow, 4 * r, 16)])
    ins = (
        [(me.reshape(1), SMEM_SPEC)]
        + [(array, ANY_SPEC) for array in weights.arrays]
        + [(feats, full_spec(feats.shape)), (x, tile_spec(tile, width))]
    )
    outs = [(feats.shape, F32, full_spec(feats.shape))]
    outs += [((16, width), F32, full_spec((16, width)))]
    outs += [((tokens, width), BF16, tile_spec(tile, width))] * 4
    return call(
        functools.partial(project_body, weights, tile, row_length),
        "project",
        (tokens // tile,),
        ins,
        outs,
        weights.scratch(),
        14,
    )


def same_document(seg_ref, bias_ref, block):
    @pl.when(block == 0)
    def _():
        row = seg_ref[0].astype(F32)
        column = jnp.transpose(jnp.broadcast_to(row, (128, row.shape[1])))[:, :1]
        bias_ref[...] = jnp.where(column == row, 0.0, -1e30)


def own_lanes(shape, head, head_dim):
    lanes = lax.broadcasted_iota(jnp.int32, shape, len(shape) - 1)
    return (lanes // head_dim) == head


def attend_body(head_dim, seg_ref, q_ref, k_ref, v_ref, out_ref, log_ref, bias_ref):
    same_document(seg_ref, bias_ref, pl.program_id(1))
    queries, key_rows, values = q_ref[...], k_ref[...], v_ref[...]
    scale = 1.0 / math.sqrt(head_dim)
    per = queries.shape[1] // head_dim
    total = None
    for head in range(per):
        mine = own_lanes(queries.shape, head, head_dim)
        keys_own = jnp.where(mine, key_rows * BF16(scale), BF16(0))
        scores = matmul_right(keys_own, queries) + bias_ref[...]
        top = jnp.max(scores, axis=0, keepdims=True)
        raised = jnp.exp(scores - top)
        amount = jnp.sum(raised, axis=0, keepdims=True)
        log_ref[0, 0, pl.ds(head, 1), :] = top + jnp.log(amount)
        soft_low = (raised * (1.0 / amount)).astype(BF16)
        context = matmul_left(soft_low, values)
        total = context if total is None else jnp.where(mine, context, total)
    out_ref[...] = total.astype(BF16)


def attend_back_body(
    head_dim, seg_ref, q_ref, k_ref, v_ref, log_ref, g_ref, gq_ref, gk_ref, gv_ref, sums_ref, rows_ref, bias_ref
):
    same_document(seg_ref, bias_ref, pl.program_id(1))
    queries, key_rows, values, grads = q_ref[...], k_ref[...], v_ref[...], g_ref[...]
    scale = 1.0 / math.sqrt(head_dim)
    per = queries.shape[1] // head_dim
    totals = None
    for head in range(per):
        mine = own_lanes(queries.shape, head, head_dim)
        keys_own = jnp.where(mine, key_rows * BF16(scale), BF16(0))
        scores = matmul_right(keys_own, queries) + bias_ref[...]
        soft = jnp.exp(scores - log_ref[0, 0, pl.ds(head, 1), :])
        grad_soft = matmul_right(jnp.where(mine, values, BF16(0)), grads)
        inner_sum = jnp.sum(soft * grad_soft, axis=0, keepdims=True)
        grad_scores = (soft * (grad_soft - inner_sum)).astype(BF16)
        parts = (
            matmul_left(grad_scores, key_rows),
            matmul(grad_scores, queries),
            matmul(soft.astype(BF16), grads),
        )
        if totals is None:
            totals = parts
        else:
            totals = tuple(jnp.where(mine, part, total) for part, total in zip(parts, totals))
    gq = (totals[0] * scale).astype(BF16)
    gv = totals[2].astype(BF16)
    gq_ref[...] = gq
    gk = (totals[1] * scale).astype(BF16)
    gk_ref[...] = gk
    gv_ref[...] = gv
    sums = [jnp.sum(part.astype(F32), axis=0, keepdims=True) for part in (gq, gk, gv)]
    zero = jnp.zeros_like(sums[0])
    sums_ref[...] = jnp.concatenate([sums[0], sums[2]] + [zero] * 6)
    rows_ref[...] = jnp.concatenate(sums + [zero] * 5)


def attention_args(segments, start, lanes, head_dim):
    row_length, per = segments.shape[1], lanes // head_dim
    segs = pl.BlockSpec((1, 1, row_length), lambda i, j: (start + i, 0, 0))
    block = pl.BlockSpec((row_length, lanes), lambda i, j: (start + i, j))
    log_spec = pl.BlockSpec((1, 1, per, row_length), lambda i, j: (start + i, j, 0, 0))
    return [(segments[:, None, :], segs)], block, log_spec


def attend(queries, key_rows, values, segments, lanes=256):
    rows, row_length = segments.shape
    tokens, width = queries.shape
    head_dim = width // H
    blocks, per = width // lanes, lanes // head_dim
    masks, block, log_spec = attention_args(segments, 0, lanes, head_dim)
    return call(
        functools.partial(attend_body, head_dim),
        "attend",
        (rows, blocks),
        masks + [(array, block) for array in (queries, key_rows, values)],
        [
            ((tokens, width), BF16, block),
            ((rows, blocks, per, row_length), F32, log_spec),
        ],
        [pltpu.VMEM((row_length, row_length), F32)],
        24,
    )


def attend_back(queries, key_rows, values, segments, log_total, grad_context, row, bases=(), lanes=256):
    rows, row_length = segments.shape
    tokens, width = queries.shape
    head_dim = width // H
    masks, block, log_spec = attention_args(segments, row, lanes, head_dim)
    return call(
        functools.partial(attend_back_body, head_dim),
        "attend_back",
        (1, width // lanes),
        masks
        + [(array, block) for array in (queries, key_rows, values)]
        + [(log_total, log_spec), (grad_context, block)],
        [((tokens, width), BF16, block)] * 3
        + [((8, width), F32, pl.BlockSpec((8, lanes), lambda i, j: (0, j)))] * 2,
        [pltpu.VMEM((row_length, row_length), F32)],
        19,
        bases,
    )


def add_to(ref, value, step):
    part = jnp.sum(value, axis=0, keepdims=True)

    @pl.when(step == 0)
    def _():
        ref[...] = part

    @pl.when(step != 0)
    def _():
        ref[...] += part


def add_lines(ref, values, step):
    zero = jnp.zeros((1, ref.shape[1]), F32)
    sums = {line: jnp.sum(value, axis=0, keepdims=True) for line, value in values.items()}
    part = jnp.concatenate([sums.get(line, zero) for line in range(ref.shape[0])])

    @pl.when(step == 0)
    def _():
        ref[...] = part

    @pl.when(step != 0)
    def _():
        ref[...] += part


def ffn_in_body(weights, tile, row_length, chunk, me_ref, *refs):
    count = len(weights.arrays)
    arrays, refs = refs[:count], refs[count:]
    context_ref, x_ref, temb_ref, lines_ref = refs[:4]
    first_low_ref, normed_ref, spread_ref, active_ref, slope_ref = refs[4:9]
    ow, iw, sems = refs[9:12]
    me, step = me_ref[0], pl.program_id(0)

    @pl.when(step == 0)
    def _():
        for w, held in enumerate((ow, iw)):
            weights.start(w, me, arrays, held, sems)
        weights.wait(0, me, arrays, ow, sems)

    row = step * tile // row_length
    stream = x_ref[...].astype(F32) + temb_ref[pl.ds(row, 1), :]
    mixed = stream + (matmul(context_ref[...], flat(ow[...])) + lines_ref[2:3])
    normed, spread = normalize(mixed)
    normed_ref[...] = normed
    spread_ref[...] = spread
    first = normed * lines_ref[4:5] + lines_ref[5:6]
    low = first.astype(BF16)
    first_low_ref[...] = low

    @pl.when(step == 0)
    def _():
        weights.wait(1, me, arrays, iw, sems)

    width, hidden = ow.shape[3], iw.shape[3]

    def inner(start):
        pre = matmul(low, flat(iw[:, :, :, start : start + chunk]))
        line, place = 8 + start // width, start % width
        return pre + lines_ref[line : line + 1, place : place + chunk]

    later = inner(0)
    for start in range(0, hidden, chunk):
        pre = later
        if start + chunk < hidden:
            later = inner(start + chunk)
        columns = slice(start, start + chunk)
        normal_cdf = 0.5 * (1.0 + lax.erf(pre * INV_ROOT_TWO))
        normal_pdf = jnp.exp(-0.5 * pre * pre) * INV_ROOT_TAU
        active_ref[:, columns] = (pre * normal_cdf).astype(BF16)
        slope_ref[:, columns] = (normal_cdf + pre * normal_pdf).astype(BF16)


def ffn_in(net, me, flow, context, x, temb, lines, hidden, row_length, tile=256, chunk=512):
    tokens, width = x.shape
    r = width // net.n
    blocks = range(r, r + hidden // width * r, r)
    weights = Weights(net, me, [(flow, 0, r), (flow, blocks, r)])
    tile = min(tile, row_length)
    tiled, wide, thin = (tile_spec(tile, columns) for columns in (width, hidden, 1))
    ins = (
        [(me.reshape(1), SMEM_SPEC)]
        + [(array, ANY_SPEC) for array in weights.arrays]
        + [(context, tiled), (x, tiled)]
        + [(array, full_spec(array.shape)) for array in (temb, lines)]
    )
    outs = [
        ((tokens, width), BF16, tiled),
        ((tokens, width), F32, tiled),
        ((tokens, 1), F32, thin),
        ((tokens, hidden), BF16, wide),
        ((tokens, hidden), BF16, wide),
    ]
    return call(
        functools.partial(ffn_in_body, weights, tile, row_length, chunk),
        "ffn_in",
        (tokens // tile,),
        ins,
        outs,
        weights.scratch(),
        30,
    )


def ffn_out_body(weights, me_ref, *refs):
    count = len(weights.arrays)
    arrays, refs = refs[:count], refs[count:]
    active_ref, normed_ref, cot_ref, lines_ref = refs[:4]
    out_ref, gs_ref, gs_low_ref, sums_ref = refs[4:8]
    uw, sems = refs[8:10]
    me, step = me_ref[0], pl.program_id(0)

    @pl.when(step == 0)
    def _():
        weights.start(0, me, arrays, uw, sems)
        weights.wait(0, me, arrays, uw, sems)

    first = normed_ref[...] * lines_ref[4:5] + lines_ref[5:6]
    second = first + (matmul(active_ref[...], flat(uw[...])) + lines_ref[3:4])
    normed_second, spread_second = normalize(second)
    out_ref[...] = (normed_second * lines_ref[6:7] + lines_ref[7:8]).astype(BF16)
    grad_out = cot_ref[...].astype(F32)
    grad_second = norm_back(grad_out * lines_ref[6:7], normed_second, spread_second)
    gs_ref[...] = grad_second
    low = grad_second.astype(BF16)
    gs_low_ref[...] = low
    add_lines(sums_ref, {3: low.astype(F32), 6: grad_out * normed_second, 7: grad_out}, step)


def ffn_out(net, me, flow, active, normed, cotangent, vectors, tile=256):
    tokens, width = normed.shape
    hidden = active.shape[1]
    weights = Weights(net, me, [(flow, 0, hidden // net.n)])
    tiled, wide = tile_spec(tile, width), tile_spec(tile, hidden)
    ins = (
        [(me.reshape(1), SMEM_SPEC)]
        + [(array, ANY_SPEC) for array in weights.arrays]
        + [(active, wide), (normed, tiled), (cotangent, tiled)]
        + [(vector, full_spec(vector.shape)) for vector in vectors]
    )
    outs = [
        ((tokens, width), BF16, tiled),
        ((tokens, width), F32, tiled),
        ((tokens, width), BF16, tiled),
        ((8, width), F32, full_spec((8, width))),
    ]
    return call(
        functools.partial(ffn_out_body, weights),
        "ffn_out",
        (tokens // tile,),
        ins,
        outs,
        weights.scratch(),
        20,
    )


def ffn_back_body(weights, tile, row_length, me_ref, *refs):
    count = len(weights.arrays)
    arrays, refs = refs[:count], refs[count:]
    (gs_ref, gs_low_ref, slope_ref, normed_ref, spread_ref, lines_ref) = refs[:6]
    (gi_ref, gm_ref, gm_low_ref, gc_ref, ibg_ref, sums_ref, rows_ref) = refs[6:13]
    uw, ow, iw, sems, held_ref = refs[13:18]
    me, step = me_ref[0], pl.program_id(0)
    last = pl.num_programs(0) - 1

    @pl.when(step == 0)
    def _():
        for w, held in ((0, uw), (2, iw), (1, ow)):
            weights.start(w, me, arrays, held, sems)
        sums_ref[...] = jnp.zeros_like(sums_ref)
        rows_ref[...] = jnp.zeros_like(rows_ref)
        ibg_ref[...] = jnp.zeros_like(ibg_ref)
        weights.wait(0, me, arrays, uw, sems)

    def through_hidden(first_time=False):
        part = gi_ref.shape[1] // uw.shape[0]
        for z in range(uw.shape[0]):
            columns = slice(z * part, (z + 1) * part)
            grad_active = matmul_right(gs_low_ref[...], flat(uw[z]))
            gi = (grad_active * slope_ref[:, columns].astype(F32)).astype(BF16)
            gi_ref[:, columns] = gi
            ibg_ref[:, columns] += jnp.sum(gi.astype(F32), axis=0, keepdims=True)
        if first_time:
            weights.wait(2, me, arrays, iw, sems)
        return gs_ref[...] + matmul_right(gi_ref[...], flat(iw[...]))

    def through_norm(grad_first):
        normed = normed_ref[...]
        grad_mixed = norm_back(grad_first * lines_ref[4:5], normed, spread_ref[...])
        gm_ref[...] = grad_mixed
        low = grad_mixed.astype(BF16)
        gm_low_ref[...] = low
        row = pl.ds((step - 1) * tile // row_length, 1)
        rows_ref[row, :] += jnp.sum(grad_mixed, axis=0, keepdims=True)
        values = {2: low.astype(F32), 4: grad_first * normed, 5: grad_first}
        for line, value in values.items():
            sums_ref[line : line + 1] += jnp.sum(value, axis=0, keepdims=True)
        gc_ref[...] = matmul_right(low, flat(ow[...])).astype(BF16)

    @pl.when(step == 0)
    def _():
        held_ref[...] = through_hidden(True)
        weights.wait(1, me, arrays, ow, sems)

    @pl.when((step > 0) & (step < last))
    def _():
        grad_first = held_ref[...]
        later = through_hidden()
        through_norm(grad_first)
        held_ref[...] = later

    @pl.when(step == last)
    def _():
        through_norm(held_ref[...])


def ffn_back(net, me, flow_u, flow_io, gs, gs_low, slope, normed, spread, lines, row_length, tile=256):
    tokens, width = gs.shape
    hidden = slope.shape[1]
    r = width // net.n
    weights = Weights(
        net,
        me,
        [
            (flow_u, 0, hidden // net.n),
            (flow_io, 0, r),
            (flow_io, range(r, r + hidden // width * r, r), r),
        ],
    )
    tile = min(tile, row_length)
    steps = tokens // tile

    def ahead(columns):
        return pl.BlockSpec((tile, columns), lambda i: (jnp.minimum(i, steps - 1), 0))

    def behind(columns):
        return pl.BlockSpec((tile, columns), lambda i: (jnp.maximum(i - 1, 0), 0))

    ins = (
        [(me.reshape(1), SMEM_SPEC)]
        + [(array, ANY_SPEC) for array in weights.arrays]
        + [(gs, ahead(width)), (gs_low, ahead(width)), (slope, ahead(hidden))]
        + [(normed, behind(width)), (spread, behind(1)), (lines, full_spec(lines.shape))]
    )
    outs = [
        ((tokens, hidden), BF16, ahead(hidden)),
        ((tokens, width), F32, behind(width)),
        ((tokens, width), BF16, behind(width)),
        ((tokens, width), BF16, behind(width)),
        ((1, hidden), F32, full_spec((1, hidden))),
        ((8, width), F32, full_spec((8, width))),
        ((8, width), F32, full_spec((8, width))),
    ]
    return call(
        functools.partial(ffn_back_body, weights, tile, row_length),
        "ffn_back",
        (steps + 1,),
        ins,
        outs,
        weights.scratch() + [pltpu.VMEM((tile, width), F32)],
        36,
    )


def deal(me_ref, total, rows, keep_ref, send_ref, kind=0):
    core = me_ref[0] & 1
    total = total.reshape(-1, 2, rows, total.shape[-1])
    low, high = total[:, 0], total[:, 1]
    place = slice(kind * rows, (kind + 1) * rows)
    keep_ref[:, place] = jnp.where(core == 0, low, high).astype(BF16)
    send_ref[:, place] = jnp.where(core == 0, high, low).astype(BF16)


def product_body(rows, me_ref, a_ref, b_ref, keep_ref, send_ref):
    deal(me_ref, matmul_left(a_ref[...], b_ref[...]), rows, keep_ref, send_ref)


def product(net, me, left, right, tile=1024):
    tokens, width = left.shape
    columns = right.shape[1]
    rows = width // net.n
    shape = (net.n // 2, rows, columns)
    block = pl.BlockSpec((tile // (2 * rows), rows, columns), lambda i: (i, 0, 0))
    return call(
        functools.partial(product_body, rows),
        "product",
        (width // tile,),
        [
            (me.reshape(1), SMEM_SPEC),
            (left, pl.BlockSpec((tokens, tile), lambda i: (0, i))),
            (right, full_spec((tokens, columns))),
        ],
        [(shape, BF16, block), (shape, BF16, block)],
        [],
        15,
    )


def inner_body(rows, me_ref, context_ref, first_ref, gm_ref, gi_ref, keep_ref, send_ref):
    total = matmul_left(first_ref[...], gi_ref[...])
    width = gm_ref.shape[1]
    deal(me_ref, matmul_left(context_ref[...], gm_ref[...]), rows, keep_ref, send_ref, 0)
    for k in range(total.shape[1] // width):
        part = total[:, k * width : (k + 1) * width]
        deal(me_ref, part, rows, keep_ref, send_ref, k + 1)


def inner_product(net, me, context, first_low, gm_low, gi, tile=256):
    tokens, width = context.shape
    hidden = gi.shape[1]
    rows = width // net.n
    kinds = 1 + hidden // width
    shape = (net.n // 2, kinds * rows, width)
    block = pl.BlockSpec((tile // (2 * rows), kinds * rows, width), lambda i: (i, 0, 0))
    left = pl.BlockSpec((tokens, tile), lambda i: (0, i))
    return call(
        functools.partial(inner_body, rows),
        "inner_product",
        (width // tile,),
        [
            (me.reshape(1), SMEM_SPEC),
            (context, left),
            (first_low, left),
            (gm_low, full_spec((tokens, width))),
            (gi, full_spec((tokens, hidden))),
        ],
        [(shape, BF16, block), (shape, BF16, block)],
        [],
        18,
    )


def triple_body(rows, me_ref, lines_ref, a_ref, q_ref, k_ref, v_ref, keep_ref, send_ref):
    for w, ref in enumerate((q_ref, k_ref, v_ref)):
        deal(me_ref, matmul_left(a_ref[...], ref[...]), rows, keep_ref, send_ref, w)
    core = me_ref[0] & 1
    low, high = lines_ref[:, 0:8], lines_ref[:, 8:16]
    place = slice(3 * rows, 3 * rows + 8)
    keep_ref[:, place] = jnp.where(core == 0, low, high).astype(BF16)
    send_ref[:, place] = jnp.where(core == 0, high, low).astype(BF16)


def triple_product(net, me, lines, left, gq, gk, gv, tile=256):
    tokens, width = left.shape
    rows = width // net.n
    shape = (net.n // 2, 3 * rows + 8, width)
    chips = tile // (2 * rows)
    block = pl.BlockSpec((chips, 3 * rows + 8, width), lambda i: (i, 0, 0))
    full = full_spec((tokens, width))
    return call(
        functools.partial(triple_body, rows),
        "triple_product",
        (width // tile,),
        [
            (me.reshape(1), SMEM_SPEC),
            (lines, pl.BlockSpec((chips, 16, width), lambda i: (i, 0, 0))),
            (left, pl.BlockSpec((tokens, tile), lambda i: (0, i))),
            (gq, full),
            (gk, full),
            (gv, full),
        ],
        [(shape, BF16, block), (shape, BF16, block)],
        [],
        13,
    )


def stream_back_body(weights, rows, me_ref, *refs):
    count = len(weights.arrays)
    arrays, refs = refs[:count], refs[count:]
    gm_ref, gq_ref, gk_ref, gv_ref = refs[:4]
    sum_refs, refs = refs[4 : 4 + rows], refs[4 + rows :]
    out_ref, outs = refs[0], refs[1:]
    qw, kw, vw, sems = outs[-4:]
    me, step = me_ref[0], pl.program_id(0)

    @pl.when(step == 0)
    def _():
        for w, held in enumerate((qw, kw, vw)):
            weights.start(w, me, arrays, held, sems)
        for w, held in enumerate((qw, kw, vw)):
            weights.wait(w, me, arrays, held, sems)
        if sum_refs:
            total = sum_refs[0][...]
            for w, held in enumerate((qw, kw, vw)):
                lines = [ref[w : w + 1] for ref in sum_refs[1:]]
                lines += [jnp.zeros_like(lines[0])] * (8 - len(lines))
                total += matmul_right(jnp.concatenate(lines).astype(BF16), flat(held[...]))
            outs[0][...] = total

    out_ref[...] = (
        gm_ref[...]
        + matmul_right(gq_ref[...], flat(qw[...]))
        + matmul_right(gk_ref[...], flat(kw[...]))
        + matmul_right(gv_ref[...], flat(vw[...]))
    )


def stream_back(net, me, flow, gm, gq, gk, gv, row, row_length, base=None, sums=(), tile=256):
    tokens, width = gm.shape
    tile = min(tile, row_length)
    r = width // net.n
    weights = Weights(net, me, [(flow, w * r, r) for w in (1, 2, 3)])
    start = row * (row_length // tile)
    tiled = pl.BlockSpec((tile, width), lambda i: (start + i, 0))
    ins = (
        [(me.reshape(1), SMEM_SPEC)]
        + [(array, ANY_SPEC) for array in weights.arrays]
        + [(array, tiled) for array in (gm, gq, gk, gv)]
        + [(array, full_spec((8, width))) for array in sums]
    )
    outs = [((tokens, width), F32, tiled)]
    if sums:
        outs.append(((8, width), F32, full_spec((8, width))))
    return call(
        functools.partial(stream_back_body, weights, len(sums)),
        "stream_back",
        (row_length // tile,),
        ins,
        outs,
        weights.scratch(),
        10,
        () if base is None else (base,),
    )


def in_order(net, me, sources, blocks):
    order = jnp.asarray(sources, jnp.int32)
    spot = jnp.zeros((net.n,), jnp.int32).at[order].set(jnp.arange(net.n, dtype=jnp.int32))
    return blocks[spot[jnp.arange(net.n) ^ me]]


def held(state, others):
    return after(state[0], others), state[1]


def stream_ends(state, unit, sizes):
    if not state.plain:
        total = state.net.scatter_end(state.state)
        found, start = [total[w * unit : (w + 1) * unit] for w in range(3)], 0
        for size in sizes:
            found.append(total[3 * unit, start : start + size])
            start += size
        return found
    rows, columns = state.rows, state.columns
    step_block = ((1, rows, columns), lambda i, at: (at, 0, 0))
    ins = state.sources(0, step_block)
    ins += [(term, step_block[0], lambda i, me: (0, 0, 0)) for term in state.terms[4:]]
    shapes = [(unit, columns)] * 3 + [(1, size) for size in sizes]
    outs = [(shape, F32, shape, lambda i, me: (0, 0)) for shape in shapes]

    def body(me_ref, *refs):
        total = refs[0][0].astype(F32)
        for ref in refs[1 : len(ins)]:
            total = total + ref[0].astype(F32)
        outs = refs[len(ins) :]
        for w in range(3):
            outs[w][...] = total[w * unit : (w + 1) * unit]
        start = 0
        for out_ref, size in zip(outs[3:], sizes):
            out_ref[...] = total[3 * unit : 3 * unit + 1, start : start + size]
            start += size

    results = sum_call(state.me, "stream_end", 1, ins, None, outs, body)
    return list(results[:3]) + [result[0] for result in results[3:]]


def on_device(
    net,
    inputs,
    timesteps,
    segments,
    cotangent,
    query_weight,
    key_weight,
    value_weight,
    output_weight,
    inner_weight,
    outer_weight,
    time_weight,
    *vectors,
):
    n = net.n
    me = lax.axis_index("fsdp").astype(jnp.int32)
    batch_count, row_count, row_length, model_width = inputs.shape
    rows = batch_count * row_count
    tokens = rows * row_length
    feats = features(timesteps.reshape(rows)).astype(BF16)
    order = (0, 1, 2, 4, 5, 6, 7, 8, 3)
    sizes = [vectors[i].shape[0] for i in order]
    r = model_width // n

    shards = (time_weight, query_weight, key_weight, value_weight)
    lines = [vectors[i] for i in order[:8]]
    far = net.gather_far(pack(me, shards, lines, vectors[3], timesteps.reshape(rows)))
    hidden = inner_weight.shape[1]
    inner_blocks = [
        inner_weight[:, start : start + model_width] for start in range(0, hidden, model_width)
    ]
    shard_io = after(jnp.concatenate([output_weight] + inner_blocks), far)
    far_io = net.gather_far(shard_io)
    far = net.stacked(far, me)
    near = net.gather_near(far)
    pieces, corners, _ = net.gather_corner(far, near)
    flow = net.gather_core(pieces)
    far_io, corners, shard_u = after((net.stacked(far_io, me), corners, outer_weight), ())
    near_io = net.gather_near(far_io)
    flow += net.gather_core(corners)
    far_u = net.gather_far(after(shard_u, flow))

    segments = segments.reshape(rows, row_length)
    x = inputs.reshape(tokens, model_width)
    feats_in = after(feats, far_io)
    temb, lines, stream_low, queries, key_rows, values = project(
        net, me, flow, feats_in, x, row_length
    )
    far_u = net.stacked(after(far_u, queries), me)
    near_u = net.gather_near(far_u)
    near_io, queries = after((near_io, queries), far_u)
    pieces, corners, sent = net.gather_corner(far_io, near_io)
    queries = after(queries, sent)
    context, log_total = attend(queries, key_rows, values, segments)
    near_u, context, pieces = after((near_u, context, pieces), ())
    flow_io = net.gather_core(pieces)
    pieces, corners_u, sent = net.gather_corner(far_u, near_u)
    context, corners = after((context, corners), sent)
    flow_io += net.gather_core(corners)
    corners = corners_u
    first_low, normed_first, spread_first, active_low, slope = ffn_in(
        net, me, flow_io, context, x, temb, lines, hidden, row_length
    )
    corners, active_low = after((corners, active_low), ())
    flow_u = net.gather_core(pieces) + net.gather_core(corners)
    (
        layer_output,
        grad_second,
        grad_second_low,
        sums_out,
    ) = ffn_out(
        net,
        me,
        flow_u,
        active_low,
        normed_first,
        cotangent.reshape(tokens, model_width),
        (lines,),
    )
    outer_halves = product(net, me, active_low, grad_second_low)
    outer_sum = Reduction(net, me, *outer_halves)
    slope = after(slope, outer_halves)
    (
        grad_inner_low,
        grad_mixed,
        grad_mixed_low,
        grad_context,
        inner_bias_grad,
        sums_back,
        mixed_rows,
    ) = ffn_back(
        net,
        me,
        flow_u,
        flow_io,
        grad_second,
        grad_second_low,
        slope,
        normed_first,
        spread_first,
        lines,
        row_length,
    )
    sent = outer_sum.hold(grad_mixed_low).corner()
    grad_mixed_low = after(grad_mixed_low, sent)
    inner_halves = inner_product(net, me, context, first_low, grad_mixed_low, grad_inner_low)
    inner_sum = Reduction(net, me, *inner_halves)
    sent = outer_sum.hold(inner_halves).near()
    grad_context = after(grad_context, (inner_halves, sent))
    back = (queries, key_rows, values, segments, log_total, grad_context)
    found, sums_rows, row_sums = None, 0.0, [mixed_rows]
    for row in range(rows):
        if row == 1:
            sent = list(inner_sum.hold(found[1]).corner())
            sent += list(outer_sum.hold((found[1], sent)).far())
            found = after(found, sent)
        found = attend_back(*back, row, found or ())
        sums_rows += found[3]
        row_sums.append(found[4])
        found = found[:3]
    grad_queries, grad_keys, grad_values = found
    sent = inner_sum.hold(grad_queries).near()
    outer_sum.hold(grad_queries)
    sums = sums_rows + sums_out + sums_back
    sums = sums.reshape(8, n, r).transpose(1, 0, 2).reshape(n, 8 * r)
    sums = jnp.concatenate([sums, inner_bias_grad.reshape(n, -1)], axis=1)
    sums = jnp.pad(sums, ((0, 0), (0, model_width - sums.shape[1]))).astype(BF16)
    sums = jnp.broadcast_to(sums[:, None], (n, 8, model_width)).reshape(n // 2, 16, model_width)
    stream_low, sums = after((stream_low, sums), (sent, outer_sum.received()))
    stream_halves = triple_product(
        net, me, sums, stream_low, grad_queries, grad_keys, grad_values
    )
    stream_sum = Reduction(net, me, *stream_halves)
    grad_mixed = after(grad_mixed, stream_halves)
    back = (flow, grad_mixed, grad_queries, grad_keys, grad_values)
    grad_stream, grad_temb = stream_back(net, me, *back, 0, row_length, sums=row_sums)
    ends = grad_temb[:rows][None]
    sources, ends = net.gather_round([0], ends, net.masks(net.core))
    sent = list(stream_sum.hold(grad_temb).corner())
    sent += list(inner_sum.hold((grad_temb, sent)).far())
    ends = after(ends, sent)
    sent = stream_sum.hold(sent).near()
    grad_stream = after(grad_stream, sent)
    for row in range(1, rows):
        (grad_stream,) = stream_back(net, me, *back, row, row_length, grad_stream)
    inner_sum.hold(grad_stream), outer_sum.hold(grad_stream)
    ends = after(ends, (grad_stream, inner_sum.received()))
    sources, ends = net.gather_round(sources, ends, net.masks(net.near))
    sent = stream_sum.hold(grad_stream).far()
    inner_sum.hold(sent), outer_sum.hold(sent)
    output_weight_grad, inner_weight_grad = inner_sum.end([1, hidden // model_width], r)
    (outer_weight_grad,) = outer_sum.end([1], outer_weight.shape[0])
    sources, ends = net.gather_round(sources, after(ends, sent), net.masks(net.middle))
    sources, ends = net.gather_round(
        sources, after(ends, stream_sum.received()), net.masks(net.outer)
    )
    temb_all = in_order(net, me, sources, ends).reshape(n * rows, model_width)
    query_weight_grad, key_weight_grad, value_weight_grad, *parts = stream_ends(
        stream_sum, r, sizes
    )
    own = model_width // n
    steps_all = after(lines, grad_stream)
    steps_all = (steps_all[12] * 64.0 + steps_all[13])[: n * rows]
    feats_own = own_features(steps_all, me * own, own).astype(BF16).astype(F32)
    time_weight_grad = lax.dot_general(
        feats_own,
        temb_all,
        (((0,), (0,)), ((), ())),
        precision=lax.Precision.HIGHEST,
    )
    parts = dict(zip(order, parts))
    vector_outs = [parts[i] for i in range(len(order))]

    shape = inputs.shape
    return (
        layer_output.reshape(shape),
        grad_stream.reshape(shape),
        query_weight_grad,
        key_weight_grad,
        value_weight_grad,
        output_weight_grad,
        inner_weight_grad,
        outer_weight_grad,
        time_weight_grad,
    ) + tuple(vector_outs)


def solution(mesh):
    matrix, vector = P("fsdp", None), P("fsdp")
    batch = P(None, "fsdp", None, None)
    return jax.shard_map(
        functools.partial(on_device, Net(mesh.shape["fsdp"])),
        mesh=mesh,
        in_specs=(batch, P(None, "fsdp"), P(None, "fsdp", None), batch)
        + (matrix,) * 7
        + (vector,) * 9,
        out_specs=(batch, batch) + (matrix,) * 7 + (vector,) * 9,
        check_vma=False,
    )
```

```python
import functools
import math

import jax
import jax.numpy as jnp
from jax import lax
from jax.experimental import pallas as pl
from jax.experimental.pallas import tpu as pltpu
from jax.sharding import PartitionSpec as P

D = 1024
H = 16


INV_ROOT_TWO = 0.7071067811865476
INV_ROOT_TAU = 0.3989422804014327
F32 = jnp.float32
BF16 = jnp.bfloat16


def matmul(operand, factor):
    return jnp.dot(operand, factor, preferred_element_type=F32)


def matmul_left(operand, factor):
    return lax.dot_general(
        operand, factor, (((0,), (0,)), ((), ())), preferred_element_type=F32
    )


def matmul_right(operand, factor):
    return lax.dot_general(
        operand, factor, (((1,), (1,)), ((), ())), preferred_element_type=F32
    )


def features(step_ids):
    half_width = D // 2
    freqs = jnp.exp(-math.log(10000.0) * jnp.arange(half_width, dtype=F32) / half_width)
    angles = step_ids.astype(F32)[..., None] * freqs
    return jnp.concatenate([jnp.sin(angles), jnp.cos(angles)], axis=-1)


def own_features(step_ids, first, count):
    half_width = D // 2
    columns = first + jnp.arange(count, dtype=jnp.int32)
    places = (columns % half_width).astype(F32)
    freqs = jnp.exp(-math.log(10000.0) * places / half_width)
    angles = step_ids[:, None] * freqs
    return jnp.where(columns < half_width, jnp.sin(angles), jnp.cos(angles))


def normalize(values_in):
    center = values_in - jnp.mean(values_in, axis=-1, keepdims=True)
    spread = lax.rsqrt(jnp.mean(center * center, axis=-1, keepdims=True) + 1e-05)
    return (center * spread, spread)


def norm_back(grad_normed, normed, spread):
    mean_grad = jnp.mean(grad_normed, axis=-1, keepdims=True)
    mean_cross = jnp.mean(grad_normed * normed, axis=-1, keepdims=True)
    return spread * (grad_normed - mean_grad - normed * mean_cross)


def halves_body(low_in, high_in, low_out, high_out):
    low_out[...] = low_in[...]
    high_out[...] = high_in[...]


def halves(low_of, high_of):
    count, half = low_of.shape[0], low_of.shape[0] // 2
    block = (1,) + low_of.shape[1:]
    return pl.pallas_call(
        halves_body,
        grid=(half,),
        in_specs=[
            pl.BlockSpec(block, lambda i: (i, 0, 0)),
            pl.BlockSpec(block, lambda i: (half + i, 0, 0)),
        ],
        out_specs=[pl.BlockSpec(block, lambda i: (i, 0, 0))] * 2,
        out_shape=[jax.ShapeDtypeStruct((half,) + low_of.shape[1:], low_of.dtype)] * 2,
        compiler_params=pltpu.CompilerParams(vmem_limit_bytes=16 << 20),
        cost_estimate=pl.CostEstimate(flops=1000, bytes_accessed=1000, transcendentals=0),
        name="halves",
    )(low_of, high_of)


class Net:
    def __init__(self, n):
        self.n = n
        self.bits = n.bit_length() - 1
        chip = self.bits - 1
        sizes = [(chip + 2 - i) // 3 for i in range(3)]
        groups, top = [], self.bits - 1
        for size in sizes:
            groups.append(tuple(range(top, top - size, -1)))
            top -= size
        self.outer, self.middle, self.near = groups
        self.core = (0,)

    def masks(self, group):
        found = []
        for pick in range(1, 1 << len(group)):
            mask = 0
            for place, bit in enumerate(group):
                if pick >> place & 1:
                    mask |= 1 << bit
            found.append(mask)
        return found

    def swap(self, array, mask):
        return lax.ppermute(array, "fsdp", [(i, i ^ mask) for i in range(self.n)])

    def gather_far(self, shard):
        return [shard] + [self.swap(shard, mask) for mask in self.masks(self.outer)]

    def stacked(self, parts, me):
        low = self.bits - len(self.outer)
        masks = [mask >> low for mask in [0] + self.masks(self.outer)]
        count, shape = len(parts), parts[0].shape

        def body(me_ref, *refs):
            for mask, ref in zip(masks, refs):
                refs[-1][me_ref[0] >> low ^ mask] = ref[...]

        whole = pl.BlockSpec(shape, lambda i: (0, 0))
        return pl.pallas_call(
            body,
            grid=(1,),
            in_specs=[pl.BlockSpec(memory_space=pltpu.SMEM)] + [whole] * count,
            out_specs=pl.BlockSpec((count,) + shape, lambda i: (0, 0, 0)),
            out_shape=jax.ShapeDtypeStruct((count,) + shape, parts[0].dtype),
            compiler_params=pltpu.CompilerParams(vmem_limit_bytes=16 << 20),
            cost_estimate=pl.CostEstimate(flops=1000, bytes_accessed=1000, transcendentals=0),
            name="stacked",
        )(me.reshape(1), *parts)

    def gather_near(self, own):
        return [
            [(mask, self.swap(own, mask)) for mask in self.masks(group)]
            for group in (self.near, self.middle)
        ]

    def gather_corner(self, own, near):
        half = own.shape[0] // 2
        pieces, corners, sent = [(0, 0, own)], [], []
        for group in near:
            pieces += [(0, mask, array) for mask, array in group]
        for mask_x, array_x in near[0]:
            for mask_y, array_y in near[1]:
                low, high = halves(array_y, array_x)
                sent += [low, high]
                corners.append((0, mask_x ^ mask_y, self.swap(low, mask_x)))
                corners.append((half, mask_x ^ mask_y, self.swap(high, mask_y)))
        return pieces, corners, sent

    def gather_core(self, pieces):
        return pieces + [(first, mask ^ 1, self.swap(array, 1)) for first, mask, array in pieces]

    def inner_masks(self):
        near, middle = self.masks(self.near), self.masks(self.middle)
        return near + middle + [x | y for x in near for y in middle]

    def gather_round(self, sources, array, masks):
        array = jnp.concatenate([array] + [self.swap(array, mask) for mask in masks])
        return [source ^ mask for mask in [0] + masks for source in sources], array

    def take(self, term, bits, mask, present, me):
        present = list(present)
        for bit in bits:
            place = present.index(bit)
            low = 1 << (len(present) - 1 - place)
            value = (me >> bit & 1) ^ (mask >> bit & 1)
            rest = term.shape[1:]
            term = term.reshape((1 << place, 2, low) + rest)
            term = lax.dynamic_index_in_dim(term, value, 1, keepdims=False)
            term = term.reshape((low << place,) + rest)
            present.remove(bit)
        return term

    def scatter_core(self, halves):
        keep, send = halves
        return [keep, self.swap(send, 1)], list(range(self.bits - 1, 0, -1))

    def added(self, parts, dtype):
        parts = [part.astype(F32) for part in parts]
        return sum(parts[1:], parts[0]).astype(dtype)

    def scatter_step(self, state, group, me):
        terms, present = state
        sent = []
        for mask in self.masks(group):
            parts = [self.take(term, group, mask, present, me) for term in terms]
            sent.append(self.added(parts, terms[0].dtype))
        received = [self.swap(part, mask) for part, mask in zip(sent, self.masks(group))]
        terms = [self.take(term, group, 0, present, me) for term in terms] + received
        return (terms, [bit for bit in present if bit not in group]), sent

    def scatter_corner(self, state, me):
        terms, present = state
        left = [bit for bit in present if bit not in self.near]
        found, sent = [], []
        for mask_x in self.masks(self.near):
            row = [self.take(term, self.near, mask_x, present, me) for term in terms]
            for mask_y in self.masks(self.middle):
                parts = [self.take(term, self.middle, mask_y, left, me) for term in row]
                half = parts[0].shape[0] // 2
                low = self.added([part[:half] for part in parts], terms[0].dtype)
                high = self.added([part[half:] for part in parts], terms[0].dtype)
                sent += [low, high]
                found.append((mask_x, mask_y, self.swap(low, mask_x), self.swap(high, mask_y)))
        return found, sent

    def scatter_near(self, state, corner, me):
        terms, present = state
        left = [bit for bit in present if bit not in self.near]
        mine, received, sent = [self.take(t, self.near, 0, present, me) for t in terms], [], []
        for mask_x in self.masks(self.near):
            row = [self.take(term, self.near, mask_x, present, me) for term in terms]
            parts = [self.take(term, self.middle, 0, left, me) for term in row]
            for mask, _, _, high in corner:
                if mask == mask_x:
                    parts.append(jnp.concatenate([jnp.zeros_like(high), high]))
            sent.append((self.added(parts, terms[0].dtype), mask_x))
        for mask_y in self.masks(self.middle):
            parts = [self.take(term, self.middle, mask_y, left, me) for term in mine]
            for _, mask, low, _ in corner:
                if mask == mask_y:
                    parts.append(jnp.concatenate([low, jnp.zeros_like(low)]))
            sent.append((self.added(parts, terms[0].dtype), mask_y))
        received = [self.swap(part, mask) for part, mask in sent]
        terms = [self.take(term, self.middle, 0, left, me) for term in mine] + received
        left = [bit for bit in left if bit not in self.middle]
        return (terms, left), [part for part, _ in sent]

    def scatter_far(self, state, me):
        return self.scatter_step(state, self.outer, me)

    def scatter_end(self, state):
        return self.added(state[0], F32)[0]

    def scatter(self, halves, order, me):
        state = self.scatter_core(halves)
        for group in order:
            state, _ = self.scatter_step(state, group, me)
        return self.scatter_end(state)

    def scatter_whole(self, whole, order, me):
        present = list(range(self.bits - 1, -1, -1))
        halves = [self.take(whole, self.core, mask, present, me) for mask in (0, 1)]
        return self.scatter(halves, order, me)


def after(values, others):
    leaves, tree = jax.tree.flatten(values)
    arrays = [leaf for leaf in leaves if not isinstance(leaf, int)]
    others = [leaf for leaf in jax.tree.leaves(others) if not isinstance(leaf, int)]
    tied = iter(lax.optimization_barrier(tuple(arrays + others)))
    return jax.tree.unflatten(
        tree, [leaf if isinstance(leaf, int) else next(tied) for leaf in leaves]
    )


class Weights:
    def __init__(self, net, me, wanted):
        self.arrays, self.plans, self.shapes = [], [], []
        seen = {}
        outer = 1 << len(net.outer)
        low = net.n // outer
        self.low = low
        for pieces, places, rows in wanted:
            places = (places,) if isinstance(places, int) else tuple(places)
            columns = pieces[0][2].shape[-1]
            plan = []
            if rows % 16:
                blocks = [
                    jnp.concatenate([array[:, place : place + rows] for _, _, array in pieces])
                    for place in places
                ]
                blocks = jnp.concatenate(blocks, axis=2)
                order = [
                    (first + j) * low + (me % low ^ mask)
                    for first, mask, array in pieces
                    for j in range(array.shape[0])
                ]
                spot = jnp.zeros((net.n,), jnp.int32).at[jnp.stack(order)].set(jnp.arange(net.n))
                whole = blocks[spot].reshape(outer, low * rows // 16, 16, len(places) * columns)
                plan.append((len(self.arrays), None, None, None))
                self.arrays.append(whole)
                self.shapes.append(whole.shape)
            else:
                for first, mask, array in pieces:
                    if id(array) not in seen:
                        seen[id(array)] = len(self.arrays)
                        self.arrays.append(array)
                    for k, place in enumerate(places):
                        own = (slice(None), pl.ds(place, rows))
                        aim = (pl.ds(first, array.shape[0]), pl.ds(k * columns, columns))
                        plan.append((seen[id(array)], own, mask, aim))
                self.shapes.append((outer, low, rows, len(places) * columns))
            self.plans.append(plan)
        self.slots = max(len(plan) for plan in self.plans)

    def scratch(self):
        return [pltpu.VMEM(shape, BF16) for shape in self.shapes] + [
            pltpu.SemaphoreType.DMA((len(self.plans), self.slots))
        ]

    def copies(self, w, me, array_refs, held_ref, sems):
        found = []
        for slot, (array, own, mask, aim) in enumerate(self.plans[w]):
            if own is None:
                pair = (array_refs[array], held_ref)
            else:
                spot = me % self.low ^ mask
                pair = (array_refs[array].at[own], held_ref.at[aim[0], spot, :, aim[1]])
            found.append(pltpu.make_async_copy(*pair, sems.at[w, slot]))
        return found

    def start(self, w, *refs):
        for copy in self.copies(w, *refs):
            copy.start()

    def wait(self, w, *refs):
        for copy in self.copies(w, *refs):
            copy.wait()


def flat(held):
    return held.reshape(-1, held.shape[-1])


SMEM_SPEC = pl.BlockSpec(memory_space=pltpu.SMEM)
ANY_SPEC = pl.BlockSpec(memory_space=pltpu.HBM)


def full_spec(shape):
    return pl.BlockSpec(shape, lambda *_: (0,) * len(shape))


def tile_spec(tile, columns):
    return pl.BlockSpec((tile, columns), lambda i: (i, 0))


def call(body, name, grid, ins, outs, scratch, us, bases=()):
    count = len(ins)

    def run(*refs):
        body(*refs[:count], *refs[count + len(bases) :])

    return pl.pallas_call(
        run,
        grid=grid,
        in_specs=[spec for _, spec in ins] + [ANY_SPEC] * len(bases),
        out_specs=[spec for _, _, spec in outs],
        out_shape=[jax.ShapeDtypeStruct(shape, dtype) for shape, dtype, _ in outs],
        scratch_shapes=scratch,
        input_output_aliases={count + i: i for i in range(len(bases))},
        compiler_params=pltpu.CompilerParams(
            vmem_limit_bytes=60 << 20,
            dimension_semantics=("arbitrary",) * len(grid),
        ),
        cost_estimate=pl.CostEstimate(
            flops=int(us * 2e10), bytes_accessed=int(us * 5e7), transcendentals=0
        ),
        name=name,
    )(*[array for array, _ in ins], *bases)


def sum_body(groups, me_ref, *refs):
    step = pl.program_id(0)
    outs = refs[len(refs) - len(groups) :]
    for out_ref, addends in zip(outs, groups):
        total = None
        for place, (low, high) in addends:
            part = refs[place][...].astype(F32)
            if low is not None:
                part = jnp.where((step >= low) & (step < high), part, 0.0)
            total = part if total is None else total + part
        out_ref[...] = total.astype(out_ref.dtype)


def sum_call(me, name, grid, ins, groups, outs, body=None, us=0.01):
    grid_spec = pltpu.PrefetchScalarGridSpec(
        num_scalar_prefetch=1,
        grid=(grid,),
        in_specs=[
            pl.BlockSpec(block, lambda i, me_ref, place=place: place(i, me_ref[0]))
            for _, block, place in ins
        ],
        out_specs=[
            pl.BlockSpec(block, lambda i, me_ref, place=place: place(i, me_ref[0]))
            for _, _, block, place in outs
        ],
    )
    return pl.pallas_call(
        body or functools.partial(sum_body, groups),
        grid_spec=grid_spec,
        out_shape=[jax.ShapeDtypeStruct(shape, dtype) for shape, dtype, _, _ in outs],
        compiler_params=pltpu.CompilerParams(
            vmem_limit_bytes=60 << 20, dimension_semantics=("arbitrary",)
        ),
        cost_estimate=pl.CostEstimate(flops=int(us * 2e10), bytes_accessed=int(us * 5e7), transcendentals=0),
        name=name,
    )(me.reshape(1), *[array for array, _, _ in ins])


class Reduction:
    def __init__(self, net, me, keep, send):
        self.net, self.me = net, me
        self.terms = [keep, net.swap(send, 1)]
        self.rows, self.columns = keep.shape[1:]
        self.plain = len(net.near) == 1 and len(net.middle) == 1 and self.rows % 8 == 0
        self.state = None

    def block(self):
        return (1, self.rows, self.columns)

    def parted(self, term):
        return term.reshape(-1, 4, self.rows, self.columns)

    def blocks(self, far):
        shape = (far, self.rows, self.columns)
        return (far, None, self.rows, self.columns), shape

    def hold(self, others):
        if self.plain:
            self.terms = after(self.terms, others)
        else:
            state = self.state or (self.terms, list(range(self.net.bits - 1, 0, -1)))
            self.state = held(state, others)
            if getattr(self, "corner_pieces", None) is not None:
                self.corner_pieces = after(self.corner_pieces, others)
        return self

    def corner(self):
        net = self.net
        if not self.plain:
            state = self.state or (self.terms, list(range(net.bits - 1, 0, -1)))
            self.state = state
            self.corner_pieces, sent = net.scatter_corner(state, self.me)
            return sent
        far = 1 << (len(net.outer) - 1)

        def place(shift):
            return lambda i, me: ((i + shift) * 4 + (me >> 1 & 3 ^ 3), 0, 0)

        ins = [(term, self.block(), place(shift)) for shift in (0, far) for term in self.terms]
        out = ((far, self.rows, self.columns), BF16, self.block(), lambda i, me: (i, 0, 0))
        always = (None, None)
        groups = [[(0, always), (1, always)], [(2, always), (3, always)]]
        low, high = sum_call(self.me, "corner_sum", far, ins, groups, [out, out])
        self.terms += [net.swap(low, 1 << net.near[0]), net.swap(high, 1 << net.middle[0])]
        return [low, high]

    def near(self):
        net = self.net
        if not self.plain:
            self.state, sent = net.scatter_near(self.state, self.corner_pieces, self.me)
            self.corner_pieces = None
            return sent
        far = 1 << (len(net.outer) - 1)
        keep, other, low, high = self.terms

        def place(flip):
            return lambda i, me: (i, me >> 1 & 3 ^ flip, 0, 0)

        block, shape = self.blocks(far)
        pair = (self.parted(keep), self.parted(other))
        ins = [(term, block, place(flip)) for flip in (1, 2) for term in pair]
        ins += [(term, shape, lambda i, me: (0, 0, 0)) for term in (high, low)]
        always = (None, None)
        groups = [
            [(0, always), (1, always), (4, (1, 2))],
            [(2, always), (3, always), (5, (0, 1))],
        ]
        whole = (2 * far, self.rows, self.columns)
        out = (whole, BF16, shape, lambda i, me: (i, 0, 0))
        sent = sum_call(self.me, "near_sum", 2, ins, groups, [out, out])
        received = [
            net.swap(part, 1 << group[0]) for part, group in zip(sent, (net.near, net.middle))
        ]
        self.terms = [keep, other] + received
        return sent

    def sources(self, flip, step_block):
        keep, other, row, column = self.terms[:4]
        found = []
        for term in (keep, other):
            found.append((term, lambda me: ((me >> 3 ^ flip) * 4 + (me >> 1 & 3))))
        for term in (row, column):
            found.append((term, lambda me: (me >> 3 ^ flip)))
        return [
            (term, step_block[0], lambda i, me, at=at: step_block[1](i, at(me)))
            for term, at in found
        ]

    def far(self):
        net = self.net
        if not self.plain:
            self.state, sent = net.scatter_step(self.state, net.outer, self.me)
            return sent
        parts = 2 if self.rows % 32 == 0 else 1
        step_block = ((1, self.rows // parts, self.columns), lambda i, at: (at, i, 0))
        masks = net.masks(net.outer)
        ins, groups = [], []
        for mask in masks:
            groups.append([(len(ins) + j, (None, None)) for j in range(4)])
            ins += self.sources(mask >> 3, step_block)
        out = ((1, self.rows, self.columns), BF16, step_block[0], lambda i, me: (0, i, 0))
        sent = sum_call(self.me, "far_sum", parts, ins, groups, [out] * len(masks))
        self.terms += [net.swap(part, mask) for part, mask in zip(sent, masks)]
        return sent

    def received(self):
        return self.terms[-1] if self.plain else self.state[0][-1]

    def end(self, lots, unit):
        if not self.plain:
            total = self.net.scatter_end(self.state)
            results, start = [], 0
            for count in lots:
                blocks = [
                    total[(start + j) * unit : (start + j + 1) * unit] for j in range(count)
                ]
                results.append(jnp.concatenate(blocks, axis=1))
                start += count
            return results
        step_block = ((1, unit, self.columns), lambda i, at: (at, i, 0))
        ins = self.sources(0, step_block)
        ins += [(term, step_block[0], lambda i, me: (0, i, 0)) for term in self.terms[4:]]
        outs, bounds, start = [], [], 0
        for count in lots:

            def place(i, me, start=start, count=count):
                return (0, jnp.clip(i - start, 0, count - 1))

            outs.append(((unit, count * self.columns), F32, (unit, self.columns), place))
            bounds.append((start, start + count))
            start += count

        def body(me_ref, *refs):
            step, addends = pl.program_id(0), refs[: len(ins)]
            total = addends[0][0].astype(F32)
            for ref in addends[1:]:
                total = total + ref[0].astype(F32)
            for out_ref, (low, high) in zip(refs[len(ins) :], bounds):

                @pl.when((step >= low) & (step < high))
                def _():
                    out_ref[...] = total

        return sum_call(self.me, "end_sum", start, ins, None, outs, body, 4)


def pack_body(sizes, me_ref, times_ref, small_ref, *refs):
    shards, out_ref = refs[:-1], refs[-1]
    start = 0
    for ref in shards:
        out_ref[start : start + ref.shape[0]] = ref[...]
        start += ref.shape[0]
    me, width = me_ref[0], out_ref.shape[1]

    small = small_ref[...]
    step, inner_size, steps = sizes

    def spread(first, count, offset):
        spots = lax.broadcasted_iota(jnp.int32, (small.shape[1], width), 0) - first
        lanes = lax.broadcasted_iota(jnp.int32, (small.shape[1], width), 1)
        hits = (spots >= 0) & (spots < count) & (lanes == spots + offset)
        return matmul(small, jnp.where(hits, 1.0, 0.0).astype(BF16))

    vectors = spread(0, step, me * step)
    place = me * inner_size
    inner = spread(step, inner_size, lax.rem(place, width))
    row = lax.broadcasted_iota(jnp.int32, inner.shape, 0)
    inner = jnp.where(row == place // width, inner, 0.0)
    lane = lax.broadcasted_iota(jnp.int32, inner.shape, 1)
    for j in range(steps):
        time = times_ref[j]
        digit = jnp.where(row == 4, time >> 6, jnp.where(row == 5, time & 63, 0))
        inner += jnp.where(lane == me * steps + j, digit, 0).astype(F32)
    out_ref[start:] = jnp.concatenate([vectors, inner]).astype(BF16)


def pack(me, shards, vectors, inner, times):
    step, width = shards[0].shape
    sizes = (step, inner.shape[0], times.shape[0])
    small = 0.0
    for line, vector in enumerate(vectors):
        small += jnp.pad(vector.astype(F32)[None], ((line, 7 - line), (0, 256 - step)))
    rest = 256 - sizes[1] - step
    small += jnp.pad(inner.astype(F32)[None], ((0, 0), (step, rest)))
    small = small.astype(BF16)
    rows = len(shards) * step + 16
    return call(
        functools.partial(pack_body, sizes),
        "pack",
        (1,),
        [(me.reshape(1), SMEM_SPEC), (times, SMEM_SPEC)]
        + [(array, full_spec(array.shape)) for array in (small, *shards)],
        [((rows, width), BF16, full_spec((rows, width)))],
        [],
        1,
    )[0]


def project_body(weights, tile, row_length, me_ref, *refs):
    count = len(weights.arrays)
    arrays, refs = refs[:count], refs[count:]
    feats_ref, x_ref = refs[:2]
    temb_ref, lines_ref, low_ref, q_ref, k_ref, v_ref = refs[2:8]
    tw, qw, kw, vw, lw, sems = refs[8:14]
    me, step = me_ref[0], pl.program_id(0)

    @pl.when(step == 0)
    def _():
        for w, held in enumerate((tw, qw, kw, vw, lw)):
            weights.start(w, me, arrays, held, sems)
        weights.wait(0, me, arrays, tw, sems)
        temb_ref[...] = matmul(feats_ref[...], flat(tw[...]))
        weights.wait(4, me, arrays, lw, sems)
        lines_ref[...] = jnp.sum(lw[...].astype(F32), axis=(0, 1))
        for w, held in ((1, qw), (2, kw), (3, vw)):
            weights.wait(w, me, arrays, held, sems)

    row = step * tile // row_length
    low = (x_ref[...].astype(F32) + temb_ref[pl.ds(row, 1), :]).astype(BF16)
    low_ref[...] = low
    q_ref[...] = (matmul(low, flat(qw[...])) + lines_ref[0:1]).astype(BF16)
    k_ref[...] = matmul(low, flat(kw[...])).astype(BF16)
    v_ref[...] = (matmul(low, flat(vw[...])) + lines_ref[1:2]).astype(BF16)


def project(net, me, flow, feats, x, row_length):
    tokens, width = x.shape
    tile = min(256, row_length)
    r = width // net.n
    weights = Weights(net, me, [(flow, w * r, r) for w in range(4)] + [(flow, 4 * r, 16)])
    ins = (
        [(me.reshape(1), SMEM_SPEC)]
        + [(array, ANY_SPEC) for array in weights.arrays]
        + [(feats, full_spec(feats.shape)), (x, tile_spec(tile, width))]
    )
    outs = [(feats.shape, F32, full_spec(feats.shape))]
    outs += [((16, width), F32, full_spec((16, width)))]
    outs += [((tokens, width), BF16, tile_spec(tile, width))] * 4
    return call(
        functools.partial(project_body, weights, tile, row_length),
        "project",
        (tokens // tile,),
        ins,
        outs,
        weights.scratch(),
        14,
    )


def same_document(seg_ref, bias_ref, block):
    @pl.when(block == 0)
    def _():
        row = seg_ref[0].astype(F32)
        column = jnp.transpose(jnp.broadcast_to(row, (128, row.shape[1])))[:, :1]
        bias_ref[...] = jnp.where(column == row, 0.0, -1e30)


def own_lanes(shape, head, head_dim):
    lanes = lax.broadcasted_iota(jnp.int32, shape, len(shape) - 1)
    return (lanes // head_dim) == head


def attend_body(head_dim, seg_ref, q_ref, k_ref, v_ref, out_ref, log_ref, bias_ref):
    same_document(seg_ref, bias_ref, pl.program_id(1))
    queries, key_rows, values = q_ref[...], k_ref[...], v_ref[...]
    scale = 1.0 / math.sqrt(head_dim)
    per = queries.shape[1] // head_dim
    total = None
    for head in range(per):
        mine = own_lanes(queries.shape, head, head_dim)
        keys_own = jnp.where(mine, key_rows * BF16(scale), BF16(0))
        scores = matmul_right(keys_own, queries) + bias_ref[...]
        top = jnp.max(scores, axis=0, keepdims=True)
        raised = jnp.exp(scores - top)
        amount = jnp.sum(raised, axis=0, keepdims=True)
        log_ref[0, 0, pl.ds(head, 1), :] = top + jnp.log(amount)
        soft_low = (raised * (1.0 / amount)).astype(BF16)
        context = matmul_left(soft_low, values)
        total = context if total is None else jnp.where(mine, context, total)
    out_ref[...] = total.astype(BF16)


def attend_back_body(
    head_dim, seg_ref, q_ref, k_ref, v_ref, log_ref, g_ref, gq_ref, gk_ref, gv_ref, sums_ref, rows_ref, bias_ref
):
    same_document(seg_ref, bias_ref, pl.program_id(1))
    queries, key_rows, values, grads = q_ref[...], k_ref[...], v_ref[...], g_ref[...]
    scale = 1.0 / math.sqrt(head_dim)
    per = queries.shape[1] // head_dim
    totals = None
    for head in range(per):
        mine = own_lanes(queries.shape, head, head_dim)
        keys_own = jnp.where(mine, key_rows * BF16(scale), BF16(0))
        scores = matmul_right(keys_own, queries) + bias_ref[...]
        soft = jnp.exp(scores - log_ref[0, 0, pl.ds(head, 1), :])
        grad_soft = matmul_right(jnp.where(mine, values, BF16(0)), grads)
        inner_sum = jnp.sum(soft * grad_soft, axis=0, keepdims=True)
        grad_scores = (soft * (grad_soft - inner_sum)).astype(BF16)
        parts = (
            matmul_left(grad_scores, key_rows),
            matmul(grad_scores, queries),
            matmul(soft.astype(BF16), grads),
        )
        if totals is None:
            totals = parts
        else:
            totals = tuple(jnp.where(mine, part, total) for part, total in zip(parts, totals))
    gq = (totals[0] * scale).astype(BF16)
    gv = totals[2].astype(BF16)
    gq_ref[...] = gq
    gk = (totals[1] * scale).astype(BF16)
    gk_ref[...] = gk
    gv_ref[...] = gv
    sums = [jnp.sum(part.astype(F32), axis=0, keepdims=True) for part in (gq, gk, gv)]
    zero = jnp.zeros_like(sums[0])
    sums_ref[...] = jnp.concatenate([sums[0], sums[2]] + [zero] * 6)
    rows_ref[...] = jnp.concatenate(sums + [zero] * 5)


def attention_args(segments, start, lanes, head_dim):
    row_length, per = segments.shape[1], lanes // head_dim
    segs = pl.BlockSpec((1, 1, row_length), lambda i, j: (start + i, 0, 0))
    block = pl.BlockSpec((row_length, lanes), lambda i, j: (start + i, j))
    log_spec = pl.BlockSpec((1, 1, per, row_length), lambda i, j: (start + i, j, 0, 0))
    return [(segments[:, None, :], segs)], block, log_spec


def attend(queries, key_rows, values, segments, lanes=256):
    rows, row_length = segments.shape
    tokens, width = queries.shape
    head_dim = width // H
    blocks, per = width // lanes, lanes // head_dim
    masks, block, log_spec = attention_args(segments, 0, lanes, head_dim)
    return call(
        functools.partial(attend_body, head_dim),
        "attend",
        (rows, blocks),
        masks + [(array, block) for array in (queries, key_rows, values)],
        [
            ((tokens, width), BF16, block),
            ((rows, blocks, per, row_length), F32, log_spec),
        ],
        [pltpu.VMEM((row_length, row_length), F32)],
        24,
    )


def attend_back(queries, key_rows, values, segments, log_total, grad_context, row, bases=(), lanes=256):
    rows, row_length = segments.shape
    tokens, width = queries.shape
    head_dim = width // H
    masks, block, log_spec = attention_args(segments, row, lanes, head_dim)
    return call(
        functools.partial(attend_back_body, head_dim),
        "attend_back",
        (1, width // lanes),
        masks
        + [(array, block) for array in (queries, key_rows, values)]
        + [(log_total, log_spec), (grad_context, block)],
        [((tokens, width), BF16, block)] * 3
        + [((8, width), F32, pl.BlockSpec((8, lanes), lambda i, j: (0, j)))] * 2,
        [pltpu.VMEM((row_length, row_length), F32)],
        19,
        bases,
    )


def add_to(ref, value, step):
    part = jnp.sum(value, axis=0, keepdims=True)

    @pl.when(step == 0)
    def _():
        ref[...] = part

    @pl.when(step != 0)
    def _():
        ref[...] += part


def add_lines(ref, values, step):
    zero = jnp.zeros((1, ref.shape[1]), F32)
    sums = {line: jnp.sum(value, axis=0, keepdims=True) for line, value in values.items()}
    part = jnp.concatenate([sums.get(line, zero) for line in range(ref.shape[0])])

    @pl.when(step == 0)
    def _():
        ref[...] = part

    @pl.when(step != 0)
    def _():
        ref[...] += part


def ffn_in_body(weights, tile, row_length, chunk, me_ref, *refs):
    count = len(weights.arrays)
    arrays, refs = refs[:count], refs[count:]
    context_ref, x_ref, temb_ref, lines_ref = refs[:4]
    first_low_ref, normed_ref, spread_ref, active_ref, slope_ref = refs[4:9]
    ow, iw, sems = refs[9:12]
    me, step = me_ref[0], pl.program_id(0)

    @pl.when(step == 0)
    def _():
        for w, held in enumerate((ow, iw)):
            weights.start(w, me, arrays, held, sems)
        weights.wait(0, me, arrays, ow, sems)

    row = step * tile // row_length
    stream = x_ref[...].astype(F32) + temb_ref[pl.ds(row, 1), :]
    mixed = stream + (matmul(context_ref[...], flat(ow[...])) + lines_ref[2:3])
    normed, spread = normalize(mixed)
    normed_ref[...] = normed
    spread_ref[...] = spread
    first = normed * lines_ref[4:5] + lines_ref[5:6]
    low = first.astype(BF16)
    first_low_ref[...] = low

    @pl.when(step == 0)
    def _():
        weights.wait(1, me, arrays, iw, sems)

    width, hidden = ow.shape[3], iw.shape[3]

    def inner(start):
        pre = matmul(low, flat(iw[:, :, :, start : start + chunk]))
        line, place = 8 + start // width, start % width
        return pre + lines_ref[line : line + 1, place : place + chunk]

    later = inner(0)
    for start in range(0, hidden, chunk):
        pre = later
        if start + chunk < hidden:
            later = inner(start + chunk)
        columns = slice(start, start + chunk)
        normal_cdf = 0.5 * (1.0 + lax.erf(pre * INV_ROOT_TWO))
        normal_pdf = jnp.exp(-0.5 * pre * pre) * INV_ROOT_TAU
        active_ref[:, columns] = (pre * normal_cdf).astype(BF16)
        slope_ref[:, columns] = (normal_cdf + pre * normal_pdf).astype(BF16)


def ffn_in(net, me, flow, context, x, temb, lines, hidden, row_length, tile=256, chunk=512):
    tokens, width = x.shape
    r = width // net.n
    blocks = range(r, r + hidden // width * r, r)
    weights = Weights(net, me, [(flow, 0, r), (flow, blocks, r)])
    tile = min(tile, row_length)
    tiled, wide, thin = (tile_spec(tile, columns) for columns in (width, hidden, 1))
    ins = (
        [(me.reshape(1), SMEM_SPEC)]
        + [(array, ANY_SPEC) for array in weights.arrays]
        + [(context, tiled), (x, tiled)]
        + [(array, full_spec(array.shape)) for array in (temb, lines)]
    )
    outs = [
        ((tokens, width), BF16, tiled),
        ((tokens, width), F32, tiled),
        ((tokens, 1), F32, thin),
        ((tokens, hidden), BF16, wide),
        ((tokens, hidden), BF16, wide),
    ]
    return call(
        functools.partial(ffn_in_body, weights, tile, row_length, chunk),
        "ffn_in",
        (tokens // tile,),
        ins,
        outs,
        weights.scratch(),
        30,
    )


def ffn_out_body(weights, me_ref, *refs):
    count = len(weights.arrays)
    arrays, refs = refs[:count], refs[count:]
    active_ref, normed_ref, cot_ref, lines_ref = refs[:4]
    out_ref, gs_ref, gs_low_ref, sums_ref = refs[4:8]
    uw, sems = refs[8:10]
    me, step = me_ref[0], pl.program_id(0)

    @pl.when(step == 0)
    def _():
        weights.start(0, me, arrays, uw, sems)
        weights.wait(0, me, arrays, uw, sems)

    first = normed_ref[...] * lines_ref[4:5] + lines_ref[5:6]
    second = first + (matmul(active_ref[...], flat(uw[...])) + lines_ref[3:4])
    normed_second, spread_second = normalize(second)
    out_ref[...] = (normed_second * lines_ref[6:7] + lines_ref[7:8]).astype(BF16)
    grad_out = cot_ref[...].astype(F32)
    grad_second = norm_back(grad_out * lines_ref[6:7], normed_second, spread_second)
    gs_ref[...] = grad_second
    low = grad_second.astype(BF16)
    gs_low_ref[...] = low
    add_lines(sums_ref, {3: low.astype(F32), 6: grad_out * normed_second, 7: grad_out}, step)


def ffn_out(net, me, flow, active, normed, cotangent, vectors, tile=256):
    tokens, width = normed.shape
    hidden = active.shape[1]
    weights = Weights(net, me, [(flow, 0, hidden // net.n)])
    tiled, wide = tile_spec(tile, width), tile_spec(tile, hidden)
    ins = (
        [(me.reshape(1), SMEM_SPEC)]
        + [(array, ANY_SPEC) for array in weights.arrays]
        + [(active, wide), (normed, tiled), (cotangent, tiled)]
        + [(vector, full_spec(vector.shape)) for vector in vectors]
    )
    outs = [
        ((tokens, width), BF16, tiled),
        ((tokens, width), F32, tiled),
        ((tokens, width), BF16, tiled),
        ((8, width), F32, full_spec((8, width))),
    ]
    return call(
        functools.partial(ffn_out_body, weights),
        "ffn_out",
        (tokens // tile,),
        ins,
        outs,
        weights.scratch(),
        20,
    )


def ffn_back_body(weights, tile, row_length, me_ref, *refs):
    count = len(weights.arrays)
    arrays, refs = refs[:count], refs[count:]
    (gs_ref, gs_low_ref, slope_ref, normed_ref, spread_ref, lines_ref) = refs[:6]
    (gi_ref, gm_ref, gm_low_ref, gc_ref, ibg_ref, sums_ref, rows_ref) = refs[6:13]
    uw, ow, iw, sems, held_ref = refs[13:18]
    me, step = me_ref[0], pl.program_id(0)
    last = pl.num_programs(0) - 1

    @pl.when(step == 0)
    def _():
        for w, held in ((0, uw), (2, iw), (1, ow)):
            weights.start(w, me, arrays, held, sems)
        sums_ref[...] = jnp.zeros_like(sums_ref)
        rows_ref[...] = jnp.zeros_like(rows_ref)
        ibg_ref[...] = jnp.zeros_like(ibg_ref)
        weights.wait(0, me, arrays, uw, sems)

    def through_hidden(first_time=False):
        part = gi_ref.shape[1] // uw.shape[0]
        for z in range(uw.shape[0]):
            columns = slice(z * part, (z + 1) * part)
            grad_active = matmul_right(gs_low_ref[...], flat(uw[z]))
            gi = (grad_active * slope_ref[:, columns].astype(F32)).astype(BF16)
            gi_ref[:, columns] = gi
            ibg_ref[:, columns] += jnp.sum(gi.astype(F32), axis=0, keepdims=True)
        if first_time:
            weights.wait(2, me, arrays, iw, sems)
        return gs_ref[...] + matmul_right(gi_ref[...], flat(iw[...]))

    def through_norm(grad_first):
        normed = normed_ref[...]
        grad_mixed = norm_back(grad_first * lines_ref[4:5], normed, spread_ref[...])
        gm_ref[...] = grad_mixed
        low = grad_mixed.astype(BF16)
        gm_low_ref[...] = low
        row = pl.ds((step - 1) * tile // row_length, 1)
        rows_ref[row, :] += jnp.sum(grad_mixed, axis=0, keepdims=True)
        values = {2: low.astype(F32), 4: grad_first * normed, 5: grad_first}
        for line, value in values.items():
            sums_ref[line : line + 1] += jnp.sum(value, axis=0, keepdims=True)
        gc_ref[...] = matmul_right(low, flat(ow[...])).astype(BF16)

    @pl.when(step == 0)
    def _():
        held_ref[...] = through_hidden(True)
        weights.wait(1, me, arrays, ow, sems)

    @pl.when((step > 0) & (step < last))
    def _():
        grad_first = held_ref[...]
        later = through_hidden()
        through_norm(grad_first)
        held_ref[...] = later

    @pl.when(step == last)
    def _():
        through_norm(held_ref[...])


def ffn_back(net, me, flow_u, flow_io, gs, gs_low, slope, normed, spread, lines, row_length, tile=256):
    tokens, width = gs.shape
    hidden = slope.shape[1]
    r = width // net.n
    weights = Weights(
        net,
        me,
        [
            (flow_u, 0, hidden // net.n),
            (flow_io, 0, r),
            (flow_io, range(r, r + hidden // width * r, r), r),
        ],
    )
    tile = min(tile, row_length)
    steps = tokens // tile

    def ahead(columns):
        return pl.BlockSpec((tile, columns), lambda i: (jnp.minimum(i, steps - 1), 0))

    def behind(columns):
        return pl.BlockSpec((tile, columns), lambda i: (jnp.maximum(i - 1, 0), 0))

    ins = (
        [(me.reshape(1), SMEM_SPEC)]
        + [(array, ANY_SPEC) for array in weights.arrays]
        + [(gs, ahead(width)), (gs_low, ahead(width)), (slope, ahead(hidden))]
        + [(normed, behind(width)), (spread, behind(1)), (lines, full_spec(lines.shape))]
    )
    outs = [
        ((tokens, hidden), BF16, ahead(hidden)),
        ((tokens, width), F32, behind(width)),
        ((tokens, width), BF16, behind(width)),
        ((tokens, width), BF16, behind(width)),
        ((1, hidden), F32, full_spec((1, hidden))),
        ((8, width), F32, full_spec((8, width))),
        ((8, width), F32, full_spec((8, width))),
    ]
    return call(
        functools.partial(ffn_back_body, weights, tile, row_length),
        "ffn_back",
        (steps + 1,),
        ins,
        outs,
        weights.scratch() + [pltpu.VMEM((tile, width), F32)],
        36,
    )


def deal(me_ref, total, rows, keep_ref, send_ref, kind=0):
    core = me_ref[0] & 1
    total = total.reshape(-1, 2, rows, total.shape[-1])
    low, high = total[:, 0], total[:, 1]
    place = slice(kind * rows, (kind + 1) * rows)
    keep_ref[:, place] = jnp.where(core == 0, low, high).astype(BF16)
    send_ref[:, place] = jnp.where(core == 0, high, low).astype(BF16)


def product_body(rows, me_ref, a_ref, b_ref, keep_ref, send_ref):
    deal(me_ref, matmul_left(a_ref[...], b_ref[...]), rows, keep_ref, send_ref)


def product(net, me, left, right, tile=1024):
    tokens, width = left.shape
    columns = right.shape[1]
    rows = width // net.n
    shape = (net.n // 2, rows, columns)
    block = pl.BlockSpec((tile // (2 * rows), rows, columns), lambda i: (i, 0, 0))
    return call(
        functools.partial(product_body, rows),
        "product",
        (width // tile,),
        [
            (me.reshape(1), SMEM_SPEC),
            (left, pl.BlockSpec((tokens, tile), lambda i: (0, i))),
            (right, full_spec((tokens, columns))),
        ],
        [(shape, BF16, block), (shape, BF16, block)],
        [],
        15,
    )


def inner_body(rows, me_ref, context_ref, first_ref, gm_ref, gi_ref, keep_ref, send_ref):
    total = matmul_left(first_ref[...], gi_ref[...])
    width = gm_ref.shape[1]
    deal(me_ref, matmul_left(context_ref[...], gm_ref[...]), rows, keep_ref, send_ref, 0)
    for k in range(total.shape[1] // width):
        part = total[:, k * width : (k + 1) * width]
        deal(me_ref, part, rows, keep_ref, send_ref, k + 1)


def inner_product(net, me, context, first_low, gm_low, gi, tile=256):
    tokens, width = context.shape
    hidden = gi.shape[1]
    rows = width // net.n
    kinds = 1 + hidden // width
    shape = (net.n // 2, kinds * rows, width)
    block = pl.BlockSpec((tile // (2 * rows), kinds * rows, width), lambda i: (i, 0, 0))
    left = pl.BlockSpec((tokens, tile), lambda i: (0, i))
    return call(
        functools.partial(inner_body, rows),
        "inner_product",
        (width // tile,),
        [
            (me.reshape(1), SMEM_SPEC),
            (context, left),
            (first_low, left),
            (gm_low, full_spec((tokens, width))),
            (gi, full_spec((tokens, hidden))),
        ],
        [(shape, BF16, block), (shape, BF16, block)],
        [],
        18,
    )


def triple_body(rows, me_ref, lines_ref, a_ref, q_ref, k_ref, v_ref, keep_ref, send_ref):
    for w, ref in enumerate((q_ref, k_ref, v_ref)):
        deal(me_ref, matmul_left(a_ref[...], ref[...]), rows, keep_ref, send_ref, w)
    core = me_ref[0] & 1
    low, high = lines_ref[:, 0:8], lines_ref[:, 8:16]
    place = slice(3 * rows, 3 * rows + 8)
    keep_ref[:, place] = jnp.where(core == 0, low, high).astype(BF16)
    send_ref[:, place] = jnp.where(core == 0, high, low).astype(BF16)


def triple_product(net, me, lines, left, gq, gk, gv, tile=256):
    tokens, width = left.shape
    rows = width // net.n
    shape = (net.n // 2, 3 * rows + 8, width)
    chips = tile // (2 * rows)
    block = pl.BlockSpec((chips, 3 * rows + 8, width), lambda i: (i, 0, 0))
    full = full_spec((tokens, width))
    return call(
        functools.partial(triple_body, rows),
        "triple_product",
        (width // tile,),
        [
            (me.reshape(1), SMEM_SPEC),
            (lines, pl.BlockSpec((chips, 16, width), lambda i: (i, 0, 0))),
            (left, pl.BlockSpec((tokens, tile), lambda i: (0, i))),
            (gq, full),
            (gk, full),
            (gv, full),
        ],
        [(shape, BF16, block), (shape, BF16, block)],
        [],
        13,
    )


def stream_back_body(weights, rows, me_ref, *refs):
    count = len(weights.arrays)
    arrays, refs = refs[:count], refs[count:]
    gm_ref, gq_ref, gk_ref, gv_ref = refs[:4]
    sum_refs, refs = refs[4 : 4 + rows], refs[4 + rows :]
    out_ref, outs = refs[0], refs[1:]
    qw, kw, vw, sems = outs[-4:]
    me, step = me_ref[0], pl.program_id(0)

    @pl.when(step == 0)
    def _():
        for w, held in enumerate((qw, kw, vw)):
            weights.start(w, me, arrays, held, sems)
        for w, held in enumerate((qw, kw, vw)):
            weights.wait(w, me, arrays, held, sems)
        if sum_refs:
            total = sum_refs[0][...]
            for w, held in enumerate((qw, kw, vw)):
                lines = [ref[w : w + 1] for ref in sum_refs[1:]]
                lines += [jnp.zeros_like(lines[0])] * (8 - len(lines))
                total += matmul_right(jnp.concatenate(lines).astype(BF16), flat(held[...]))
            outs[0][...] = total

    out_ref[...] = (
        gm_ref[...]
        + matmul_right(gq_ref[...], flat(qw[...]))
        + matmul_right(gk_ref[...], flat(kw[...]))
        + matmul_right(gv_ref[...], flat(vw[...]))
    )


def stream_back(net, me, flow, gm, gq, gk, gv, row, row_length, base=None, sums=(), tile=256):
    tokens, width = gm.shape
    tile = min(tile, row_length)
    r = width // net.n
    weights = Weights(net, me, [(flow, w * r, r) for w in (1, 2, 3)])
    start = row * (row_length // tile)
    tiled = pl.BlockSpec((tile, width), lambda i: (start + i, 0))
    ins = (
        [(me.reshape(1), SMEM_SPEC)]
        + [(array, ANY_SPEC) for array in weights.arrays]
        + [(array, tiled) for array in (gm, gq, gk, gv)]
        + [(array, full_spec((8, width))) for array in sums]
    )
    outs = [((tokens, width), F32, tiled)]
    if sums:
        outs.append(((8, width), F32, full_spec((8, width))))
    return call(
        functools.partial(stream_back_body, weights, len(sums)),
        "stream_back",
        (row_length // tile,),
        ins,
        outs,
        weights.scratch(),
        10,
        () if base is None else (base,),
    )


def in_order(net, me, sources, blocks):
    order = jnp.asarray(sources, jnp.int32)
    spot = jnp.zeros((net.n,), jnp.int32).at[order].set(jnp.arange(net.n, dtype=jnp.int32))
    return blocks[spot[jnp.arange(net.n) ^ me]]


def held(state, others):
    return after(state[0], others), state[1]


def stream_ends(state, unit, sizes):
    if not state.plain:
        total = state.net.scatter_end(state.state)
        found, start = [total[w * unit : (w + 1) * unit] for w in range(3)], 0
        for size in sizes:
            found.append(total[3 * unit, start : start + size])
            start += size
        return found
    rows, columns = state.rows, state.columns
    step_block = ((1, rows, columns), lambda i, at: (at, 0, 0))
    ins = state.sources(0, step_block)
    ins += [(term, step_block[0], lambda i, me: (0, 0, 0)) for term in state.terms[4:]]
    shapes = [(unit, columns)] * 3 + [(1, size) for size in sizes]
    outs = [(shape, F32, shape, lambda i, me: (0, 0)) for shape in shapes]

    def body(me_ref, *refs):
        total = refs[0][0].astype(F32)
        for ref in refs[1 : len(ins)]:
            total = total + ref[0].astype(F32)
        outs = refs[len(ins) :]
        for w in range(3):
            outs[w][...] = total[w * unit : (w + 1) * unit]
        start = 0
        for out_ref, size in zip(outs[3:], sizes):
            out_ref[...] = total[3 * unit : 3 * unit + 1, start : start + size]
            start += size

    results = sum_call(state.me, "stream_end", 1, ins, None, outs, body)
    return list(results[:3]) + [result[0] for result in results[3:]]


def on_device(
    net,
    inputs,
    timesteps,
    segments,
    cotangent,
    query_weight,
    key_weight,
    value_weight,
    output_weight,
    inner_weight,
    outer_weight,
    time_weight,
    *vectors,
):
    n = net.n
    me = lax.axis_index("fsdp").astype(jnp.int32)
    batch_count, row_count, row_length, model_width = inputs.shape
    rows = batch_count * row_count
    tokens = rows * row_length
    feats = features(timesteps.reshape(rows)).astype(BF16)
    order = (0, 1, 2, 4, 5, 6, 7, 8, 3)
    sizes = [vectors[i].shape[0] for i in order]
    r = model_width // n

    shards = (time_weight, query_weight, key_weight, value_weight)
    lines = [vectors[i] for i in order[:8]]
    far = net.gather_far(pack(me, shards, lines, vectors[3], timesteps.reshape(rows)))
    hidden = inner_weight.shape[1]
    inner_blocks = [
        inner_weight[:, start : start + model_width] for start in range(0, hidden, model_width)
    ]
    shard_io = after(jnp.concatenate([output_weight] + inner_blocks), far)
    far_io = net.gather_far(shard_io)
    far = net.stacked(far, me)
    near = net.gather_near(far)
    pieces, corners, _ = net.gather_corner(far, near)
    flow = net.gather_core(pieces)
    far_io, corners, shard_u = after((net.stacked(far_io, me), corners, outer_weight), ())
    near_io = net.gather_near(far_io)
    flow += net.gather_core(corners)
    far_u = net.gather_far(after(shard_u, flow))

    segments = segments.reshape(rows, row_length)
    x = inputs.reshape(tokens, model_width)
    feats_in = after(feats, far_io)
    temb, lines, stream_low, queries, key_rows, values = project(
        net, me, flow, feats_in, x, row_length
    )
    far_u = net.stacked(after(far_u, queries), me)
    near_u = net.gather_near(far_u)
    near_io, queries = after((near_io, queries), far_u)
    pieces, corners, sent = net.gather_corner(far_io, near_io)
    queries = after(queries, sent)
    context, log_total = attend(queries, key_rows, values, segments)
    near_u, context, pieces = after((near_u, context, pieces), ())
    flow_io = net.gather_core(pieces)
    pieces, corners_u, sent = net.gather_corner(far_u, near_u)
    context, corners = after((context, corners), sent)
    flow_io += net.gather_core(corners)
    corners = corners_u
    first_low, normed_first, spread_first, active_low, slope = ffn_in(
        net, me, flow_io, context, x, temb, lines, hidden, row_length
    )
    corners, active_low = after((corners, active_low), ())
    flow_u = net.gather_core(pieces) + net.gather_core(corners)
    (
        layer_output,
        grad_second,
        grad_second_low,
        sums_out,
    ) = ffn_out(
        net,
        me,
        flow_u,
        active_low,
        normed_first,
        cotangent.reshape(tokens, model_width),
        (lines,),
    )
    outer_halves = product(net, me, active_low, grad_second_low)
    outer_sum = Reduction(net, me, *outer_halves)
    slope = after(slope, outer_halves)
    (
        grad_inner_low,
        grad_mixed,
        grad_mixed_low,
        grad_context,
        inner_bias_grad,
        sums_back,
        mixed_rows,
    ) = ffn_back(
        net,
        me,
        flow_u,
        flow_io,
        grad_second,
        grad_second_low,
        slope,
        normed_first,
        spread_first,
        lines,
        row_length,
    )
    sent = outer_sum.hold(grad_mixed_low).corner()
    grad_mixed_low = after(grad_mixed_low, sent)
    inner_halves = inner_product(net, me, context, first_low, grad_mixed_low, grad_inner_low)
    inner_sum = Reduction(net, me, *inner_halves)
    sent = outer_sum.hold(inner_halves).near()
    grad_context = after(grad_context, (inner_halves, sent))
    back = (queries, key_rows, values, segments, log_total, grad_context)
    found, sums_rows, row_sums = None, 0.0, [mixed_rows]
    for row in range(rows):
        if row == 1:
            sent = list(inner_sum.hold(found[1]).corner())
            sent += list(outer_sum.hold((found[1], sent)).far())
            found = after(found, sent)
        found = attend_back(*back, row, found or ())
        sums_rows += found[3]
        row_sums.append(found[4])
        found = found[:3]
    grad_queries, grad_keys, grad_values = found
    sent = inner_sum.hold(grad_queries).near()
    outer_sum.hold(grad_queries)
    sums = sums_rows + sums_out + sums_back
    sums = sums.reshape(8, n, r).transpose(1, 0, 2).reshape(n, 8 * r)
    sums = jnp.concatenate([sums, inner_bias_grad.reshape(n, -1)], axis=1)
    sums = jnp.pad(sums, ((0, 0), (0, model_width - sums.shape[1]))).astype(BF16)
    sums = jnp.broadcast_to(sums[:, None], (n, 8, model_width)).reshape(n // 2, 16, model_width)
    stream_low, sums = after((stream_low, sums), (sent, outer_sum.received()))
    stream_halves = triple_product(
        net, me, sums, stream_low, grad_queries, grad_keys, grad_values
    )
    stream_sum = Reduction(net, me, *stream_halves)
    grad_mixed = after(grad_mixed, stream_halves)
    back = (flow, grad_mixed, grad_queries, grad_keys, grad_values)
    grad_stream, grad_temb = stream_back(net, me, *back, 0, row_length, sums=row_sums)
    ends = grad_temb[:rows][None]
    sources, ends = net.gather_round([0], ends, net.masks(net.core))
    sent = list(stream_sum.hold(grad_temb).corner())
    sent += list(inner_sum.hold((grad_temb, sent)).far())
    ends = after(ends, sent)
    sent = stream_sum.hold(sent).near()
    grad_stream = after(grad_stream, sent)
    for row in range(1, rows):
        (grad_stream,) = stream_back(net, me, *back, row, row_length, grad_stream)
    inner_sum.hold(grad_stream), outer_sum.hold(grad_stream)
    sent = stream_sum.hold(grad_stream).far()
    ends = after(ends, (sent, inner_sum.received()))
    sources, ends = net.gather_round(sources, ends, net.masks(net.near))
    inner_sum.hold(sent), outer_sum.hold(sent)
    output_weight_grad, inner_weight_grad = inner_sum.end([1, hidden // model_width], r)
    (outer_weight_grad,) = outer_sum.end([1], outer_weight.shape[0])
    sources, ends = net.gather_round(sources, ends, net.masks(net.middle))
    others = (stream_sum.received(), inner_weight_grad, outer_weight_grad)
    sources, ends = net.gather_round(sources, after(ends, others), net.masks(net.outer))
    temb_all = in_order(net, me, sources, ends).reshape(n * rows, model_width)
    query_weight_grad, key_weight_grad, value_weight_grad, *parts = stream_ends(
        stream_sum, r, sizes
    )
    own = model_width // n
    steps_all = after(lines, grad_stream)
    steps_all = (steps_all[12] * 64.0 + steps_all[13])[: n * rows]
    feats_own = own_features(steps_all, me * own, own).astype(BF16).astype(F32)
    time_weight_grad = lax.dot_general(
        feats_own,
        temb_all,
        (((0,), (0,)), ((), ())),
        precision=lax.Precision.HIGHEST,
    )
    parts = dict(zip(order, parts))
    vector_outs = [parts[i] for i in range(len(order))]

    shape = inputs.shape
    return (
        layer_output.reshape(shape),
        grad_stream.reshape(shape),
        query_weight_grad,
        key_weight_grad,
        value_weight_grad,
        output_weight_grad,
        inner_weight_grad,
        outer_weight_grad,
        time_weight_grad,
    ) + tuple(vector_outs)


def solution(mesh):
    matrix, vector = P("fsdp", None), P("fsdp")
    batch = P(None, "fsdp", None, None)
    return jax.shard_map(
        functools.partial(on_device, Net(mesh.shape["fsdp"])),
        mesh=mesh,
        in_specs=(batch, P(None, "fsdp"), P(None, "fsdp", None), batch)
        + (matrix,) * 7
        + (vector,) * 9,
        out_specs=(batch, batch) + (matrix,) * 7 + (vector,) * 9,
        check_vma=False,
    )
```

```python
import functools
import math

import jax
import jax.numpy as jnp
from jax import lax
from jax.experimental import pallas as pl
from jax.experimental.pallas import tpu as pltpu
from jax.sharding import PartitionSpec as P

D = 1024
H = 16


INV_ROOT_TWO = 0.7071067811865476
INV_ROOT_TAU = 0.3989422804014327
F32 = jnp.float32
BF16 = jnp.bfloat16


def matmul(operand, factor):
    return jnp.dot(operand, factor, preferred_element_type=F32)


def matmul_left(operand, factor):
    return lax.dot_general(
        operand, factor, (((0,), (0,)), ((), ())), preferred_element_type=F32
    )


def matmul_right(operand, factor):
    return lax.dot_general(
        operand, factor, (((1,), (1,)), ((), ())), preferred_element_type=F32
    )


def features(step_ids):
    half_width = D // 2
    freqs = jnp.exp(-math.log(10000.0) * jnp.arange(half_width, dtype=F32) / half_width)
    angles = step_ids.astype(F32)[..., None] * freqs
    return jnp.concatenate([jnp.sin(angles), jnp.cos(angles)], axis=-1)


def own_features(step_ids, first, count):
    half_width = D // 2
    columns = first + jnp.arange(count, dtype=jnp.int32)
    places = (columns % half_width).astype(F32)
    freqs = jnp.exp(-math.log(10000.0) * places / half_width)
    angles = step_ids[:, None] * freqs
    return jnp.where(columns < half_width, jnp.sin(angles), jnp.cos(angles))


def normalize(values_in):
    center = values_in - jnp.mean(values_in, axis=-1, keepdims=True)
    spread = lax.rsqrt(jnp.mean(center * center, axis=-1, keepdims=True) + 1e-05)
    return (center * spread, spread)


def norm_back(grad_normed, normed, spread):
    mean_grad = jnp.mean(grad_normed, axis=-1, keepdims=True)
    mean_cross = jnp.mean(grad_normed * normed, axis=-1, keepdims=True)
    return spread * (grad_normed - mean_grad - normed * mean_cross)


def halves_body(low_in, high_in, low_out, high_out):
    low_out[...] = low_in[...]
    high_out[...] = high_in[...]


def halves(low_of, high_of):
    count, half = low_of.shape[0], low_of.shape[0] // 2
    block = (1,) + low_of.shape[1:]
    return pl.pallas_call(
        halves_body,
        grid=(half,),
        in_specs=[
            pl.BlockSpec(block, lambda i: (i, 0, 0)),
            pl.BlockSpec(block, lambda i: (half + i, 0, 0)),
        ],
        out_specs=[pl.BlockSpec(block, lambda i: (i, 0, 0))] * 2,
        out_shape=[jax.ShapeDtypeStruct((half,) + low_of.shape[1:], low_of.dtype)] * 2,
        compiler_params=pltpu.CompilerParams(vmem_limit_bytes=16 << 20),
        cost_estimate=pl.CostEstimate(flops=1000, bytes_accessed=1000, transcendentals=0),
        name="halves",
    )(low_of, high_of)


class Net:
    def __init__(self, n):
        self.n = n
        self.bits = n.bit_length() - 1
        chip = self.bits - 1
        sizes = [(chip + 2 - i) // 3 for i in range(3)]
        groups, top = [], self.bits - 1
        for size in sizes:
            groups.append(tuple(range(top, top - size, -1)))
            top -= size
        self.outer, self.middle, self.near = groups
        self.core = (0,)

    def masks(self, group):
        found = []
        for pick in range(1, 1 << len(group)):
            mask = 0
            for place, bit in enumerate(group):
                if pick >> place & 1:
                    mask |= 1 << bit
            found.append(mask)
        return found

    def swap(self, array, mask):
        return lax.ppermute(array, "fsdp", [(i, i ^ mask) for i in range(self.n)])

    def gather_far(self, shard):
        return [shard] + [self.swap(shard, mask) for mask in self.masks(self.outer)]

    def stacked(self, parts, me):
        low = self.bits - len(self.outer)
        masks = [mask >> low for mask in [0] + self.masks(self.outer)]
        count, shape = len(parts), parts[0].shape

        def body(me_ref, *refs):
            for mask, ref in zip(masks, refs):
                refs[-1][me_ref[0] >> low ^ mask] = ref[...]

        whole = pl.BlockSpec(shape, lambda i: (0, 0))
        return pl.pallas_call(
            body,
            grid=(1,),
            in_specs=[pl.BlockSpec(memory_space=pltpu.SMEM)] + [whole] * count,
            out_specs=pl.BlockSpec((count,) + shape, lambda i: (0, 0, 0)),
            out_shape=jax.ShapeDtypeStruct((count,) + shape, parts[0].dtype),
            compiler_params=pltpu.CompilerParams(vmem_limit_bytes=16 << 20),
            cost_estimate=pl.CostEstimate(flops=1000, bytes_accessed=1000, transcendentals=0),
            name="stacked",
        )(me.reshape(1), *parts)

    def gather_near(self, own):
        return [
            [(mask, self.swap(own, mask)) for mask in self.masks(group)]
            for group in (self.near, self.middle)
        ]

    def gather_corner(self, own, near):
        half = own.shape[0] // 2
        pieces, corners, sent = [(0, 0, own)], [], []
        for group in near:
            pieces += [(0, mask, array) for mask, array in group]
        for mask_x, array_x in near[0]:
            for mask_y, array_y in near[1]:
                low, high = halves(array_y, array_x)
                sent += [low, high]
                corners.append((0, mask_x ^ mask_y, self.swap(low, mask_x)))
                corners.append((half, mask_x ^ mask_y, self.swap(high, mask_y)))
        return pieces, corners, sent

    def gather_core(self, pieces):
        return pieces + [(first, mask ^ 1, self.swap(array, 1)) for first, mask, array in pieces]

    def inner_masks(self):
        near, middle = self.masks(self.near), self.masks(self.middle)
        return near + middle + [x | y for x in near for y in middle]

    def gather_round(self, sources, array, masks):
        array = jnp.concatenate([array] + [self.swap(array, mask) for mask in masks])
        return [source ^ mask for mask in [0] + masks for source in sources], array

    def take(self, term, bits, mask, present, me):
        present = list(present)
        for bit in bits:
            place = present.index(bit)
            low = 1 << (len(present) - 1 - place)
            value = (me >> bit & 1) ^ (mask >> bit & 1)
            rest = term.shape[1:]
            term = term.reshape((1 << place, 2, low) + rest)
            term = lax.dynamic_index_in_dim(term, value, 1, keepdims=False)
            term = term.reshape((low << place,) + rest)
            present.remove(bit)
        return term

    def scatter_core(self, halves):
        keep, send = halves
        return [keep, self.swap(send, 1)], list(range(self.bits - 1, 0, -1))

    def added(self, parts, dtype):
        parts = [part.astype(F32) for part in parts]
        return sum(parts[1:], parts[0]).astype(dtype)

    def scatter_step(self, state, group, me):
        terms, present = state
        sent = []
        for mask in self.masks(group):
            parts = [self.take(term, group, mask, present, me) for term in terms]
            sent.append(self.added(parts, terms[0].dtype))
        received = [self.swap(part, mask) for part, mask in zip(sent, self.masks(group))]
        terms = [self.take(term, group, 0, present, me) for term in terms] + received
        return (terms, [bit for bit in present if bit not in group]), sent

    def scatter_corner(self, state, me):
        terms, present = state
        left = [bit for bit in present if bit not in self.near]
        found, sent = [], []
        for mask_x in self.masks(self.near):
            row = [self.take(term, self.near, mask_x, present, me) for term in terms]
            for mask_y in self.masks(self.middle):
                parts = [self.take(term, self.middle, mask_y, left, me) for term in row]
                half = parts[0].shape[0] // 2
                low = self.added([part[:half] for part in parts], terms[0].dtype)
                high = self.added([part[half:] for part in parts], terms[0].dtype)
                sent += [low, high]
                found.append((mask_x, mask_y, self.swap(low, mask_x), self.swap(high, mask_y)))
        return found, sent

    def scatter_near(self, state, corner, me):
        terms, present = state
        left = [bit for bit in present if bit not in self.near]
        mine, received, sent = [self.take(t, self.near, 0, present, me) for t in terms], [], []
        for mask_x in self.masks(self.near):
            row = [self.take(term, self.near, mask_x, present, me) for term in terms]
            parts = [self.take(term, self.middle, 0, left, me) for term in row]
            for mask, _, _, high in corner:
                if mask == mask_x:
                    parts.append(jnp.concatenate([jnp.zeros_like(high), high]))
            sent.append((self.added(parts, terms[0].dtype), mask_x))
        for mask_y in self.masks(self.middle):
            parts = [self.take(term, self.middle, mask_y, left, me) for term in mine]
            for _, mask, low, _ in corner:
                if mask == mask_y:
                    parts.append(jnp.concatenate([low, jnp.zeros_like(low)]))
            sent.append((self.added(parts, terms[0].dtype), mask_y))
        received = [self.swap(part, mask) for part, mask in sent]
        terms = [self.take(term, self.middle, 0, left, me) for term in mine] + received
        left = [bit for bit in left if bit not in self.middle]
        return (terms, left), [part for part, _ in sent]

    def scatter_far(self, state, me):
        return self.scatter_step(state, self.outer, me)

    def scatter_end(self, state):
        return self.added(state[0], F32)[0]

    def scatter(self, halves, order, me):
        state = self.scatter_core(halves)
        for group in order:
            state, _ = self.scatter_step(state, group, me)
        return self.scatter_end(state)

    def scatter_whole(self, whole, order, me):
        present = list(range(self.bits - 1, -1, -1))
        halves = [self.take(whole, self.core, mask, present, me) for mask in (0, 1)]
        return self.scatter(halves, order, me)


def after(values, others):
    leaves, tree = jax.tree.flatten(values)
    arrays = [leaf for leaf in leaves if not isinstance(leaf, int)]
    others = [leaf for leaf in jax.tree.leaves(others) if not isinstance(leaf, int)]
    tied = iter(lax.optimization_barrier(tuple(arrays + others)))
    return jax.tree.unflatten(
        tree, [leaf if isinstance(leaf, int) else next(tied) for leaf in leaves]
    )


class Weights:
    def __init__(self, net, me, wanted):
        self.arrays, self.plans, self.shapes = [], [], []
        seen = {}
        outer = 1 << len(net.outer)
        low = net.n // outer
        self.low = low
        for pieces, places, rows in wanted:
            places = (places,) if isinstance(places, int) else tuple(places)
            columns = pieces[0][2].shape[-1]
            plan = []
            if rows % 16:
                blocks = [
                    jnp.concatenate([array[:, place : place + rows] for _, _, array in pieces])
                    for place in places
                ]
                blocks = jnp.concatenate(blocks, axis=2)
                order = [
                    (first + j) * low + (me % low ^ mask)
                    for first, mask, array in pieces
                    for j in range(array.shape[0])
                ]
                spot = jnp.zeros((net.n,), jnp.int32).at[jnp.stack(order)].set(jnp.arange(net.n))
                whole = blocks[spot].reshape(outer, low * rows // 16, 16, len(places) * columns)
                plan.append((len(self.arrays), None, None, None))
                self.arrays.append(whole)
                self.shapes.append(whole.shape)
            else:
                for first, mask, array in pieces:
                    if id(array) not in seen:
                        seen[id(array)] = len(self.arrays)
                        self.arrays.append(array)
                    for k, place in enumerate(places):
                        own = (slice(None), pl.ds(place, rows))
                        aim = (pl.ds(first, array.shape[0]), pl.ds(k * columns, columns))
                        plan.append((seen[id(array)], own, mask, aim))
                self.shapes.append((outer, low, rows, len(places) * columns))
            self.plans.append(plan)
        self.slots = max(len(plan) for plan in self.plans)

    def scratch(self):
        return [pltpu.VMEM(shape, BF16) for shape in self.shapes] + [
            pltpu.SemaphoreType.DMA((len(self.plans), self.slots))
        ]

    def copies(self, w, me, array_refs, held_ref, sems):
        found = []
        for slot, (array, own, mask, aim) in enumerate(self.plans[w]):
            if own is None:
                pair = (array_refs[array], held_ref)
            else:
                spot = me % self.low ^ mask
                pair = (array_refs[array].at[own], held_ref.at[aim[0], spot, :, aim[1]])
            found.append(pltpu.make_async_copy(*pair, sems.at[w, slot]))
        return found

    def start(self, w, *refs):
        for copy in self.copies(w, *refs):
            copy.start()

    def wait(self, w, *refs):
        for copy in self.copies(w, *refs):
            copy.wait()


def flat(held):
    return held.reshape(-1, held.shape[-1])


SMEM_SPEC = pl.BlockSpec(memory_space=pltpu.SMEM)
ANY_SPEC = pl.BlockSpec(memory_space=pltpu.HBM)


def full_spec(shape):
    return pl.BlockSpec(shape, lambda *_: (0,) * len(shape))


def tile_spec(tile, columns):
    return pl.BlockSpec((tile, columns), lambda i: (i, 0))


def call(body, name, grid, ins, outs, scratch, us, bases=()):
    count = len(ins)

    def run(*refs):
        body(*refs[:count], *refs[count + len(bases) :])

    return pl.pallas_call(
        run,
        grid=grid,
        in_specs=[spec for _, spec in ins] + [ANY_SPEC] * len(bases),
        out_specs=[spec for _, _, spec in outs],
        out_shape=[jax.ShapeDtypeStruct(shape, dtype) for shape, dtype, _ in outs],
        scratch_shapes=scratch,
        input_output_aliases={count + i: i for i in range(len(bases))},
        compiler_params=pltpu.CompilerParams(
            vmem_limit_bytes=60 << 20,
            dimension_semantics=("arbitrary",) * len(grid),
        ),
        cost_estimate=pl.CostEstimate(
            flops=int(us * 2e10), bytes_accessed=int(us * 5e7), transcendentals=0
        ),
        name=name,
    )(*[array for array, _ in ins], *bases)


def sum_body(groups, me_ref, *refs):
    step = pl.program_id(0)
    outs = refs[len(refs) - len(groups) :]
    for out_ref, addends in zip(outs, groups):
        total = None
        for place, (low, high) in addends:
            part = refs[place][...].astype(F32)
            if low is not None:
                part = jnp.where((step >= low) & (step < high), part, 0.0)
            total = part if total is None else total + part
        out_ref[...] = total.astype(out_ref.dtype)


def sum_call(me, name, grid, ins, groups, outs, body=None, us=0.01):
    grid_spec = pltpu.PrefetchScalarGridSpec(
        num_scalar_prefetch=1,
        grid=(grid,),
        in_specs=[
            pl.BlockSpec(block, lambda i, me_ref, place=place: place(i, me_ref[0]))
            for _, block, place in ins
        ],
        out_specs=[
            pl.BlockSpec(block, lambda i, me_ref, place=place: place(i, me_ref[0]))
            for _, _, block, place in outs
        ],
    )
    return pl.pallas_call(
        body or functools.partial(sum_body, groups),
        grid_spec=grid_spec,
        out_shape=[jax.ShapeDtypeStruct(shape, dtype) for shape, dtype, _, _ in outs],
        compiler_params=pltpu.CompilerParams(
            vmem_limit_bytes=60 << 20, dimension_semantics=("arbitrary",)
        ),
        cost_estimate=pl.CostEstimate(flops=int(us * 2e10), bytes_accessed=int(us * 5e7), transcendentals=0),
        name=name,
    )(me.reshape(1), *[array for array, _, _ in ins])


class Reduction:
    def __init__(self, net, me, keep, send):
        self.net, self.me = net, me
        self.terms = [keep, net.swap(send, 1)]
        self.rows, self.columns = keep.shape[1:]
        self.plain = len(net.near) == 1 and len(net.middle) == 1 and self.rows % 8 == 0
        self.state = None

    def block(self):
        return (1, self.rows, self.columns)

    def parted(self, term):
        return term.reshape(-1, 4, self.rows, self.columns)

    def blocks(self, far):
        shape = (far, self.rows, self.columns)
        return (far, None, self.rows, self.columns), shape

    def hold(self, others):
        if self.plain:
            self.terms = after(self.terms, others)
        else:
            state = self.state or (self.terms, list(range(self.net.bits - 1, 0, -1)))
            self.state = held(state, others)
            if getattr(self, "corner_pieces", None) is not None:
                self.corner_pieces = after(self.corner_pieces, others)
        return self

    def corner(self):
        net = self.net
        if not self.plain:
            state = self.state or (self.terms, list(range(net.bits - 1, 0, -1)))
            self.state = state
            self.corner_pieces, sent = net.scatter_corner(state, self.me)
            return sent
        far = 1 << (len(net.outer) - 1)

        def place(shift):
            return lambda i, me: ((i + shift) * 4 + (me >> 1 & 3 ^ 3), 0, 0)

        ins = [(term, self.block(), place(shift)) for shift in (0, far) for term in self.terms]
        out = ((far, self.rows, self.columns), BF16, self.block(), lambda i, me: (i, 0, 0))
        always = (None, None)
        groups = [[(0, always), (1, always)], [(2, always), (3, always)]]
        low, high = sum_call(self.me, "corner_sum", far, ins, groups, [out, out])
        self.terms += [net.swap(low, 1 << net.near[0]), net.swap(high, 1 << net.middle[0])]
        return [low, high]

    def near(self):
        net = self.net
        if not self.plain:
            self.state, sent = net.scatter_near(self.state, self.corner_pieces, self.me)
            self.corner_pieces = None
            return sent
        far = 1 << (len(net.outer) - 1)
        keep, other, low, high = self.terms

        def place(flip):
            return lambda i, me: (i, me >> 1 & 3 ^ flip, 0, 0)

        block, shape = self.blocks(far)
        pair = (self.parted(keep), self.parted(other))
        ins = [(term, block, place(flip)) for flip in (1, 2) for term in pair]
        ins += [(term, shape, lambda i, me: (0, 0, 0)) for term in (high, low)]
        always = (None, None)
        groups = [
            [(0, always), (1, always), (4, (1, 2))],
            [(2, always), (3, always), (5, (0, 1))],
        ]
        whole = (2 * far, self.rows, self.columns)
        out = (whole, BF16, shape, lambda i, me: (i, 0, 0))
        sent = sum_call(self.me, "near_sum", 2, ins, groups, [out, out])
        received = [
            net.swap(part, 1 << group[0]) for part, group in zip(sent, (net.near, net.middle))
        ]
        self.terms = [keep, other] + received
        return sent

    def sources(self, flip, step_block):
        keep, other, row, column = self.terms[:4]
        found = []
        for term in (keep, other):
            found.append((term, lambda me: ((me >> 3 ^ flip) * 4 + (me >> 1 & 3))))
        for term in (row, column):
            found.append((term, lambda me: (me >> 3 ^ flip)))
        return [
            (term, step_block[0], lambda i, me, at=at: step_block[1](i, at(me)))
            for term, at in found
        ]

    def far(self):
        net = self.net
        if not self.plain:
            self.state, sent = net.scatter_step(self.state, net.outer, self.me)
            return sent
        parts = 2 if self.rows % 32 == 0 else 1
        step_block = ((1, self.rows // parts, self.columns), lambda i, at: (at, i, 0))
        masks = net.masks(net.outer)
        ins, groups = [], []
        for mask in masks:
            groups.append([(len(ins) + j, (None, None)) for j in range(4)])
            ins += self.sources(mask >> 3, step_block)
        out = ((1, self.rows, self.columns), BF16, step_block[0], lambda i, me: (0, i, 0))
        sent = sum_call(self.me, "far_sum", parts, ins, groups, [out] * len(masks))
        self.terms += [net.swap(part, mask) for part, mask in zip(sent, masks)]
        return sent

    def received(self):
        return self.terms[-1] if self.plain else self.state[0][-1]

    def end(self, lots, unit):
        if not self.plain:
            total = self.net.scatter_end(self.state)
            results, start = [], 0
            for count in lots:
                blocks = [
                    total[(start + j) * unit : (start + j + 1) * unit] for j in range(count)
                ]
                results.append(jnp.concatenate(blocks, axis=1))
                start += count
            return results
        step_block = ((1, unit, self.columns), lambda i, at: (at, i, 0))
        ins = self.sources(0, step_block)
        ins += [(term, step_block[0], lambda i, me: (0, i, 0)) for term in self.terms[4:]]
        outs, bounds, start = [], [], 0
        for count in lots:

            def place(i, me, start=start, count=count):
                return (0, jnp.clip(i - start, 0, count - 1))

            outs.append(((unit, count * self.columns), F32, (unit, self.columns), place))
            bounds.append((start, start + count))
            start += count

        def body(me_ref, *refs):
            step, addends = pl.program_id(0), refs[: len(ins)]
            total = addends[0][0].astype(F32)
            for ref in addends[1:]:
                total = total + ref[0].astype(F32)
            for out_ref, (low, high) in zip(refs[len(ins) :], bounds):

                @pl.when((step >= low) & (step < high))
                def _():
                    out_ref[...] = total

        return sum_call(self.me, "end_sum", start, ins, None, outs, body, 4)


def pack_body(sizes, me_ref, times_ref, small_ref, *refs):
    shards, out_ref = refs[:-1], refs[-1]
    start = 0
    for ref in shards:
        out_ref[start : start + ref.shape[0]] = ref[...]
        start += ref.shape[0]
    me, width = me_ref[0], out_ref.shape[1]

    small = small_ref[...]
    step, inner_size, steps = sizes

    def spread(first, count, offset):
        spots = lax.broadcasted_iota(jnp.int32, (small.shape[1], width), 0) - first
        lanes = lax.broadcasted_iota(jnp.int32, (small.shape[1], width), 1)
        hits = (spots >= 0) & (spots < count) & (lanes == spots + offset)
        return matmul(small, jnp.where(hits, 1.0, 0.0).astype(BF16))

    vectors = spread(0, step, me * step)
    place = me * inner_size
    inner = spread(step, inner_size, lax.rem(place, width))
    row = lax.broadcasted_iota(jnp.int32, inner.shape, 0)
    inner = jnp.where(row == place // width, inner, 0.0)
    lane = lax.broadcasted_iota(jnp.int32, inner.shape, 1)
    for j in range(steps):
        time = times_ref[j]
        digit = jnp.where(row == 4, time >> 6, jnp.where(row == 5, time & 63, 0))
        inner += jnp.where(lane == me * steps + j, digit, 0).astype(F32)
    out_ref[start:] = jnp.concatenate([vectors, inner]).astype(BF16)


def pack(me, shards, vectors, inner, times):
    step, width = shards[0].shape
    sizes = (step, inner.shape[0], times.shape[0])
    small = 0.0
    for line, vector in enumerate(vectors):
        small += jnp.pad(vector.astype(F32)[None], ((line, 7 - line), (0, 256 - step)))
    rest = 256 - sizes[1] - step
    small += jnp.pad(inner.astype(F32)[None], ((0, 0), (step, rest)))
    small = small.astype(BF16)
    rows = len(shards) * step + 16
    return call(
        functools.partial(pack_body, sizes),
        "pack",
        (1,),
        [(me.reshape(1), SMEM_SPEC), (times, SMEM_SPEC)]
        + [(array, full_spec(array.shape)) for array in (small, *shards)],
        [((rows, width), BF16, full_spec((rows, width)))],
        [],
        1,
    )[0]


def project_body(weights, tile, row_length, me_ref, *refs):
    count = len(weights.arrays)
    arrays, refs = refs[:count], refs[count:]
    feats_ref, x_ref = refs[:2]
    temb_ref, lines_ref, low_ref, q_ref, k_ref, v_ref = refs[2:8]
    tw, qw, kw, vw, lw, sems = refs[8:14]
    me, step = me_ref[0], pl.program_id(0)

    @pl.when(step == 0)
    def _():
        for w, held in enumerate((tw, qw, kw, vw, lw)):
            weights.start(w, me, arrays, held, sems)
        weights.wait(0, me, arrays, tw, sems)
        temb_ref[...] = matmul(feats_ref[...], flat(tw[...]))
        weights.wait(4, me, arrays, lw, sems)
        lines_ref[...] = jnp.sum(lw[...].astype(F32), axis=(0, 1))
        for w, held in ((1, qw), (2, kw), (3, vw)):
            weights.wait(w, me, arrays, held, sems)

    row = step * tile // row_length
    low = (x_ref[...].astype(F32) + temb_ref[pl.ds(row, 1), :]).astype(BF16)
    low_ref[...] = low
    q_ref[...] = (matmul(low, flat(qw[...])) + lines_ref[0:1]).astype(BF16)
    k_ref[...] = matmul(low, flat(kw[...])).astype(BF16)
    v_ref[...] = (matmul(low, flat(vw[...])) + lines_ref[1:2]).astype(BF16)


def project(net, me, flow, feats, x, row_length):
    tokens, width = x.shape
    tile = min(256, row_length)
    r = width // net.n
    weights = Weights(net, me, [(flow, w * r, r) for w in range(4)] + [(flow, 4 * r, 16)])
    ins = (
        [(me.reshape(1), SMEM_SPEC)]
        + [(array, ANY_SPEC) for array in weights.arrays]
        + [(feats, full_spec(feats.shape)), (x, tile_spec(tile, width))]
    )
    outs = [(feats.shape, F32, full_spec(feats.shape))]
    outs += [((16, width), F32, full_spec((16, width)))]
    outs += [((tokens, width), BF16, tile_spec(tile, width))] * 4
    return call(
        functools.partial(project_body, weights, tile, row_length),
        "project",
        (tokens // tile,),
        ins,
        outs,
        weights.scratch(),
        14,
    )


def same_document(seg_ref, bias_ref, block):
    @pl.when(block == 0)
    def _():
        row = seg_ref[0].astype(F32)
        column = jnp.transpose(jnp.broadcast_to(row, (128, row.shape[1])))[:, :1]
        bias_ref[...] = jnp.where(column == row, 0.0, -1e30)


def own_lanes(shape, head, head_dim):
    lanes = lax.broadcasted_iota(jnp.int32, shape, len(shape) - 1)
    return (lanes // head_dim) == head


def attend_body(head_dim, seg_ref, q_ref, k_ref, v_ref, out_ref, log_ref, bias_ref):
    same_document(seg_ref, bias_ref, pl.program_id(1))
    queries, key_rows, values = q_ref[...], k_ref[...], v_ref[...]
    scale = 1.0 / math.sqrt(head_dim)
    per = queries.shape[1] // head_dim
    total = None
    for head in range(per):
        mine = own_lanes(queries.shape, head, head_dim)
        keys_own = jnp.where(mine, key_rows * BF16(scale), BF16(0))
        scores = matmul_right(keys_own, queries) + bias_ref[...]
        top = jnp.max(scores, axis=0, keepdims=True)
        raised = jnp.exp(scores - top)
        amount = jnp.sum(raised, axis=0, keepdims=True)
        log_ref[0, 0, pl.ds(head, 1), :] = top + jnp.log(amount)
        soft_low = (raised * (1.0 / amount)).astype(BF16)
        context = matmul_left(soft_low, values)
        total = context if total is None else jnp.where(mine, context, total)
    out_ref[...] = total.astype(BF16)


def attend_back_body(
    head_dim, seg_ref, q_ref, k_ref, v_ref, log_ref, g_ref, gq_ref, gk_ref, gv_ref, sums_ref, rows_ref, bias_ref
):
    same_document(seg_ref, bias_ref, pl.program_id(1))
    queries, key_rows, values, grads = q_ref[...], k_ref[...], v_ref[...], g_ref[...]
    scale = 1.0 / math.sqrt(head_dim)
    per = queries.shape[1] // head_dim
    totals = None
    for head in range(per):
        mine = own_lanes(queries.shape, head, head_dim)
        keys_own = jnp.where(mine, key_rows * BF16(scale), BF16(0))
        scores = matmul_right(keys_own, queries) + bias_ref[...]
        soft = jnp.exp(scores - log_ref[0, 0, pl.ds(head, 1), :])
        grad_soft = matmul_right(jnp.where(mine, values, BF16(0)), grads)
        inner_sum = jnp.sum(soft * grad_soft, axis=0, keepdims=True)
        grad_scores = (soft * (grad_soft - inner_sum)).astype(BF16)
        parts = (
            matmul_left(grad_scores, key_rows),
            matmul(grad_scores, queries),
            matmul(soft.astype(BF16), grads),
        )
        if totals is None:
            totals = parts
        else:
            totals = tuple(jnp.where(mine, part, total) for part, total in zip(parts, totals))
    gq = (totals[0] * scale).astype(BF16)
    gv = totals[2].astype(BF16)
    gq_ref[...] = gq
    gk = (totals[1] * scale).astype(BF16)
    gk_ref[...] = gk
    gv_ref[...] = gv
    sums = [jnp.sum(part.astype(F32), axis=0, keepdims=True) for part in (gq, gk, gv)]
    zero = jnp.zeros_like(sums[0])
    sums_ref[...] = jnp.concatenate([sums[0], sums[2]] + [zero] * 6)
    rows_ref[...] = jnp.concatenate(sums + [zero] * 5)


def attention_args(segments, start, lanes, head_dim):
    row_length, per = segments.shape[1], lanes // head_dim
    segs = pl.BlockSpec((1, 1, row_length), lambda i, j: (start + i, 0, 0))
    block = pl.BlockSpec((row_length, lanes), lambda i, j: (start + i, j))
    log_spec = pl.BlockSpec((1, 1, per, row_length), lambda i, j: (start + i, j, 0, 0))
    return [(segments[:, None, :], segs)], block, log_spec


def attend(queries, key_rows, values, segments, lanes=256):
    rows, row_length = segments.shape
    tokens, width = queries.shape
    head_dim = width // H
    blocks, per = width // lanes, lanes // head_dim
    masks, block, log_spec = attention_args(segments, 0, lanes, head_dim)
    return call(
        functools.partial(attend_body, head_dim),
        "attend",
        (rows, blocks),
        masks + [(array, block) for array in (queries, key_rows, values)],
        [
            ((tokens, width), BF16, block),
            ((rows, blocks, per, row_length), F32, log_spec),
        ],
        [pltpu.VMEM((row_length, row_length), F32)],
        24,
    )


def attend_back(queries, key_rows, values, segments, log_total, grad_context, row, bases=(), lanes=256):
    rows, row_length = segments.shape
    tokens, width = queries.shape
    head_dim = width // H
    masks, block, log_spec = attention_args(segments, row, lanes, head_dim)
    return call(
        functools.partial(attend_back_body, head_dim),
        "attend_back",
        (1, width // lanes),
        masks
        + [(array, block) for array in (queries, key_rows, values)]
        + [(log_total, log_spec), (grad_context, block)],
        [((tokens, width), BF16, block)] * 3
        + [((8, width), F32, pl.BlockSpec((8, lanes), lambda i, j: (0, j)))] * 2,
        [pltpu.VMEM((row_length, row_length), F32)],
        19,
        bases,
    )


def add_to(ref, value, step):
    part = jnp.sum(value, axis=0, keepdims=True)

    @pl.when(step == 0)
    def _():
        ref[...] = part

    @pl.when(step != 0)
    def _():
        ref[...] += part


def add_lines(ref, values, step):
    zero = jnp.zeros((1, ref.shape[1]), F32)
    sums = {line: jnp.sum(value, axis=0, keepdims=True) for line, value in values.items()}
    part = jnp.concatenate([sums.get(line, zero) for line in range(ref.shape[0])])

    @pl.when(step == 0)
    def _():
        ref[...] = part

    @pl.when(step != 0)
    def _():
        ref[...] += part


def ffn_in_body(weights, tile, row_length, chunk, me_ref, *refs):
    count = len(weights.arrays)
    arrays, refs = refs[:count], refs[count:]
    context_ref, x_ref, temb_ref, lines_ref = refs[:4]
    first_low_ref, normed_ref, spread_ref, active_ref, slope_ref = refs[4:9]
    ow, iw, sems = refs[9:12]
    me, step = me_ref[0], pl.program_id(0)

    @pl.when(step == 0)
    def _():
        for w, held in enumerate((ow, iw)):
            weights.start(w, me, arrays, held, sems)
        weights.wait(0, me, arrays, ow, sems)

    row = step * tile // row_length
    stream = x_ref[...].astype(F32) + temb_ref[pl.ds(row, 1), :]
    mixed = stream + (matmul(context_ref[...], flat(ow[...])) + lines_ref[2:3])
    normed, spread = normalize(mixed)
    normed_ref[...] = normed
    spread_ref[...] = spread
    first = normed * lines_ref[4:5] + lines_ref[5:6]
    low = first.astype(BF16)
    first_low_ref[...] = low

    @pl.when(step == 0)
    def _():
        weights.wait(1, me, arrays, iw, sems)

    width, hidden = ow.shape[3], iw.shape[3]

    def inner(start):
        pre = matmul(low, flat(iw[:, :, :, start : start + chunk]))
        line, place = 8 + start // width, start % width
        return pre + lines_ref[line : line + 1, place : place + chunk]

    later = inner(0)
    for start in range(0, hidden, chunk):
        pre = later
        if start + chunk < hidden:
            later = inner(start + chunk)
        columns = slice(start, start + chunk)
        normal_cdf = 0.5 * (1.0 + lax.erf(pre * INV_ROOT_TWO))
        normal_pdf = jnp.exp(-0.5 * pre * pre) * INV_ROOT_TAU
        active_ref[:, columns] = (pre * normal_cdf).astype(BF16)
        slope_ref[:, columns] = (normal_cdf + pre * normal_pdf).astype(BF16)


def ffn_in(net, me, flow, context, x, temb, lines, hidden, row_length, tile=256, chunk=512):
    tokens, width = x.shape
    r = width // net.n
    blocks = range(r, r + hidden // width * r, r)
    weights = Weights(net, me, [(flow, 0, r), (flow, blocks, r)])
    tile = min(tile, row_length)
    tiled, wide, thin = (tile_spec(tile, columns) for columns in (width, hidden, 1))
    ins = (
        [(me.reshape(1), SMEM_SPEC)]
        + [(array, ANY_SPEC) for array in weights.arrays]
        + [(context, tiled), (x, tiled)]
        + [(array, full_spec(array.shape)) for array in (temb, lines)]
    )
    outs = [
        ((tokens, width), BF16, tiled),
        ((tokens, width), F32, tiled),
        ((tokens, 1), F32, thin),
        ((tokens, hidden), BF16, wide),
        ((tokens, hidden), BF16, wide),
    ]
    return call(
        functools.partial(ffn_in_body, weights, tile, row_length, chunk),
        "ffn_in",
        (tokens // tile,),
        ins,
        outs,
        weights.scratch(),
        30,
    )


def ffn_out_body(weights, me_ref, *refs):
    count = len(weights.arrays)
    arrays, refs = refs[:count], refs[count:]
    active_ref, normed_ref, cot_ref, lines_ref = refs[:4]
    out_ref, gs_ref, gs_low_ref, sums_ref = refs[4:8]
    uw, sems = refs[8:10]
    me, step = me_ref[0], pl.program_id(0)

    @pl.when(step == 0)
    def _():
        weights.start(0, me, arrays, uw, sems)
        weights.wait(0, me, arrays, uw, sems)

    first = normed_ref[...] * lines_ref[4:5] + lines_ref[5:6]
    second = first + (matmul(active_ref[...], flat(uw[...])) + lines_ref[3:4])
    normed_second, spread_second = normalize(second)
    out_ref[...] = (normed_second * lines_ref[6:7] + lines_ref[7:8]).astype(BF16)
    grad_out = cot_ref[...].astype(F32)
    grad_second = norm_back(grad_out * lines_ref[6:7], normed_second, spread_second)
    gs_ref[...] = grad_second
    low = grad_second.astype(BF16)
    gs_low_ref[...] = low
    add_lines(sums_ref, {3: low.astype(F32), 6: grad_out * normed_second, 7: grad_out}, step)


def ffn_out(net, me, flow, active, normed, cotangent, vectors, tile=256):
    tokens, width = normed.shape
    hidden = active.shape[1]
    weights = Weights(net, me, [(flow, 0, hidden // net.n)])
    tiled, wide = tile_spec(tile, width), tile_spec(tile, hidden)
    ins = (
        [(me.reshape(1), SMEM_SPEC)]
        + [(array, ANY_SPEC) for array in weights.arrays]
        + [(active, wide), (normed, tiled), (cotangent, tiled)]
        + [(vector, full_spec(vector.shape)) for vector in vectors]
    )
    outs = [
        ((tokens, width), BF16, tiled),
        ((tokens, width), F32, tiled),
        ((tokens, width), BF16, tiled),
        ((8, width), F32, full_spec((8, width))),
    ]
    return call(
        functools.partial(ffn_out_body, weights),
        "ffn_out",
        (tokens // tile,),
        ins,
        outs,
        weights.scratch(),
        20,
    )


def ffn_back_body(weights, tile, row_length, me_ref, *refs):
    count = len(weights.arrays)
    arrays, refs = refs[:count], refs[count:]
    (gs_ref, gs_low_ref, slope_ref, normed_ref, spread_ref, lines_ref) = refs[:6]
    (gi_ref, gm_ref, gm_low_ref, gc_ref, ibg_ref, sums_ref, rows_ref) = refs[6:13]
    uw, ow, iw, sems, held_ref = refs[13:18]
    me, step = me_ref[0], pl.program_id(0)
    last = pl.num_programs(0) - 1

    @pl.when(step == 0)
    def _():
        for w, held in ((0, uw), (2, iw), (1, ow)):
            weights.start(w, me, arrays, held, sems)
        sums_ref[...] = jnp.zeros_like(sums_ref)
        rows_ref[...] = jnp.zeros_like(rows_ref)
        ibg_ref[...] = jnp.zeros_like(ibg_ref)
        weights.wait(0, me, arrays, uw, sems)

    def through_hidden(first_time=False):
        part = gi_ref.shape[1] // uw.shape[0]
        for z in range(uw.shape[0]):
            columns = slice(z * part, (z + 1) * part)
            grad_active = matmul_right(gs_low_ref[...], flat(uw[z]))
            gi = (grad_active * slope_ref[:, columns].astype(F32)).astype(BF16)
            gi_ref[:, columns] = gi
            ibg_ref[:, columns] += jnp.sum(gi.astype(F32), axis=0, keepdims=True)
        if first_time:
            weights.wait(2, me, arrays, iw, sems)
        return gs_ref[...] + matmul_right(gi_ref[...], flat(iw[...]))

    def through_norm(grad_first):
        normed = normed_ref[...]
        grad_mixed = norm_back(grad_first * lines_ref[4:5], normed, spread_ref[...])
        gm_ref[...] = grad_mixed
        low = grad_mixed.astype(BF16)
        gm_low_ref[...] = low
        row = pl.ds((step - 1) * tile // row_length, 1)
        rows_ref[row, :] += jnp.sum(grad_mixed, axis=0, keepdims=True)
        values = {2: low.astype(F32), 4: grad_first * normed, 5: grad_first}
        for line, value in values.items():
            sums_ref[line : line + 1] += jnp.sum(value, axis=0, keepdims=True)
        gc_ref[...] = matmul_right(low, flat(ow[...])).astype(BF16)

    @pl.when(step == 0)
    def _():
        held_ref[...] = through_hidden(True)
        weights.wait(1, me, arrays, ow, sems)

    @pl.when((step > 0) & (step < last))
    def _():
        grad_first = held_ref[...]
        later = through_hidden()
        through_norm(grad_first)
        held_ref[...] = later

    @pl.when(step == last)
    def _():
        through_norm(held_ref[...])


def ffn_back(net, me, flow_u, flow_io, gs, gs_low, slope, normed, spread, lines, row_length, tile=256):
    tokens, width = gs.shape
    hidden = slope.shape[1]
    r = width // net.n
    weights = Weights(
        net,
        me,
        [
            (flow_u, 0, hidden // net.n),
            (flow_io, 0, r),
            (flow_io, range(r, r + hidden // width * r, r), r),
        ],
    )
    tile = min(tile, row_length)
    steps = tokens // tile

    def ahead(columns):
        return pl.BlockSpec((tile, columns), lambda i: (jnp.minimum(i, steps - 1), 0))

    def behind(columns):
        return pl.BlockSpec((tile, columns), lambda i: (jnp.maximum(i - 1, 0), 0))

    ins = (
        [(me.reshape(1), SMEM_SPEC)]
        + [(array, ANY_SPEC) for array in weights.arrays]
        + [(gs, ahead(width)), (gs_low, ahead(width)), (slope, ahead(hidden))]
        + [(normed, behind(width)), (spread, behind(1)), (lines, full_spec(lines.shape))]
    )
    outs = [
        ((tokens, hidden), BF16, ahead(hidden)),
        ((tokens, width), F32, behind(width)),
        ((tokens, width), BF16, behind(width)),
        ((tokens, width), BF16, behind(width)),
        ((1, hidden), F32, full_spec((1, hidden))),
        ((8, width), F32, full_spec((8, width))),
        ((8, width), F32, full_spec((8, width))),
    ]
    return call(
        functools.partial(ffn_back_body, weights, tile, row_length),
        "ffn_back",
        (steps + 1,),
        ins,
        outs,
        weights.scratch() + [pltpu.VMEM((tile, width), F32)],
        36,
    )


def deal(me_ref, total, rows, keep_ref, send_ref, kind=0):
    core = me_ref[0] & 1
    total = total.reshape(-1, 2, rows, total.shape[-1])
    low, high = total[:, 0], total[:, 1]
    place = slice(kind * rows, (kind + 1) * rows)
    keep_ref[:, place] = jnp.where(core == 0, low, high).astype(BF16)
    send_ref[:, place] = jnp.where(core == 0, high, low).astype(BF16)


def product_body(rows, me_ref, a_ref, b_ref, keep_ref, send_ref):
    deal(me_ref, matmul_left(a_ref[...], b_ref[...]), rows, keep_ref, send_ref)


def product(net, me, left, right, tile=1024):
    tokens, width = left.shape
    columns = right.shape[1]
    rows = width // net.n
    shape = (net.n // 2, rows, columns)
    block = pl.BlockSpec((tile // (2 * rows), rows, columns), lambda i: (i, 0, 0))
    return call(
        functools.partial(product_body, rows),
        "product",
        (width // tile,),
        [
            (me.reshape(1), SMEM_SPEC),
            (left, pl.BlockSpec((tokens, tile), lambda i: (0, i))),
            (right, full_spec((tokens, columns))),
        ],
        [(shape, BF16, block), (shape, BF16, block)],
        [],
        15,
    )


def inner_body(rows, me_ref, context_ref, first_ref, gm_ref, gi_ref, keep_ref, send_ref):
    total = matmul_left(first_ref[...], gi_ref[...])
    width = gm_ref.shape[1]
    deal(me_ref, matmul_left(context_ref[...], gm_ref[...]), rows, keep_ref, send_ref, 0)
    for k in range(total.shape[1] // width):
        part = total[:, k * width : (k + 1) * width]
        deal(me_ref, part, rows, keep_ref, send_ref, k + 1)


def inner_product(net, me, context, first_low, gm_low, gi, tile=256):
    tokens, width = context.shape
    hidden = gi.shape[1]
    rows = width // net.n
    kinds = 1 + hidden // width
    shape = (net.n // 2, kinds * rows, width)
    block = pl.BlockSpec((tile // (2 * rows), kinds * rows, width), lambda i: (i, 0, 0))
    left = pl.BlockSpec((tokens, tile), lambda i: (0, i))
    return call(
        functools.partial(inner_body, rows),
        "inner_product",
        (width // tile,),
        [
            (me.reshape(1), SMEM_SPEC),
            (context, left),
            (first_low, left),
            (gm_low, full_spec((tokens, width))),
            (gi, full_spec((tokens, hidden))),
        ],
        [(shape, BF16, block), (shape, BF16, block)],
        [],
        18,
    )


def triple_body(rows, me_ref, lines_ref, a_ref, q_ref, k_ref, v_ref, keep_ref, send_ref):
    for w, ref in enumerate((q_ref, k_ref, v_ref)):
        deal(me_ref, matmul_left(a_ref[...], ref[...]), rows, keep_ref, send_ref, w)
    core = me_ref[0] & 1
    low, high = lines_ref[:, 0:16], lines_ref[:, 16:32]
    place = slice(3 * rows, 3 * rows + 16)
    keep_ref[:, place] = jnp.where(core == 0, low, high).astype(BF16)
    send_ref[:, place] = jnp.where(core == 0, high, low).astype(BF16)


def triple_product(net, me, lines, left, gq, gk, gv, tile=256):
    tokens, width = left.shape
    rows = width // net.n
    shape = (net.n // 2, 3 * rows + 16, width)
    chips = tile // (2 * rows)
    block = pl.BlockSpec((chips, 3 * rows + 16, width), lambda i: (i, 0, 0))
    full = full_spec((tokens, width))
    return call(
        functools.partial(triple_body, rows),
        "triple_product",
        (width // tile,),
        [
            (me.reshape(1), SMEM_SPEC),
            (lines, pl.BlockSpec((chips, 32, width), lambda i: (i, 0, 0))),
            (left, pl.BlockSpec((tokens, tile), lambda i: (0, i))),
            (gq, full),
            (gk, full),
            (gv, full),
        ],
        [(shape, BF16, block), (shape, BF16, block)],
        [],
        13,
    )


def stream_back_body(weights, rows, me_ref, *refs):
    count = len(weights.arrays)
    arrays, refs = refs[:count], refs[count:]
    gm_ref, gq_ref, gk_ref, gv_ref = refs[:4]
    sum_refs, refs = refs[4 : 4 + rows], refs[4 + rows :]
    out_ref, outs = refs[0], refs[1:]
    qw, kw, vw, sems = outs[-4:]
    me, step = me_ref[0], pl.program_id(0)

    @pl.when(step == 0)
    def _():
        for w, held in enumerate((qw, kw, vw)):
            weights.start(w, me, arrays, held, sems)
        for w, held in enumerate((qw, kw, vw)):
            weights.wait(w, me, arrays, held, sems)
        if sum_refs:
            total = sum_refs[0][...]
            for w, held in enumerate((qw, kw, vw)):
                lines = [ref[w : w + 1] for ref in sum_refs[1:]]
                lines += [jnp.zeros_like(lines[0])] * (8 - len(lines))
                total += matmul_right(jnp.concatenate(lines).astype(BF16), flat(held[...]))
            outs[0][...] = total

    out_ref[...] = (
        gm_ref[...]
        + matmul_right(gq_ref[...], flat(qw[...]))
        + matmul_right(gk_ref[...], flat(kw[...]))
        + matmul_right(gv_ref[...], flat(vw[...]))
    )


def stream_back(net, me, flow, gm, gq, gk, gv, row, row_length, base=None, sums=(), tile=256):
    tokens, width = gm.shape
    tile = min(tile, row_length)
    r = width // net.n
    weights = Weights(net, me, [(flow, w * r, r) for w in (1, 2, 3)])
    start = row * (row_length // tile)
    tiled = pl.BlockSpec((tile, width), lambda i: (start + i, 0))
    ins = (
        [(me.reshape(1), SMEM_SPEC)]
        + [(array, ANY_SPEC) for array in weights.arrays]
        + [(array, tiled) for array in (gm, gq, gk, gv)]
        + [(array, full_spec((8, width))) for array in sums]
    )
    outs = [((tokens, width), F32, tiled)]
    if sums:
        outs.append(((8, width), F32, full_spec((8, width))))
    return call(
        functools.partial(stream_back_body, weights, len(sums)),
        "stream_back",
        (row_length // tile,),
        ins,
        outs,
        weights.scratch(),
        10,
        () if base is None else (base,),
    )


def in_order(net, me, sources, blocks):
    order = jnp.asarray(sources, jnp.int32)
    spot = jnp.zeros((net.n,), jnp.int32).at[order].set(jnp.arange(net.n, dtype=jnp.int32))
    return blocks[spot[jnp.arange(net.n) ^ me]]


def held(state, others):
    return after(state[0], others), state[1]


def stream_ends(state, unit, sizes):
    if not state.plain:
        total = state.net.scatter_end(state.state)
        found, start = [total[w * unit : (w + 1) * unit] for w in range(3)], 0
        for size in sizes:
            found.append(total[3 * unit, start : start + size])
            start += size
        return found
    rows, columns = state.rows, state.columns
    step_block = ((1, rows, columns), lambda i, at: (at, 0, 0))
    ins = state.sources(0, step_block)
    ins += [(term, step_block[0], lambda i, me: (0, 0, 0)) for term in state.terms[4:]]
    shapes = [(unit, columns)] * 3 + [(1, size) for size in sizes]
    outs = [(shape, F32, shape, lambda i, me: (0, 0)) for shape in shapes]

    def body(me_ref, *refs):
        total = refs[0][0].astype(F32)
        for ref in refs[1 : len(ins)]:
            total = total + ref[0].astype(F32)
        outs = refs[len(ins) :]
        for w in range(3):
            outs[w][...] = total[w * unit : (w + 1) * unit]
        start = 0
        for out_ref, size in zip(outs[3:], sizes):
            out_ref[...] = total[3 * unit : 3 * unit + 1, start : start + size]
            start += size

    results = sum_call(state.me, "stream_end", 1, ins, None, outs, body)
    return list(results[:3]) + [result[0] for result in results[3:]]


def on_device(
    net,
    inputs,
    timesteps,
    segments,
    cotangent,
    query_weight,
    key_weight,
    value_weight,
    output_weight,
    inner_weight,
    outer_weight,
    time_weight,
    *vectors,
):
    n = net.n
    me = lax.axis_index("fsdp").astype(jnp.int32)
    batch_count, row_count, row_length, model_width = inputs.shape
    rows = batch_count * row_count
    tokens = rows * row_length
    feats = features(timesteps.reshape(rows)).astype(BF16)
    order = (0, 1, 2, 4, 5, 6, 7, 8, 3)
    sizes = [vectors[i].shape[0] for i in order]
    r = model_width // n

    shards = (time_weight, query_weight, key_weight, value_weight)
    lines = [vectors[i] for i in order[:8]]
    far = net.gather_far(pack(me, shards, lines, vectors[3], timesteps.reshape(rows)))
    hidden = inner_weight.shape[1]
    inner_blocks = [
        inner_weight[:, start : start + model_width] for start in range(0, hidden, model_width)
    ]
    shard_io = after(jnp.concatenate([output_weight] + inner_blocks), far)
    far_io = net.gather_far(shard_io)
    far = net.stacked(far, me)
    near = net.gather_near(far)
    pieces, corners, _ = net.gather_corner(far, near)
    flow = net.gather_core(pieces)
    far_io, corners, shard_u = after((net.stacked(far_io, me), corners, outer_weight), ())
    near_io = net.gather_near(far_io)
    flow += net.gather_core(corners)
    far_u = net.gather_far(after(shard_u, flow))

    segments = segments.reshape(rows, row_length)
    x = inputs.reshape(tokens, model_width)
    feats_in = after(feats, far_io)
    temb, lines, stream_low, queries, key_rows, values = project(
        net, me, flow, feats_in, x, row_length
    )
    far_u = net.stacked(after(far_u, queries), me)
    near_u = net.gather_near(far_u)
    near_io, queries = after((near_io, queries), far_u)
    pieces, corners, sent = net.gather_corner(far_io, near_io)
    queries = after(queries, sent)
    context, log_total = attend(queries, key_rows, values, segments)
    near_u, context, pieces = after((near_u, context, pieces), ())
    flow_io = net.gather_core(pieces)
    pieces, corners_u, sent = net.gather_corner(far_u, near_u)
    context, corners = after((context, corners), sent)
    flow_io += net.gather_core(corners)
    corners = corners_u
    first_low, normed_first, spread_first, active_low, slope = ffn_in(
        net, me, flow_io, context, x, temb, lines, hidden, row_length
    )
    corners, active_low = after((corners, active_low), ())
    flow_u = net.gather_core(pieces) + net.gather_core(corners)
    (
        layer_output,
        grad_second,
        grad_second_low,
        sums_out,
    ) = ffn_out(
        net,
        me,
        flow_u,
        active_low,
        normed_first,
        cotangent.reshape(tokens, model_width),
        (lines,),
    )
    outer_halves = product(net, me, active_low, grad_second_low)
    outer_sum = Reduction(net, me, *outer_halves)
    slope = after(slope, outer_halves)
    (
        grad_inner_low,
        grad_mixed,
        grad_mixed_low,
        grad_context,
        inner_bias_grad,
        sums_back,
        mixed_rows,
    ) = ffn_back(
        net,
        me,
        flow_u,
        flow_io,
        grad_second,
        grad_second_low,
        slope,
        normed_first,
        spread_first,
        lines,
        row_length,
    )
    sent = outer_sum.hold(grad_mixed_low).corner()
    grad_mixed_low = after(grad_mixed_low, sent)
    inner_halves = inner_product(net, me, context, first_low, grad_mixed_low, grad_inner_low)
    inner_sum = Reduction(net, me, *inner_halves)
    sent = outer_sum.hold(inner_halves).near()
    grad_context = after(grad_context, (inner_halves, sent))
    back = (queries, key_rows, values, segments, log_total, grad_context)
    found, sums_rows, row_sums = None, 0.0, [mixed_rows]
    for row in range(rows):
        if row == 1:
            sent = list(inner_sum.hold(found[1]).corner())
            sent += list(outer_sum.hold((found[1], sent)).far())
            found = after(found, sent)
        found = attend_back(*back, row, found or ())
        sums_rows += found[3]
        row_sums.append(found[4])
        found = found[:3]
    grad_queries, grad_keys, grad_values = found
    sent = inner_sum.hold(grad_queries).near()
    outer_sum.hold(grad_queries)
    sums = sums_rows + sums_out + sums_back
    sums = sums.reshape(8, n, r).transpose(1, 0, 2).reshape(n, 8 * r)
    sums = jnp.concatenate([sums, inner_bias_grad.reshape(n, -1)], axis=1)
    sums = jnp.pad(sums, ((0, 0), (0, model_width - sums.shape[1]))).astype(BF16)
    sums = jnp.broadcast_to(sums[:, None], (n, 16, model_width))
    sums = sums.reshape(n // 2, 32, model_width)
    stream_low, sums = after((stream_low, sums), (sent, outer_sum.received()))
    stream_halves = triple_product(
        net, me, sums, stream_low, grad_queries, grad_keys, grad_values
    )
    stream_sum = Reduction(net, me, *stream_halves)
    grad_mixed = after(grad_mixed, stream_halves)
    back = (flow, grad_mixed, grad_queries, grad_keys, grad_values)
    grad_stream, grad_temb = stream_back(net, me, *back, 0, row_length, sums=row_sums)
    ends = grad_temb[:rows][None]
    sources, ends = net.gather_round([0], ends, net.masks(net.core))
    sent = list(stream_sum.hold(grad_temb).corner())
    sent += list(inner_sum.hold((grad_temb, sent)).far())
    ends = after(ends, sent)
    sent = stream_sum.hold(sent).near()
    grad_stream = after(grad_stream, sent)
    for row in range(1, rows):
        (grad_stream,) = stream_back(net, me, *back, row, row_length, grad_stream)
    inner_sum.hold(grad_stream), outer_sum.hold(grad_stream)
    sent = stream_sum.hold(grad_stream).far()
    ends = after(ends, (sent, inner_sum.received()))
    sources, ends = net.gather_round(sources, ends, net.masks(net.near))
    inner_sum.hold(sent), outer_sum.hold(sent)
    output_weight_grad, inner_weight_grad = inner_sum.end([1, hidden // model_width], r)
    (outer_weight_grad,) = outer_sum.end([1], outer_weight.shape[0])
    sources, ends = net.gather_round(sources, ends, net.masks(net.middle))
    others = (stream_sum.received(), inner_weight_grad, outer_weight_grad)
    sources, ends = net.gather_round(sources, after(ends, others), net.masks(net.outer))
    temb_all = in_order(net, me, sources, ends).reshape(n * rows, model_width)
    query_weight_grad, key_weight_grad, value_weight_grad, *parts = stream_ends(
        stream_sum, r, sizes
    )
    own = model_width // n
    steps_all = after(lines, grad_stream)
    steps_all = (steps_all[12] * 64.0 + steps_all[13])[: n * rows]
    feats_own = own_features(steps_all, me * own, own).astype(BF16).astype(F32)
    time_weight_grad = lax.dot_general(
        feats_own,
        temb_all,
        (((0,), (0,)), ((), ())),
        precision=lax.Precision.HIGHEST,
    )
    parts = dict(zip(order, parts))
    vector_outs = [parts[i] for i in range(len(order))]

    shape = inputs.shape
    return (
        layer_output.reshape(shape),
        grad_stream.reshape(shape),
        query_weight_grad,
        key_weight_grad,
        value_weight_grad,
        output_weight_grad,
        inner_weight_grad,
        outer_weight_grad,
        time_weight_grad,
    ) + tuple(vector_outs)


def solution(mesh):
    matrix, vector = P("fsdp", None), P("fsdp")
    batch = P(None, "fsdp", None, None)
    return jax.shard_map(
        functools.partial(on_device, Net(mesh.shape["fsdp"])),
        mesh=mesh,
        in_specs=(batch, P(None, "fsdp"), P(None, "fsdp", None), batch)
        + (matrix,) * 7
        + (vector,) * 9,
        out_specs=(batch, batch) + (matrix,) * 7 + (vector,) * 9,
        check_vma=False,
    )
```

```python
import functools
import math

import jax
import jax.numpy as jnp
from jax import lax
from jax.experimental import pallas as pl
from jax.experimental.pallas import tpu as pltpu
from jax.sharding import PartitionSpec as P

D = 1024
H = 16


INV_ROOT_TWO = 0.7071067811865476
INV_ROOT_TAU = 0.3989422804014327
F32 = jnp.float32
BF16 = jnp.bfloat16


def matmul(operand, factor):
    return jnp.dot(operand, factor, preferred_element_type=F32)


def matmul_left(operand, factor):
    return lax.dot_general(
        operand, factor, (((0,), (0,)), ((), ())), preferred_element_type=F32
    )


def matmul_right(operand, factor):
    return lax.dot_general(
        operand, factor, (((1,), (1,)), ((), ())), preferred_element_type=F32
    )


def features(step_ids):
    half_width = D // 2
    freqs = jnp.exp(-math.log(10000.0) * jnp.arange(half_width, dtype=F32) / half_width)
    angles = step_ids.astype(F32)[..., None] * freqs
    return jnp.concatenate([jnp.sin(angles), jnp.cos(angles)], axis=-1)


def own_features(step_ids, first, count):
    half_width = D // 2
    columns = first + jnp.arange(count, dtype=jnp.int32)
    places = (columns % half_width).astype(F32)
    freqs = jnp.exp(-math.log(10000.0) * places / half_width)
    angles = step_ids[:, None] * freqs
    return jnp.where(columns < half_width, jnp.sin(angles), jnp.cos(angles))


def normalize(values_in):
    center = values_in - jnp.mean(values_in, axis=-1, keepdims=True)
    spread = lax.rsqrt(jnp.mean(center * center, axis=-1, keepdims=True) + 1e-05)
    return (center * spread, spread)


def norm_back(grad_normed, normed, spread):
    mean_grad = jnp.mean(grad_normed, axis=-1, keepdims=True)
    mean_cross = jnp.mean(grad_normed * normed, axis=-1, keepdims=True)
    return spread * (grad_normed - mean_grad - normed * mean_cross)


def halves_body(low_in, high_in, low_out, high_out):
    low_out[...] = low_in[...]
    high_out[...] = high_in[...]


def halves(low_of, high_of):
    count, half = low_of.shape[0], low_of.shape[0] // 2
    block = (1,) + low_of.shape[1:]
    return pl.pallas_call(
        halves_body,
        grid=(half,),
        in_specs=[
            pl.BlockSpec(block, lambda i: (i, 0, 0)),
            pl.BlockSpec(block, lambda i: (half + i, 0, 0)),
        ],
        out_specs=[pl.BlockSpec(block, lambda i: (i, 0, 0))] * 2,
        out_shape=[jax.ShapeDtypeStruct((half,) + low_of.shape[1:], low_of.dtype)] * 2,
        compiler_params=pltpu.CompilerParams(vmem_limit_bytes=16 << 20),
        cost_estimate=pl.CostEstimate(flops=1000, bytes_accessed=1000, transcendentals=0),
        name="halves",
    )(low_of, high_of)


class Net:
    def __init__(self, n):
        self.n = n
        self.bits = n.bit_length() - 1
        chip = self.bits - 1
        sizes = [(chip + 2 - i) // 3 for i in range(3)]
        groups, top = [], self.bits - 1
        for size in sizes:
            groups.append(tuple(range(top, top - size, -1)))
            top -= size
        self.outer, self.middle, self.near = groups
        self.core = (0,)

    def masks(self, group):
        found = []
        for pick in range(1, 1 << len(group)):
            mask = 0
            for place, bit in enumerate(group):
                if pick >> place & 1:
                    mask |= 1 << bit
            found.append(mask)
        return found

    def swap(self, array, mask):
        return lax.ppermute(array, "fsdp", [(i, i ^ mask) for i in range(self.n)])

    def gather_far(self, shard):
        return [shard] + [self.swap(shard, mask) for mask in self.masks(self.outer)]

    def stacked(self, parts, me):
        low = self.bits - len(self.outer)
        masks = [mask >> low for mask in [0] + self.masks(self.outer)]
        count, shape = len(parts), parts[0].shape

        def body(me_ref, *refs):
            for mask, ref in zip(masks, refs):
                refs[-1][me_ref[0] >> low ^ mask] = ref[...]

        whole = pl.BlockSpec(shape, lambda i: (0, 0))
        return pl.pallas_call(
            body,
            grid=(1,),
            in_specs=[pl.BlockSpec(memory_space=pltpu.SMEM)] + [whole] * count,
            out_specs=pl.BlockSpec((count,) + shape, lambda i: (0, 0, 0)),
            out_shape=jax.ShapeDtypeStruct((count,) + shape, parts[0].dtype),
            compiler_params=pltpu.CompilerParams(vmem_limit_bytes=16 << 20),
            cost_estimate=pl.CostEstimate(flops=1000, bytes_accessed=1000, transcendentals=0),
            name="stacked",
        )(me.reshape(1), *parts)

    def gather_near(self, own):
        return [
            [(mask, self.swap(own, mask)) for mask in self.masks(group)]
            for group in (self.near, self.middle)
        ]

    def gather_corner(self, own, near):
        half = own.shape[0] // 2
        pieces, corners, sent = [(0, 0, own)], [], []
        for group in near:
            pieces += [(0, mask, array) for mask, array in group]
        for mask_x, array_x in near[0]:
            for mask_y, array_y in near[1]:
                low, high = halves(array_y, array_x)
                sent += [low, high]
                corners.append((0, mask_x ^ mask_y, self.swap(low, mask_x)))
                corners.append((half, mask_x ^ mask_y, self.swap(high, mask_y)))
        return pieces, corners, sent

    def gather_core(self, pieces):
        return pieces + [(first, mask ^ 1, self.swap(array, 1)) for first, mask, array in pieces]

    def inner_masks(self):
        near, middle = self.masks(self.near), self.masks(self.middle)
        return near + middle + [x | y for x in near for y in middle]

    def gather_round(self, sources, array, masks):
        array = jnp.concatenate([array] + [self.swap(array, mask) for mask in masks])
        return [source ^ mask for mask in [0] + masks for source in sources], array

    def take(self, term, bits, mask, present, me):
        present = list(present)
        for bit in bits:
            place = present.index(bit)
            low = 1 << (len(present) - 1 - place)
            value = (me >> bit & 1) ^ (mask >> bit & 1)
            rest = term.shape[1:]
            term = term.reshape((1 << place, 2, low) + rest)
            term = lax.dynamic_index_in_dim(term, value, 1, keepdims=False)
            term = term.reshape((low << place,) + rest)
            present.remove(bit)
        return term

    def scatter_core(self, halves):
        keep, send = halves
        return [keep, self.swap(send, 1)], list(range(self.bits - 1, 0, -1))

    def added(self, parts, dtype):
        parts = [part.astype(F32) for part in parts]
        return sum(parts[1:], parts[0]).astype(dtype)

    def scatter_step(self, state, group, me):
        terms, present = state
        sent = []
        for mask in self.masks(group):
            parts = [self.take(term, group, mask, present, me) for term in terms]
            sent.append(self.added(parts, terms[0].dtype))
        received = [self.swap(part, mask) for part, mask in zip(sent, self.masks(group))]
        terms = [self.take(term, group, 0, present, me) for term in terms] + received
        return (terms, [bit for bit in present if bit not in group]), sent

    def scatter_corner(self, state, me):
        terms, present = state
        left = [bit for bit in present if bit not in self.near]
        found, sent = [], []
        for mask_x in self.masks(self.near):
            row = [self.take(term, self.near, mask_x, present, me) for term in terms]
            for mask_y in self.masks(self.middle):
                parts = [self.take(term, self.middle, mask_y, left, me) for term in row]
                half = parts[0].shape[0] // 2
                low = self.added([part[:half] for part in parts], terms[0].dtype)
                high = self.added([part[half:] for part in parts], terms[0].dtype)
                sent += [low, high]
                found.append((mask_x, mask_y, self.swap(low, mask_x), self.swap(high, mask_y)))
        return found, sent

    def scatter_near(self, state, corner, me):
        terms, present = state
        left = [bit for bit in present if bit not in self.near]
        mine, received, sent = [self.take(t, self.near, 0, present, me) for t in terms], [], []
        for mask_x in self.masks(self.near):
            row = [self.take(term, self.near, mask_x, present, me) for term in terms]
            parts = [self.take(term, self.middle, 0, left, me) for term in row]
            for mask, _, _, high in corner:
                if mask == mask_x:
                    parts.append(jnp.concatenate([jnp.zeros_like(high), high]))
            sent.append((self.added(parts, terms[0].dtype), mask_x))
        for mask_y in self.masks(self.middle):
            parts = [self.take(term, self.middle, mask_y, left, me) for term in mine]
            for _, mask, low, _ in corner:
                if mask == mask_y:
                    parts.append(jnp.concatenate([low, jnp.zeros_like(low)]))
            sent.append((self.added(parts, terms[0].dtype), mask_y))
        received = [self.swap(part, mask) for part, mask in sent]
        terms = [self.take(term, self.middle, 0, left, me) for term in mine] + received
        left = [bit for bit in left if bit not in self.middle]
        return (terms, left), [part for part, _ in sent]

    def scatter_far(self, state, me):
        return self.scatter_step(state, self.outer, me)

    def scatter_end(self, state):
        return self.added(state[0], F32)[0]

    def scatter(self, halves, order, me):
        state = self.scatter_core(halves)
        for group in order:
            state, _ = self.scatter_step(state, group, me)
        return self.scatter_end(state)

    def scatter_whole(self, whole, order, me):
        present = list(range(self.bits - 1, -1, -1))
        halves = [self.take(whole, self.core, mask, present, me) for mask in (0, 1)]
        return self.scatter(halves, order, me)


def after(values, others):
    leaves, tree = jax.tree.flatten(values)
    arrays = [leaf for leaf in leaves if not isinstance(leaf, int)]
    others = [leaf for leaf in jax.tree.leaves(others) if not isinstance(leaf, int)]
    tied = iter(lax.optimization_barrier(tuple(arrays + others)))
    return jax.tree.unflatten(
        tree, [leaf if isinstance(leaf, int) else next(tied) for leaf in leaves]
    )


class Weights:
    def __init__(self, net, me, wanted):
        self.arrays, self.plans, self.shapes = [], [], []
        seen = {}
        outer = 1 << len(net.outer)
        low = net.n // outer
        self.low = low
        for pieces, places, rows in wanted:
            places = (places,) if isinstance(places, int) else tuple(places)
            columns = pieces[0][2].shape[-1]
            plan = []
            if rows % 16:
                blocks = [
                    jnp.concatenate([array[:, place : place + rows] for _, _, array in pieces])
                    for place in places
                ]
                blocks = jnp.concatenate(blocks, axis=2)
                order = [
                    (first + j) * low + (me % low ^ mask)
                    for first, mask, array in pieces
                    for j in range(array.shape[0])
                ]
                spot = jnp.zeros((net.n,), jnp.int32).at[jnp.stack(order)].set(jnp.arange(net.n))
                whole = blocks[spot].reshape(outer, low * rows // 16, 16, len(places) * columns)
                plan.append((len(self.arrays), None, None, None))
                self.arrays.append(whole)
                self.shapes.append(whole.shape)
            else:
                for first, mask, array in pieces:
                    if id(array) not in seen:
                        seen[id(array)] = len(self.arrays)
                        self.arrays.append(array)
                    for k, place in enumerate(places):
                        own = (slice(None), pl.ds(place, rows))
                        aim = (pl.ds(first, array.shape[0]), pl.ds(k * columns, columns))
                        plan.append((seen[id(array)], own, mask, aim))
                self.shapes.append((outer, low, rows, len(places) * columns))
            self.plans.append(plan)
        self.slots = max(len(plan) for plan in self.plans)

    def scratch(self):
        return [pltpu.VMEM(shape, BF16) for shape in self.shapes] + [
            pltpu.SemaphoreType.DMA((len(self.plans), self.slots))
        ]

    def copies(self, w, me, array_refs, held_ref, sems):
        found = []
        for slot, (array, own, mask, aim) in enumerate(self.plans[w]):
            if own is None:
                pair = (array_refs[array], held_ref)
            else:
                spot = me % self.low ^ mask
                pair = (array_refs[array].at[own], held_ref.at[aim[0], spot, :, aim[1]])
            found.append(pltpu.make_async_copy(*pair, sems.at[w, slot]))
        return found

    def start(self, w, *refs):
        for copy in self.copies(w, *refs):
            copy.start()

    def wait(self, w, *refs):
        for copy in self.copies(w, *refs):
            copy.wait()


def flat(held):
    return held.reshape(-1, held.shape[-1])


SMEM_SPEC = pl.BlockSpec(memory_space=pltpu.SMEM)
ANY_SPEC = pl.BlockSpec(memory_space=pltpu.HBM)


def full_spec(shape):
    return pl.BlockSpec(shape, lambda *_: (0,) * len(shape))


def tile_spec(tile, columns):
    return pl.BlockSpec((tile, columns), lambda i: (i, 0))


def call(body, name, grid, ins, outs, scratch, us, bases=()):
    count = len(ins)

    def run(*refs):
        body(*refs[:count], *refs[count + len(bases) :])

    return pl.pallas_call(
        run,
        grid=grid,
        in_specs=[spec for _, spec in ins] + [ANY_SPEC] * len(bases),
        out_specs=[spec for _, _, spec in outs],
        out_shape=[jax.ShapeDtypeStruct(shape, dtype) for shape, dtype, _ in outs],
        scratch_shapes=scratch,
        input_output_aliases={count + i: i for i in range(len(bases))},
        compiler_params=pltpu.CompilerParams(
            vmem_limit_bytes=60 << 20,
            dimension_semantics=("arbitrary",) * len(grid),
        ),
        cost_estimate=pl.CostEstimate(
            flops=int(us * 2e10), bytes_accessed=int(us * 5e7), transcendentals=0
        ),
        name=name,
    )(*[array for array, _ in ins], *bases)


def sum_body(groups, me_ref, *refs):
    step = pl.program_id(0)
    outs = refs[len(refs) - len(groups) :]
    for out_ref, addends in zip(outs, groups):
        total = None
        for place, (low, high) in addends:
            part = refs[place][...].astype(F32)
            if low is not None:
                part = jnp.where((step >= low) & (step < high), part, 0.0)
            total = part if total is None else total + part
        out_ref[...] = total.astype(out_ref.dtype)


def sum_call(me, name, grid, ins, groups, outs, body=None, us=0.01):
    grid_spec = pltpu.PrefetchScalarGridSpec(
        num_scalar_prefetch=1,
        grid=(grid,),
        in_specs=[
            pl.BlockSpec(block, lambda i, me_ref, place=place: place(i, me_ref[0]))
            for _, block, place in ins
        ],
        out_specs=[
            pl.BlockSpec(block, lambda i, me_ref, place=place: place(i, me_ref[0]))
            for _, _, block, place in outs
        ],
    )
    return pl.pallas_call(
        body or functools.partial(sum_body, groups),
        grid_spec=grid_spec,
        out_shape=[jax.ShapeDtypeStruct(shape, dtype) for shape, dtype, _, _ in outs],
        compiler_params=pltpu.CompilerParams(
            vmem_limit_bytes=60 << 20, dimension_semantics=("arbitrary",)
        ),
        cost_estimate=pl.CostEstimate(flops=int(us * 2e10), bytes_accessed=int(us * 5e7), transcendentals=0),
        name=name,
    )(me.reshape(1), *[array for array, _, _ in ins])


class Reduction:
    def __init__(self, net, me, keep, send):
        self.net, self.me = net, me
        self.terms = [keep, net.swap(send, 1)]
        self.rows, self.columns = keep.shape[1:]
        self.plain = len(net.near) == 1 and len(net.middle) == 1 and self.rows % 8 == 0
        self.state = None

    def block(self):
        return (1, self.rows, self.columns)

    def parted(self, term):
        return term.reshape(-1, 4, self.rows, self.columns)

    def blocks(self, far):
        shape = (far, self.rows, self.columns)
        return (far, None, self.rows, self.columns), shape

    def hold(self, others):
        if self.plain:
            self.terms = after(self.terms, others)
        else:
            state = self.state or (self.terms, list(range(self.net.bits - 1, 0, -1)))
            self.state = held(state, others)
            if getattr(self, "corner_pieces", None) is not None:
                self.corner_pieces = after(self.corner_pieces, others)
        return self

    def corner(self):
        net = self.net
        if not self.plain:
            state = self.state or (self.terms, list(range(net.bits - 1, 0, -1)))
            self.state = state
            self.corner_pieces, sent = net.scatter_corner(state, self.me)
            return sent
        far = 1 << (len(net.outer) - 1)

        def place(shift):
            return lambda i, me: ((i + shift) * 4 + (me >> 1 & 3 ^ 3), 0, 0)

        ins = [(term, self.block(), place(shift)) for shift in (0, far) for term in self.terms]
        out = ((far, self.rows, self.columns), BF16, self.block(), lambda i, me: (i, 0, 0))
        always = (None, None)
        groups = [[(0, always), (1, always)], [(2, always), (3, always)]]
        low, high = sum_call(self.me, "corner_sum", far, ins, groups, [out, out])
        self.terms += [net.swap(low, 1 << net.near[0]), net.swap(high, 1 << net.middle[0])]
        return [low, high]

    def near(self):
        net = self.net
        if not self.plain:
            self.state, sent = net.scatter_near(self.state, self.corner_pieces, self.me)
            self.corner_pieces = None
            return sent
        far = 1 << (len(net.outer) - 1)
        keep, other, low, high = self.terms

        def place(flip):
            return lambda i, me: (i, me >> 1 & 3 ^ flip, 0, 0)

        block, shape = self.blocks(far)
        pair = (self.parted(keep), self.parted(other))
        ins = [(term, block, place(flip)) for flip in (1, 2) for term in pair]
        ins += [(term, shape, lambda i, me: (0, 0, 0)) for term in (high, low)]
        always = (None, None)
        groups = [
            [(0, always), (1, always), (4, (1, 2))],
            [(2, always), (3, always), (5, (0, 1))],
        ]
        whole = (2 * far, self.rows, self.columns)
        out = (whole, BF16, shape, lambda i, me: (i, 0, 0))
        sent = sum_call(self.me, "near_sum", 2, ins, groups, [out, out])
        received = [
            net.swap(part, 1 << group[0]) for part, group in zip(sent, (net.near, net.middle))
        ]
        self.terms = [keep, other] + received
        return sent

    def sources(self, flip, step_block):
        keep, other, row, column = self.terms[:4]
        found = []
        for term in (keep, other):
            found.append((term, lambda me: ((me >> 3 ^ flip) * 4 + (me >> 1 & 3))))
        for term in (row, column):
            found.append((term, lambda me: (me >> 3 ^ flip)))
        return [
            (term, step_block[0], lambda i, me, at=at: step_block[1](i, at(me)))
            for term, at in found
        ]

    def far(self):
        net = self.net
        if not self.plain:
            self.state, sent = net.scatter_step(self.state, net.outer, self.me)
            return sent
        parts = 2 if self.rows % 32 == 0 else 1
        step_block = ((1, self.rows // parts, self.columns), lambda i, at: (at, i, 0))
        masks = net.masks(net.outer)
        ins, groups = [], []
        for mask in masks:
            groups.append([(len(ins) + j, (None, None)) for j in range(4)])
            ins += self.sources(mask >> 3, step_block)
        out = ((1, self.rows, self.columns), BF16, step_block[0], lambda i, me: (0, i, 0))
        sent = sum_call(self.me, "far_sum", parts, ins, groups, [out] * len(masks))
        self.terms += [net.swap(part, mask) for part, mask in zip(sent, masks)]
        return sent

    def received(self):
        return self.terms[-1] if self.plain else self.state[0][-1]

    def end(self, lots, unit):
        if not self.plain:
            total = self.net.scatter_end(self.state)
            results, start = [], 0
            for count in lots:
                blocks = [
                    total[(start + j) * unit : (start + j + 1) * unit] for j in range(count)
                ]
                results.append(jnp.concatenate(blocks, axis=1))
                start += count
            return results
        step_block = ((1, unit, self.columns), lambda i, at: (at, i, 0))
        ins = self.sources(0, step_block)
        ins += [(term, step_block[0], lambda i, me: (0, i, 0)) for term in self.terms[4:]]
        outs, bounds, start = [], [], 0
        for count in lots:

            def place(i, me, start=start, count=count):
                return (0, jnp.clip(i - start, 0, count - 1))

            outs.append(((unit, count * self.columns), F32, (unit, self.columns), place))
            bounds.append((start, start + count))
            start += count

        def body(me_ref, *refs):
            step, addends = pl.program_id(0), refs[: len(ins)]
            total = addends[0][0].astype(F32)
            for ref in addends[1:]:
                total = total + ref[0].astype(F32)
            for out_ref, (low, high) in zip(refs[len(ins) :], bounds):

                @pl.when((step >= low) & (step < high))
                def _():
                    out_ref[...] = total

        return sum_call(self.me, "end_sum", start, ins, None, outs, body, 4)


def pack_body(sizes, me_ref, times_ref, small_ref, *refs):
    shards, out_ref = refs[:-1], refs[-1]
    start = 0
    for ref in shards:
        out_ref[start : start + ref.shape[0]] = ref[...]
        start += ref.shape[0]
    me, width = me_ref[0], out_ref.shape[1]

    small = small_ref[...]
    step, inner_size, steps = sizes

    def spread(first, count, offset):
        spots = lax.broadcasted_iota(jnp.int32, (small.shape[1], width), 0) - first
        lanes = lax.broadcasted_iota(jnp.int32, (small.shape[1], width), 1)
        hits = (spots >= 0) & (spots < count) & (lanes == spots + offset)
        return matmul(small, jnp.where(hits, 1.0, 0.0).astype(BF16))

    vectors = spread(0, step, me * step)
    place = me * inner_size
    inner = spread(step, inner_size, lax.rem(place, width))
    row = lax.broadcasted_iota(jnp.int32, inner.shape, 0)
    inner = jnp.where(row == place // width, inner, 0.0)
    lane = lax.broadcasted_iota(jnp.int32, inner.shape, 1)
    for j in range(steps):
        time = times_ref[j]
        digit = jnp.where(row == 4, time >> 6, jnp.where(row == 5, time & 63, 0))
        inner += jnp.where(lane == me * steps + j, digit, 0).astype(F32)
    out_ref[start:] = jnp.concatenate([vectors, inner]).astype(BF16)


def pack(me, shards, vectors, inner, times):
    step, width = shards[0].shape
    sizes = (step, inner.shape[0], times.shape[0])
    small = 0.0
    for line, vector in enumerate(vectors):
        small += jnp.pad(vector.astype(F32)[None], ((line, 7 - line), (0, 256 - step)))
    rest = 256 - sizes[1] - step
    small += jnp.pad(inner.astype(F32)[None], ((0, 0), (step, rest)))
    small = small.astype(BF16)
    rows = len(shards) * step + 16
    return call(
        functools.partial(pack_body, sizes),
        "pack",
        (1,),
        [(me.reshape(1), SMEM_SPEC), (times, SMEM_SPEC)]
        + [(array, full_spec(array.shape)) for array in (small, *shards)],
        [((rows, width), BF16, full_spec((rows, width)))],
        [],
        1,
    )[0]


def project_body(weights, tile, row_length, me_ref, *refs):
    count = len(weights.arrays)
    arrays, refs = refs[:count], refs[count:]
    feats_ref, x_ref = refs[:2]
    temb_ref, lines_ref, low_ref, q_ref, k_ref, v_ref = refs[2:8]
    tw, qw, kw, vw, lw, sems = refs[8:14]
    me, step = me_ref[0], pl.program_id(0)

    @pl.when(step == 0)
    def _():
        for w, held in enumerate((tw, qw, kw, vw, lw)):
            weights.start(w, me, arrays, held, sems)
        weights.wait(0, me, arrays, tw, sems)
        temb_ref[...] = matmul(feats_ref[...], flat(tw[...]))
        weights.wait(4, me, arrays, lw, sems)
        lines_ref[...] = jnp.sum(lw[...].astype(F32), axis=(0, 1))
        for w, held in ((1, qw), (2, kw), (3, vw)):
            weights.wait(w, me, arrays, held, sems)

    row = step * tile // row_length
    low = (x_ref[...].astype(F32) + temb_ref[pl.ds(row, 1), :]).astype(BF16)
    low_ref[...] = low
    q_ref[...] = (matmul(low, flat(qw[...])) + lines_ref[0:1]).astype(BF16)
    k_ref[...] = matmul(low, flat(kw[...])).astype(BF16)
    v_ref[...] = (matmul(low, flat(vw[...])) + lines_ref[1:2]).astype(BF16)


def project(net, me, flow, feats, x, row_length):
    tokens, width = x.shape
    tile = min(256, row_length)
    r = width // net.n
    weights = Weights(net, me, [(flow, w * r, r) for w in range(4)] + [(flow, 4 * r, 16)])
    ins = (
        [(me.reshape(1), SMEM_SPEC)]
        + [(array, ANY_SPEC) for array in weights.arrays]
        + [(feats, full_spec(feats.shape)), (x, tile_spec(tile, width))]
    )
    outs = [(feats.shape, F32, full_spec(feats.shape))]
    outs += [((16, width), F32, full_spec((16, width)))]
    outs += [((tokens, width), BF16, tile_spec(tile, width))] * 4
    return call(
        functools.partial(project_body, weights, tile, row_length),
        "project",
        (tokens // tile,),
        ins,
        outs,
        weights.scratch(),
        14,
    )


def same_document(seg_ref, bias_ref, block):
    @pl.when(block == 0)
    def _():
        row = seg_ref[0].astype(F32)
        column = jnp.transpose(jnp.broadcast_to(row, (128, row.shape[1])))[:, :1]
        bias_ref[...] = jnp.where(column == row, 0.0, -1e30)


def own_lanes(shape, head, head_dim):
    lanes = lax.broadcasted_iota(jnp.int32, shape, len(shape) - 1)
    return (lanes // head_dim) == head


def attend_body(head_dim, seg_ref, q_ref, k_ref, v_ref, out_ref, log_ref, bias_ref):
    same_document(seg_ref, bias_ref, pl.program_id(1))
    queries, key_rows, values = q_ref[...], k_ref[...], v_ref[...]
    scale = 1.0 / math.sqrt(head_dim)
    per = queries.shape[1] // head_dim
    total = None
    for head in range(per):
        mine = own_lanes(queries.shape, head, head_dim)
        keys_own = jnp.where(mine, key_rows * BF16(scale), BF16(0))
        scores = matmul_right(keys_own, queries) + bias_ref[...]
        top = jnp.max(scores, axis=0, keepdims=True)
        raised = jnp.exp(scores - top)
        amount = jnp.sum(raised, axis=0, keepdims=True)
        log_ref[0, 0, pl.ds(head, 1), :] = top + jnp.log(amount)
        soft_low = (raised * (1.0 / amount)).astype(BF16)
        context = matmul_left(soft_low, values)
        total = context if total is None else jnp.where(mine, context, total)
    out_ref[...] = total.astype(BF16)


def attend_back_body(
    head_dim, seg_ref, q_ref, k_ref, v_ref, log_ref, g_ref, gq_ref, gk_ref, gv_ref, sums_ref, rows_ref, bias_ref
):
    same_document(seg_ref, bias_ref, pl.program_id(1))
    queries, key_rows, values, grads = q_ref[...], k_ref[...], v_ref[...], g_ref[...]
    scale = 1.0 / math.sqrt(head_dim)
    per = queries.shape[1] // head_dim
    totals = None
    for head in range(per):
        mine = own_lanes(queries.shape, head, head_dim)
        keys_own = jnp.where(mine, key_rows * BF16(scale), BF16(0))
        scores = matmul_right(keys_own, queries) + bias_ref[...]
        soft = jnp.exp(scores - log_ref[0, 0, pl.ds(head, 1), :])
        grad_soft = matmul_right(jnp.where(mine, values, BF16(0)), grads)
        inner_sum = jnp.sum(soft * grad_soft, axis=0, keepdims=True)
        grad_scores = (soft * (grad_soft - inner_sum)).astype(BF16)
        parts = (
            matmul_left(grad_scores, key_rows),
            matmul(grad_scores, queries),
            matmul(soft.astype(BF16), grads),
        )
        if totals is None:
            totals = parts
        else:
            totals = tuple(jnp.where(mine, part, total) for part, total in zip(parts, totals))
    gq = (totals[0] * scale).astype(BF16)
    gv = totals[2].astype(BF16)
    gq_ref[...] = gq
    gk = (totals[1] * scale).astype(BF16)
    gk_ref[...] = gk
    gv_ref[...] = gv
    sums = [jnp.sum(part.astype(F32), axis=0, keepdims=True) for part in (gq, gk, gv)]
    zero = jnp.zeros_like(sums[0])
    sums_ref[...] = jnp.concatenate([sums[0], sums[2]] + [zero] * 6)
    rows_ref[...] = jnp.concatenate(sums + [zero] * 5)


def attention_args(segments, start, lanes, head_dim):
    row_length, per = segments.shape[1], lanes // head_dim
    segs = pl.BlockSpec((1, 1, row_length), lambda i, j: (start + i, 0, 0))
    block = pl.BlockSpec((row_length, lanes), lambda i, j: (start + i, j))
    log_spec = pl.BlockSpec((1, 1, per, row_length), lambda i, j: (start + i, j, 0, 0))
    return [(segments[:, None, :], segs)], block, log_spec


def attend(queries, key_rows, values, segments, lanes=256):
    rows, row_length = segments.shape
    tokens, width = queries.shape
    head_dim = width // H
    blocks, per = width // lanes, lanes // head_dim
    masks, block, log_spec = attention_args(segments, 0, lanes, head_dim)
    return call(
        functools.partial(attend_body, head_dim),
        "attend",
        (rows, blocks),
        masks + [(array, block) for array in (queries, key_rows, values)],
        [
            ((tokens, width), BF16, block),
            ((rows, blocks, per, row_length), F32, log_spec),
        ],
        [pltpu.VMEM((row_length, row_length), F32)],
        24,
    )


def attend_back(queries, key_rows, values, segments, log_total, grad_context, row, bases=(), lanes=256):
    rows, row_length = segments.shape
    tokens, width = queries.shape
    head_dim = width // H
    masks, block, log_spec = attention_args(segments, row, lanes, head_dim)
    return call(
        functools.partial(attend_back_body, head_dim),
        "attend_back",
        (1, width // lanes),
        masks
        + [(array, block) for array in (queries, key_rows, values)]
        + [(log_total, log_spec), (grad_context, block)],
        [((tokens, width), BF16, block)] * 3
        + [((8, width), F32, pl.BlockSpec((8, lanes), lambda i, j: (0, j)))] * 2,
        [pltpu.VMEM((row_length, row_length), F32)],
        19,
        bases,
    )


def add_to(ref, value, step):
    part = jnp.sum(value, axis=0, keepdims=True)

    @pl.when(step == 0)
    def _():
        ref[...] = part

    @pl.when(step != 0)
    def _():
        ref[...] += part


def add_lines(ref, values, step):
    zero = jnp.zeros((1, ref.shape[1]), F32)
    sums = {line: jnp.sum(value, axis=0, keepdims=True) for line, value in values.items()}
    part = jnp.concatenate([sums.get(line, zero) for line in range(ref.shape[0])])

    @pl.when(step == 0)
    def _():
        ref[...] = part

    @pl.when(step != 0)
    def _():
        ref[...] += part


def ffn_in_body(weights, tile, row_length, chunk, me_ref, *refs):
    count = len(weights.arrays)
    arrays, refs = refs[:count], refs[count:]
    context_ref, x_ref, temb_ref, lines_ref = refs[:4]
    first_low_ref, normed_ref, spread_ref, active_ref, slope_ref = refs[4:9]
    ow, iw, sems = refs[9:12]
    me, step = me_ref[0], pl.program_id(0)

    @pl.when(step == 0)
    def _():
        for w, held in enumerate((ow, iw)):
            weights.start(w, me, arrays, held, sems)
        weights.wait(0, me, arrays, ow, sems)

    row = step * tile // row_length
    stream = x_ref[...].astype(F32) + temb_ref[pl.ds(row, 1), :]
    mixed = stream + (matmul(context_ref[...], flat(ow[...])) + lines_ref[2:3])
    normed, spread = normalize(mixed)
    normed_ref[...] = normed
    spread_ref[...] = spread
    first = normed * lines_ref[4:5] + lines_ref[5:6]
    low = first.astype(BF16)
    first_low_ref[...] = low

    @pl.when(step == 0)
    def _():
        weights.wait(1, me, arrays, iw, sems)

    width, hidden = ow.shape[3], iw.shape[3]

    def inner(start):
        pre = matmul(low, flat(iw[:, :, :, start : start + chunk]))
        line, place = 8 + start // width, start % width
        return pre + lines_ref[line : line + 1, place : place + chunk]

    later = inner(0)
    for start in range(0, hidden, chunk):
        pre = later
        if start + chunk < hidden:
            later = inner(start + chunk)
        columns = slice(start, start + chunk)
        normal_cdf = 0.5 * (1.0 + lax.erf(pre * INV_ROOT_TWO))
        normal_pdf = jnp.exp(-0.5 * pre * pre) * INV_ROOT_TAU
        active_ref[:, columns] = (pre * normal_cdf).astype(BF16)
        slope_ref[:, columns] = (normal_cdf + pre * normal_pdf).astype(BF16)


def ffn_in(net, me, flow, context, x, temb, lines, hidden, row_length, tile=256, chunk=512):
    tokens, width = x.shape
    r = width // net.n
    blocks = range(r, r + hidden // width * r, r)
    weights = Weights(net, me, [(flow, 0, r), (flow, blocks, r)])
    tile = min(tile, row_length)
    tiled, wide, thin = (tile_spec(tile, columns) for columns in (width, hidden, 1))
    ins = (
        [(me.reshape(1), SMEM_SPEC)]
        + [(array, ANY_SPEC) for array in weights.arrays]
        + [(context, tiled), (x, tiled)]
        + [(array, full_spec(array.shape)) for array in (temb, lines)]
    )
    outs = [
        ((tokens, width), BF16, tiled),
        ((tokens, width), F32, tiled),
        ((tokens, 1), F32, thin),
        ((tokens, hidden), BF16, wide),
        ((tokens, hidden), BF16, wide),
    ]
    return call(
        functools.partial(ffn_in_body, weights, tile, row_length, chunk),
        "ffn_in",
        (tokens // tile,),
        ins,
        outs,
        weights.scratch(),
        30,
    )


def ffn_out_body(weights, me_ref, *refs):
    count = len(weights.arrays)
    arrays, refs = refs[:count], refs[count:]
    active_ref, normed_ref, cot_ref, lines_ref = refs[:4]
    out_ref, gs_ref, gs_low_ref, sums_ref = refs[4:8]
    uw, sems = refs[8:10]
    me, step = me_ref[0], pl.program_id(0)

    @pl.when(step == 0)
    def _():
        weights.start(0, me, arrays, uw, sems)
        weights.wait(0, me, arrays, uw, sems)

    first = normed_ref[...] * lines_ref[4:5] + lines_ref[5:6]
    second = first + (matmul(active_ref[...], flat(uw[...])) + lines_ref[3:4])
    normed_second, spread_second = normalize(second)
    out_ref[...] = (normed_second * lines_ref[6:7] + lines_ref[7:8]).astype(BF16)
    grad_out = cot_ref[...].astype(F32)
    grad_second = norm_back(grad_out * lines_ref[6:7], normed_second, spread_second)
    gs_ref[...] = grad_second
    low = grad_second.astype(BF16)
    gs_low_ref[...] = low
    add_lines(sums_ref, {3: low.astype(F32), 6: grad_out * normed_second, 7: grad_out}, step)


def ffn_out(net, me, flow, active, normed, cotangent, vectors, tile=256):
    tokens, width = normed.shape
    hidden = active.shape[1]
    weights = Weights(net, me, [(flow, 0, hidden // net.n)])
    tiled, wide = tile_spec(tile, width), tile_spec(tile, hidden)
    ins = (
        [(me.reshape(1), SMEM_SPEC)]
        + [(array, ANY_SPEC) for array in weights.arrays]
        + [(active, wide), (normed, tiled), (cotangent, tiled)]
        + [(vector, full_spec(vector.shape)) for vector in vectors]
    )
    outs = [
        ((tokens, width), BF16, tiled),
        ((tokens, width), F32, tiled),
        ((tokens, width), BF16, tiled),
        ((8, width), F32, full_spec((8, width))),
    ]
    return call(
        functools.partial(ffn_out_body, weights),
        "ffn_out",
        (tokens // tile,),
        ins,
        outs,
        weights.scratch(),
        20,
    )


def ffn_back_body(weights, tile, row_length, me_ref, *refs):
    count = len(weights.arrays)
    arrays, refs = refs[:count], refs[count:]
    (gs_ref, gs_low_ref, slope_ref, normed_ref, spread_ref, lines_ref) = refs[:6]
    (gi_ref, gm_ref, gm_low_ref, gc_ref, ibg_ref, sums_ref, rows_ref) = refs[6:13]
    uw, ow, iw, sems, held_ref = refs[13:18]
    me, step = me_ref[0], pl.program_id(0)
    last = pl.num_programs(0) - 1

    @pl.when(step == 0)
    def _():
        for w, held in ((0, uw), (2, iw), (1, ow)):
            weights.start(w, me, arrays, held, sems)
        sums_ref[...] = jnp.zeros_like(sums_ref)
        rows_ref[...] = jnp.zeros_like(rows_ref)
        ibg_ref[...] = jnp.zeros_like(ibg_ref)
        weights.wait(0, me, arrays, uw, sems)

    def through_hidden(first_time=False):
        part = gi_ref.shape[1] // uw.shape[0]
        for z in range(uw.shape[0]):
            columns = slice(z * part, (z + 1) * part)
            grad_active = matmul_right(gs_low_ref[...], flat(uw[z]))
            gi = (grad_active * slope_ref[:, columns].astype(F32)).astype(BF16)
            gi_ref[:, columns] = gi
            ibg_ref[:, columns] += jnp.sum(gi.astype(F32), axis=0, keepdims=True)
        if first_time:
            weights.wait(2, me, arrays, iw, sems)
        return gs_ref[...] + matmul_right(gi_ref[...], flat(iw[...]))

    def through_norm(grad_first):
        normed = normed_ref[...]
        grad_mixed = norm_back(grad_first * lines_ref[4:5], normed, spread_ref[...])
        gm_ref[...] = grad_mixed
        low = grad_mixed.astype(BF16)
        gm_low_ref[...] = low
        row = pl.ds((step - 1) * tile // row_length, 1)
        rows_ref[row, :] += jnp.sum(grad_mixed, axis=0, keepdims=True)
        values = {2: low.astype(F32), 4: grad_first * normed, 5: grad_first}
        for line, value in values.items():
            sums_ref[line : line + 1] += jnp.sum(value, axis=0, keepdims=True)
        gc_ref[...] = matmul_right(low, flat(ow[...])).astype(BF16)

    @pl.when(step == 0)
    def _():
        held_ref[...] = through_hidden(True)
        weights.wait(1, me, arrays, ow, sems)

    @pl.when((step > 0) & (step < last))
    def _():
        grad_first = held_ref[...]
        later = through_hidden()
        through_norm(grad_first)
        held_ref[...] = later

    @pl.when(step == last)
    def _():
        through_norm(held_ref[...])


def ffn_back(net, me, flow_u, flow_io, gs, gs_low, slope, normed, spread, lines, row_length, tile=256):
    tokens, width = gs.shape
    hidden = slope.shape[1]
    r = width // net.n
    weights = Weights(
        net,
        me,
        [
            (flow_u, 0, hidden // net.n),
            (flow_io, 0, r),
            (flow_io, range(r, r + hidden // width * r, r), r),
        ],
    )
    tile = min(tile, row_length)
    steps = tokens // tile

    def ahead(columns):
        return pl.BlockSpec((tile, columns), lambda i: (jnp.minimum(i, steps - 1), 0))

    def behind(columns):
        return pl.BlockSpec((tile, columns), lambda i: (jnp.maximum(i - 1, 0), 0))

    ins = (
        [(me.reshape(1), SMEM_SPEC)]
        + [(array, ANY_SPEC) for array in weights.arrays]
        + [(gs, ahead(width)), (gs_low, ahead(width)), (slope, ahead(hidden))]
        + [(normed, behind(width)), (spread, behind(1)), (lines, full_spec(lines.shape))]
    )
    outs = [
        ((tokens, hidden), BF16, ahead(hidden)),
        ((tokens, width), F32, behind(width)),
        ((tokens, width), BF16, behind(width)),
        ((tokens, width), BF16, behind(width)),
        ((1, hidden), F32, full_spec((1, hidden))),
        ((8, width), F32, full_spec((8, width))),
        ((8, width), F32, full_spec((8, width))),
    ]
    return call(
        functools.partial(ffn_back_body, weights, tile, row_length),
        "ffn_back",
        (steps + 1,),
        ins,
        outs,
        weights.scratch() + [pltpu.VMEM((tile, width), F32)],
        36,
    )


def deal(me_ref, total, rows, keep_ref, send_ref, kind=0):
    core = me_ref[0] & 1
    total = total.reshape(-1, 2, rows, total.shape[-1])
    low, high = total[:, 0], total[:, 1]
    place = slice(kind * rows, (kind + 1) * rows)
    keep_ref[:, place] = jnp.where(core == 0, low, high).astype(BF16)
    send_ref[:, place] = jnp.where(core == 0, high, low).astype(BF16)


def product_body(rows, me_ref, a_ref, b_ref, keep_ref, send_ref):
    deal(me_ref, matmul_left(a_ref[...], b_ref[...]), rows, keep_ref, send_ref)


def product(net, me, left, right, tile=1024):
    tokens, width = left.shape
    columns = right.shape[1]
    rows = width // net.n
    shape = (net.n // 2, rows, columns)
    block = pl.BlockSpec((tile // (2 * rows), rows, columns), lambda i: (i, 0, 0))
    return call(
        functools.partial(product_body, rows),
        "product",
        (width // tile,),
        [
            (me.reshape(1), SMEM_SPEC),
            (left, pl.BlockSpec((tokens, tile), lambda i: (0, i))),
            (right, full_spec((tokens, columns))),
        ],
        [(shape, BF16, block), (shape, BF16, block)],
        [],
        15,
    )


def inner_body(rows, me_ref, context_ref, first_ref, gm_ref, gi_ref, keep_ref, send_ref):
    total = matmul_left(first_ref[...], gi_ref[...])
    width = gm_ref.shape[1]
    deal(me_ref, matmul_left(context_ref[...], gm_ref[...]), rows, keep_ref, send_ref, 0)
    for k in range(total.shape[1] // width):
        part = total[:, k * width : (k + 1) * width]
        deal(me_ref, part, rows, keep_ref, send_ref, k + 1)


def inner_product(net, me, context, first_low, gm_low, gi, tile=256):
    tokens, width = context.shape
    hidden = gi.shape[1]
    rows = width // net.n
    kinds = 1 + hidden // width
    shape = (net.n // 2, kinds * rows, width)
    block = pl.BlockSpec((tile // (2 * rows), kinds * rows, width), lambda i: (i, 0, 0))
    left = pl.BlockSpec((tokens, tile), lambda i: (0, i))
    return call(
        functools.partial(inner_body, rows),
        "inner_product",
        (width // tile,),
        [
            (me.reshape(1), SMEM_SPEC),
            (context, left),
            (first_low, left),
            (gm_low, full_spec((tokens, width))),
            (gi, full_spec((tokens, hidden))),
        ],
        [(shape, BF16, block), (shape, BF16, block)],
        [],
        18,
    )


def triple_body(rows, me_ref, lines_ref, a_ref, q_ref, k_ref, v_ref, keep_ref, send_ref):
    for w, ref in enumerate((q_ref, k_ref, v_ref)):
        deal(me_ref, matmul_left(a_ref[...], ref[...]), rows, keep_ref, send_ref, w)
    core = me_ref[0] & 1
    low, high = lines_ref[:, 0:1], lines_ref[:, 1:2]
    place, shape = slice(3 * rows, 3 * rows + 16), (low.shape[0], 16, low.shape[2])
    keep_ref[:, place] = jnp.broadcast_to(jnp.where(core == 0, low, high), shape).astype(BF16)
    send_ref[:, place] = jnp.broadcast_to(jnp.where(core == 0, high, low), shape).astype(BF16)


def triple_product(net, me, lines, left, gq, gk, gv, tile=256):
    tokens, width = left.shape
    rows = width // net.n
    shape = (net.n // 2, 3 * rows + 16, width)
    chips = tile // (2 * rows)
    block = pl.BlockSpec((chips, 3 * rows + 16, width), lambda i: (i, 0, 0))
    full = full_spec((tokens, width))
    return call(
        functools.partial(triple_body, rows),
        "triple_product",
        (width // tile,),
        [
            (me.reshape(1), SMEM_SPEC),
            (lines, pl.BlockSpec((chips, 2, width), lambda i: (i, 0, 0))),
            (left, pl.BlockSpec((tokens, tile), lambda i: (0, i))),
            (gq, full),
            (gk, full),
            (gv, full),
        ],
        [(shape, BF16, block), (shape, BF16, block)],
        [],
        13,
    )


def stream_back_body(weights, rows, me_ref, *refs):
    count = len(weights.arrays)
    arrays, refs = refs[:count], refs[count:]
    gm_ref, gq_ref, gk_ref, gv_ref = refs[:4]
    sum_refs, refs = refs[4 : 4 + rows], refs[4 + rows :]
    out_ref, outs = refs[0], refs[1:]
    qw, kw, vw, sems = outs[-4:]
    me, step = me_ref[0], pl.program_id(0)

    @pl.when(step == 0)
    def _():
        for w, held in enumerate((qw, kw, vw)):
            weights.start(w, me, arrays, held, sems)
        for w, held in enumerate((qw, kw, vw)):
            weights.wait(w, me, arrays, held, sems)
        if sum_refs:
            total = sum_refs[0][...]
            for w, held in enumerate((qw, kw, vw)):
                lines = [ref[w : w + 1] for ref in sum_refs[1:]]
                lines += [jnp.zeros_like(lines[0])] * (8 - len(lines))
                total += matmul_right(jnp.concatenate(lines).astype(BF16), flat(held[...]))
            outs[0][...] = total

    out_ref[...] = (
        gm_ref[...]
        + matmul_right(gq_ref[...], flat(qw[...]))
        + matmul_right(gk_ref[...], flat(kw[...]))
        + matmul_right(gv_ref[...], flat(vw[...]))
    )


def stream_back(net, me, flow, gm, gq, gk, gv, row, row_length, base=None, sums=(), tile=256):
    tokens, width = gm.shape
    tile = min(tile, row_length)
    r = width // net.n
    weights = Weights(net, me, [(flow, w * r, r) for w in (1, 2, 3)])
    start = row * (row_length // tile)
    tiled = pl.BlockSpec((tile, width), lambda i: (start + i, 0))
    ins = (
        [(me.reshape(1), SMEM_SPEC)]
        + [(array, ANY_SPEC) for array in weights.arrays]
        + [(array, tiled) for array in (gm, gq, gk, gv)]
        + [(array, full_spec((8, width))) for array in sums]
    )
    outs = [((tokens, width), F32, tiled)]
    if sums:
        outs.append(((8, width), F32, full_spec((8, width))))
    return call(
        functools.partial(stream_back_body, weights, len(sums)),
        "stream_back",
        (row_length // tile,),
        ins,
        outs,
        weights.scratch(),
        10,
        () if base is None else (base,),
    )


def in_order(net, me, sources, blocks):
    order = jnp.asarray(sources, jnp.int32)
    spot = jnp.zeros((net.n,), jnp.int32).at[order].set(jnp.arange(net.n, dtype=jnp.int32))
    return blocks[spot[jnp.arange(net.n) ^ me]]


def held(state, others):
    return after(state[0], others), state[1]


def stream_ends(state, unit, sizes):
    if not state.plain:
        total = state.net.scatter_end(state.state)
        found, start = [total[w * unit : (w + 1) * unit] for w in range(3)], 0
        for size in sizes:
            found.append(total[3 * unit, start : start + size])
            start += size
        return found
    rows, columns = state.rows, state.columns
    step_block = ((1, rows, columns), lambda i, at: (at, 0, 0))
    ins = state.sources(0, step_block)
    ins += [(term, step_block[0], lambda i, me: (0, 0, 0)) for term in state.terms[4:]]
    shapes = [(unit, columns)] * 3 + [(1, size) for size in sizes]
    outs = [(shape, F32, shape, lambda i, me: (0, 0)) for shape in shapes]

    def body(me_ref, *refs):
        total = refs[0][0].astype(F32)
        for ref in refs[1 : len(ins)]:
            total = total + ref[0].astype(F32)
        outs = refs[len(ins) :]
        for w in range(3):
            outs[w][...] = total[w * unit : (w + 1) * unit]
        start = 0
        for out_ref, size in zip(outs[3:], sizes):
            out_ref[...] = total[3 * unit : 3 * unit + 1, start : start + size]
            start += size

    results = sum_call(state.me, "stream_end", 1, ins, None, outs, body)
    return list(results[:3]) + [result[0] for result in results[3:]]


def on_device(
    net,
    inputs,
    timesteps,
    segments,
    cotangent,
    query_weight,
    key_weight,
    value_weight,
    output_weight,
    inner_weight,
    outer_weight,
    time_weight,
    *vectors,
):
    n = net.n
    me = lax.axis_index("fsdp").astype(jnp.int32)
    batch_count, row_count, row_length, model_width = inputs.shape
    rows = batch_count * row_count
    tokens = rows * row_length
    feats = features(timesteps.reshape(rows)).astype(BF16)
    order = (0, 1, 2, 4, 5, 6, 7, 8, 3)
    sizes = [vectors[i].shape[0] for i in order]
    r = model_width // n

    shards = (time_weight, query_weight, key_weight, value_weight)
    lines = [vectors[i] for i in order[:8]]
    far = net.gather_far(pack(me, shards, lines, vectors[3], timesteps.reshape(rows)))
    hidden = inner_weight.shape[1]
    inner_blocks = [
        inner_weight[:, start : start + model_width] for start in range(0, hidden, model_width)
    ]
    shard_io = after(jnp.concatenate([output_weight] + inner_blocks), far)
    far_io = net.gather_far(shard_io)
    far = net.stacked(far, me)
    near = net.gather_near(far)
    pieces, corners, _ = net.gather_corner(far, near)
    flow = net.gather_core(pieces)
    far_io, corners, shard_u = after((net.stacked(far_io, me), corners, outer_weight), ())
    near_io = net.gather_near(far_io)
    flow += net.gather_core(corners)
    far_u = net.gather_far(after(shard_u, flow))

    segments = segments.reshape(rows, row_length)
    x = inputs.reshape(tokens, model_width)
    feats_in = after(feats, far_io)
    temb, lines, stream_low, queries, key_rows, values = project(
        net, me, flow, feats_in, x, row_length
    )
    far_u = net.stacked(after(far_u, queries), me)
    near_u = net.gather_near(far_u)
    near_io, queries = after((near_io, queries), far_u)
    pieces, corners, sent = net.gather_corner(far_io, near_io)
    queries = after(queries, sent)
    context, log_total = attend(queries, key_rows, values, segments)
    near_u, context, pieces = after((near_u, context, pieces), ())
    flow_io = net.gather_core(pieces)
    pieces, corners_u, sent = net.gather_corner(far_u, near_u)
    context, corners = after((context, corners), sent)
    flow_io += net.gather_core(corners)
    corners = corners_u
    first_low, normed_first, spread_first, active_low, slope = ffn_in(
        net, me, flow_io, context, x, temb, lines, hidden, row_length
    )
    corners, active_low = after((corners, active_low), ())
    flow_u = net.gather_core(pieces) + net.gather_core(corners)
    (
        layer_output,
        grad_second,
        grad_second_low,
        sums_out,
    ) = ffn_out(
        net,
        me,
        flow_u,
        active_low,
        normed_first,
        cotangent.reshape(tokens, model_width),
        (lines,),
    )
    outer_halves = product(net, me, active_low, grad_second_low)
    outer_sum = Reduction(net, me, *outer_halves)
    slope = after(slope, outer_halves)
    (
        grad_inner_low,
        grad_mixed,
        grad_mixed_low,
        grad_context,
        inner_bias_grad,
        sums_back,
        mixed_rows,
    ) = ffn_back(
        net,
        me,
        flow_u,
        flow_io,
        grad_second,
        grad_second_low,
        slope,
        normed_first,
        spread_first,
        lines,
        row_length,
    )
    sent = outer_sum.hold(grad_mixed_low).corner()
    grad_mixed_low = after(grad_mixed_low, sent)
    inner_halves = inner_product(net, me, context, first_low, grad_mixed_low, grad_inner_low)
    inner_sum = Reduction(net, me, *inner_halves)
    sent = outer_sum.hold(inner_halves).near()
    grad_context = after(grad_context, (inner_halves, sent))
    back = (queries, key_rows, values, segments, log_total, grad_context)
    found, sums_rows, row_sums = None, 0.0, [mixed_rows]
    for row in range(rows):
        if row == 1:
            sent = list(inner_sum.hold(found[1]).corner())
            sent += list(outer_sum.hold((found[1], sent)).far())
            found = after(found, sent)
        found = attend_back(*back, row, found or ())
        sums_rows += found[3]
        row_sums.append(found[4])
        found = found[:3]
    grad_queries, grad_keys, grad_values = found
    sent = inner_sum.hold(grad_queries).near()
    outer_sum.hold(grad_queries)
    sums = sums_rows + sums_out + sums_back
    sums = sums.reshape(8, n, r).transpose(1, 0, 2).reshape(n, 8 * r)
    sums = jnp.concatenate([sums, inner_bias_grad.reshape(n, -1)], axis=1)
    sums = jnp.pad(sums, ((0, 0), (0, model_width - sums.shape[1])))
    sums = sums.reshape(n // 2, 2, model_width)
    stream_low, sums = after((stream_low, sums), (sent, outer_sum.received()))
    stream_halves = triple_product(
        net, me, sums, stream_low, grad_queries, grad_keys, grad_values
    )
    stream_sum = Reduction(net, me, *stream_halves)
    grad_mixed = after(grad_mixed, stream_halves)
    back = (flow, grad_mixed, grad_queries, grad_keys, grad_values)
    grad_stream, grad_temb = stream_back(net, me, *back, 0, row_length, sums=row_sums)
    ends = grad_temb[:rows][None]
    sources, ends = net.gather_round([0], ends, net.masks(net.core))
    sent = list(stream_sum.hold(grad_temb).corner())
    sent += list(inner_sum.hold((grad_temb, sent)).far())
    ends = after(ends, sent)
    sent = stream_sum.hold(sent).near()
    grad_stream = after(grad_stream, sent)
    for row in range(1, rows):
        (grad_stream,) = stream_back(net, me, *back, row, row_length, grad_stream)
    inner_sum.hold(grad_stream), outer_sum.hold(grad_stream)
    sent = stream_sum.hold(grad_stream).far()
    ends = after(ends, (sent, inner_sum.received()))
    sources, ends = net.gather_round(sources, ends, net.masks(net.near))
    inner_sum.hold(sent), outer_sum.hold(sent)
    output_weight_grad, inner_weight_grad = inner_sum.end([1, hidden // model_width], r)
    (outer_weight_grad,) = outer_sum.end([1], outer_weight.shape[0])
    sources, ends = net.gather_round(sources, ends, net.masks(net.middle))
    others = (stream_sum.received(), inner_weight_grad, outer_weight_grad)
    sources, ends = net.gather_round(sources, after(ends, others), net.masks(net.outer))
    temb_all = in_order(net, me, sources, ends).reshape(n * rows, model_width)
    query_weight_grad, key_weight_grad, value_weight_grad, *parts = stream_ends(
        stream_sum, r, sizes
    )
    own = model_width // n
    steps_all = after(lines, grad_stream)
    steps_all = (steps_all[12] * 64.0 + steps_all[13])[: n * rows]
    feats_own = own_features(steps_all, me * own, own).astype(BF16).astype(F32)
    time_weight_grad = lax.dot_general(
        feats_own,
        temb_all,
        (((0,), (0,)), ((), ())),
        precision=lax.Precision.HIGHEST,
    )
    parts = dict(zip(order, parts))
    vector_outs = [parts[i] for i in range(len(order))]

    shape = inputs.shape
    return (
        layer_output.reshape(shape),
        grad_stream.reshape(shape),
        query_weight_grad,
        key_weight_grad,
        value_weight_grad,
        output_weight_grad,
        inner_weight_grad,
        outer_weight_grad,
        time_weight_grad,
    ) + tuple(vector_outs)


def solution(mesh):
    matrix, vector = P("fsdp", None), P("fsdp")
    batch = P(None, "fsdp", None, None)
    return jax.shard_map(
        functools.partial(on_device, Net(mesh.shape["fsdp"])),
        mesh=mesh,
        in_specs=(batch, P(None, "fsdp"), P(None, "fsdp", None), batch)
        + (matrix,) * 7
        + (vector,) * 9,
        out_specs=(batch, batch) + (matrix,) * 7 + (vector,) * 9,
        check_vma=False,
    )
```
